32 devices in a mesh: head: 4 (over z), blk: 8 (over y, x, core).
Axes of the slice: x: 2, y: 2, z: 4, core: 2. Of those that a mesh axis runs over, the one named last changes fastest.
Arguments:
- inputs: bfloat16 [4096, 768], P(('head', 'blk')), may hold values from -6 to 6
- cotangent: bfloat16 [4096, 768], P(('head', 'blk')), may hold values from -6 to 6
- segment: int32 [4096], P(('head', 'blk')), may hold values from 0 to 3, as said below
- position: int32 [4096], P(('head', 'blk')), may hold values from 0 to 1023, as said below
- routes: int32 [4096, 2], P(('head', 'blk')), may hold values from 0 to 11, all different within a row; in each aligned block of 128 rows (0 to 127, 128 to 255, ...) at most 24 rows name the same one
- gate_residual: float32 [4096, 12], P(('head', 'blk')), may hold values from -1.8 to 1.8
- first_gain: bfloat16 [768], P(('head', 'blk')), may hold values from 0.5 to 1.5
- second_gain: bfloat16 [768], P(('head', 'blk')), may hold values from 0.5 to 1.5
- query_key_weight: bfloat16 [768, 1536], P(('head', 'blk')), may hold values from -0.3125 to 0.3125
- value_weight: bfloat16 [768, 768], P(('head', 'blk')), may hold values from -0.21875 to 0.21875
- output_weight: bfloat16 [768, 768], P(('head', 'blk')), may hold values from -2.5 to 2.5
- router_weight: bfloat16 [768, 12], P(('head', 'blk')), may hold values from -0.15625 to 0.15625
- const_gate: bfloat16 [768, 4], P(('head', 'blk')), may hold values from -0.21875 to 0.21875
- const_vectors: bfloat16 [768, 2], P(('head', 'blk')), may hold values from -6 to 6
- gate_weight: bfloat16 [768, 16384], P('head', 'blk'), may hold values from -0.21875 to 0.21875
- up_weight: bfloat16 [768, 16384], P('head', 'blk'), may hold values from -0.21875 to 0.21875
- down_weight: bfloat16 [16384, 768], P('blk', 'head'), may hold values from -0.1875 to 0.1875
Outputs:
- layer_out: bfloat16 [4096, 768], P(('head', 'blk'))
- grad_input: float32 [4096, 768], P(('head', 'blk'))
- grad_residual: float32 [4096, 12], P(('head', 'blk'))
- grad_first_gain: float32 [768], P(('head', 'blk'))
- grad_second_gain: float32 [768], P(('head', 'blk'))
- grad_query_key: float32 [768, 1536], P(('head', 'blk'))
- grad_value: float32 [768, 768], P(('head', 'blk'))
- grad_output: float32 [768, 768], P(('head', 'blk'))
- grad_router: float32 [768, 12], P(('head', 'blk'))
- grad_const_gate: float32 [768, 4], P(('head', 'blk'))
- grad_const_vectors: float32 [768, 2], P(('head', 'blk'))
- grad_gate: float32 [768, 16384], P('head', 'blk')
- grad_up: float32 [768, 16384], P('head', 'blk')
- grad_down: float32 [16384, 768], P('blk', 'head')
The draws below stay inside these ranges and needn't reach their ends.
Inputs may be any that keep to these rules, and one draw needn't show every extreme that they name: `segment`: for g from 0 to 1, g * 2 marks the 1024 tokens of group g's prompt and g * 2 + 1 to g * 2 + 1 its continuations of 1024 tokens each; the 128 tokens of one device belong to one sequence; every index of blk holds one device's block of every group's prompt. `position`: every prompt's tokens hold positions 0 to 1023 once each and every continuation's tokens positions 0 to 1023 once each; the tokens of one device are consecutive positions in order. `routes`: each row names two different experts; among the 128 rows of one device no expert is named more than 24 times.
All inputs are finite; a program needn't handle non-finite values.
Results may differ from the reference program's by a relative error of at most 0.02.
Values may be sent and summed in bfloat16 or wider, within the bound.
A program may use at most 320 MiB of HBM per device.

```python
import math
from functools import partial
import jax
import jax.numpy as jnp
import numpy as np
from jax import lax

D = 768
HEADS = 12
HEAD_DIM = 64
FF = 2048
EXPERTS = 8
ROUTED = 12
TOP = 2
TOK_DEV = 128
CONT_LEN = 1024
TOKENS = 4096
PROMPT = 1024
CONTS = 1
PERIOD = 2
GROUPS = 2
CAP = 24
DEVICES = 32


def layout_numbers(key):
    block_count = PROMPT // TOK_DEV
    row_count = TOKENS // PROMPT
    group_count = row_count // 2
    key_rows, key_prompt, key_rest = jax.random.split(key, 3)
    row_order = jax.vmap(lambda sub_key: jax.random.permutation(sub_key, row_count))(jax.random.split(key_rows, block_count))
    row_place = jnp.argsort(row_order, axis=1).astype(jnp.int32)
    prompt_order = jax.vmap(lambda sub_key: jax.random.permutation(sub_key, block_count))(jax.random.split(key_prompt, group_count))
    rest_order = jax.random.permutation(key_rest, block_count * group_count)
    device = jnp.arange(block_count * row_count, dtype=jnp.int32)
    row_index = device // block_count
    column = device % block_count
    device_place = row_place[column, row_index]
    holder = (device_place < group_count).astype(jnp.int32)
    rest_flag = 1 - holder
    earlier = jnp.cumsum(rest_flag) - rest_flag
    others = jnp.clip(earlier, 0, block_count * group_count - 1)
    prompt_group = jnp.clip(device_place, 0, group_count - 1)
    prompt_unit = prompt_group * 2 * block_count + prompt_order[prompt_group, column]
    rest_pick = rest_order[others]
    rest_unit = rest_pick // block_count * 2 * block_count + block_count + rest_pick % block_count
    unit_index = jnp.where(holder == 1, prompt_unit, rest_unit)
    natural = (unit_index[:, None] * TOK_DEV + jnp.arange(TOK_DEV, dtype=jnp.int32)[None, :]).reshape(-1)
    group_of = natural // (2 * PROMPT)
    offset_in = natural % (2 * PROMPT)
    segment = group_of * (CONTS + 1) + jnp.where(offset_in < PROMPT, 0, 1 + (offset_in - PROMPT) // CONT_LEN)
    place = jnp.where(offset_in < PROMPT, offset_in, (offset_in - PROMPT) % CONT_LEN)
    return (segment.astype(jnp.int32), place.astype(jnp.int32))


def draw_segment(key, part):
    segment, place = layout_numbers(key)
    return segment


def draw_position(key, part):
    segment, place = layout_numbers(key)
    return place


def steps_of(rng, extent, cuts, low, high):
    def one(dim, shards_of):
        heights = jax.random.uniform(jax.random.fold_in(jax.random.fold_in(rng, 6), dim), (shards_of,), jnp.float32, low / len(cuts), high / len(cuts))
        return jnp.repeat(jnp.exp(heights), extent[dim] // shards_of).reshape((-1,) + (1,) * (len(extent) - dim - 1))

    level = one(*cuts[0])
    for cut in cuts[1:]:
        level = level * one(*cut)
    return level


def routed_block(rng, own, number, rows, amount, top, bound, skew):
    order = jax.random.permutation(rng, amount)
    crowded, ordinary = shares(amount, rows * top, bound, skew, True), shares(amount, rows * top, bound, skew, False)
    places = jnp.arange(amount)

    def named(sizes, offset_by):
        used = int((sizes > 0).sum())
        fixed = max(1, used // 4)
        moved = fixed + (places - fixed + offset_by * (used - fixed)) % max(1, amount - fixed)
        return jnp.zeros((amount,), jnp.int32).at[order[jnp.where(places < fixed, places, moved)]].set(jnp.asarray(sizes, jnp.int32))

    sizes = jnp.where(number % 4 == 0, named(crowded, number // 4), named(ordinary, number - number // 4 - 1))
    mixed = jax.random.permutation(jax.random.fold_in(own, 3), amount)
    source_of, sink = mixed[0:amount // 2 * 2:2], mixed[1:amount // 2 * 2:2]
    margin = jnp.minimum(sizes[source_of] - 1, bound - sizes[sink]) // 2
    margin = jnp.where((source_of == order[0]) | (sink == order[0]) | (sizes[sink] == 0), 0, jnp.maximum(margin, 0))
    moved = jax.random.randint(jax.random.fold_in(own, 4), (amount // 2,), 0, 1 << 20) % (margin + 1)
    sizes = sizes.at[source_of].add(-moved).at[sink].add(moved)
    members = jnp.searchsorted(jnp.cumsum(sizes), jnp.arange(rows * top), side="right").astype(jnp.int32)
    table = members.reshape(top, rows).T
    table = table[jax.random.permutation(jax.random.fold_in(own, 1), rows)]
    offset_by = jax.random.randint(jax.random.fold_in(own, 2), (rows, 1), 0, top)
    return jnp.take_along_axis(table, (jnp.arange(top)[None, :] + offset_by) % top, axis=1)


def shares(number_of, total, bound, skew, full):
    weights = [(1 << 20) // math.isqrt(grade ** skew) + 1 for grade in range(1, number_of + 1)]
    largest = bound if full else min(bound, max(-(-total // number_of), total * weights[0] // sum(weights)))
    least = 1 if total - largest >= number_of - 1 else 0
    holding, spare = [largest] + [least] * (number_of - 1), total - largest - least * (number_of - 1)
    while spare > 0:
        movable = [i for i in range(1, number_of) if holding[i] < largest] or [i for i in range(1, number_of) if holding[i] < bound]
        whole, remaining = sum([weights[i] for i in movable]), spare
        for i in movable:
            addition = min(bound - holding[i], max(1, remaining * weights[i] // whole), spare)
            holding[i] = holding[i] + addition
            spare = spare - addition
    return np.array(holding)


def normal_values(stream_key, extent, spread, limit, cuts=(), kind=jnp.bfloat16):
    values = spread * jax.random.normal(stream_key, extent, jnp.float32)
    if cuts:
        values = values * steps_of(stream_key, extent, cuts, -0.22, 0.18)
    return jnp.clip(values, -limit, limit).astype(kind)


def setup_inputs(seed: int = 0) -> dict:
    streams_of = jax.random.split(jax.random.key(seed), 18)
    inputs = normal_values(streams_of[0], (TOKENS, D), 1.0, 6.0, ((0, 32),))
    cotangent = normal_values(streams_of[1], (TOKENS, D), 1.0, 6.0, ((0, 32),))
    segment = draw_segment(jax.random.fold_in(streams_of[17], 71), 0)
    position = draw_position(jax.random.fold_in(streams_of[17], 71), 0)
    routes_keys = jax.random.split(jax.random.fold_in(streams_of[4], 1), TOKENS // TOK_DEV)
    routes_turns = jax.random.permutation(jax.random.fold_in(streams_of[4], 3), TOKENS // TOK_DEV)
    routes = jax.vmap(lambda own, number: routed_block(jax.random.fold_in(streams_of[4], 2), own, number, TOK_DEV, ROUTED, TOP, CAP, 1))(routes_keys, routes_turns).reshape((TOKENS, TOP))
    gate_residual = normal_values(streams_of[5], (TOKENS, ROUTED), 0.3, 1.8, ((0, 32),), jnp.float32)
    first_gain = jnp.clip(1.0 + 0.1 * jax.random.normal(streams_of[6], (D,), jnp.float32), 0.5, 1.5).astype(jnp.bfloat16)
    second_gain = jnp.clip(1.0 + 0.1 * jax.random.normal(streams_of[7], (D,), jnp.float32), 0.5, 1.5).astype(jnp.bfloat16)
    query_key_weight = normal_values(streams_of[8], (D, 2 * D), (D // 2) ** -0.5, 0.3125, ((0, 32),))
    value_weight = normal_values(streams_of[9], (D, D), D ** -0.5, 0.21875, ((0, 32),))
    output_weight = normal_values(streams_of[10], (D, D), (D // 128) ** -0.5, 2.5, ((0, 32),))
    router_weight = normal_values(streams_of[11], (D, ROUTED), (2 * D) ** -0.5, 0.15625, ((0, 32),))
    const_gate = normal_values(streams_of[12], (D, 4), D ** -0.5, 0.21875, ((0, 32),))
    const_vectors = normal_values(streams_of[13], (D, 2), 1.0, 6.0, ((0, 32),))
    gate_weight = normal_values(streams_of[14], (D, EXPERTS * FF), D ** -0.5, 0.21875, ((0, 4), (1, 8)))
    up_weight = normal_values(streams_of[15], (D, EXPERTS * FF), D ** -0.5, 0.21875, ((0, 4), (1, 8)))
    down_weight = normal_values(streams_of[16], (EXPERTS * FF, D), (FF // 2) ** -0.5, 0.1875, ((0, 8), (1, 4)))
    return dict(inputs=inputs, cotangent=cotangent, segment=segment, position=position, routes=routes, gate_residual=gate_residual, first_gain=first_gain, second_gain=second_gain, query_key_weight=query_key_weight, value_weight=value_weight, output_weight=output_weight, router_weight=router_weight, const_gate=const_gate, const_vectors=const_vectors, gate_weight=gate_weight, up_weight=up_weight, down_weight=down_weight)


EPS = 1e-06
HIGH = lax.Precision.HIGHEST

@jax.custom_vjp
def low(v):
    return lax.optimization_barrier(v.astype(jnp.bfloat16)).astype(jnp.float32)

@jax.custom_vjp
def low_back(v):
    return v

def low_keep(v):
    return (low(v), None)

def low_pass(kept, grad):
    return (grad,)

def back_keep(v):
    return (v, None)

def back_low(kept, grad):
    return (low(grad),)
low.defvjp(low_keep, low_pass)
low_back.defvjp(back_keep, back_low)

def rms_norm(values, gain):
    return values * lax.rsqrt(lax.optimization_barrier(jnp.mean(values * values, axis=-1, keepdims=True)) + EPS) * gain

def softmax_rows(scores):
    highest = lax.optimization_barrier(jnp.max(scores, axis=-1, keepdims=True))
    raised = jnp.exp(scores - highest)
    return raised / lax.optimization_barrier(jnp.sum(raised, axis=-1, keepdims=True))

def attend(queries, key_rows, value_rows, visible):
    scores = jnp.einsum('qhd,khd->hqk', queries, key_rows, precision=HIGH) * HEAD_DIM ** (-0.5)
    scores = low_back(jnp.where(visible[None], scores, -jnp.inf))
    weights = low(softmax_rows(scores))
    return jnp.einsum('hqk,khd->qhd', weights, value_rows, precision=HIGH)

def prompt_attention(queries, key_rows, value_rows):
    block_size = math.gcd(PROMPT, 512)
    block_count = PROMPT // block_size
    query_blocks = queries.reshape(block_count, block_size, HEADS, HEAD_DIM)
    first_rows = jnp.arange(block_count, dtype=jnp.int32) * block_size
    key_index = jnp.arange(PROMPT, dtype=jnp.int32)

    def one_block(operands):
        block, first_row = operands
        query_index = first_row + jnp.arange(block_size, dtype=jnp.int32)
        return attend(block, key_rows, value_rows, key_index[None, :] <= query_index[:, None])
    return lax.map(jax.checkpoint(one_block), (query_blocks, first_rows)).reshape(PROMPT, HEADS, HEAD_DIM)

def continuation_attention(queries, key_rows, value_rows, prompt_keys, prompt_values):
    local_index = jnp.arange(CONT_LEN, dtype=jnp.int32)
    visible = jnp.concatenate([jnp.ones((CONT_LEN, PROMPT), jnp.bool_), local_index[None, :] <= local_index[:, None]], axis=1)

    def one_sequence(operands):
        block, own_keys, own_values = operands
        return attend(block, jnp.concatenate([prompt_keys, own_keys], 0), jnp.concatenate([prompt_values, own_values], 0), visible)
    return lax.map(jax.checkpoint(one_sequence), (queries, key_rows, value_rows))

def run_expert(operands):
    slot_rows, gate_part, up_part, down_part = operands
    gate_pre = low_back(jnp.dot(slot_rows, gate_part, precision=HIGH))
    up_pre = low_back(jnp.dot(slot_rows, up_part, precision=HIGH))
    hidden = low(jax.nn.silu(gate_pre) * up_pre)
    return low_back(jnp.dot(hidden, down_part, precision=HIGH))

def layer(segment, position, routes, inputs, first_gain, second_gain, query_key_weight, value_weight, output_weight, router_weight, const_gate, const_vectors, gate_weight, up_weight, down_weight, gate_residual):
    normed_one = low(rms_norm(inputs, first_gain))
    joined = jnp.dot(normed_one, query_key_weight, precision=HIGH)
    queries = low_back(low(joined[:, :D])).reshape(TOKENS, HEADS, HEAD_DIM)
    key_rows = low_back(low(joined[:, D:])).reshape(TOKENS, HEADS, HEAD_DIM)
    value_rows = low_back(low(jnp.dot(normed_one, value_weight, precision=HIGH))).reshape(TOKENS, HEADS, HEAD_DIM)
    period = PERIOD
    group_of = (segment // period).astype(jnp.int32)
    within = (segment % period).astype(jnp.int32)
    natural = (group_of * (2 * PROMPT) + jnp.where(within == 0, position, PROMPT + (within - 1) * CONT_LEN + position)).astype(jnp.int32)
    inverse = jnp.zeros((TOKENS,), jnp.int32).at[natural].set(jnp.arange(TOKENS, dtype=jnp.int32))
    queries_nat = queries[inverse]
    keys_nat = key_rows[inverse]
    values_nat = value_rows[inverse]
    cont_shape = (CONTS, CONT_LEN, HEADS, HEAD_DIM)
    outputs = []
    for group_index in range(GROUPS):
        base = group_index * 2 * PROMPT
        group_queries = queries_nat[base:base + 2 * PROMPT]
        group_keys = keys_nat[base:base + 2 * PROMPT]
        group_values = values_nat[base:base + 2 * PROMPT]
        prompt_out = prompt_attention(group_queries[:PROMPT], group_keys[:PROMPT], group_values[:PROMPT])
        cont_out = continuation_attention(group_queries[PROMPT:].reshape(cont_shape), group_keys[PROMPT:].reshape(cont_shape), group_values[PROMPT:].reshape(cont_shape), group_keys[:PROMPT], group_values[:PROMPT])
        outputs.append(prompt_out)
        outputs.append(cont_out.reshape(PROMPT, HEADS, HEAD_DIM))
    attended = jnp.concatenate(outputs, 0)[natural]
    attended = low_back(low(attended.reshape(TOKENS, D)))
    middle = inputs + low_back(jnp.dot(attended, output_weight, precision=HIGH))
    normed_two = low(rms_norm(middle, second_gain))
    logits = jnp.dot(normed_two, router_weight, precision=HIGH) + gate_residual
    choose = (routes[:, :, None] == jnp.arange(ROUTED, dtype=jnp.int32)[None, None, :]).astype(jnp.float32)
    picked = lax.optimization_barrier(jnp.sum(choose * logits[:, None, :], axis=-1))
    weighting = softmax_rows(picked)
    pair_expert = routes.reshape(DEVICES, TOK_DEV * TOP)
    ffn_onehot = (pair_expert[:, :, None] == jnp.arange(EXPERTS, dtype=jnp.int32)[None, None, :]).astype(jnp.int32)
    pair_rank = lax.optimization_barrier(jnp.sum((jnp.cumsum(ffn_onehot, axis=1) - ffn_onehot) * ffn_onehot, axis=-1)).astype(jnp.int32)
    is_ffn = pair_expert < EXPERTS
    device_ids = jnp.broadcast_to(jnp.arange(DEVICES, dtype=jnp.int32)[:, None], pair_expert.shape)
    token_ids = device_ids * TOK_DEV + jnp.arange(TOK_DEV * TOP, dtype=jnp.int32)[None, :] // TOP
    target = jnp.where(is_ffn, pair_expert, EXPERTS).astype(jnp.int32)
    slot_token = jnp.zeros((DEVICES, EXPERTS, CAP), jnp.int32).at[device_ids, target, pair_rank].set(token_ids, mode='drop')
    slot_live = jnp.zeros((DEVICES, EXPERTS, CAP), jnp.float32).at[device_ids, target, pair_rank].set(1.0, mode='drop')
    slot_rows = normed_two[slot_token] * slot_live[..., None]
    slot_rows = slot_rows.transpose(1, 0, 2, 3).reshape(EXPERTS, DEVICES * CAP, D)
    gate_parts = gate_weight.reshape(D, EXPERTS, FF).transpose(1, 0, 2)
    up_parts = up_weight.reshape(D, EXPERTS, FF).transpose(1, 0, 2)
    down_parts = down_weight.reshape(EXPERTS, FF, D)
    expert_out = lax.map(jax.checkpoint(run_expert), (slot_rows, gate_parts, up_parts, down_parts))
    expert_out = expert_out.reshape(EXPERTS, DEVICES, CAP, D)
    safe_expert = jnp.where(is_ffn, pair_expert, 0).astype(jnp.int32)
    safe_rank = jnp.where(is_ffn, pair_rank, 0).astype(jnp.int32)
    pair_out = expert_out[safe_expert, device_ids, safe_rank] * is_ffn[..., None].astype(jnp.float32)
    pair_out = pair_out.reshape(TOKENS, TOP, D)
    mixing = softmax_rows(jnp.dot(normed_two, const_gate, precision=HIGH).reshape(TOKENS, 2, 2))
    special = (routes == EXPERTS + 1).astype(jnp.float32)[..., None] * normed_two[:, None, :]
    for const_index in range(2):
        const_out = mixing[:, const_index, 0:1] * normed_two + mixing[:, const_index, 1:2] * const_vectors[:, const_index][None, :]
        special = special + (routes == EXPERTS + 2 + const_index).astype(jnp.float32)[..., None] * const_out[:, None, :]
    mixture = lax.optimization_barrier(jnp.sum(weighting[..., None] * (pair_out + special), axis=1))
    return middle + mixture

def reference(inputs, cotangent, segment, position, routes, gate_residual, first_gain, second_gain, query_key_weight, value_weight, output_weight, router_weight, const_gate, const_vectors, gate_weight, up_weight, down_weight):
    primals = tuple((array.astype(jnp.float32) for array in (inputs, first_gain, second_gain, query_key_weight, value_weight, output_weight, router_weight, const_gate, const_vectors, gate_weight, up_weight, down_weight, gate_residual)))
    result, pullback = jax.vjp(partial(layer, segment, position, routes), *primals)
    grads_all = pullback(cotangent.astype(jnp.float32))
    return (result.astype(jnp.bfloat16), grads_all[0], grads_all[12], grads_all[1], grads_all[2], grads_all[3], grads_all[4], grads_all[5], grads_all[6], grads_all[7], grads_all[8], grads_all[9], grads_all[10], grads_all[11])
```

```python
import functools

import jax
import jax.numpy as jnp
from jax import lax
from jax.experimental import pallas as pl
from jax.experimental.pallas import tpu as pltpu
from jax.sharding import PartitionSpec as P

HEADS = 12
HEAD_DIM = 64
EXPERTS = 8
ROUTED = 12
TOP = 2
CONT_LEN = 1024
CAP = 24


EPS = 1e-06
HIGH = lax.Precision.HIGHEST


def silu_slope(pre):
    sigmoid_value = jax.nn.sigmoid(pre)
    return sigmoid_value * (1.0 + pre * (1.0 - sigmoid_value))


def visible_pairs(query_segment, query_position, key_segment, key_position, period):
    same_sequence = (query_segment[:, None] == key_segment[None, :]) & (
        key_position[None, :] <= query_position[:, None]
    )
    same_group = query_segment[:, None] // period == key_segment[None, :] // period
    shared = (
        (key_segment[None, :] % period == 0) & (query_segment[:, None] % period != 0) & same_group
    )
    return same_sequence | shared


def norm_back(grad_normed, source, inverse, gain):
    scaled = grad_normed * gain
    grad_source = inverse * scaled - source * inverse**3 * jnp.mean(
        scaled * source, axis=-1, keepdims=True
    )
    grad_gain = jnp.sum(grad_normed * source * inverse, axis=0)
    return (grad_source, grad_gain)


def around_blocks(pieces, combine, initial):
    return combine(
        initial,
        (
            lax.all_gather(pieces[0], "blk", axis=0, tiled=True),
            lax.all_gather(pieces[1], "blk", axis=0, tiled=True),
        ),
        jnp.int32(0),
    )


def softmax_last(logits):
    highest = jnp.max(logits, axis=-1, keepdims=True)
    raised = jnp.exp(logits - highest)
    return raised / jnp.sum(raised, axis=-1, keepdims=True)


def shards(
    inputs,
    cotangent,
    segment,
    position,
    routes,
    gate_residual,
    first_gain,
    second_gain,
    query_key_weight,
    value_weight,
    output_weight,
    router_weight,
    const_gate,
    const_vectors,
    gate_weight,
    up_weight,
    down_weight,
):
    tok_rows, width = inputs.shape
    head_count = lax.axis_size("head")
    blk_count = lax.axis_size("blk")
    local_heads = HEADS // head_count
    query_rows = head_count * tok_rows
    head_width = width // head_count
    width_split = blk_count // EXPERTS
    score_scale = HEAD_DIM ** (-0.5)
    period = tok_rows * blk_count // CONT_LEN + 1
    gathered = (
        lax.all_gather(first_gain, ("head", "blk"), axis=0, tiled=True),
        lax.all_gather(second_gain, ("head", "blk"), axis=0, tiled=True),
        lax.all_gather(query_key_weight, ("head", "blk"), axis=0, tiled=True),
        lax.all_gather(value_weight, ("head", "blk"), axis=0, tiled=True),
        lax.all_gather(output_weight, ("head", "blk"), axis=0, tiled=True),
        lax.all_gather(router_weight, ("head", "blk"), axis=0, tiled=True),
        lax.all_gather(const_gate, ("head", "blk"), axis=0, tiled=True),
        lax.all_gather(const_vectors, ("head", "blk"), axis=0, tiled=True),
        lax.all_gather(segment, ("head", "blk"), axis=0, tiled=True),
        lax.all_gather(position, ("head", "blk"), axis=0, tiled=True),
    )
    (
        gain_one,
        gain_two,
        full_joint,
        full_value,
        full_output,
        full_router,
        full_const,
        full_vectors,
        segment_all,
        position_all,
    ) = gathered
    gate_columns, up_columns, down_rows = (
        lax.all_gather(gate_weight, "head", axis=0, tiled=True),
        lax.all_gather(up_weight, "head", axis=0, tiled=True),
        lax.all_gather(down_weight, "head", axis=1, tiled=True),
    )
    gain_one = gain_one.astype(jnp.float32)
    gain_two = gain_two.astype(jnp.float32)
    source = inputs.astype(jnp.float32)
    inverse_one = lax.rsqrt(jnp.mean(source * source, axis=-1, keepdims=True) + EPS)
    normed_one = (source * inverse_one * gain_one).astype(jnp.bfloat16)
    joined = jnp.dot(normed_one, full_joint, preferred_element_type=jnp.float32)
    value_proj = jnp.dot(normed_one, full_value, preferred_element_type=jnp.float32)

    def head_layout(array):
        return array.astype(jnp.bfloat16).reshape(tok_rows, head_count, head_width)

    query_heads, key_heads, value_heads = (
        lax.all_to_all(
            head_layout(joined[:, :width]), "head", split_axis=1, concat_axis=0, tiled=True
        ),
        lax.all_to_all(
            head_layout(joined[:, width:]), "head", split_axis=1, concat_axis=0, tiled=True
        ),
        lax.all_to_all(head_layout(value_proj), "head", split_axis=1, concat_axis=0, tiled=True),
    )
    query_heads = query_heads.reshape(query_rows, local_heads, HEAD_DIM)
    key_heads = key_heads.reshape(query_rows, head_width)
    value_heads = value_heads.reshape(query_rows, head_width)
    blk_index = lax.axis_index("blk")
    segment_grid = segment_all.reshape(head_count, blk_count, tok_rows)
    position_grid = position_all.reshape(head_count, blk_count, tok_rows)
    query_segment = lax.dynamic_index_in_dim(segment_grid, blk_index, 1, keepdims=False).reshape(
        query_rows
    )
    query_position = lax.dynamic_index_in_dim(position_grid, blk_index, 1, keepdims=False).reshape(
        query_rows
    )
    key_segment = segment_grid.transpose(1, 0, 2).reshape(blk_count * query_rows)
    key_position = position_grid.transpose(1, 0, 2).reshape(blk_count * query_rows)

    def key_slices(pieces):
        piece_rows = pieces[0].shape[0]
        step_count = piece_rows // tok_rows
        return (
            pieces[0].reshape(step_count, tok_rows, local_heads, HEAD_DIM),
            pieces[1].reshape(step_count, tok_rows, local_heads, HEAD_DIM),
            key_segment.reshape(step_count, tok_rows),
            key_position.reshape(step_count, tok_rows),
        )

    def masked_scores(queries, block_keys, visible):
        scores = (
            jnp.einsum("qhd,khd->hqk", queries, block_keys, preferred_element_type=jnp.float32)
            * score_scale
        )
        return jnp.where(visible[None], scores, -jnp.inf)

    def attend_block(carried, block):
        block_keys, block_values, block_segment, block_position = block
        visible = visible_pairs(
            query_segment, query_position, block_segment, block_position, period
        )

        def attend_compute(state):
            top_score, running_total, weighted = state
            scores = masked_scores(query_heads, block_keys, visible)
            new_top = jnp.maximum(top_score, jnp.max(scores, axis=-1))
            anchor = jnp.where(new_top == -jnp.inf, 0.0, new_top)
            raised = jnp.exp(scores - anchor[..., None])
            factor = jnp.exp(top_score - anchor)
            running_total = running_total * factor + jnp.sum(raised, axis=-1)
            weighted = weighted * factor[..., None] + jnp.einsum(
                "hqk,khd->hqd",
                raised.astype(jnp.bfloat16),
                block_values,
                preferred_element_type=jnp.float32,
            )
            return (new_top, running_total, weighted)

        def unchanged(state):
            return state

        return (lax.cond(jnp.any(visible), attend_compute, unchanged, carried), None)

    def attend_piece(carried, pieces, first_row):
        result, unused = lax.scan(attend_block, carried, key_slices(pieces))
        return result

    start_state = (
        jnp.full((local_heads, query_rows), -jnp.inf, jnp.float32),
        jnp.zeros((local_heads, query_rows), jnp.float32),
        jnp.zeros((local_heads, query_rows, HEAD_DIM), jnp.float32),
    )
    top_score, running_total, weighted = around_blocks(
        (key_heads, value_heads), attend_piece, start_state
    )
    log_total = top_score + jnp.log(running_total)
    attended_local = (weighted / running_total[..., None]).transpose(1, 0, 2).astype(jnp.bfloat16)
    attended = lax.all_to_all(
        attended_local.reshape(query_rows, 1, head_width),
        "head",
        split_axis=0,
        concat_axis=1,
        tiled=True,
    ).reshape(tok_rows, width)
    middle = source + jnp.dot(attended, full_output, preferred_element_type=jnp.float32)
    inverse_two = lax.rsqrt(jnp.mean(middle * middle, axis=-1, keepdims=True) + EPS)
    normed_two = (middle * inverse_two * gain_two).astype(jnp.bfloat16)
    normed_float = normed_two.astype(jnp.float32)
    logits = jnp.dot(normed_two, full_router, preferred_element_type=jnp.float32) + gate_residual
    choose = (routes[:, :, None] == jnp.arange(ROUTED, dtype=jnp.int32)[None, None, :]).astype(
        jnp.float32
    )
    picked = jnp.sum(choose * logits[:, None, :], axis=-1)
    weighting = softmax_last(picked)
    pair_expert = routes.reshape(tok_rows * TOP)
    ffn_onehot = (pair_expert[:, None] == jnp.arange(EXPERTS, dtype=jnp.int32)[None, :]).astype(
        jnp.int32
    )
    pair_rank = jnp.sum((jnp.cumsum(ffn_onehot, axis=0) - ffn_onehot) * ffn_onehot, axis=-1)
    slot_match = (
        pair_rank[None, None, :] == jnp.arange(CAP, dtype=jnp.int32)[None, :, None]
    ).astype(jnp.int32)
    placement = (
        (ffn_onehot.T[:, None, :] * slot_match)
        .reshape(EXPERTS, CAP, tok_rows, TOP)
        .astype(jnp.float32)
    )
    select = jnp.sum(placement, axis=-1)
    gate_slot = jnp.einsum("ectj,tj->ect", placement, weighting, precision=HIGH)
    send_rows = jnp.einsum(
        "ect,td->ecd", select.astype(jnp.bfloat16), normed_two, preferred_element_type=jnp.float32
    ).astype(jnp.bfloat16)
    upstream = cotangent.astype(jnp.float32)
    slot_grad = jnp.einsum("ect,td->ecd", gate_slot, upstream, precision=HIGH).astype(jnp.bfloat16)
    rows_in = lax.all_to_all(
        jnp.repeat(send_rows, width_split, axis=0), "blk", split_axis=0, concat_axis=0, tiled=True
    )
    grads_in = lax.all_to_all(
        jnp.repeat(slot_grad, width_split, axis=0), "blk", split_axis=0, concat_axis=0, tiled=True
    )
    gate_pre = jnp.einsum("scd,df->scf", rows_in, gate_columns, preferred_element_type=jnp.float32)
    up_pre = jnp.einsum("scd,df->scf", rows_in, up_columns, preferred_element_type=jnp.float32)
    activated = jax.nn.silu(gate_pre)
    hidden = (activated * up_pre).astype(jnp.bfloat16)
    partial_out = jnp.einsum("scf,fd->scd", hidden, down_rows, preferred_element_type=jnp.float32)
    grad_hidden = jnp.einsum("scd,fd->scf", grads_in, down_rows, preferred_element_type=jnp.float32)
    grad_gate_pre = (grad_hidden * up_pre * silu_slope(gate_pre)).astype(jnp.bfloat16)
    grad_up_pre = (grad_hidden * activated).astype(jnp.bfloat16)
    grad_part = jnp.einsum(
        "scf,df->scd", grad_gate_pre, gate_columns, preferred_element_type=jnp.float32
    ) + jnp.einsum("scf,df->scd", grad_up_pre, up_columns, preferred_element_type=jnp.float32)
    back_out = lax.all_to_all(
        partial_out.astype(jnp.bfloat16), "blk", split_axis=0, concat_axis=0, tiled=True
    ).astype(partial_out.dtype)
    back_grad = lax.all_to_all(
        grad_part.astype(jnp.bfloat16), "blk", split_axis=0, concat_axis=0, tiled=True
    ).astype(grad_part.dtype)
    returned, grad_back, kept_rows, kept_grads, hidden, grad_gate_pre, grad_up_pre = (
        back_out,
        back_grad,
        rows_in,
        grads_in,
        hidden,
        grad_gate_pre,
        grad_up_pre,
    )
    expert_out = returned.reshape(EXPERTS, width_split, CAP, width).sum(axis=1)
    ffn_sum = jnp.einsum("ect,ecd->td", gate_slot, expert_out, precision=HIGH)
    mixing = softmax_last(
        jnp.dot(normed_two, full_const, preferred_element_type=jnp.float32).reshape(tok_rows, 2, 2)
    )
    vectors = full_vectors.astype(jnp.float32)
    copy_share = jnp.sum(weighting * (routes == EXPERTS + 1).astype(jnp.float32), axis=-1)
    const_share = jnp.stack(
        [
            jnp.sum(weighting * (routes == EXPERTS + 2 + const_index).astype(jnp.float32), axis=-1)
            for const_index in range(2)
        ],
        axis=1,
    )
    const_outs = [
        mixing[:, const_index, 0:1] * normed_float
        + mixing[:, const_index, 1:2] * vectors[:, const_index][None, :]
        for const_index in range(2)
    ]
    mixture = ffn_sum + copy_share[:, None] * normed_float
    for const_index in range(2):
        mixture = mixture + const_share[:, const_index : const_index + 1] * const_outs[const_index]
    layer_out = (middle + mixture).astype(jnp.bfloat16)
    output_dots = jnp.einsum("ecd,td->ect", expert_out, upstream, precision=HIGH)
    grad_weighting = jnp.einsum("ectj,ect->tj", placement, output_dots, precision=HIGH)
    copy_dot = jnp.sum(upstream * normed_float, axis=-1)
    grad_weighting = (
        grad_weighting + (routes == EXPERTS + 1).astype(jnp.float32) * copy_dot[:, None]
    )
    for const_index in range(2):
        const_dot = jnp.sum(upstream * const_outs[const_index], axis=-1)
        grad_weighting = (
            grad_weighting
            + (routes == EXPERTS + 2 + const_index).astype(jnp.float32) * const_dot[:, None]
        )
    grad_picked = weighting * (
        grad_weighting - jnp.sum(weighting * grad_weighting, axis=-1, keepdims=True)
    )
    grad_logits = jnp.einsum("tj,tjr->tr", grad_picked, choose, precision=HIGH)
    vector_dots = jnp.dot(upstream, vectors, precision=HIGH)
    grad_mixing = const_share[:, :, None] * jnp.stack(
        [jnp.broadcast_to(copy_dot[:, None], vector_dots.shape), vector_dots], axis=-1
    )
    grad_mix = (
        mixing * (grad_mixing - jnp.sum(mixing * grad_mixing, axis=-1, keepdims=True))
    ).reshape(tok_rows, 4)
    grad_const_weight = jnp.dot(normed_float.T, grad_mix, precision=HIGH)
    grad_vectors = jnp.einsum("ti,td->di", const_share * mixing[:, :, 1], upstream, precision=HIGH)
    grad_router_weight = jnp.dot(normed_float.T, grad_logits, precision=HIGH)
    direct_share = (
        copy_share + const_share[:, 0] * mixing[:, 0, 0] + const_share[:, 1] * mixing[:, 1, 0]
    )
    grad_normed_two = direct_share[:, None] * upstream
    grad_normed_two = grad_normed_two + jnp.dot(
        grad_mix, full_const.astype(jnp.float32).T, precision=HIGH
    )
    grad_normed_two = grad_normed_two + jnp.dot(
        grad_logits, full_router.astype(jnp.float32).T, precision=HIGH
    )
    grad_down_local = jnp.einsum(
        "scf,scd->fd", hidden, kept_grads, preferred_element_type=jnp.float32
    )
    grad_gate_local = jnp.einsum(
        "scd,scf->df", kept_rows, grad_gate_pre, preferred_element_type=jnp.float32
    )
    grad_up_local = jnp.einsum(
        "scd,scf->df", kept_rows, grad_up_pre, preferred_element_type=jnp.float32
    )
    grad_slots = grad_back.reshape(EXPERTS, width_split, CAP, width).sum(axis=1)
    grad_normed_two = grad_normed_two + jnp.einsum(
        "ect,ecd->td", select, grad_slots, precision=HIGH
    )
    grad_gate_sum, grad_up_sum, grad_down_sum = (
        lax.psum_scatter(
            grad_gate_local.astype(jnp.bfloat16), "head", scatter_dimension=0, tiled=True
        ).astype(jnp.float32),
        lax.psum_scatter(
            grad_up_local.astype(jnp.bfloat16), "head", scatter_dimension=0, tiled=True
        ).astype(jnp.float32),
        lax.psum_scatter(
            grad_down_local.astype(jnp.bfloat16), "head", scatter_dimension=1, tiled=True
        ).astype(jnp.float32),
    )
    grad_from_norm, grad_gain_two = norm_back(grad_normed_two, middle, inverse_two, gain_two)
    grad_middle = upstream + grad_from_norm
    branch_grad = grad_middle.astype(jnp.bfloat16)
    grad_out_weight = jnp.einsum(
        "tc,td->cd", attended, branch_grad, preferred_element_type=jnp.float32
    )
    grad_attended = jnp.einsum(
        "td,cd->tc", branch_grad, full_output, preferred_element_type=jnp.float32
    ).astype(jnp.bfloat16)
    grad_heads = lax.all_to_all(
        grad_attended.reshape(tok_rows, head_count, head_width),
        "head",
        split_axis=1,
        concat_axis=0,
        tiled=True,
    )
    grad_heads = grad_heads.reshape(query_rows, local_heads, HEAD_DIM)
    offset = jnp.sum(grad_heads.astype(jnp.float32) * attended_local.astype(jnp.float32), axis=-1).T

    def probe_block(queries, grads, lse_rows, offset_rows, block_keys, block_values, visible):
        scores = masked_scores(queries, block_keys, visible)
        probabilities = jnp.exp(scores - lse_rows[..., None])
        grad_probs = jnp.einsum(
            "qhd,khd->hqk", grads, block_values, preferred_element_type=jnp.float32
        )
        grad_scores = (probabilities * (grad_probs - offset_rows[..., None])).astype(jnp.bfloat16)
        return (probabilities, grad_scores)

    zero_query = jnp.zeros((query_rows, local_heads, HEAD_DIM), jnp.float32)

    def backward_block(grad_query, block):
        block_keys, block_values, block_segment, block_position = block
        visible = visible_pairs(
            query_segment, query_position, block_segment, block_position, period
        )

        def backward_compute(accumulated):
            probabilities, grad_scores = probe_block(
                query_heads, grad_heads, log_total, offset, block_keys, block_values, visible
            )
            grad_values = jnp.einsum(
                "hqk,qhd->khd",
                probabilities.astype(jnp.bfloat16),
                grad_heads,
                preferred_element_type=jnp.float32,
            )
            accumulated = (
                accumulated
                + jnp.einsum(
                    "hqk,khd->qhd", grad_scores, block_keys, preferred_element_type=jnp.float32
                )
                * score_scale
            )
            grad_keys = (
                jnp.einsum(
                    "hqk,qhd->khd", grad_scores, query_heads, preferred_element_type=jnp.float32
                )
                * score_scale
            )
            return (accumulated, jnp.concatenate([grad_keys, grad_values], axis=-1))

        def skipped(accumulated):
            return (
                accumulated,
                jnp.zeros((block_keys.shape[0], local_heads, 2 * HEAD_DIM), jnp.float32),
            )

        return lax.cond(jnp.any(visible), backward_compute, skipped, grad_query)

    def fold_back(carried, pieces, first_row):
        grad_query, stacked = lax.scan(backward_block, carried[0], key_slices(pieces))
        term_piece = stacked.reshape(pieces[0].shape[0], local_heads * 2 * HEAD_DIM)
        return (grad_query, term_piece)

    zero_term = jnp.zeros((blk_count * query_rows, local_heads * 2 * HEAD_DIM), jnp.float32)
    grad_query, key_term = around_blocks(
        (key_heads, value_heads), fold_back, (zero_query, zero_term)
    )
    key_sums = lax.psum_scatter(key_term, "blk", scatter_dimension=0, tiled=True).reshape(
        query_rows, local_heads, 2, HEAD_DIM
    )
    grad_key_heads = key_sums[:, :, 0].astype(jnp.bfloat16).reshape(query_rows, 1, head_width)
    grad_value_heads = key_sums[:, :, 1].astype(jnp.bfloat16).reshape(query_rows, 1, head_width)
    grad_query_heads = grad_query.astype(jnp.bfloat16).reshape(query_rows, 1, head_width)
    grad_query_tok, grad_key_tok, grad_value_tok = (
        lax.all_to_all(grad_query_heads, "head", split_axis=0, concat_axis=1, tiled=True),
        lax.all_to_all(grad_key_heads, "head", split_axis=0, concat_axis=1, tiled=True),
        lax.all_to_all(grad_value_heads, "head", split_axis=0, concat_axis=1, tiled=True),
    )
    grad_joined = jnp.concatenate(
        [grad_query_tok.reshape(tok_rows, width), grad_key_tok.reshape(tok_rows, width)], axis=1
    )
    grad_value_tok = grad_value_tok.reshape(tok_rows, width)
    grad_normed_one = jnp.einsum(
        "tc,dc->td", grad_joined, full_joint, preferred_element_type=jnp.float32
    ) + jnp.einsum("tc,dc->td", grad_value_tok, full_value, preferred_element_type=jnp.float32)
    grad_joint_weight = jnp.einsum(
        "td,tc->dc", normed_one, grad_joined, preferred_element_type=jnp.float32
    )
    grad_value_weight = jnp.einsum(
        "td,tc->dc", normed_one, grad_value_tok, preferred_element_type=jnp.float32
    )
    grad_from_first, grad_gain_one = norm_back(grad_normed_one, source, inverse_one, gain_one)
    grad_input = grad_middle + grad_from_first
    summed = (
        lax.psum_scatter(grad_gain_one, ("head", "blk"), scatter_dimension=0, tiled=True),
        lax.psum_scatter(grad_gain_two, ("head", "blk"), scatter_dimension=0, tiled=True),
        lax.psum_scatter(grad_joint_weight, ("head", "blk"), scatter_dimension=0, tiled=True),
        lax.psum_scatter(grad_value_weight, ("head", "blk"), scatter_dimension=0, tiled=True),
        lax.psum_scatter(grad_out_weight, ("head", "blk"), scatter_dimension=0, tiled=True),
        lax.psum_scatter(grad_router_weight, ("head", "blk"), scatter_dimension=0, tiled=True),
        lax.psum_scatter(grad_const_weight, ("head", "blk"), scatter_dimension=0, tiled=True),
        lax.psum_scatter(grad_vectors, ("head", "blk"), scatter_dimension=0, tiled=True),
    )
    return (
        layer_out,
        grad_input,
        grad_logits,
        summed[0],
        summed[1],
        summed[2],
        summed[3],
        summed[4],
        summed[5],
        summed[6],
        summed[7],
        grad_gate_sum,
        grad_up_sum,
        grad_down_sum,
    )


MESH = pl.DeviceIdType.MESH
SMALL = 24
ROUTER_AT, MIX_AT, VECTOR_AT, GAIN_ONE_AT, GAIN_TWO_AT = 0, 12, 16, 18, 19
PAD = 32
CHUNK = 4
FAR = 1 << 20
NT = (((1,), (1,)), ((), ()))
TN = (((0,), (0,)), ((), ()))


def mul(left, right):
    return jnp.dot(left, right, preferred_element_type=jnp.float32)


def mul_nt(left, right):
    return lax.dot_general(left, right, NT, preferred_element_type=jnp.float32)


def mul_tn(left, right):
    return lax.dot_general(left, right, TN, preferred_element_type=jnp.float32)


def low(values):
    return values.astype(jnp.bfloat16)


def wide(values):
    return values.astype(jnp.float32)


def halves(values):
    high = low(values)
    return high, low(values - wide(high))


def shape(dims, dtype=jnp.bfloat16):
    return jax.ShapeDtypeStruct(dims, dtype)


def compute(body, outs, ins, scratch=(), smem=0):
    specs = [pl.BlockSpec(memory_space=pltpu.SMEM)] * smem
    specs += [pl.BlockSpec(memory_space=pltpu.VMEM)] * (len(ins) - smem)
    return pl.pallas_call(
        body,
        out_shape=outs,
        in_specs=specs,
        out_specs=[pl.BlockSpec(memory_space=pltpu.VMEM)] * len(outs),
        scratch_shapes=list(scratch),
        compiler_params=pltpu.CompilerParams(vmem_limit_bytes=52 * 2**20),
    )(*ins)


def exchange(body, outs, ins, scratch, number):
    return pl.pallas_call(
        body,
        out_shape=outs,
        in_specs=[pl.BlockSpec(memory_space=pl.ANY)] * len(ins),
        out_specs=[pl.BlockSpec(memory_space=pl.ANY)] * len(outs),
        scratch_shapes=list(scratch),
        compiler_params=pltpu.CompilerParams(
            collective_id=number, has_side_effects=True, vmem_limit_bytes=32 * 2**20
        ),
    )(*ins)


def meet(devices):
    barrier = pltpu.get_barrier_semaphore()
    for device in devices:
        pl.semaphore_signal(barrier, inc=1, device_id=device, device_id_type=MESH)
    pl.semaphore_wait(barrier, len(devices))


class Place:
    def __init__(self, head_count, blk_count):
        self.head_count, self.blk_count = head_count, blk_count
        self.head, self.blk = lax.axis_index("head"), lax.axis_index("blk")
        self.half = blk_count // 2
        self.chip, self.core = self.blk // 2, self.blk % 2
        self.twin = self.blk + 1 - 2 * self.core

    def along(self, axis):
        if axis == "head":
            return self.head, self.head_count
        return self.blk, self.blk_count

    def device(self, axis, index):
        return (index, self.blk) if axis == "head" else (self.head, index)

    def others(self, axis):
        me, size = self.along(axis)
        return [self.device(axis, (me + step) % size) for step in range(1, size)]

    def chips(self):
        return [((self.chip + step) % self.half) * 2 + self.core for step in range(1, self.half)]

    def near(self):
        return [(self.head, self.twin)] + [(self.head, blk) for blk in self.chips()]


def dma(*dims):
    return pltpu.SemaphoreType.DMA(dims)


def send(source, target, sent, got, device):
    copy = pltpu.make_async_remote_copy(
        src_ref=source,
        dst_ref=target,
        send_sem=sent,
        recv_sem=got,
        device_id=device,
        device_id_type=MESH,
    )
    copy.start()
    return copy


def keep(source, target, done):
    copy = pltpu.make_async_copy(source, target, done)
    copy.start()
    return copy


def scatter(place, axis, source, target, sent, got):
    me, size = place.along(axis)
    copies = []
    for step in range(1, size):
        other = (me + step) % size
        copies.append(
            send(
                source.at[other],
                target.at[me],
                sent.at[step - 1],
                got.at[step - 1],
                place.device(axis, other),
            )
        )
    return copies


def gather(place, axis, source, target, sent, got):
    me, size = place.along(axis)
    copies = []
    for step in range(1, size):
        other = (me + step) % size
        copies.append(
            send(
                source, target.at[me], sent.at[step - 1], got.at[step - 1], place.device(axis, other)
            )
        )
    return copies


def spread(place, refs, sent, got):
    def pass_on(number, lane, slot, blk):
        return send(
            refs[number].at[slot],
            refs[number].at[slot],
            sent.at[number, lane],
            got.at[number, lane],
            (place.head, blk),
        )

    numbers = range(len(refs))
    direct = [
        [pass_on(number, step, place.blk, blk) for step, blk in enumerate(place.chips(), 1)]
        for number in numbers
    ]
    rest = [pass_on(number, 0, place.blk, place.twin) for number in numbers]
    for step in range(1, place.half):
        slot = ((place.chip + place.half - step) % place.half) * 2 + place.core
        for number in numbers:
            direct[number][step - 1].wait_recv()
            rest.append(pass_on(number, place.half - 1 + step, slot, place.twin))
    for number in numbers:
        for copy in direct[number]:
            copy.wait_send()
    for copy in rest:
        copy.wait()


def wait_all(*groups):
    for group in groups:
        for copy in group:
            copy.wait()


def send_tokens_and_weights(sizes, x, joint, packed, facts, x_all, joint_all, packed_all, facts_all, local, sent, got, sent_blk, got_blk):
    place = Place(*sizes)
    head, blk = place.head, place.blk
    own = [
        keep(joint.at[head], joint_all.at[blk, head], local.at[0]),
        keep(packed, packed_all.at[blk, head], local.at[1]),
        keep(facts, facts_all.at[blk, head], local.at[2]),
    ]
    own_x = keep(x, x_all.at[head], local.at[3])
    meet(place.others("head") + place.near())
    weights = scatter(place, "head", joint, joint_all.at[blk], sent.at[0], got.at[0])
    weights += gather(place, "head", packed, packed_all.at[blk], sent.at[1], got.at[1])
    weights += gather(place, "head", facts, facts_all.at[blk], sent.at[2], got.at[2])
    tokens = gather(place, "head", x, x_all, sent.at[3], got.at[3])
    wait_all(own, weights)
    spread(place, [joint_all, packed_all, facts_all], sent_blk, got_blk)
    wait_all(tokens, [own_x])


def send_keys(sizes, pairs, g, pairs_all, g_all, local, sent, got, sent_blk, got_blk):
    place = Place(*sizes)
    own = keep(pairs, pairs_all.at[place.blk], local.at[0])
    own_g = keep(g, g_all.at[place.head], local.at[1])
    meet(place.others("head") + place.near())
    upstream = gather(place, "head", g, g_all, sent, got)
    own.wait()
    spread(place, [pairs_all], sent_blk, got_blk)
    wait_all(upstream, [own_g])


def send_attended(sizes, attended, slots, attended_all, slots_in, local, sent, got, sent_blk, got_blk):
    place = Place(*sizes)
    own = keep(attended, attended_all.at[place.head], local.at[0])
    own_slots = keep(slots.at[place.blk], slots_in.at[place.blk], local.at[1])
    meet(place.others("head") + place.others("blk"))
    rows = gather(place, "head", attended, attended_all, sent, got)
    routed = scatter(place, "blk", slots, slots_in, sent_blk, got_blk)
    wait_all(rows, routed, [own, own_slots])


def send_slots(sizes, slots, slots_in, local, sent, got):
    place = Place(*sizes)
    own = keep(slots.at[place.blk], slots_in.at[place.blk], local.at[0])
    meet(place.others("blk"))
    wait_all(scatter(place, "blk", slots, slots_in, sent, got), [own])


def send_shares(sizes, parts, slots, parts_in, slots_in, local, sent, got, sent_blk, got_blk):
    place = Place(*sizes)
    own = keep(parts.at[place.head], parts_in.at[place.head], local.at[0])
    own_slots = keep(slots.at[place.blk], slots_in.at[place.blk], local.at[1])
    meet(place.others("head") + place.others("blk"))
    shares = scatter(place, "head", parts, parts_in, sent, got)
    routed = scatter(place, "blk", slots, slots_in, sent_blk, got_blk)
    wait_all(shares, routed, [own, own_slots])


def send_middle(sizes, rows, rows_all, local, sent, got):
    place = Place(*sizes)
    own = keep(rows, rows_all.at[place.head], local.at[0])
    meet(place.others("head"))
    wait_all(gather(place, "head", rows, rows_all, sent, got), [own])


def send_key_sums(sizes, terms, parts, sums, parts_in, mine, theirs, local, sent, got, sent_twin, got_twin, sent_blk, got_blk):
    place = Place(*sizes)
    half = place.half
    own_parts = keep(parts.at[place.head], parts_in.at[place.head], local.at[half])
    own = [
        keep(terms.at[step * 2 + place.core], mine.at[step], local.at[step])
        for step in range(half)
    ]
    meet(place.others("head") + place.near())
    shares = scatter(place, "head", parts, parts_in, sent, got)
    twin = (place.head, place.twin)
    across = []
    for step in range(half):
        chip = (place.chip + step + 1) % half
        across.append(
            send(
                terms.at[chip * 2 + 1 - place.core],
                theirs.at[step],
                sent_twin.at[step],
                got_twin.at[step],
                twin,
            )
        )
    for copy in own:
        copy.wait()
    onward = []
    for step in range(half):
        chip = (place.chip + step + 1) % half
        across[step].wait_recv()
        theirs[step] = low(wide(theirs[step]) + wide(mine[chip]))
        if step < half - 1:
            onward.append(
                send(
                    theirs.at[step],
                    sums.at[place.chip],
                    sent_blk.at[step],
                    got_blk.at[step],
                    (place.head, chip * 2 + place.core),
                )
            )
    last = keep(theirs.at[half - 1], sums.at[place.chip], local.at[half + 1])
    for copy in across:
        copy.wait_send()
    wait_all(onward, shares, [own_parts, last])


def send_gradients(sizes, rows, joint, out, small, rows_in, joint_in, out_in, small_in, local, sent, got, sent_blk, got_blk):
    place = Place(*sizes)
    head, blk = place.head, place.blk
    own = [
        keep(rows.at[head], rows_in.at[head], local.at[0]),
        keep(joint.at[blk], joint_in.at[blk], local.at[1]),
        keep(out.at[blk], out_in.at[blk], local.at[2]),
        keep(small.at[blk], small_in.at[blk], local.at[3]),
    ]
    meet(place.others("head") + place.others("blk"))
    tokens = scatter(place, "head", rows, rows_in, sent, got)
    weights = scatter(place, "blk", joint, joint_in, sent_blk.at[0], got_blk.at[0])
    weights += scatter(place, "blk", out, out_in, sent_blk.at[1], got_blk.at[1])
    weights += scatter(place, "blk", small, small_in, sent_blk.at[2], got_blk.at[2])
    wait_all(own, tokens, weights)


def send_weight_sums(sizes, joint, small, joint_in, small_in, local, sent, got):
    place = Place(*sizes)
    head = place.head
    own = [
        keep(joint.at[head], joint_in.at[head], local.at[0]),
        keep(small.at[head], small_in.at[head], local.at[1]),
    ]
    meet(place.others("head"))
    copies = scatter(place, "head", joint, joint_in, sent.at[0], got.at[0])
    copies += scatter(place, "head", small, small_in, sent.at[1], got.at[1])
    wait_all(own, copies)


def project(sizes, x, joint_all, packed_all, normed, queries, pairs, joint, output, small, joint_wide, output_wide, small_wide):
    head_count, blk_count = sizes
    rows = joint.shape[0] // (head_count * blk_count)
    for head in range(head_count):
        for blk in range(blk_count):
            place = pl.ds((head * blk_count + blk) * rows, rows)
            joint_wide[place, :] = wide(joint_all[blk, head])[:rows]
            piece = wide(packed_all[blk, head])[:rows]
            output_wide[place, :] = piece[:, : output.shape[1]]
            small_wide[place, :] = piece[:, output.shape[1] :]
    joint[...] = low(joint_wide[...])
    output[...] = low(output_wide[...])
    small_rows = small_wide[...].T
    small[...] = small_rows[:SMALL]
    source = wide(x[...])
    inverse = lax.rsqrt(jnp.mean(source * source, axis=-1, keepdims=True) + EPS)
    normed[...] = low(source * inverse * small_rows[GAIN_ONE_AT : GAIN_ONE_AT + 1])
    product = mul(normed[...], joint[...])
    split = queries.shape[1]
    queries[...] = low(product[:, :split])
    pairs[...] = low(product[:, split:])


def slots_of(head_count, facts, first, second):
    tokens = first.shape[2]
    earlier = low(
        wide(
            lax.broadcasted_iota(jnp.int32, (tokens, tokens), 0)
            < lax.broadcasted_iota(jnp.int32, (tokens, tokens), 1)
        )
    )
    expert = wide(lax.broadcasted_iota(jnp.int32, (2 * EXPERTS, tokens), 0))
    expert_at = wide(lax.broadcasted_iota(jnp.int32, (EXPERTS, CAP, tokens), 0))
    rank_at = wide(lax.broadcasted_iota(jnp.int32, (EXPERTS, CAP, tokens), 1))
    for head in range(head_count):
        routes = [facts[head, 2 + choice : 3 + choice, :] for choice in range(TOP)]
        named = jnp.where((routes[0] == expert) | (routes[1] == expert), 1.0, 0.0)
        count = mul(low(named), earlier)[:EXPERTS]
        fits = count[:, None, :] == rank_at
        for choice, out in enumerate((first, second)):
            match = (routes[choice][None] == expert_at) & fits
            out[head] = low(jnp.where(match, 1.0, 0.0).reshape(EXPERTS * CAP, tokens))


def fill_slots(head_count, width, placed, rows_of, slots):
    parts = []
    for head in range(head_count):
        chosen = placed[0][head] + placed[1][head]
        parts.append(mul(chosen, rows_of(head)).reshape(EXPERTS, CAP, width))
    slots[:, :, :width] = low(jnp.concatenate(parts, axis=1))


def place_upstream(sizes, facts_all, g_all, first, second, slots):
    head_count, blk_count = sizes
    facts = facts_all.at[lax.axis_index("blk")]
    slots_of(head_count, facts, first, second)
    fill_slots(head_count, slots.shape[2], (first, second), lambda head: g_all[head], slots)


def visible_blocks(segment, position, period, me, count, chosen, shift):
    def look(block, found):
        same = segment[block] == segment[me]
        shared = (
            (segment[block] // period == segment[me] // period)
            & (segment[block] % period == 0)
            & (segment[me] % period != 0)
        )
        seen = (same & (position[block] <= position[me])) | shared
        chosen[found] = block
        shift[found] = jnp.where(same & (position[block] == position[me]), 0, -FAR)
        return found + seen.astype(jnp.int32)

    found = lax.fori_loop(0, count, look, jnp.int32(0))
    for extra in range(CHUNK):
        chosen[found + extra] = jnp.int32(0)
        shift[found + extra] = jnp.int32(FAR)
    return (found + CHUNK - 1) // CHUNK


def chunk_mask(tokens, heads, shift, start):
    row = lax.broadcasted_iota(jnp.int32, (tokens, tokens), 0)
    column = lax.broadcasted_iota(jnp.int32, (tokens, tokens), 1)
    gap = row - column
    parts = [
        jnp.where(gap + shift[start + step] <= 0, 1.0, 0.0) for step in range(CHUNK)
    ]
    mask = jnp.concatenate(parts, axis=0)
    return jnp.concatenate([mask] * heads, axis=1) > 0.5


def chunk_rows(pairs, chosen, start, low_lane, high_lane):
    return jnp.concatenate(
        [pairs[chosen[start + step], :, low_lane:high_lane] for step in range(CHUNK)], axis=0
    )


def lanes_at(rows, first, last):
    lane = lax.broadcasted_iota(jnp.int32, rows.shape, 1)
    return jnp.where((lane >= first) & (lane < last), rows, jnp.zeros_like(rows))


def query_rows_of(queries, head, tokens):
    rows = queries[pl.ds(head * tokens, tokens), :]
    rows = low(wide(rows) * HEAD_DIM ** (-0.5))
    return jnp.concatenate(
        [lanes_at(rows, part * HEAD_DIM, (part + 1) * HEAD_DIM) for part in range(3)], axis=0
    )


def attend(sizes, period, segment, position, queries, pairs, attended, totals, chosen, shift):
    head_count, blk_count = sizes
    blocks, tokens, lanes = pairs.shape
    heads = 3
    blk = lax.axis_index("blk")
    for head in range(head_count):
        chunks = visible_blocks(
            segment, position, period, blk * head_count + head, blocks, chosen, shift
        )
        asked = query_rows_of(queries, head, tokens)

        def step(number, carried):
            top, total, weighted = carried
            start = number * CHUNK
            scores = mul_nt(chunk_rows(pairs, chosen, start, 0, 256), asked)
            scores = jnp.where(chunk_mask(tokens, heads, shift, start), scores, -jnp.inf)
            new_top = jnp.maximum(top, jnp.max(scores, axis=0, keepdims=True))
            raised = jnp.exp(scores - new_top)
            factor = jnp.exp(top - new_top)
            total = total * factor + jnp.sum(raised, axis=0, keepdims=True)
            mixed = mul_tn(chunk_rows(pairs, chosen, start, 128, lanes), low(raised))
            mixed = jnp.concatenate(
                [mixed[128:192, 0:128], mixed[192:256, 128:256], mixed[64:128, 256:384]], axis=1
            )
            return (new_top, total, weighted * factor + mixed)

        wide_lanes = heads * tokens
        top, total, weighted = lax.fori_loop(
            0,
            chunks,
            step,
            (
                jnp.full((1, wide_lanes), -1e30, jnp.float32),
                jnp.zeros((1, wide_lanes), jnp.float32),
                jnp.zeros((HEAD_DIM, wide_lanes), jnp.float32),
            ),
        )
        outcome = low(weighted / total)
        totals[head] = jnp.broadcast_to(top + jnp.log(total), totals.shape[1:])
        for part in range(heads):
            attended[part * HEAD_DIM : (part + 1) * HEAD_DIM, head * tokens : (head + 1) * tokens] = (
                outcome[:, part * tokens : (part + 1) * tokens]
            )


def attend_back(sizes, period, segment, position, queries, pairs, attended, totals, middle_grad, output, query_grad, pair_grad, output_grad, chosen, shift, summed):
    head_count, blk_count = sizes
    blocks, tokens, lanes = pairs.shape
    heads = 3
    blk, mine = lax.axis_index("blk"), lax.axis_index("head")
    head_rows = heads * HEAD_DIM
    weight = output[pl.ds(pl.multiple_of(mine * head_rows, head_rows), head_rows), :]
    turned = jnp.concatenate(
        [jnp.zeros((HEAD_DIM, weight.shape[1]), weight.dtype), weight[128:192], weight[0:128]], axis=0
    )
    grads = middle_grad[...]
    product = mul(attended[...], grads)
    rows = head_rows // blk_count
    filler = jnp.zeros((PAD - rows, product.shape[1]), jnp.float32)
    for part in range(blk_count):
        output_grad[part] = low(
            jnp.concatenate([product[part * rows : (part + 1) * rows], filler], axis=0)
        )
    given = low(mul_nt(grads, turned))
    given_turned = wide(low(mul_nt(weight, grads)))
    dots = given_turned * wide(attended[...])
    summed[...] = jnp.zeros_like(summed)
    for head in range(head_count):
        chunks = visible_blocks(
            segment, position, period, blk * head_count + head, blocks, chosen, shift
        )
        asked = query_rows_of(queries, head, tokens)
        own = given[head * tokens : (head + 1) * tokens]
        back = jnp.concatenate(
            [lanes_at(own, 128, 192), lanes_at(own, 192, 256), lanes_at(own, 64, 128)], axis=0
        )
        offset = jnp.concatenate(
            [
                jnp.sum(
                    dots[
                        part * HEAD_DIM : (part + 1) * HEAD_DIM,
                        head * tokens : (head + 1) * tokens,
                    ],
                    axis=0,
                    keepdims=True,
                )
                for part in range(heads)
            ],
            axis=1,
        )
        total = totals[head, 0:1, :]

        def step(number, carried):
            start = number * CHUNK
            keys = chunk_rows(pairs, chosen, start, 0, 256)
            values = chunk_rows(pairs, chosen, start, 128, lanes)
            scores = mul_nt(keys, asked)
            raised = jnp.where(
                chunk_mask(tokens, heads, shift, start), jnp.exp(scores - total), 0.0
            )
            grad_raised = mul_nt(values, back)
            grad_scores = low(raised * (grad_raised - offset))
            key_part = mul(grad_scores, asked)
            value_part = mul(low(raised), back)
            both = jnp.concatenate(
                [
                    key_part[:, :128],
                    key_part[:, 128:] + value_part[:, :128],
                    value_part[:, 128:],
                ],
                axis=1,
            )
            for block in range(CHUNK):
                at = chosen[start + block]
                summed[at] = summed[at] + both[block * tokens : (block + 1) * tokens]
            found = mul_tn(keys, grad_scores)
            return carried + jnp.concatenate(
                [found[0:64, 0:128], found[64:128, 128:256], found[128:192, 256:384]], axis=1
            )

        found = lax.fori_loop(
            0, chunks, step, jnp.zeros((HEAD_DIM, heads * tokens), jnp.float32)
        )
        found = found * HEAD_DIM ** (-0.5)
        stacked = jnp.concatenate(
            [found[:, part * tokens : (part + 1) * tokens] for part in range(heads)]
            + [jnp.zeros((HEAD_DIM, tokens), jnp.float32)],
            axis=0,
        )
        query_grad[pl.ds(head * tokens, tokens), :] = low(stacked.T)
    pair_grad[...] = low(summed[...])


def route(sizes, x_all, attended_all, output, small, facts_all, first, second, slots, middle_home, normed_home, weights, middle, normed):
    head_count, blk_count = sizes
    tokens, width = middle_home.shape
    facts = facts_all.at[lax.axis_index("blk")]
    mine = lax.axis_index("head")
    rows = attended_all[...].T
    middle[...] = wide(x_all[...]) + mul(rows, output[...])
    source = middle[...]
    inverse = lax.rsqrt(jnp.mean(source * source, axis=-1, keepdims=True) + EPS)
    normed[...] = low(source * inverse * small[GAIN_TWO_AT : GAIN_TWO_AT + 1])
    here = pl.ds(pl.multiple_of(mine * tokens, tokens), tokens)
    middle_home[...] = middle[here, :]
    normed_home[...] = normed[here, :]
    router = low(small[0:16])
    expert = wide(lax.broadcasted_iota(jnp.int32, (16, tokens), 0))
    lane = lax.broadcasted_iota(jnp.int32, (EXPERTS * CAP, 128), 1)
    tails = []
    for head in range(head_count):
        logits = mul_nt(router, normed[pl.ds(head * tokens, tokens), :]) + facts[head, 8:24, :]
        picked = [
            jnp.sum(
                jnp.where(facts[head, 2 + choice : 3 + choice, :] == expert, logits, 0.0),
                axis=0,
                keepdims=True,
            )
            for choice in range(TOP)
        ]
        highest = jnp.maximum(picked[0], picked[1])
        raised = [jnp.exp(value - highest) for value in picked]
        total = raised[0] + raised[1]
        share = [value / total for value in raised]
        weights[head] = jnp.concatenate(share + [jnp.zeros((6, tokens), jnp.float32)], axis=0)
        of_slot = jnp.sum(
            wide(first[head]) * share[0] + wide(second[head]) * share[1], axis=1, keepdims=True
        )
        high, rest = halves(of_slot)
        tail = jnp.where(lane < 64, wide(high), wide(rest))
        tails.append(tail.reshape(EXPERTS, CAP, 128))
    fill_slots(
        head_count,
        width,
        (first, second),
        lambda head: normed[pl.ds(head * tokens, tokens), :],
        slots,
    )
    slots[:, :, width:] = low(jnp.concatenate(tails, axis=1))


def run_experts(sizes, slots_in, grads_in, piece_0, piece_1, piece_2, piece_3, back, outs, weight_grads, weights, hidden, grad_gate, grad_up, scaled):
    head_count, blk_count = sizes
    mine = lax.axis_index("head")
    width = outs.shape[2]
    columns = weights.shape[3]
    rows = outs.shape[1]
    for step, piece in enumerate((piece_0, piece_1, piece_2, piece_3)):
        source = (mine + head_count - step) % head_count
        for kind in range(3):
            weights[kind, source] = piece[kind]
    depth = head_count * weights.shape[2]
    group = 2 * rows

    def chunk(number, unused):
        at = pl.ds(number * 2, 2)
        here = pl.ds(pl.multiple_of(number * group, group), group)
        gate = weights[0].reshape(depth, columns)
        up = weights[1].reshape(depth, columns)
        down = weights[2].reshape(depth, columns)
        entry = slots_in[at].reshape(group, width + 128)
        taken = entry[:, :width]
        tail = wide(entry[:, width:])
        share = tail[:, 0:1] + tail[:, 64:65]
        scaled_rows = low(share * wide(grads_in[at].reshape(group, width)))
        scaled[here, :] = scaled_rows
        gate_pre = mul(taken, gate)
        up_pre = mul(taken, up)
        sigmoid = 1.0 / (1.0 + jnp.exp(-gate_pre))
        activated = gate_pre * sigmoid
        hidden_rows = low(activated * up_pre)
        hidden[here, :] = hidden_rows
        grad_hidden = mul(scaled_rows, down)
        gate_rows = low(grad_hidden * up_pre * sigmoid * (1.0 + gate_pre * (1.0 - sigmoid)))
        up_rows = low(grad_hidden * activated)
        grad_gate[here, :] = gate_rows
        grad_up[here, :] = up_rows
        dots = jnp.sum(wide(hidden_rows) * grad_hidden, axis=1, keepdims=True)
        grad_rows = mul_nt(gate_rows, gate) + mul_nt(up_rows, up)
        high, rest = halves(dots)
        lane = lax.broadcasted_iota(jnp.int32, (group, 128), 1)
        tail_out = jnp.where(lane < 64, wide(high), wide(rest))
        back[at] = low(jnp.concatenate([grad_rows, tail_out], axis=1)).reshape(2, rows, width + 128)
        outs[at] = low(mul_nt(hidden_rows, down)).reshape(2, rows, width)
        return unused

    lax.fori_loop(0, blk_count // 2, chunk, 0)
    rows_turned = slots_in[:, :, :width].reshape(blk_count * rows, width).T
    scaled_turned = scaled[...].T
    for kind, (left, right) in enumerate(
        ((rows_turned, grad_gate), (rows_turned, grad_up), (scaled_turned, hidden))
    ):
        weight_grads[:, kind] = low(mul(left, right[...])).reshape(
            head_count, depth // head_count, columns
        )


def slots_of_head(rows, head):
    taken = rows[:, head * CAP : (head + 1) * CAP]
    return low(taken.reshape(EXPERTS * CAP, rows.shape[2]))


def combine_grads(sizes, back_in, first, second, parts):
    head_count, blk_count = sizes
    width = parts.shape[2] - 128
    tokens = parts.shape[1]
    rows = wide(back_in[...])
    lane = lax.broadcasted_iota(jnp.int32, (tokens, 128), 1)
    for head in range(head_count):
        taken = slots_of_head(rows, head)
        found = [mul_tn(placed[head], taken) for placed in (first, second)]
        tail = jnp.zeros((tokens, 128), jnp.float32)
        for choice in range(TOP):
            high, rest = halves(
                found[choice][:, width : width + 1] + found[choice][:, width + 64 : width + 65]
            )
            tail = jnp.where(lane // 32 == 2 * choice, wide(high), tail)
            tail = jnp.where(lane // 32 == 2 * choice + 1, wide(rest), tail)
        parts[head, :, :width] = low(found[0][:, :width] + found[1][:, :width])
        parts[head, :, width:] = low(tail)


def combine_outs(sizes, outs_in, first, second, weights, parts):
    head_count, blk_count = sizes
    rows = wide(outs_in[...])
    for head in range(head_count):
        taken = slots_of_head(rows, head)
        columns = weights[head].T
        total = 0.0
        for choice, placed in enumerate((first, second)):
            total = total + columns[:, choice : choice + 1] * mul_tn(placed[head], taken)
        parts[head] = low(total)


def at_home(sizes, parts, middle, normed, g, small, weights, facts_all, middle_grad, middle_low, residual_grad, small_grad, mixture):
    head_count, blk_count = sizes
    tokens, width = middle.shape
    mine = lax.axis_index("head")
    facts = facts_all[lax.axis_index("blk"), mine]
    share_rows = weights[mine]
    columns = jnp.concatenate([share_rows, facts[0:8]], axis=0).T
    share = [columns[:, choice : choice + 1] for choice in range(TOP)]
    route_of = [columns[:, 10 + choice : 11 + choice] for choice in range(TOP)]
    upstream = wide(g[...])
    normed_wide = wide(normed[...])
    source = middle[...]
    small_low = low(small[...])
    seen = mul_nt(normed[...], small_low)
    met = mul_nt(g[...], small_low)

    def weight_of(expert):
        return sum(
            share[choice] * jnp.where(route_of[choice] == expert, 1.0, 0.0)
            for choice in range(TOP)
        )

    copy_share = weight_of(EXPERTS + 1)
    const_share = [weight_of(EXPERTS + 2 + const) for const in range(2)]
    mixing = []
    for const in range(2):
        at = MIX_AT + 2 * const
        pair = [seen[:, at + part : at + part + 1] for part in range(2)]
        highest = jnp.maximum(pair[0], pair[1])
        raised = [jnp.exp(value - highest) for value in pair]
        total = raised[0] + raised[1]
        mixing.append([value / total for value in raised])
    copy_dot = jnp.sum(upstream * normed_wide, axis=-1, keepdims=True)
    vector_dot = [met[:, VECTOR_AT + const : VECTOR_AT + const + 1] for const in range(2)]
    const_dot = [
        mixing[const][0] * copy_dot + mixing[const][1] * vector_dot[const] for const in range(2)
    ]
    total = wide(parts[0])
    for head in range(1, head_count):
        total = total + wide(parts[head])
    tail = total[:, width:]
    product = []
    for choice in range(TOP):
        value = tail[:, 64 * choice : 64 * choice + 1] + tail[:, 64 * choice + 32 : 64 * choice + 33]
        special = jnp.where(route_of[choice] == EXPERTS + 1, copy_dot, 0.0)
        for const in range(2):
            special = special + jnp.where(
                route_of[choice] == EXPERTS + 2 + const, const_dot[const], 0.0
            )
        product.append(value + share[choice] * special)
    both = product[0] + product[1]
    lane = lax.broadcasted_iota(jnp.int32, (tokens, 128), 1)
    lane_wide = wide(lane)
    routing = jnp.zeros((tokens, 128), jnp.float32)
    for choice in range(TOP):
        routing = routing + jnp.where(
            lane_wide == route_of[choice], product[choice] - share[choice] * both, 0.0
        )
    residual_grad[...] = routing
    vector_share = jnp.zeros((tokens, 128), jnp.float32)
    spread_grad = routing
    for const in range(2):
        grad_mix = [const_share[const] * copy_dot, const_share[const] * vector_dot[const]]
        mean = mixing[const][0] * grad_mix[0] + mixing[const][1] * grad_mix[1]
        for part in range(2):
            spread_grad = spread_grad + jnp.where(
                lane == MIX_AT + 2 * const + part,
                mixing[const][part] * (grad_mix[part] - mean),
                0.0,
            )
        vector_share = vector_share + jnp.where(
            lane == VECTOR_AT + const, const_share[const] * mixing[const][1], 0.0
        )
    direct = (
        copy_share + const_share[0] * mixing[0][0] + const_share[1] * mixing[1][0]
    )
    table = jnp.concatenate(
        [small_low[0:16], jnp.zeros((128 - 16, width), jnp.bfloat16)], axis=0
    )
    spread_high, spread_rest = halves(spread_grad)
    grad_normed = (
        direct * upstream + total[:, :width] + mul(spread_high, table) + mul(spread_rest, table)
    )
    inverse = lax.rsqrt(jnp.mean(source * source, axis=-1, keepdims=True) + EPS)
    scaled = grad_normed * small[GAIN_TWO_AT : GAIN_TWO_AT + 1]
    result = (
        upstream
        + inverse * scaled
        - source * inverse**3 * jnp.mean(scaled * source, axis=-1, keepdims=True)
    )
    middle_grad[...] = result
    middle_low[...] = low(result)
    gain_row = jnp.sum(grad_normed * source * inverse, axis=0, keepdims=True)
    vector_high, vector_rest = halves(vector_share)
    by_normed = mul_tn(spread_high, normed[...]) + mul_tn(spread_rest, normed[...])
    by_upstream = mul_tn(vector_high, g[...]) + mul_tn(vector_rest, g[...])
    row = lax.broadcasted_iota(jnp.int32, (SMALL, width), 0)
    small_grad[...] = jnp.where(
        row == GAIN_TWO_AT, gain_row, by_normed[:SMALL] + by_upstream[:SMALL]
    )
    vectors = [small[VECTOR_AT + const : VECTOR_AT + const + 1] for const in range(2)]
    mixed = copy_share * normed_wide
    for const in range(2):
        mixed = mixed + const_share[const] * (
            mixing[const][0] * normed_wide + mixing[const][1] * vectors[const]
        )
    mixture[...] = source + mixed


def project_back(sizes, key_sums, query_grad, joint, normed, x_all, small_grad, row_parts, joint_parts, small_parts):
    head_count, blk_count = sizes
    tokens, width = row_parts.shape[1:]
    total = wide(key_sums[0])
    for step in range(1, key_sums.shape[0]):
        total = total + wide(key_sums[step])
    grads = jnp.concatenate([query_grad[...], low(total)], axis=1)
    grad_normed = mul_nt(grads, joint[...])
    row_parts[...] = low(grad_normed).reshape(head_count, tokens, width)
    source = wide(x_all[...])
    inverse = lax.rsqrt(jnp.mean(source * source, axis=-1, keepdims=True) + EPS)
    gain_row = jnp.sum(grad_normed * source * inverse, axis=0, keepdims=True)
    product = mul_tn(normed[...], grads)
    row = lax.broadcasted_iota(jnp.int32, (SMALL, width), 0)
    rows_all = jnp.where(row == GAIN_ONE_AT, gain_row, small_grad[...])
    turned = jnp.concatenate(
        [rows_all, jnp.zeros((128 - SMALL, width), jnp.float32)], axis=0
    ).T
    rows = width // (head_count * blk_count)
    filler = jnp.zeros((PAD - rows, product.shape[1]), jnp.float32)
    for head in range(head_count):
        for blk in range(blk_count):
            at = (head * blk_count + blk) * rows
            joint_parts[blk, head] = low(
                jnp.concatenate([product[at : at + rows], filler], axis=0)
            )
            small_parts[blk, head] = turned[at : at + rows]


def finish(sizes, rows_in, joint_in, out_in, small_in, x, small, middle_grad, input_grad, joint_sums, output_grad, small_sums):
    head_count, blk_count = sizes

    def total_of(ref):
        total = wide(ref[0])
        for step in range(1, ref.shape[0]):
            total = total + wide(ref[step])
        return total

    grad_normed = total_of(rows_in)
    source = wide(x[...])
    inverse = lax.rsqrt(jnp.mean(source * source, axis=-1, keepdims=True) + EPS)
    scaled = grad_normed * small[GAIN_ONE_AT : GAIN_ONE_AT + 1]
    input_grad[...] = (
        middle_grad[...]
        + inverse * scaled
        - source * inverse**3 * jnp.mean(scaled * source, axis=-1, keepdims=True)
    )
    joint_sums[...] = low(total_of(joint_in))
    output_grad[...] = total_of(out_in)[: output_grad.shape[0]]
    small_sums[...] = total_of(small_in)


def finish_layer(sizes, mixture, parts, layer_out):
    total = mixture[...]
    for step in range(parts.shape[0]):
        total = total + wide(parts[step])
    layer_out[...] = low(total)


def finish_experts(sizes, piece_0, piece_1, piece_2, piece_3, gate, up, down):
    head_count, blk_count = sizes
    mine = lax.axis_index("head")
    columns = piece_0.shape[2]
    for step, piece in enumerate((piece_0, piece_1, piece_2, piece_3)):
        source = (mine + head_count - step) % head_count
        at = pl.ds(pl.multiple_of(source * columns, columns), columns)
        gate[:, at] = wide(piece[0])
        up[:, at] = wide(piece[1])
        down[at, :] = wide(piece[2]).T


def after(values, *signals):
    return lax.optimization_barrier((values, signals))[0]


def around_heads(pieces_of, head_count):
    mine = lax.axis_index("head")
    pieces = []
    for step in range(head_count):
        piece = lax.dynamic_index_in_dim(
            pieces_of, (mine + step) % head_count, 0, keepdims=False
        )
        if step:
            piece = lax.ppermute(
                piece, "head", [(i, (i + step) % head_count) for i in range(head_count)]
            )
        pieces.append(piece)
    return pieces


def fast_shards(
    inputs,
    cotangent,
    segment,
    position,
    routes,
    gate_residual,
    first_gain,
    second_gain,
    query_key_weight,
    value_weight,
    output_weight,
    router_weight,
    const_gate,
    const_vectors,
    gate_weight,
    up_weight,
    down_weight,
):
    tokens, width = inputs.shape
    head_count = lax.axis_size("head")
    blk_count = lax.axis_size("blk")
    sizes = (head_count, blk_count)
    part = functools.partial
    half = blk_count // 2
    period = tokens * blk_count // CONT_LEN + 1
    head_width = width // head_count
    column_rows = head_count * tokens
    weight_rows = query_key_weight.shape[0]
    columns = gate_weight.shape[1] // head_count
    slot_rows = head_count * CAP

    def by_head(weight):
        return weight.reshape(weight_rows, head_count, head_width)

    query_part = by_head(query_key_weight[:, :width])
    key_part = by_head(query_key_weight[:, width:])
    value_part = by_head(value_weight)
    two = 2 * HEAD_DIM
    joint_pieces = jnp.concatenate(
        [
            query_part,
            jnp.zeros((weight_rows, head_count, HEAD_DIM), jnp.bfloat16),
            key_part,
            value_part[:, :, two:],
            value_part[:, :, :two],
        ],
        axis=2,
    ).transpose(1, 0, 2)
    joint_pieces = jnp.pad(joint_pieces, ((0, 0), (0, PAD - weight_rows), (0, 0)))
    joint_width = joint_pieces.shape[2]
    packed = jnp.concatenate(
        [
            output_weight,
            router_weight,
            const_gate,
            const_vectors,
            first_gain[:, None],
            second_gain[:, None],
        ],
        axis=1,
    )
    packed = jnp.pad(
        packed, ((0, PAD - weight_rows), (0, width + 128 - packed.shape[1]))
    )
    facts = jnp.concatenate(
        [
            jnp.stack([segment, position, routes[:, 0], routes[:, 1]]).astype(jnp.float32),
            jnp.zeros((4, tokens), jnp.float32),
            gate_residual.T,
            jnp.zeros((24 - 8 - ROUTED, tokens), jnp.float32),
        ],
        axis=0,
    )

    x_all, joint_all, packed_all, facts_all = exchange(
        part(send_tokens_and_weights, sizes),
        [
            shape((head_count, tokens, width)),
            shape((blk_count, head_count, PAD, joint_width)),
            shape((blk_count, head_count, PAD, width + 128)),
            shape((blk_count, head_count, 24, tokens), jnp.float32),
        ],
        [inputs, joint_pieces, packed, facts],
        [
            dma(4),
            dma(4, head_count - 1),
            dma(4, head_count - 1),
            dma(3, blk_count),
            dma(3, blk_count),
        ],
        0,
    )
    x_all = x_all.reshape(column_rows, width)
    expert_weights = jnp.stack([gate_weight, up_weight, down_weight.T])
    expert_weights = expert_weights.reshape(3, head_width, head_count, columns)
    expert_weights = after(expert_weights.transpose(2, 0, 1, 3), facts_all)
    expert_pieces = around_heads(expert_weights, head_count)

    normed, queries, pairs, joint, output, small = compute(
        part(project, sizes),
        [
            shape((column_rows, width)),
            shape((column_rows, 4 * HEAD_DIM)),
            shape((column_rows, 6 * HEAD_DIM)),
            shape((width, joint_width)),
            shape((width, width)),
            shape((SMALL, width), jnp.float32),
        ],
        [x_all, joint_all, packed_all],
        [
            pltpu.VMEM((width, joint_width), jnp.float32),
            pltpu.VMEM((width, width), jnp.float32),
            pltpu.VMEM((width, 128), jnp.float32),
        ],
    )
    pairs_all, g_all = exchange(
        part(send_keys, sizes),
        [shape((blk_count,) + pairs.shape), shape((head_count, tokens, width))],
        [pairs, cotangent],
        [
            dma(2),
            dma(head_count - 1),
            dma(head_count - 1),
            dma(1, blk_count),
            dma(1, blk_count),
        ],
        1,
    )
    pairs_all = pairs_all.reshape(blk_count * head_count, tokens, pairs.shape[1])
    marks = facts_all[:, :, 0:2, 0].astype(jnp.int32).reshape(blk_count * head_count, 2)
    segments, positions = marks[:, 0], marks[:, 1]
    lists = [
        pltpu.SMEM((blk_count * head_count + CHUNK,), jnp.int32),
        pltpu.SMEM((blk_count * head_count + CHUNK,), jnp.int32),
    ]
    attended, totals = compute(
        part(attend, sizes, period),
        [
            shape((head_width, column_rows)),
            shape((head_count, 8, 3 * tokens), jnp.float32),
        ],
        [segments, positions, queries, pairs_all],
        lists,
        2,
    )
    first, second, upstream_slots = compute(
        part(place_upstream, sizes),
        [
            shape((head_count, EXPERTS * CAP, tokens)),
            shape((head_count, EXPERTS * CAP, tokens)),
            shape((EXPERTS, slot_rows, width)),
        ],
        [facts_all, g_all],
    )
    attended_all, grads_in = exchange(
        part(send_attended, sizes),
        [shape((head_count, head_width, column_rows)), shape((blk_count, slot_rows, width))],
        [attended, upstream_slots],
        [
            dma(2),
            dma(head_count - 1),
            dma(head_count - 1),
            dma(blk_count - 1),
            dma(blk_count - 1),
        ],
        2,
    )
    slots, middle, normed_two, weights = compute(
        part(route, sizes),
        [
            shape((EXPERTS, slot_rows, width + 128)),
            shape((tokens, width), jnp.float32),
            shape((tokens, width)),
            shape((head_count, 8, tokens), jnp.float32),
        ],
        [
            x_all,
            attended_all.reshape(width, column_rows),
            output,
            small,
            facts_all,
            first,
            second,
        ],
        [
            pltpu.VMEM((column_rows, width), jnp.float32),
            pltpu.VMEM((column_rows, width), jnp.bfloat16),
        ],
    )
    (slots_in,) = exchange(
        part(send_slots, sizes),
        [shape(slots.shape)],
        [slots],
        [dma(1), dma(blk_count - 1), dma(blk_count - 1)],
        3,
    )
    slot_total = blk_count * slot_rows
    back, outs, weight_grads = compute(
        part(run_experts, sizes),
        [
            shape((blk_count, slot_rows, width + 128)),
            shape((blk_count, slot_rows, width)),
            shape((head_count, 3, head_width, columns)),
        ],
        [slots_in, grads_in] + expert_pieces,
        [
            pltpu.VMEM((3, head_count, head_width, columns), jnp.bfloat16),
            pltpu.VMEM((slot_total, columns), jnp.bfloat16),
            pltpu.VMEM((slot_total, columns), jnp.bfloat16),
            pltpu.VMEM((slot_total, columns), jnp.bfloat16),
            pltpu.VMEM((slot_total, width), jnp.bfloat16),
        ],
    )
    (back_in,) = exchange(
        part(send_slots, sizes),
        [shape(back.shape)],
        [back],
        [dma(1), dma(blk_count - 1), dma(blk_count - 1)],
        4,
    )
    (grad_parts,) = compute(
        part(combine_grads, sizes),
        [shape((head_count, tokens, width + 128))],
        [back_in, first, second],
    )
    parts_in, outs_in = exchange(
        part(send_shares, sizes),
        [shape(grad_parts.shape), shape(outs.shape)],
        [grad_parts, outs],
        [
            dma(2),
            dma(head_count - 1),
            dma(head_count - 1),
            dma(blk_count - 1),
            dma(blk_count - 1),
        ],
        5,
    )
    middle_grad, middle_low, residual_grad, small_grad, mixture = compute(
        part(at_home, sizes),
        [
            shape((tokens, width), jnp.float32),
            shape((tokens, width)),
            shape((tokens, 128), jnp.float32),
            shape((SMALL, width), jnp.float32),
            shape((tokens, width), jnp.float32),
        ],
        [parts_in, middle, normed_two, cotangent, small, weights, facts_all],
    )
    (middle_all,) = exchange(
        part(send_middle, sizes),
        [shape((head_count, tokens, width))],
        [middle_low],
        [dma(1), dma(head_count - 1), dma(head_count - 1)],
        6,
    )
    weight_grads = after(weight_grads, middle_all)
    grad_pieces = around_heads(weight_grads, head_count)
    (out_parts,) = compute(
        part(combine_outs, sizes),
        [shape((head_count, tokens, width))],
        [outs_in, first, second, weights],
    )
    query_grad, pair_grad, output_parts = compute(
        part(attend_back, sizes, period),
        [
            shape(queries.shape),
            shape(pairs_all.shape),
            shape((blk_count, PAD, width)),
        ],
        [
            segments,
            positions,
            queries,
            pairs_all,
            attended,
            totals,
            middle_all.reshape(column_rows, width),
            output,
        ],
        lists + [pltpu.VMEM(pairs_all.shape, jnp.float32)],
        2,
    )
    key_sums, out_parts_in = exchange(
        part(send_key_sums, sizes),
        [shape((half, column_rows, pairs.shape[1])), shape(out_parts.shape)],
        [pair_grad.reshape(blk_count, column_rows, pairs.shape[1]), out_parts],
        [
            pltpu.VMEM((half, column_rows, pairs.shape[1]), jnp.bfloat16),
            pltpu.VMEM((half, column_rows, pairs.shape[1]), jnp.bfloat16),
            dma(half + 2),
            dma(head_count - 1),
            dma(head_count - 1),
            dma(half),
            dma(half),
            dma(half - 1),
            dma(half - 1),
        ],
        7,
    )
    row_parts, joint_parts, small_parts = compute(
        part(project_back, sizes),
        [
            shape((head_count, tokens, width)),
            shape((blk_count, head_count, PAD, joint_width)),
            shape((blk_count, head_count, weight_rows, 128), jnp.float32),
        ],
        [key_sums, query_grad, joint, normed, x_all, small_grad],
    )
    rows_in, joint_in, out_in, small_in = exchange(
        part(send_gradients, sizes),
        [
            shape(row_parts.shape),
            shape(joint_parts.shape),
            shape(output_parts.shape),
            shape(small_parts.shape, jnp.float32),
        ],
        [row_parts, joint_parts, output_parts, small_parts],
        [
            dma(4),
            dma(head_count - 1),
            dma(head_count - 1),
            dma(3, blk_count - 1),
            dma(3, blk_count - 1),
        ],
        8,
    )
    input_grad, joint_sums, output_grad, small_sums = compute(
        part(finish, sizes),
        [
            shape((tokens, width), jnp.float32),
            shape((head_count, PAD, joint_width)),
            shape((weight_rows, width), jnp.float32),
            shape((head_count, weight_rows, 128), jnp.float32),
        ],
        [rows_in, joint_in, out_in, small_in, inputs, small, middle_grad],
    )
    joint_out, small_out = exchange(
        part(send_weight_sums, sizes),
        [shape(joint_sums.shape), shape(small_sums.shape, jnp.float32)],
        [joint_sums, small_sums],
        [dma(2), dma(2, head_count - 1), dma(2, head_count - 1)],
        9,
    )
    (layer_out,) = compute(
        part(finish_layer, sizes), [shape((tokens, width))], [mixture, out_parts_in]
    )
    grad_pieces = after(grad_pieces, joint_out)
    gate_grad, up_grad, down_grad = compute(
        part(finish_experts, sizes),
        [
            shape(gate_weight.shape, jnp.float32),
            shape(up_weight.shape, jnp.float32),
            shape(down_weight.shape, jnp.float32),
        ],
        grad_pieces,
    )
    joint_rows = joint_out[:, :weight_rows].astype(jnp.float32).transpose(1, 0, 2)

    def lanes_of(*spans):
        return jnp.concatenate(
            [joint_rows[:, :, first:last] for first, last in spans], axis=2
        ).reshape(weight_rows, width)

    small_total = jnp.sum(small_out, axis=0)
    joint_grad = jnp.concatenate([lanes_of((0, 192)), lanes_of((256, 448))], axis=1)
    value_grad = lanes_of((512, 640), (448, 512))
    return (
        layer_out,
        input_grad,
        residual_grad[:, :ROUTED],
        small_total[:, GAIN_ONE_AT],
        small_total[:, GAIN_TWO_AT],
        joint_grad,
        value_grad,
        output_grad,
        small_total[:, ROUTER_AT : ROUTER_AT + ROUTED],
        small_total[:, MIX_AT : MIX_AT + 4],
        small_total[:, VECTOR_AT : VECTOR_AT + 2],
        gate_grad,
        up_grad,
        down_grad,
    )


def solution(mesh):
    body = fast_shards if mesh.shape["blk"] == EXPERTS else shards
    in_specs = (
        P(("head", "blk"), None),
        P(("head", "blk"), None),
        P(("head", "blk")),
        P(("head", "blk")),
        P(("head", "blk"), None),
        P(("head", "blk"), None),
        P(("head", "blk")),
        P(("head", "blk")),
        P(("head", "blk"), None),
        P(("head", "blk"), None),
        P(("head", "blk"), None),
        P(("head", "blk"), None),
        P(("head", "blk"), None),
        P(("head", "blk"), None),
        P("head", "blk"),
        P("head", "blk"),
        P("blk", "head"),
    )
    out_specs = (
        P(("head", "blk"), None),
        P(("head", "blk"), None),
        P(("head", "blk"), None),
        P(("head", "blk")),
        P(("head", "blk")),
        P(("head", "blk"), None),
        P(("head", "blk"), None),
        P(("head", "blk"), None),
        P(("head", "blk"), None),
        P(("head", "blk"), None),
        P(("head", "blk"), None),
        P("head", "blk"),
        P("head", "blk"),
        P("blk", "head"),
    )
    return jax.shard_map(body, mesh=mesh, in_specs=in_specs, out_specs=out_specs, check_vma=False)
```

```python
import functools

import jax
import jax.numpy as jnp
from jax import lax
from jax.experimental import pallas as pl
from jax.experimental.pallas import tpu as pltpu
from jax.sharding import PartitionSpec as P

HEADS = 12
HEAD_DIM = 64
EXPERTS = 8
ROUTED = 12
TOP = 2
CONT_LEN = 1024
CAP = 24


EPS = 1e-06
HIGH = lax.Precision.HIGHEST


def silu_slope(pre):
    sigmoid_value = jax.nn.sigmoid(pre)
    return sigmoid_value * (1.0 + pre * (1.0 - sigmoid_value))


def visible_pairs(query_segment, query_position, key_segment, key_position, period):
    same_sequence = (query_segment[:, None] == key_segment[None, :]) & (
        key_position[None, :] <= query_position[:, None]
    )
    same_group = query_segment[:, None] // period == key_segment[None, :] // period
    shared = (
        (key_segment[None, :] % period == 0) & (query_segment[:, None] % period != 0) & same_group
    )
    return same_sequence | shared


def norm_back(grad_normed, source, inverse, gain):
    scaled = grad_normed * gain
    grad_source = inverse * scaled - source * inverse**3 * jnp.mean(
        scaled * source, axis=-1, keepdims=True
    )
    grad_gain = jnp.sum(grad_normed * source * inverse, axis=0)
    return (grad_source, grad_gain)


def around_blocks(pieces, combine, initial):
    return combine(
        initial,
        (
            lax.all_gather(pieces[0], "blk", axis=0, tiled=True),
            lax.all_gather(pieces[1], "blk", axis=0, tiled=True),
        ),
        jnp.int32(0),
    )


def softmax_last(logits):
    highest = jnp.max(logits, axis=-1, keepdims=True)
    raised = jnp.exp(logits - highest)
    return raised / jnp.sum(raised, axis=-1, keepdims=True)


def shards(
    inputs,
    cotangent,
    segment,
    position,
    routes,
    gate_residual,
    first_gain,
    second_gain,
    query_key_weight,
    value_weight,
    output_weight,
    router_weight,
    const_gate,
    const_vectors,
    gate_weight,
    up_weight,
    down_weight,
):
    tok_rows, width = inputs.shape
    head_count = lax.axis_size("head")
    blk_count = lax.axis_size("blk")
    local_heads = HEADS // head_count
    query_rows = head_count * tok_rows
    head_width = width // head_count
    width_split = blk_count // EXPERTS
    score_scale = HEAD_DIM ** (-0.5)
    period = tok_rows * blk_count // CONT_LEN + 1
    gathered = (
        lax.all_gather(first_gain, ("head", "blk"), axis=0, tiled=True),
        lax.all_gather(second_gain, ("head", "blk"), axis=0, tiled=True),
        lax.all_gather(query_key_weight, ("head", "blk"), axis=0, tiled=True),
        lax.all_gather(value_weight, ("head", "blk"), axis=0, tiled=True),
        lax.all_gather(output_weight, ("head", "blk"), axis=0, tiled=True),
        lax.all_gather(router_weight, ("head", "blk"), axis=0, tiled=True),
        lax.all_gather(const_gate, ("head", "blk"), axis=0, tiled=True),
        lax.all_gather(const_vectors, ("head", "blk"), axis=0, tiled=True),
        lax.all_gather(segment, ("head", "blk"), axis=0, tiled=True),
        lax.all_gather(position, ("head", "blk"), axis=0, tiled=True),
    )
    (
        gain_one,
        gain_two,
        full_joint,
        full_value,
        full_output,
        full_router,
        full_const,
        full_vectors,
        segment_all,
        position_all,
    ) = gathered
    gate_columns, up_columns, down_rows = (
        lax.all_gather(gate_weight, "head", axis=0, tiled=True),
        lax.all_gather(up_weight, "head", axis=0, tiled=True),
        lax.all_gather(down_weight, "head", axis=1, tiled=True),
    )
    gain_one = gain_one.astype(jnp.float32)
    gain_two = gain_two.astype(jnp.float32)
    source = inputs.astype(jnp.float32)
    inverse_one = lax.rsqrt(jnp.mean(source * source, axis=-1, keepdims=True) + EPS)
    normed_one = (source * inverse_one * gain_one).astype(jnp.bfloat16)
    joined = jnp.dot(normed_one, full_joint, preferred_element_type=jnp.float32)
    value_proj = jnp.dot(normed_one, full_value, preferred_element_type=jnp.float32)

    def head_layout(array):
        return array.astype(jnp.bfloat16).reshape(tok_rows, head_count, head_width)

    query_heads, key_heads, value_heads = (
        lax.all_to_all(
            head_layout(joined[:, :width]), "head", split_axis=1, concat_axis=0, tiled=True
        ),
        lax.all_to_all(
            head_layout(joined[:, width:]), "head", split_axis=1, concat_axis=0, tiled=True
        ),
        lax.all_to_all(head_layout(value_proj), "head", split_axis=1, concat_axis=0, tiled=True),
    )
    query_heads = query_heads.reshape(query_rows, local_heads, HEAD_DIM)
    key_heads = key_heads.reshape(query_rows, head_width)
    value_heads = value_heads.reshape(query_rows, head_width)
    blk_index = lax.axis_index("blk")
    segment_grid = segment_all.reshape(head_count, blk_count, tok_rows)
    position_grid = position_all.reshape(head_count, blk_count, tok_rows)
    query_segment = lax.dynamic_index_in_dim(segment_grid, blk_index, 1, keepdims=False).reshape(
        query_rows
    )
    query_position = lax.dynamic_index_in_dim(position_grid, blk_index, 1, keepdims=False).reshape(
        query_rows
    )
    key_segment = segment_grid.transpose(1, 0, 2).reshape(blk_count * query_rows)
    key_position = position_grid.transpose(1, 0, 2).reshape(blk_count * query_rows)

    def key_slices(pieces):
        piece_rows = pieces[0].shape[0]
        step_count = piece_rows // tok_rows
        return (
            pieces[0].reshape(step_count, tok_rows, local_heads, HEAD_DIM),
            pieces[1].reshape(step_count, tok_rows, local_heads, HEAD_DIM),
            key_segment.reshape(step_count, tok_rows),
            key_position.reshape(step_count, tok_rows),
        )

    def masked_scores(queries, block_keys, visible):
        scores = (
            jnp.einsum("qhd,khd->hqk", queries, block_keys, preferred_element_type=jnp.float32)
            * score_scale
        )
        return jnp.where(visible[None], scores, -jnp.inf)

    def attend_block(carried, block):
        block_keys, block_values, block_segment, block_position = block
        visible = visible_pairs(
            query_segment, query_position, block_segment, block_position, period
        )

        def attend_compute(state):
            top_score, running_total, weighted = state
            scores = masked_scores(query_heads, block_keys, visible)
            new_top = jnp.maximum(top_score, jnp.max(scores, axis=-1))
            anchor = jnp.where(new_top == -jnp.inf, 0.0, new_top)
            raised = jnp.exp(scores - anchor[..., None])
            factor = jnp.exp(top_score - anchor)
            running_total = running_total * factor + jnp.sum(raised, axis=-1)
            weighted = weighted * factor[..., None] + jnp.einsum(
                "hqk,khd->hqd",
                raised.astype(jnp.bfloat16),
                block_values,
                preferred_element_type=jnp.float32,
            )
            return (new_top, running_total, weighted)

        def unchanged(state):
            return state

        return (lax.cond(jnp.any(visible), attend_compute, unchanged, carried), None)

    def attend_piece(carried, pieces, first_row):
        result, unused = lax.scan(attend_block, carried, key_slices(pieces))
        return result

    start_state = (
        jnp.full((local_heads, query_rows), -jnp.inf, jnp.float32),
        jnp.zeros((local_heads, query_rows), jnp.float32),
        jnp.zeros((local_heads, query_rows, HEAD_DIM), jnp.float32),
    )
    top_score, running_total, weighted = around_blocks(
        (key_heads, value_heads), attend_piece, start_state
    )
    log_total = top_score + jnp.log(running_total)
    attended_local = (weighted / running_total[..., None]).transpose(1, 0, 2).astype(jnp.bfloat16)
    attended = lax.all_to_all(
        attended_local.reshape(query_rows, 1, head_width),
        "head",
        split_axis=0,
        concat_axis=1,
        tiled=True,
    ).reshape(tok_rows, width)
    middle = source + jnp.dot(attended, full_output, preferred_element_type=jnp.float32)
    inverse_two = lax.rsqrt(jnp.mean(middle * middle, axis=-1, keepdims=True) + EPS)
    normed_two = (middle * inverse_two * gain_two).astype(jnp.bfloat16)
    normed_float = normed_two.astype(jnp.float32)
    logits = jnp.dot(normed_two, full_router, preferred_element_type=jnp.float32) + gate_residual
    choose = (routes[:, :, None] == jnp.arange(ROUTED, dtype=jnp.int32)[None, None, :]).astype(
        jnp.float32
    )
    picked = jnp.sum(choose * logits[:, None, :], axis=-1)
    weighting = softmax_last(picked)
    pair_expert = routes.reshape(tok_rows * TOP)
    ffn_onehot = (pair_expert[:, None] == jnp.arange(EXPERTS, dtype=jnp.int32)[None, :]).astype(
        jnp.int32
    )
    pair_rank = jnp.sum((jnp.cumsum(ffn_onehot, axis=0) - ffn_onehot) * ffn_onehot, axis=-1)
    slot_match = (
        pair_rank[None, None, :] == jnp.arange(CAP, dtype=jnp.int32)[None, :, None]
    ).astype(jnp.int32)
    placement = (
        (ffn_onehot.T[:, None, :] * slot_match)
        .reshape(EXPERTS, CAP, tok_rows, TOP)
        .astype(jnp.float32)
    )
    select = jnp.sum(placement, axis=-1)
    gate_slot = jnp.einsum("ectj,tj->ect", placement, weighting, precision=HIGH)
    send_rows = jnp.einsum(
        "ect,td->ecd", select.astype(jnp.bfloat16), normed_two, preferred_element_type=jnp.float32
    ).astype(jnp.bfloat16)
    upstream = cotangent.astype(jnp.float32)
    slot_grad = jnp.einsum("ect,td->ecd", gate_slot, upstream, precision=HIGH).astype(jnp.bfloat16)
    rows_in = lax.all_to_all(
        jnp.repeat(send_rows, width_split, axis=0), "blk", split_axis=0, concat_axis=0, tiled=True
    )
    grads_in = lax.all_to_all(
        jnp.repeat(slot_grad, width_split, axis=0), "blk", split_axis=0, concat_axis=0, tiled=True
    )
    gate_pre = jnp.einsum("scd,df->scf", rows_in, gate_columns, preferred_element_type=jnp.float32)
    up_pre = jnp.einsum("scd,df->scf", rows_in, up_columns, preferred_element_type=jnp.float32)
    activated = jax.nn.silu(gate_pre)
    hidden = (activated * up_pre).astype(jnp.bfloat16)
    partial_out = jnp.einsum("scf,fd->scd", hidden, down_rows, preferred_element_type=jnp.float32)
    grad_hidden = jnp.einsum("scd,fd->scf", grads_in, down_rows, preferred_element_type=jnp.float32)
    grad_gate_pre = (grad_hidden * up_pre * silu_slope(gate_pre)).astype(jnp.bfloat16)
    grad_up_pre = (grad_hidden * activated).astype(jnp.bfloat16)
    grad_part = jnp.einsum(
        "scf,df->scd", grad_gate_pre, gate_columns, preferred_element_type=jnp.float32
    ) + jnp.einsum("scf,df->scd", grad_up_pre, up_columns, preferred_element_type=jnp.float32)
    back_out = lax.all_to_all(
        partial_out.astype(jnp.bfloat16), "blk", split_axis=0, concat_axis=0, tiled=True
    ).astype(partial_out.dtype)
    back_grad = lax.all_to_all(
        grad_part.astype(jnp.bfloat16), "blk", split_axis=0, concat_axis=0, tiled=True
    ).astype(grad_part.dtype)
    returned, grad_back, kept_rows, kept_grads, hidden, grad_gate_pre, grad_up_pre = (
        back_out,
        back_grad,
        rows_in,
        grads_in,
        hidden,
        grad_gate_pre,
        grad_up_pre,
    )
    expert_out = returned.reshape(EXPERTS, width_split, CAP, width).sum(axis=1)
    ffn_sum = jnp.einsum("ect,ecd->td", gate_slot, expert_out, precision=HIGH)
    mixing = softmax_last(
        jnp.dot(normed_two, full_const, preferred_element_type=jnp.float32).reshape(tok_rows, 2, 2)
    )
    vectors = full_vectors.astype(jnp.float32)
    copy_share = jnp.sum(weighting * (routes == EXPERTS + 1).astype(jnp.float32), axis=-1)
    const_share = jnp.stack(
        [
            jnp.sum(weighting * (routes == EXPERTS + 2 + const_index).astype(jnp.float32), axis=-1)
            for const_index in range(2)
        ],
        axis=1,
    )
    const_outs = [
        mixing[:, const_index, 0:1] * normed_float
        + mixing[:, const_index, 1:2] * vectors[:, const_index][None, :]
        for const_index in range(2)
    ]
    mixture = ffn_sum + copy_share[:, None] * normed_float
    for const_index in range(2):
        mixture = mixture + const_share[:, const_index : const_index + 1] * const_outs[const_index]
    layer_out = (middle + mixture).astype(jnp.bfloat16)
    output_dots = jnp.einsum("ecd,td->ect", expert_out, upstream, precision=HIGH)
    grad_weighting = jnp.einsum("ectj,ect->tj", placement, output_dots, precision=HIGH)
    copy_dot = jnp.sum(upstream * normed_float, axis=-1)
    grad_weighting = (
        grad_weighting + (routes == EXPERTS + 1).astype(jnp.float32) * copy_dot[:, None]
    )
    for const_index in range(2):
        const_dot = jnp.sum(upstream * const_outs[const_index], axis=-1)
        grad_weighting = (
            grad_weighting
            + (routes == EXPERTS + 2 + const_index).astype(jnp.float32) * const_dot[:, None]
        )
    grad_picked = weighting * (
        grad_weighting - jnp.sum(weighting * grad_weighting, axis=-1, keepdims=True)
    )
    grad_logits = jnp.einsum("tj,tjr->tr", grad_picked, choose, precision=HIGH)
    vector_dots = jnp.dot(upstream, vectors, precision=HIGH)
    grad_mixing = const_share[:, :, None] * jnp.stack(
        [jnp.broadcast_to(copy_dot[:, None], vector_dots.shape), vector_dots], axis=-1
    )
    grad_mix = (
        mixing * (grad_mixing - jnp.sum(mixing * grad_mixing, axis=-1, keepdims=True))
    ).reshape(tok_rows, 4)
    grad_const_weight = jnp.dot(normed_float.T, grad_mix, precision=HIGH)
    grad_vectors = jnp.einsum("ti,td->di", const_share * mixing[:, :, 1], upstream, precision=HIGH)
    grad_router_weight = jnp.dot(normed_float.T, grad_logits, precision=HIGH)
    direct_share = (
        copy_share + const_share[:, 0] * mixing[:, 0, 0] + const_share[:, 1] * mixing[:, 1, 0]
    )
    grad_normed_two = direct_share[:, None] * upstream
    grad_normed_two = grad_normed_two + jnp.dot(
        grad_mix, full_const.astype(jnp.float32).T, precision=HIGH
    )
    grad_normed_two = grad_normed_two + jnp.dot(
        grad_logits, full_router.astype(jnp.float32).T, precision=HIGH
    )
    grad_down_local = jnp.einsum(
        "scf,scd->fd", hidden, kept_grads, preferred_element_type=jnp.float32
    )
    grad_gate_local = jnp.einsum(
        "scd,scf->df", kept_rows, grad_gate_pre, preferred_element_type=jnp.float32
    )
    grad_up_local = jnp.einsum(
        "scd,scf->df", kept_rows, grad_up_pre, preferred_element_type=jnp.float32
    )
    grad_slots = grad_back.reshape(EXPERTS, width_split, CAP, width).sum(axis=1)
    grad_normed_two = grad_normed_two + jnp.einsum(
        "ect,ecd->td", select, grad_slots, precision=HIGH
    )
    grad_gate_sum, grad_up_sum, grad_down_sum = (
        lax.psum_scatter(
            grad_gate_local.astype(jnp.bfloat16), "head", scatter_dimension=0, tiled=True
        ).astype(jnp.float32),
        lax.psum_scatter(
            grad_up_local.astype(jnp.bfloat16), "head", scatter_dimension=0, tiled=True
        ).astype(jnp.float32),
        lax.psum_scatter(
            grad_down_local.astype(jnp.bfloat16), "head", scatter_dimension=1, tiled=True
        ).astype(jnp.float32),
    )
    grad_from_norm, grad_gain_two = norm_back(grad_normed_two, middle, inverse_two, gain_two)
    grad_middle = upstream + grad_from_norm
    branch_grad = grad_middle.astype(jnp.bfloat16)
    grad_out_weight = jnp.einsum(
        "tc,td->cd", attended, branch_grad, preferred_element_type=jnp.float32
    )
    grad_attended = jnp.einsum(
        "td,cd->tc", branch_grad, full_output, preferred_element_type=jnp.float32
    ).astype(jnp.bfloat16)
    grad_heads = lax.all_to_all(
        grad_attended.reshape(tok_rows, head_count, head_width),
        "head",
        split_axis=1,
        concat_axis=0,
        tiled=True,
    )
    grad_heads = grad_heads.reshape(query_rows, local_heads, HEAD_DIM)
    offset = jnp.sum(grad_heads.astype(jnp.float32) * attended_local.astype(jnp.float32), axis=-1).T

    def probe_block(queries, grads, lse_rows, offset_rows, block_keys, block_values, visible):
        scores = masked_scores(queries, block_keys, visible)
        probabilities = jnp.exp(scores - lse_rows[..., None])
        grad_probs = jnp.einsum(
            "qhd,khd->hqk", grads, block_values, preferred_element_type=jnp.float32
        )
        grad_scores = (probabilities * (grad_probs - offset_rows[..., None])).astype(jnp.bfloat16)
        return (probabilities, grad_scores)

    zero_query = jnp.zeros((query_rows, local_heads, HEAD_DIM), jnp.float32)

    def backward_block(grad_query, block):
        block_keys, block_values, block_segment, block_position = block
        visible = visible_pairs(
            query_segment, query_position, block_segment, block_position, period
        )

        def backward_compute(accumulated):
            probabilities, grad_scores = probe_block(
                query_heads, grad_heads, log_total, offset, block_keys, block_values, visible
            )
            grad_values = jnp.einsum(
                "hqk,qhd->khd",
                probabilities.astype(jnp.bfloat16),
                grad_heads,
                preferred_element_type=jnp.float32,
            )
            accumulated = (
                accumulated
                + jnp.einsum(
                    "hqk,khd->qhd", grad_scores, block_keys, preferred_element_type=jnp.float32
                )
                * score_scale
            )
            grad_keys = (
                jnp.einsum(
                    "hqk,qhd->khd", grad_scores, query_heads, preferred_element_type=jnp.float32
                )
                * score_scale
            )
            return (accumulated, jnp.concatenate([grad_keys, grad_values], axis=-1))

        def skipped(accumulated):
            return (
                accumulated,
                jnp.zeros((block_keys.shape[0], local_heads, 2 * HEAD_DIM), jnp.float32),
            )

        return lax.cond(jnp.any(visible), backward_compute, skipped, grad_query)

    def fold_back(carried, pieces, first_row):
        grad_query, stacked = lax.scan(backward_block, carried[0], key_slices(pieces))
        term_piece = stacked.reshape(pieces[0].shape[0], local_heads * 2 * HEAD_DIM)
        return (grad_query, term_piece)

    zero_term = jnp.zeros((blk_count * query_rows, local_heads * 2 * HEAD_DIM), jnp.float32)
    grad_query, key_term = around_blocks(
        (key_heads, value_heads), fold_back, (zero_query, zero_term)
    )
    key_sums = lax.psum_scatter(key_term, "blk", scatter_dimension=0, tiled=True).reshape(
        query_rows, local_heads, 2, HEAD_DIM
    )
    grad_key_heads = key_sums[:, :, 0].astype(jnp.bfloat16).reshape(query_rows, 1, head_width)
    grad_value_heads = key_sums[:, :, 1].astype(jnp.bfloat16).reshape(query_rows, 1, head_width)
    grad_query_heads = grad_query.astype(jnp.bfloat16).reshape(query_rows, 1, head_width)
    grad_query_tok, grad_key_tok, grad_value_tok = (
        lax.all_to_all(grad_query_heads, "head", split_axis=0, concat_axis=1, tiled=True),
        lax.all_to_all(grad_key_heads, "head", split_axis=0, concat_axis=1, tiled=True),
        lax.all_to_all(grad_value_heads, "head", split_axis=0, concat_axis=1, tiled=True),
    )
    grad_joined = jnp.concatenate(
        [grad_query_tok.reshape(tok_rows, width), grad_key_tok.reshape(tok_rows, width)], axis=1
    )
    grad_value_tok = grad_value_tok.reshape(tok_rows, width)
    grad_normed_one = jnp.einsum(
        "tc,dc->td", grad_joined, full_joint, preferred_element_type=jnp.float32
    ) + jnp.einsum("tc,dc->td", grad_value_tok, full_value, preferred_element_type=jnp.float32)
    grad_joint_weight = jnp.einsum(
        "td,tc->dc", normed_one, grad_joined, preferred_element_type=jnp.float32
    )
    grad_value_weight = jnp.einsum(
        "td,tc->dc", normed_one, grad_value_tok, preferred_element_type=jnp.float32
    )
    grad_from_first, grad_gain_one = norm_back(grad_normed_one, source, inverse_one, gain_one)
    grad_input = grad_middle + grad_from_first
    summed = (
        lax.psum_scatter(grad_gain_one, ("head", "blk"), scatter_dimension=0, tiled=True),
        lax.psum_scatter(grad_gain_two, ("head", "blk"), scatter_dimension=0, tiled=True),
        lax.psum_scatter(grad_joint_weight, ("head", "blk"), scatter_dimension=0, tiled=True),
        lax.psum_scatter(grad_value_weight, ("head", "blk"), scatter_dimension=0, tiled=True),
        lax.psum_scatter(grad_out_weight, ("head", "blk"), scatter_dimension=0, tiled=True),
        lax.psum_scatter(grad_router_weight, ("head", "blk"), scatter_dimension=0, tiled=True),
        lax.psum_scatter(grad_const_weight, ("head", "blk"), scatter_dimension=0, tiled=True),
        lax.psum_scatter(grad_vectors, ("head", "blk"), scatter_dimension=0, tiled=True),
    )
    return (
        layer_out,
        grad_input,
        grad_logits,
        summed[0],
        summed[1],
        summed[2],
        summed[3],
        summed[4],
        summed[5],
        summed[6],
        summed[7],
        grad_gate_sum,
        grad_up_sum,
        grad_down_sum,
    )


MESH = pl.DeviceIdType.MESH
SMALL = 24
ROUTER_AT, MIX_AT, VECTOR_AT, GAIN_ONE_AT, GAIN_TWO_AT = 0, 12, 16, 18, 19
PAD = 32
CHUNK = 4
FAR = 1 << 20
NT = (((1,), (1,)), ((), ()))
TN = (((0,), (0,)), ((), ()))


def mul(left, right):
    return jnp.dot(left, right, preferred_element_type=jnp.float32)


def mul_nt(left, right):
    return lax.dot_general(left, right, NT, preferred_element_type=jnp.float32)


def mul_tn(left, right):
    return lax.dot_general(left, right, TN, preferred_element_type=jnp.float32)


def low(values):
    return values.astype(jnp.bfloat16)


def wide(values):
    return values.astype(jnp.float32)


def halves(values):
    high = low(values)
    return high, low(values - wide(high))


def shape(dims, dtype=jnp.bfloat16):
    return jax.ShapeDtypeStruct(dims, dtype)


def compute(body, outs, ins, scratch=(), smem=0):
    specs = [pl.BlockSpec(memory_space=pltpu.SMEM)] * smem
    specs += [pl.BlockSpec(memory_space=pltpu.VMEM)] * (len(ins) - smem)
    return pl.pallas_call(
        body,
        out_shape=outs,
        in_specs=specs,
        out_specs=[pl.BlockSpec(memory_space=pltpu.VMEM)] * len(outs),
        scratch_shapes=list(scratch),
        compiler_params=pltpu.CompilerParams(vmem_limit_bytes=52 * 2**20),
    )(*ins)


def exchange(body, outs, ins, scratch, number, far_ins=(), far_outs=()):
    def spec(index, far):
        return pl.BlockSpec(memory_space=pl.ANY if index in far else pltpu.VMEM)

    return pl.pallas_call(
        body,
        out_shape=outs,
        in_specs=[spec(index, far_ins) for index in range(len(ins))],
        out_specs=[spec(index, far_outs) for index in range(len(outs))],
        scratch_shapes=list(scratch),
        compiler_params=pltpu.CompilerParams(
            collective_id=number, has_side_effects=True, vmem_limit_bytes=52 * 2**20
        ),
    )(*ins)


def greet(devices):
    barrier = pltpu.get_barrier_semaphore()
    for device in devices:
        pl.semaphore_signal(barrier, inc=1, device_id=device, device_id_type=MESH)


def greeted(count):
    pl.semaphore_wait(pltpu.get_barrier_semaphore(), count)


def meet(devices):
    greet(devices)
    greeted(len(devices))


class Place:
    def __init__(self, head_count, blk_count):
        self.head_count, self.blk_count = head_count, blk_count
        self.head, self.blk = lax.axis_index("head"), lax.axis_index("blk")
        self.half = blk_count // 2
        self.chip, self.core = self.blk // 2, self.blk % 2
        self.twin = self.blk + 1 - 2 * self.core

    def along(self, axis):
        if axis == "head":
            return self.head, self.head_count
        return self.blk, self.blk_count

    def device(self, axis, index):
        return (index, self.blk) if axis == "head" else (self.head, index)

    def others(self, axis):
        me, size = self.along(axis)
        return [self.device(axis, (me + step) % size) for step in range(1, size)]

    def chips(self):
        return [((self.chip + step) % self.half) * 2 + self.core for step in range(1, self.half)]

    def near(self):
        return [(self.head, self.twin)] + [(self.head, blk) for blk in self.chips()]


def dma(*dims):
    return pltpu.SemaphoreType.DMA(dims)


def send(source, target, sent, got, device):
    copy = pltpu.make_async_remote_copy(
        src_ref=source,
        dst_ref=target,
        send_sem=sent,
        recv_sem=got,
        device_id=device,
        device_id_type=MESH,
    )
    copy.start()
    return copy


def keep(source, target, done):
    copy = pltpu.make_async_copy(source, target, done)
    copy.start()
    return copy


def scatter(place, axis, source, target, sent, got):
    me, size = place.along(axis)
    copies = []
    for step in range(1, size):
        other = (me + step) % size
        copies.append(
            send(
                source.at[other],
                target.at[me],
                sent.at[step - 1],
                got.at[step - 1],
                place.device(axis, other),
            )
        )
    return copies


def gather(place, axis, source, target, sent, got):
    me, size = place.along(axis)
    copies = []
    for step in range(1, size):
        other = (me + step) % size
        copies.append(
            send(
                source, target.at[me], sent.at[step - 1], got.at[step - 1], place.device(axis, other)
            )
        )
    return copies


class Spread:
    def __init__(self, place, ref, sent, got):
        self.place, self.ref, self.sent, self.got = place, ref, sent, got
        self.direct = [
            self.pass_on(step, place.blk, blk) for step, blk in enumerate(place.chips(), 1)
        ]
        self.rest = [self.pass_on(0, place.blk, place.twin)]

    def pass_on(self, lane, slot, blk):
        return send(
            self.ref.at[slot],
            self.ref.at[slot],
            self.sent.at[lane],
            self.got.at[lane],
            (self.place.head, blk),
        )

    def relay(self):
        place = self.place
        for step in range(1, place.half):
            slot = ((place.chip + place.half - step) % place.half) * 2 + place.core
            self.direct[step - 1].wait_recv()
            self.rest.append(self.pass_on(place.half - 1 + step, slot, place.twin))

    def wait(self):
        for copy in self.direct:
            copy.wait_send()
        for copy in self.rest:
            copy.wait()


class Fold:
    def __init__(self, place, terms, theirs, arrived, sent_twin, got_twin, sent, got):
        self.place, self.terms, self.theirs, self.arrived = place, terms, theirs, arrived
        self.sent, self.got = sent, got
        self.order = [(place.chip + step + 1) % place.half for step in range(place.half)]
        self.across = [
            send(
                terms.at[chip * 2 + 1 - place.core],
                theirs.at[step],
                sent_twin.at[step],
                got_twin.at[step],
                (place.head, place.twin),
            )
            for step, chip in enumerate(self.order)
        ]
        self.onward = []

    def add(self):
        place = self.place
        for step, chip in enumerate(self.order):
            self.across[step].wait_recv()
            total = wide(self.theirs[step]) + wide(self.terms[chip * 2 + place.core])
            self.theirs[step] = total.astype(self.theirs.dtype)
            if step < place.half - 1:
                self.onward.append(
                    send(
                        self.theirs.at[step],
                        self.arrived.at[step],
                        self.sent.at[step],
                        self.got.at[step],
                        (place.head, chip * 2 + place.core),
                    )
                )

    def total(self):
        total = wide(self.theirs[self.place.half - 1])
        for step, copy in enumerate(self.onward):
            copy.wait_recv()
            total = total + wide(self.arrived[step])
        return total

    def wait(self):
        for copy in self.across + self.onward:
            copy.wait_send()


def wait_all(*groups):
    for group in groups:
        for copy in group:
            copy.wait()


def block_order(head_count):
    return list(range(1, head_count)) + [0]


def block_at(step, head_count):
    return (lax.axis_index("head") + step) % head_count


def rows_at(block, tokens):
    return pl.ds(pl.multiple_of(block * tokens, tokens), tokens)


def open_layer(
    sizes,
    x,
    joint_rows,
    value_rows,
    output_rows,
    router,
    mix,
    vectors,
    gain_one,
    gain_two,
    segment,
    position,
    routes,
    residual,
    g,
    x_all,
    facts_all,
    g_all,
    normed,
    queries,
    pairs_all,
    joint,
    output,
    small,
    joint_own,
    output_own,
    facts_own,
    joint_all,
    output_all,
    joint_wide,
    output_wide,
    local,
    sent,
    got,
    sent_joint,
    got_joint,
    sent_output,
    got_output,
    sent_facts,
    got_facts,
    sent_pairs,
    got_pairs,
):
    place = Place(*sizes)
    head_count, blk_count = sizes
    head, blk = place.head, place.blk
    tokens, width = x.shape
    rows = joint_rows.shape[0]
    head_width = width // head_count
    split = 2 * HEAD_DIM
    greet(place.others("head") + place.near())
    own_g = keep(g, g_all.at[head], local.at[0])
    x_all[head] = x[...]
    marks = jnp.concatenate(
        [wide(router[...]), wide(mix[...]), wide(vectors[...]), wide(gain_one[...]), wide(gain_two[...])],
        axis=0,
    )
    marks = jnp.concatenate([marks, jnp.zeros((128 - marks.shape[0], rows), jnp.float32)], axis=0)
    marks = jnp.concatenate([marks, jnp.zeros((128, 128 - rows), jnp.float32)], axis=1)
    marks = marks.T[:rows]
    both = wide(joint_rows[...])
    third = wide(value_rows[...])
    filler = jnp.zeros((rows, HEAD_DIM), jnp.float32)
    below = jnp.zeros((PAD - rows, joint_own.shape[2]), jnp.float32)
    for part in range(head_count):
        at = part * head_width
        piece = jnp.concatenate(
            [
                both[:, at : at + head_width],
                filler,
                both[:, width + at : width + at + head_width],
                third[:, at + split : at + head_width],
                third[:, at : at + split],
                marks,
            ],
            axis=1,
        )
        joint_own[part] = low(jnp.concatenate([piece, below], axis=0))
    output_own[...] = low(
        jnp.concatenate(
            [wide(output_rows[...]), jnp.zeros((PAD - rows, width), jnp.float32)], axis=0
        )
    )
    facts_own[...] = jnp.concatenate(
        [
            wide(segment[...]),
            wide(position[...]),
            wide(routes[...]),
            jnp.zeros((4, tokens), jnp.float32),
            residual[...],
            jnp.zeros((24 - 8 - ROUTED, tokens), jnp.float32),
        ],
        axis=0,
    )
    joint_all[blk, head] = joint_own[head]
    output_all[blk, head] = output_own[...]
    facts_all[blk, head] = facts_own[...]
    greeted(place.head_count - 1 + place.half)
    first = scatter(place, "head", joint_own, joint_all.at[blk], sent.at[0], got.at[0])
    first += gather(place, "head", facts_own, facts_all.at[blk], sent.at[1], got.at[1])
    for copy in first:
        copy.wait_send()
    tokens_in = gather(place, "head", x, x_all, sent.at[2], got.at[2])
    for copy in first:
        copy.wait_recv()
    spreads = [
        Spread(place, joint_all, sent_joint, got_joint),
        Spread(place, facts_all, sent_facts, got_facts),
    ]
    outputs_in = gather(place, "head", output_own, output_all.at[blk], sent.at[3], got.at[3])
    for spread in spreads:
        spread.relay()
    for spread in spreads:
        spread.wait()
    joint_width = joint.shape[1]
    for part in range(head_count):
        for other in range(blk_count):
            joint_wide[pl.ds((part * blk_count + other) * rows, rows), :] = wide(
                joint_all[other, part]
            )[:rows]
    joint[...] = low(joint_wide[:, :joint_width])
    small_rows = joint_wide[:, joint_width:].T
    small[...] = small_rows[:SMALL]
    gain = small_rows[GAIN_ONE_AT : GAIN_ONE_AT + 1]
    upstream = []
    pair_spreads = []
    cut = queries.shape[1]
    for step in range(head_count):
        block = (head + head_count - step) % head_count
        if step:
            tokens_in[step - 1].wait_recv()
        if step == head_count - 1:
            upstream = gather(place, "head", g, g_all, sent.at[4], got.at[4])
        source = wide(x_all[block])
        inverse = lax.rsqrt(jnp.mean(source * source, axis=-1, keepdims=True) + EPS)
        rows_normed = low(source * inverse * gain)
        here = rows_at(block, tokens)
        normed[here, :] = rows_normed
        product = mul(rows_normed, joint[...])
        queries[here, :] = low(product[:, :cut])
        pairs_all[blk, block] = low(product[:, cut:])
        pair_spreads.append(
            Spread(place, pairs_all.at[:, block], sent_pairs.at[step], got_pairs.at[step])
        )
    for copy in outputs_in:
        copy.wait_recv()
    output_spread = Spread(place, output_all, sent_output, got_output)
    for spread in pair_spreads:
        spread.relay()
    output_spread.relay()
    output_spread.wait()
    for part in range(head_count):
        for other in range(blk_count):
            output_wide[pl.ds((part * blk_count + other) * rows, rows), :] = wide(
                output_all[other, part]
            )[:rows]
    output[...] = low(output_wide[...])
    for spread in pair_spreads:
        spread.wait()
    for copy in tokens_in + outputs_in:
        copy.wait_send()
    wait_all(upstream, [own_g])


def slots_of(head_count, facts, first, second):
    tokens = first.shape[2]
    earlier = low(
        wide(
            lax.broadcasted_iota(jnp.int32, (tokens, tokens), 0)
            < lax.broadcasted_iota(jnp.int32, (tokens, tokens), 1)
        )
    )
    expert = wide(lax.broadcasted_iota(jnp.int32, (2 * EXPERTS, tokens), 0))
    expert_at = wide(lax.broadcasted_iota(jnp.int32, (EXPERTS, CAP, tokens), 0))
    rank_at = wide(lax.broadcasted_iota(jnp.int32, (EXPERTS, CAP, tokens), 1))
    for head in range(head_count):
        routes = [facts[head, 2 + choice : 3 + choice, :] for choice in range(TOP)]
        named = jnp.where((routes[0] == expert) | (routes[1] == expert), 1.0, 0.0)
        count = mul(low(named), earlier)[:EXPERTS]
        fits = count[:, None, :] == rank_at
        for choice, out in enumerate((first, second)):
            match = (routes[choice][None] == expert_at) & fits
            out[head] = low(jnp.where(match, 1.0, 0.0).reshape(EXPERTS * CAP, tokens))


def place_upstream(sizes, facts_all, g_all, first, second, slots):
    head_count, blk_count = sizes
    facts = facts_all.at[lax.axis_index("blk")]
    slots_of(head_count, facts, first, second)
    parts = []
    for step in block_order(head_count):
        block = block_at(step, head_count)
        found = mul(first[block] + second[block], g_all[block])
        parts.append(found.reshape(EXPERTS, CAP, slots.shape[2]))
    slots[...] = low(jnp.concatenate(parts, axis=1))


def visible_blocks(segment, position, period, me, count, chosen, shift):
    def look(block, found):
        same = segment[block] == segment[me]
        shared = (
            (segment[block] // period == segment[me] // period)
            & (segment[block] % period == 0)
            & (segment[me] % period != 0)
        )
        seen = (same & (position[block] <= position[me])) | shared
        chosen[found] = block
        shift[found] = jnp.where(same & (position[block] == position[me]), 0, -FAR)
        return found + seen.astype(jnp.int32)

    found = lax.fori_loop(0, count, look, jnp.int32(0))
    for extra in range(CHUNK):
        chosen[found + extra] = jnp.int32(0)
        shift[found + extra] = jnp.int32(FAR)
    return (found + CHUNK - 1) // CHUNK


def chunk_mask(tokens, heads, shift, start):
    row = lax.broadcasted_iota(jnp.int32, (tokens, tokens), 0)
    column = lax.broadcasted_iota(jnp.int32, (tokens, tokens), 1)
    gap = row - column
    parts = [
        jnp.where(gap + shift[start + step] <= 0, 1.0, 0.0) for step in range(CHUNK)
    ]
    mask = jnp.concatenate(parts, axis=0)
    return jnp.concatenate([mask] * heads, axis=1) > 0.5


def chunk_rows(pairs, chosen, start, low_lane, high_lane):
    return jnp.concatenate(
        [pairs[chosen[start + step], :, low_lane:high_lane] for step in range(CHUNK)], axis=0
    )


def lanes_at(rows, first, last):
    lane = lax.broadcasted_iota(jnp.int32, rows.shape, 1)
    return jnp.where((lane >= first) & (lane < last), rows, jnp.zeros_like(rows))


def query_rows_of(queries, head, tokens):
    rows = queries[pl.ds(head * tokens, tokens), :]
    rows = low(wide(rows) * HEAD_DIM ** (-0.5))
    return jnp.concatenate(
        [lanes_at(rows, part * HEAD_DIM, (part + 1) * HEAD_DIM) for part in range(3)], axis=0
    )


def attend(sizes, period, segment, position, queries, pairs, attended, totals, chosen, shift):
    head_count, blk_count = sizes
    blocks, tokens, lanes = pairs.shape
    heads = 3
    blk = lax.axis_index("blk")
    for head in range(head_count):
        chunks = visible_blocks(
            segment, position, period, blk * head_count + head, blocks, chosen, shift
        )
        asked = query_rows_of(queries, head, tokens)

        def step(number, carried):
            top, total, weighted = carried
            start = number * CHUNK
            scores = mul_nt(chunk_rows(pairs, chosen, start, 0, 256), asked)
            scores = jnp.where(chunk_mask(tokens, heads, shift, start), scores, -jnp.inf)
            new_top = jnp.maximum(top, jnp.max(scores, axis=0, keepdims=True))
            raised = jnp.exp(scores - new_top)
            factor = jnp.exp(top - new_top)
            total = total * factor + jnp.sum(raised, axis=0, keepdims=True)
            mixed = mul_tn(chunk_rows(pairs, chosen, start, 128, lanes), low(raised))
            mixed = jnp.concatenate(
                [mixed[128:192, 0:128], mixed[192:256, 128:256], mixed[64:128, 256:384]], axis=1
            )
            return (new_top, total, weighted * factor + mixed)

        wide_lanes = heads * tokens
        top, total, weighted = lax.fori_loop(
            0,
            chunks,
            step,
            (
                jnp.full((1, wide_lanes), -1e30, jnp.float32),
                jnp.zeros((1, wide_lanes), jnp.float32),
                jnp.zeros((HEAD_DIM, wide_lanes), jnp.float32),
            ),
        )
        outcome = low(weighted / total)
        totals[head] = jnp.broadcast_to(top + jnp.log(total), totals.shape[1:])
        for part in range(heads):
            attended[head, part * HEAD_DIM : (part + 1) * HEAD_DIM, :] = outcome[
                :, part * tokens : (part + 1) * tokens
            ]


def attend_back(sizes, period, segment, position, queries, pairs, attended, totals, middle_grad, output, query_grad, pair_grad, output_grad, chosen, shift, summed):
    head_count, blk_count = sizes
    blocks, tokens, lanes = pairs.shape
    heads = 3
    blk, mine = lax.axis_index("blk"), lax.axis_index("head")
    head_rows = heads * HEAD_DIM
    weight = output[pl.ds(pl.multiple_of(mine * head_rows, head_rows), head_rows), :]
    turned = jnp.concatenate(
        [jnp.zeros((HEAD_DIM, weight.shape[1]), weight.dtype), weight[128:192], weight[0:128]], axis=0
    )
    grads = middle_grad[...]
    product = sum(
        mul(attended[head], grads[head * tokens : (head + 1) * tokens])
        for head in range(head_count)
    )
    rows = head_rows // blk_count
    filler = jnp.zeros((PAD - rows, product.shape[1]), jnp.float32)
    for part in range(blk_count):
        output_grad[part] = low(
            jnp.concatenate([product[part * rows : (part + 1) * rows], filler], axis=0)
        )
    given = low(mul_nt(grads, turned))
    given_turned = wide(low(mul_nt(weight, grads)))
    summed[...] = jnp.zeros_like(summed)
    for head in range(head_count):
        chunks = visible_blocks(
            segment, position, period, blk * head_count + head, blocks, chosen, shift
        )
        asked = query_rows_of(queries, head, tokens)
        own = given[head * tokens : (head + 1) * tokens]
        back = jnp.concatenate(
            [lanes_at(own, 128, 192), lanes_at(own, 192, 256), lanes_at(own, 64, 128)], axis=0
        )
        dots = given_turned[:, head * tokens : (head + 1) * tokens] * wide(attended[head])
        offset = jnp.concatenate(
            [
                jnp.sum(dots[part * HEAD_DIM : (part + 1) * HEAD_DIM], axis=0, keepdims=True)
                for part in range(heads)
            ],
            axis=1,
        )
        total = totals[head, 0:1, :]

        def step(number, carried):
            start = number * CHUNK
            keys = chunk_rows(pairs, chosen, start, 0, 256)
            values = chunk_rows(pairs, chosen, start, 128, lanes)
            scores = mul_nt(keys, asked)
            raised = jnp.where(
                chunk_mask(tokens, heads, shift, start), jnp.exp(scores - total), 0.0
            )
            grad_raised = mul_nt(values, back)
            grad_scores = low(raised * (grad_raised - offset))
            key_part = mul(grad_scores, asked)
            value_part = mul(low(raised), back)
            both = jnp.concatenate(
                [
                    key_part[:, :128],
                    key_part[:, 128:] + value_part[:, :128],
                    value_part[:, 128:],
                ],
                axis=1,
            )
            for block in range(CHUNK):
                at = chosen[start + block]
                summed[at] = summed[at] + both[block * tokens : (block + 1) * tokens]
            found = mul_tn(keys, grad_scores)
            return carried + jnp.concatenate(
                [found[0:64, 0:128], found[64:128, 128:256], found[128:192, 256:384]], axis=1
            )

        found = lax.fori_loop(
            0, chunks, step, jnp.zeros((HEAD_DIM, heads * tokens), jnp.float32)
        )
        found = found * HEAD_DIM ** (-0.5)
        stacked = jnp.concatenate(
            [found[:, part * tokens : (part + 1) * tokens] for part in range(heads)]
            + [jnp.zeros((HEAD_DIM, tokens), jnp.float32)],
            axis=0,
        )
        query_grad[pl.ds(head * tokens, tokens), :] = low(stacked.T)
    pair_grad[...] = low(summed[...])


def at_home(sizes, parts, middle, normed, g, small, weights, facts_all, middle_grad, middle_low, residual_grad, small_grad, mixture):
    head_count, blk_count = sizes
    tokens, width = middle.shape
    mine = lax.axis_index("head")
    facts = facts_all[lax.axis_index("blk"), mine]
    share_rows = weights[mine]
    columns = jnp.concatenate([share_rows, facts[0:8]], axis=0).T
    share = [columns[:, choice : choice + 1] for choice in range(TOP)]
    route_of = [columns[:, 10 + choice : 11 + choice] for choice in range(TOP)]
    upstream = wide(g[...])
    normed_wide = wide(normed[...])
    source = middle[...]
    small_low = low(small[...])
    seen = mul_nt(normed[...], small_low)
    met = mul_nt(g[...], small_low)

    def weight_of(expert):
        return sum(
            share[choice] * jnp.where(route_of[choice] == expert, 1.0, 0.0)
            for choice in range(TOP)
        )

    copy_share = weight_of(EXPERTS + 1)
    const_share = [weight_of(EXPERTS + 2 + const) for const in range(2)]
    mixing = []
    for const in range(2):
        at = MIX_AT + 2 * const
        pair = [seen[:, at + part : at + part + 1] for part in range(2)]
        highest = jnp.maximum(pair[0], pair[1])
        raised = [jnp.exp(value - highest) for value in pair]
        total = raised[0] + raised[1]
        mixing.append([value / total for value in raised])
    copy_dot = jnp.sum(upstream * normed_wide, axis=-1, keepdims=True)
    vector_dot = [met[:, VECTOR_AT + const : VECTOR_AT + const + 1] for const in range(2)]
    const_dot = [
        mixing[const][0] * copy_dot + mixing[const][1] * vector_dot[const] for const in range(2)
    ]
    total = wide(parts[0])
    for head in range(1, head_count):
        total = total + wide(parts[head])
    tail = total[:, width:]
    product = []
    for choice in range(TOP):
        value = tail[:, 64 * choice : 64 * choice + 1] + tail[:, 64 * choice + 32 : 64 * choice + 33]
        special = jnp.where(route_of[choice] == EXPERTS + 1, copy_dot, 0.0)
        for const in range(2):
            special = special + jnp.where(
                route_of[choice] == EXPERTS + 2 + const, const_dot[const], 0.0
            )
        product.append(value + share[choice] * special)
    both = product[0] + product[1]
    lane = lax.broadcasted_iota(jnp.int32, (tokens, 128), 1)
    lane_wide = wide(lane)
    routing = jnp.zeros((tokens, 128), jnp.float32)
    for choice in range(TOP):
        routing = routing + jnp.where(
            lane_wide == route_of[choice], product[choice] - share[choice] * both, 0.0
        )
    residual_grad[...] = routing
    vector_share = jnp.zeros((tokens, 128), jnp.float32)
    spread_grad = routing
    for const in range(2):
        grad_mix = [const_share[const] * copy_dot, const_share[const] * vector_dot[const]]
        mean = mixing[const][0] * grad_mix[0] + mixing[const][1] * grad_mix[1]
        for part in range(2):
            spread_grad = spread_grad + jnp.where(
                lane == MIX_AT + 2 * const + part,
                mixing[const][part] * (grad_mix[part] - mean),
                0.0,
            )
        vector_share = vector_share + jnp.where(
            lane == VECTOR_AT + const, const_share[const] * mixing[const][1], 0.0
        )
    direct = (
        copy_share + const_share[0] * mixing[0][0] + const_share[1] * mixing[1][0]
    )
    table = jnp.concatenate(
        [small_low[0:16], jnp.zeros((128 - 16, width), jnp.bfloat16)], axis=0
    )
    spread_high, spread_rest = halves(spread_grad)
    grad_normed = (
        direct * upstream + total[:, :width] + mul(spread_high, table) + mul(spread_rest, table)
    )
    inverse = lax.rsqrt(jnp.mean(source * source, axis=-1, keepdims=True) + EPS)
    scaled = grad_normed * small[GAIN_TWO_AT : GAIN_TWO_AT + 1]
    result = (
        upstream
        + inverse * scaled
        - source * inverse**3 * jnp.mean(scaled * source, axis=-1, keepdims=True)
    )
    middle_grad[...] = result
    middle_low[...] = low(result)
    gain_row = jnp.sum(grad_normed * source * inverse, axis=0, keepdims=True)
    vector_high, vector_rest = halves(vector_share)
    by_normed = mul_tn(spread_high, normed[...]) + mul_tn(spread_rest, normed[...])
    by_upstream = mul_tn(vector_high, g[...]) + mul_tn(vector_rest, g[...])
    row = lax.broadcasted_iota(jnp.int32, (SMALL, width), 0)
    small_grad[...] = jnp.where(
        row == GAIN_TWO_AT, gain_row, by_normed[:SMALL] + by_upstream[:SMALL]
    )
    vectors = [small[VECTOR_AT + const : VECTOR_AT + const + 1] for const in range(2)]
    mixed = copy_share * normed_wide
    for const in range(2):
        mixed = mixed + const_share[const] * (
            mixing[const][0] * normed_wide + mixing[const][1] * vectors[const]
        )
    mixture[...] = source + mixed


def route(
    sizes,
    attended,
    upstream_slots,
    x_all,
    output,
    small,
    facts_all,
    first,
    second,
    slots_in,
    grads_in,
    middle_home,
    normed_home,
    weights,
    attended_all,
    slots,
    sent,
    got,
    sent_grads,
    got_grads,
    sent_slots,
    got_slots,
):
    place = Place(*sizes)
    head_count, blk_count = sizes
    head, blk = place.head, place.blk
    tokens, width = middle_home.shape
    order = block_order(head_count)
    greet(place.others("head") + place.others("blk"))
    attended_all[head] = attended[...]
    grads_in[blk] = upstream_slots[blk]
    greeted(head_count + blk_count - 2)
    rows_in = []
    for number, step in enumerate(order):
        copies = []
        for away in range(1, head_count):
            other = (head + away) % head_count
            block = (other + step) % head_count
            copies.append(
                send(
                    attended.at[block],
                    attended_all.at[head, block],
                    sent.at[number, away - 1],
                    got.at[number, away - 1],
                    (other, blk),
                )
            )
        rows_in.append(copies)
    routed = scatter(place, "blk", upstream_slots, grads_in, sent_grads, got_grads)
    router = low(small[0:16])
    expert = wide(lax.broadcasted_iota(jnp.int32, (16, tokens), 0))
    lane = lax.broadcasted_iota(jnp.int32, (EXPERTS * CAP, 128), 1)
    gain = small[GAIN_TWO_AT : GAIN_TWO_AT + 1]
    parts = []
    for number, step in enumerate(order):
        block = block_at(step, head_count)
        for copy in rows_in[number]:
            copy.wait_recv()
        rows = jnp.concatenate(
            [attended_all[source, block] for source in range(head_count)], axis=0
        ).T
        source = wide(x_all[block]) + mul(rows, output[...])
        inverse = lax.rsqrt(jnp.mean(source * source, axis=-1, keepdims=True) + EPS)
        normed = low(source * inverse * gain)
        if step == 0:
            middle_home[...] = source
            normed_home[...] = normed
        facts = facts_all[blk, block]
        logits = mul_nt(router, normed) + facts[8:24]
        picked = [
            jnp.sum(
                jnp.where(facts[2 + choice : 3 + choice] == expert, logits, 0.0),
                axis=0,
                keepdims=True,
            )
            for choice in range(TOP)
        ]
        highest = jnp.maximum(picked[0], picked[1])
        raised = [jnp.exp(value - highest) for value in picked]
        total = raised[0] + raised[1]
        share = [value / total for value in raised]
        weights[block] = jnp.concatenate(share + [jnp.zeros((6, tokens), jnp.float32)], axis=0)
        places = [first[block], second[block]]
        of_slot = jnp.sum(
            wide(places[0]) * share[0] + wide(places[1]) * share[1], axis=1, keepdims=True
        )
        high, rest = halves(of_slot)
        found = jnp.concatenate(
            [mul(places[0] + places[1], normed), jnp.where(lane < 64, wide(high), wide(rest))],
            axis=1,
        )
        parts.append(found.reshape(EXPERTS, CAP, width + 128))
        if number % 2:
            span = pl.ds((number - 1) * CAP, 2 * CAP)
            slots[:, span, :] = low(jnp.concatenate(parts, axis=1))
            parts = []
            slots_in[blk, span, :] = slots[blk, span, :]
            routed += scatter(
                place,
                "blk",
                slots.at[:, span],
                slots_in.at[:, span],
                sent_slots.at[number // 2],
                got_slots.at[number // 2],
            )
    for copies in rows_in:
        for copy in copies:
            copy.wait_send()
    wait_all(routed)


def experts(
    sizes,
    slots_in,
    grads_in,
    piece_0,
    piece_1,
    piece_2,
    piece_3,
    first,
    second,
    middle,
    normed,
    g,
    small,
    weights,
    facts_all,
    early_grads,
    down_in,
    out_parts,
    middle_grad,
    middle_all,
    residual_grad,
    small_grad,
    mixture,
    held,
    taken,
    hidden,
    grad_gate,
    grad_up,
    scaled,
    back,
    outs,
    back_in,
    outs_in,
    parts,
    parts_in,
    down_parts,
    middle_low,
    sent_back,
    got_back,
    sent_outs,
    got_outs,
    sent_down,
    got_down,
    sent_parts,
    got_parts,
    sent_middle,
    got_middle,
):
    place = Place(*sizes)
    head_count, blk_count = sizes
    head, blk = place.head, place.blk
    tokens, width = middle.shape
    order = block_order(head_count)
    greet(place.others("head") + place.others("blk"))
    for step, piece in enumerate((piece_0, piece_1, piece_2, piece_3)):
        source = (head + head_count - step) % head_count
        for kind in range(3):
            held[kind, source] = piece[kind]
    columns = held.shape[3]
    depth = head_count * held.shape[2]
    gate, up, down = [held[kind].reshape(depth, columns) for kind in range(3)]
    span_rows = 2 * CAP
    group = blk_count * span_rows
    lane = lax.broadcasted_iota(jnp.int32, (group, 128), 1)
    routed = []
    for number in range(head_count // 2):
        span = pl.ds(number * span_rows, span_rows)
        here = pl.ds(number * group, group)
        entry = slots_in[:, span, :].reshape(group, width + 128)
        rows = entry[:, :width]
        taken[here, :] = rows
        tail = wide(entry[:, width:])
        share = tail[:, 0:1] + tail[:, 64:65]
        scaled_rows = low(share * wide(grads_in[:, span, :].reshape(group, width)))
        scaled[here, :] = scaled_rows
        gate_pre = mul(rows, gate)
        up_pre = mul(rows, up)
        sigmoid = 1.0 / (1.0 + jnp.exp(-gate_pre))
        activated = gate_pre * sigmoid
        hidden_rows = low(activated * up_pre)
        hidden[here, :] = hidden_rows
        grad_hidden = mul(scaled_rows, down)
        gate_rows = low(grad_hidden * up_pre * sigmoid * (1.0 + gate_pre * (1.0 - sigmoid)))
        up_rows = low(grad_hidden * activated)
        grad_gate[here, :] = gate_rows
        grad_up[here, :] = up_rows
        dots = jnp.sum(wide(hidden_rows) * grad_hidden, axis=1, keepdims=True)
        grad_rows = mul_nt(gate_rows, gate) + mul_nt(up_rows, up)
        high, rest = halves(dots)
        tail_out = jnp.where(lane < 64, wide(high), wide(rest))
        back[:, span, :] = low(jnp.concatenate([grad_rows, tail_out], axis=1)).reshape(
            blk_count, span_rows, width + 128
        )
        if number == 0:
            greeted(head_count + blk_count - 2)
        back_in[blk, span, :] = back[blk, span, :]
        routed.append(
            scatter(
                place,
                "blk",
                back.at[:, span],
                back_in.at[:, span],
                sent_back.at[number],
                got_back.at[number],
            )
        )
    scaled_turned = scaled[...].T
    down_parts[...] = low(mul(scaled_turned, hidden[...])).reshape(down_parts.shape)
    down_in[head] = down_parts[head]
    down_copies = scatter(place, "head", down_parts, down_in, sent_down, got_down)
    for number in range(head_count // 2):
        span = pl.ds(number * span_rows, span_rows)
        here = pl.ds(number * group, group)
        outs[:, span, :] = low(mul_nt(hidden[here, :], down)).reshape(blk_count, span_rows, width)
    outs_in[blk] = outs[blk]
    out_copies = scatter(place, "blk", outs, outs_in, sent_outs, got_outs)
    rows_turned = taken[...].T
    for kind, right in enumerate((grad_gate, grad_up)):
        early_grads[:, kind] = low(mul(rows_turned, right[...])).reshape(
            head_count, depth // head_count, columns
        )
    narrow = lax.broadcasted_iota(jnp.int32, (tokens, 128), 1)
    share_copies = []
    for number, step in enumerate(order):
        block = block_at(step, head_count)
        if number % 2 == 0:
            for copy in routed[number // 2]:
                copy.wait_recv()
            span = pl.ds(number * CAP, span_rows)
            rows = wide(back_in[:, span, :])
        part = rows[:, (number % 2) * CAP : (number % 2 + 1) * CAP]
        part = low(part.reshape(EXPERTS * CAP, width + 128))
        found = [mul_tn(placed[block], part) for placed in (first, second)]
        tail = jnp.zeros((tokens, 128), jnp.float32)
        for choice in range(TOP):
            high, rest = halves(
                found[choice][:, width : width + 1] + found[choice][:, width + 64 : width + 65]
            )
            tail = jnp.where(narrow // 32 == 2 * choice, wide(high), tail)
            tail = jnp.where(narrow // 32 == 2 * choice + 1, wide(rest), tail)
        result = low(
            jnp.concatenate([found[0][:, :width] + found[1][:, :width], tail], axis=1)
        )
        if step:
            parts[step - 1] = result
            share_copies.append(
                send(
                    parts.at[step - 1],
                    parts_in.at[head],
                    sent_parts.at[step - 1],
                    got_parts.at[step - 1],
                    (block, blk),
                )
            )
        else:
            parts_in[head] = result
    for copy in share_copies:
        copy.wait_recv()
    at_home(
        sizes,
        parts_in,
        middle,
        normed,
        g,
        small,
        weights,
        facts_all,
        middle_grad,
        middle_low,
        residual_grad,
        small_grad,
        mixture,
    )
    middle_all[head] = middle_low[...]
    middle_copies = gather(place, "head", middle_low, middle_all, sent_middle, got_middle)
    for copy in out_copies:
        copy.wait_recv()
    for number, step in enumerate(order):
        block = block_at(step, head_count)
        if number % 2 == 0:
            rows = wide(outs_in[:, pl.ds(number * CAP, span_rows), :])
        part = rows[:, (number % 2) * CAP : (number % 2 + 1) * CAP]
        part = low(part.reshape(EXPERTS * CAP, width))
        shares = weights[block].T
        out_parts[block] = low(
            shares[:, 0:1] * mul_tn(first[block], part)
            + shares[:, 1:2] * mul_tn(second[block], part)
        )
    for copies in routed + [out_copies, share_copies]:
        for copy in copies:
            copy.wait_send()
    wait_all(down_copies, middle_copies)


def close_layer(
    sizes,
    pair_terms,
    query_grad,
    joint,
    normed,
    x_all,
    small_grad,
    out_parts,
    output_terms,
    small,
    middle_grad,
    mixture,
    input_grad,
    layer_out,
    joint_out,
    output_grad,
    small_total,
    gain_total,
    theirs_pairs,
    arrived_pairs,
    theirs_output,
    arrived_output,
    small_terms,
    theirs_small,
    arrived_small,
    joint_terms,
    theirs_joint,
    arrived_joint,
    gain_terms,
    theirs_gain,
    arrived_gain,
    row_parts,
    rows_in,
    out_in,
    joint_sums,
    small_sums,
    small_in,
    gain_sums,
    gain_in,
    turned,
    grads,
    early_rows,
    sent_out,
    got_out,
    sent_twin,
    got_twin,
    sent_blk,
    got_blk,
    sent_rows,
    got_rows,
    sent_last,
    got_last,
):
    place = Place(*sizes)
    head_count, blk_count = sizes
    head, blk = place.head, place.blk
    tokens, width = input_grad.shape
    order = block_order(head_count)
    rows = width // (head_count * blk_count)
    cut = query_grad.shape[1]
    joint_width = joint.shape[1]
    greet(place.others("head") + place.near())
    out_in[head] = out_parts[head]
    flat = jnp.concatenate(
        [small_grad[...], jnp.zeros((128 - SMALL, width), jnp.float32)], axis=0
    ).T
    for part in range(head_count):
        for other in range(blk_count):
            at = (part * blk_count + other) * rows
            small_terms[other, part * rows : (part + 1) * rows, :] = flat[at : at + rows]
    greeted(place.head_count - 1 + place.half)
    out_copies = scatter(place, "head", out_parts, out_in, sent_out, got_out)

    def fold(number, terms, theirs, arrived):
        return Fold(
            place,
            terms,
            theirs,
            arrived,
            sent_twin.at[number],
            got_twin.at[number],
            sent_blk.at[number],
            got_blk.at[number],
        )

    pair_folds = []
    for number, step in enumerate(order):
        block = block_at(step, head_count)
        pair_folds.append(
            fold(
                number,
                pair_terms.at[:, block],
                theirs_pairs.at[number],
                arrived_pairs.at[number],
            )
        )
    output_fold = fold(head_count, output_terms, theirs_output, arrived_output)
    small_fold = fold(head_count + 1, small_terms, theirs_small, arrived_small)
    for one in pair_folds:
        one.add()
    output_fold.add()
    small_fold.add()
    turned[...] = normed[...].T
    early_rows[...] = mul_nt(query_grad[...], joint[:, :cut])
    early = mul(turned[...], query_grad[...])
    row_copies = []
    gain_row = jnp.zeros((1, width), jnp.float32)
    for number, step in enumerate(order):
        block = block_at(step, head_count)
        here = rows_at(block, tokens)
        part = low(pair_folds[number].total())
        grads[here, :] = part
        grad_normed = early_rows[here, :] + mul_nt(part, joint[:, cut:])
        result = low(grad_normed)
        if step:
            row_parts[step - 1] = result
            row_copies.append(
                send(
                    row_parts.at[step - 1],
                    rows_in.at[head],
                    sent_rows.at[step - 1],
                    got_rows.at[step - 1],
                    (block, blk),
                )
            )
        else:
            rows_in[head] = result
        source = wide(x_all[block])
        inverse = lax.rsqrt(jnp.mean(source * source, axis=-1, keepdims=True) + EPS)
        gain_row = gain_row + jnp.sum(grad_normed * source * inverse, axis=0, keepdims=True)
    product = jnp.concatenate([early, mul(turned[...], grads[...])], axis=1)
    filler = jnp.zeros((PAD - rows, joint_width), jnp.float32)
    for part in range(head_count):
        for other in range(blk_count):
            at = (part * blk_count + other) * rows
            joint_terms[other, part * PAD : (part + 1) * PAD, :] = low(
                jnp.concatenate([product[at : at + rows], filler], axis=0)
            )
    joint_fold = fold(head_count + 2, joint_terms, theirs_joint, arrived_joint)
    owners = head_count * blk_count
    owner = lax.broadcasted_iota(jnp.int32, (owners, width), 0)
    column = lax.broadcasted_iota(jnp.int32, (owners, width), 1)
    owned = jnp.where(column // rows == owner, gain_row, 0.0)
    feature = lax.broadcasted_iota(jnp.int32, (width, 128), 0)
    target = lax.broadcasted_iota(jnp.int32, (width, 128), 1)
    moved = low(jnp.where(feature % rows == target, 1.0, 0.0))
    high, rest = halves(owned)
    by_owner = mul(high, moved) + mul(rest, moved)
    for other in range(blk_count):
        gain_terms[other] = jnp.concatenate(
            [
                by_owner[part * blk_count + other : part * blk_count + other + 1]
                for part in range(head_count)
            ]
            + [jnp.zeros((8 - head_count, 128), jnp.float32)],
            axis=0,
        )
    gain_fold = fold(head_count + 3, gain_terms, theirs_gain, arrived_gain)
    output_grad[...] = output_fold.total()[:rows]
    small_sums[...] = small_fold.total().reshape(head_count, rows, 128)
    small_in[head] = small_sums[head]
    last = scatter(place, "head", small_sums, small_in, sent_last.at[0], got_last.at[0])
    joint_fold.add()
    gain_fold.add()
    for copy in out_copies:
        copy.wait_recv()
    total = mixture[...]
    for part in range(head_count):
        total = total + wide(out_in[part])
    layer_out[...] = low(total)
    joint_sums[...] = low(joint_fold.total()).reshape(head_count, PAD, joint_width)
    joint_out[head] = joint_sums[head]
    last += scatter(place, "head", joint_sums, joint_out, sent_last.at[1], got_last.at[1])
    gain_now = gain_fold.total()
    for part in range(head_count):
        gain_sums[part] = jnp.broadcast_to(gain_now[part : part + 1], (8, 128))
    gain_in[head] = gain_sums[head]
    last += scatter(place, "head", gain_sums, gain_in, sent_last.at[2], got_last.at[2])
    for copy in row_copies:
        copy.wait_recv()
    grad_normed = wide(rows_in[0])
    for part in range(1, head_count):
        grad_normed = grad_normed + wide(rows_in[part])
    source = wide(x_all[head])
    inverse = lax.rsqrt(jnp.mean(source * source, axis=-1, keepdims=True) + EPS)
    scaled = grad_normed * small[GAIN_ONE_AT : GAIN_ONE_AT + 1]
    input_grad[...] = (
        middle_grad[...]
        + inverse * scaled
        - source * inverse**3 * jnp.mean(scaled * source, axis=-1, keepdims=True)
    )
    for copy in last:
        copy.wait_recv()
    small_total[...] = sum(small_in[part] for part in range(head_count))
    gain_total[...] = sum(gain_in[part] for part in range(head_count))
    for one in pair_folds + [output_fold, small_fold, joint_fold, gain_fold]:
        one.wait()
    for copy in out_copies + row_copies + last:
        copy.wait_send()


def finish_early(sizes, piece_0, piece_1, piece_2, piece_3, gate, up):
    head_count, blk_count = sizes
    mine = lax.axis_index("head")
    columns = piece_0.shape[2]
    for step, piece in enumerate((piece_0, piece_1, piece_2, piece_3)):
        source = (mine + head_count - step) % head_count
        at = pl.ds(pl.multiple_of(source * columns, columns), columns)
        gate[:, at] = wide(piece[0])
        up[:, at] = wide(piece[1])


def finish_down(sizes, down_in, down):
    head_count, blk_count = sizes
    columns = down_in.shape[2]
    for source in range(head_count):
        down[pl.ds(source * columns, columns), :] = wide(down_in[source]).T


def after(values, *signals):
    return lax.optimization_barrier((values, signals))[0]


def around_heads(pieces_of, head_count):
    mine = lax.axis_index("head")
    pieces = []
    for step in range(head_count):
        piece = lax.dynamic_index_in_dim(
            pieces_of, (mine + step) % head_count, 0, keepdims=False
        )
        if step:
            piece = lax.ppermute(
                piece, "head", [(i, (i + step) % head_count) for i in range(head_count)]
            )
        pieces.append(piece)
    return pieces


def fast_shards(
    inputs,
    cotangent,
    segment,
    position,
    routes,
    gate_residual,
    first_gain,
    second_gain,
    query_key_weight,
    value_weight,
    output_weight,
    router_weight,
    const_gate,
    const_vectors,
    gate_weight,
    up_weight,
    down_weight,
):
    tokens, width = inputs.shape
    head_count = lax.axis_size("head")
    blk_count = lax.axis_size("blk")
    sizes = (head_count, blk_count)
    part = functools.partial
    half = blk_count // 2
    period = tokens * blk_count // CONT_LEN + 1
    head_width = width // head_count
    column_rows = head_count * tokens
    weight_rows = query_key_weight.shape[0]
    columns = gate_weight.shape[1] // head_count
    slot_rows = head_count * CAP
    slot_total = blk_count * slot_rows
    joint_width = 10 * HEAD_DIM
    pair_width = 6 * HEAD_DIM
    others, near = head_count - 1, blk_count - 1

    (
        x_all,
        facts_all,
        g_all,
        normed,
        queries,
        pairs_all,
        joint,
        output,
        small,
    ) = exchange(
        part(open_layer, sizes),
        [
            shape((head_count, tokens, width)),
            shape((blk_count, head_count, 24, tokens), jnp.float32),
            shape((head_count, tokens, width)),
            shape((column_rows, width)),
            shape((column_rows, 4 * HEAD_DIM)),
            shape((blk_count, head_count, tokens, pair_width)),
            shape((width, joint_width)),
            shape((width, width)),
            shape((SMALL, width), jnp.float32),
        ],
        [
            inputs,
            query_key_weight,
            value_weight,
            output_weight,
            router_weight.T,
            const_gate.T,
            const_vectors.T,
            first_gain[None],
            second_gain[None],
            segment[None],
            position[None],
            routes.T,
            gate_residual.T,
            cotangent,
        ],
        [
            pltpu.VMEM((head_count, PAD, joint_width + 128), jnp.bfloat16),
            pltpu.VMEM((PAD, width), jnp.bfloat16),
            pltpu.VMEM((24, tokens), jnp.float32),
            pltpu.VMEM((blk_count, head_count, PAD, joint_width + 128), jnp.bfloat16),
            pltpu.VMEM((blk_count, head_count, PAD, width), jnp.bfloat16),
            pltpu.VMEM((width, joint_width + 128), jnp.float32),
            pltpu.VMEM((width, width), jnp.float32),
            dma(1),
            dma(5, others),
            dma(5, others),
            dma(near),
            dma(near),
            dma(near),
            dma(near),
            dma(near),
            dma(near),
            dma(head_count, near),
            dma(head_count, near),
        ],
        0,
        far_ins=(13,),
        far_outs=(2,),
    )
    expert_weights = jnp.stack([gate_weight, up_weight, down_weight.T])
    expert_weights = expert_weights.reshape(3, head_width, head_count, columns)
    expert_weights = after(expert_weights.transpose(2, 0, 1, 3), facts_all)
    expert_pieces = around_heads(expert_weights, head_count)
    pairs_all = pairs_all.reshape(blk_count * head_count, tokens, pair_width)
    marks = facts_all[:, :, 0:2, 0].astype(jnp.int32).reshape(blk_count * head_count, 2)
    segments, positions = marks[:, 0], marks[:, 1]
    lists = [
        pltpu.SMEM((blk_count * head_count + CHUNK,), jnp.int32),
        pltpu.SMEM((blk_count * head_count + CHUNK,), jnp.int32),
    ]
    attended, totals = compute(
        part(attend, sizes, period),
        [
            shape((head_count, head_width, tokens)),
            shape((head_count, 8, 3 * tokens), jnp.float32),
        ],
        [segments, positions, queries, pairs_all],
        lists,
        2,
    )
    first, second, upstream_slots = compute(
        part(place_upstream, sizes),
        [
            shape((head_count, EXPERTS * CAP, tokens)),
            shape((head_count, EXPERTS * CAP, tokens)),
            shape((EXPERTS, slot_rows, width)),
        ],
        [facts_all, g_all],
    )
    slots_in, grads_in, middle, normed_two, weights = exchange(
        part(route, sizes),
        [
            shape((blk_count, slot_rows, width + 128)),
            shape((blk_count, slot_rows, width)),
            shape((tokens, width), jnp.float32),
            shape((tokens, width)),
            shape((head_count, 8, tokens), jnp.float32),
        ],
        [attended, upstream_slots, x_all, output, small, facts_all, first, second],
        [
            pltpu.VMEM((head_count, head_count, head_width, tokens), jnp.bfloat16),
            pltpu.VMEM((EXPERTS, slot_rows, width + 128), jnp.bfloat16),
            dma(head_count, others),
            dma(head_count, others),
            dma(near),
            dma(near),
            dma(head_count // 2, near),
            dma(head_count // 2, near),
        ],
        1,
    )
    (
        early_grads,
        down_in,
        out_parts,
        middle_grad,
        middle_all,
        residual_grad,
        small_grad,
        mixture,
    ) = exchange(
        part(experts, sizes),
        [
            shape((head_count, 2, head_width, columns)),
            shape((head_count, head_width, columns)),
            shape((head_count, tokens, width)),
            shape((tokens, width), jnp.float32),
            shape((head_count, tokens, width)),
            shape((tokens, 128), jnp.float32),
            shape((SMALL, width), jnp.float32),
            shape((tokens, width), jnp.float32),
        ],
        [slots_in, grads_in]
        + expert_pieces
        + [first, second, middle, normed_two, cotangent, small, weights, facts_all],
        [
            pltpu.VMEM((3, head_count, head_width, columns), jnp.bfloat16),
            pltpu.VMEM((slot_total, width), jnp.bfloat16),
            pltpu.VMEM((slot_total, columns), jnp.bfloat16),
            pltpu.VMEM((slot_total, columns), jnp.bfloat16),
            pltpu.VMEM((slot_total, columns), jnp.bfloat16),
            pltpu.VMEM((slot_total, width), jnp.bfloat16),
            pltpu.VMEM((blk_count, slot_rows, width + 128), jnp.bfloat16),
            pltpu.VMEM((blk_count, slot_rows, width), jnp.bfloat16),
            pltpu.VMEM((blk_count, slot_rows, width + 128), jnp.bfloat16),
            pltpu.VMEM((blk_count, slot_rows, width), jnp.bfloat16),
            pltpu.VMEM((others, tokens, width + 128), jnp.bfloat16),
            pltpu.VMEM((head_count, tokens, width + 128), jnp.bfloat16),
            pltpu.VMEM((head_count, head_width, columns), jnp.bfloat16),
            pltpu.VMEM((tokens, width), jnp.bfloat16),
            dma(head_count // 2, near),
            dma(head_count // 2, near),
            dma(near),
            dma(near),
            dma(others),
            dma(others),
            dma(others),
            dma(others),
            dma(others),
            dma(others),
        ],
        2,
    )
    grad_pieces = around_heads(early_grads, head_count)
    query_grad, pair_grad, output_terms = compute(
        part(attend_back, sizes, period),
        [
            shape(queries.shape),
            shape(pairs_all.shape),
            shape((blk_count, PAD, width)),
        ],
        [
            segments,
            positions,
            queries,
            pairs_all,
            attended,
            totals,
            middle_all.reshape(column_rows, width),
            output,
        ],
        lists + [pltpu.VMEM(pairs_all.shape, jnp.float32)],
        2,
    )

    def vmem(*dims, dtype=jnp.bfloat16):
        return pltpu.VMEM(dims, dtype)

    wide_small = part(vmem, dtype=jnp.float32)
    input_grad, layer_out, joint_out, output_grad, small_total, gain_total = exchange(
        part(close_layer, sizes),
        [
            shape((tokens, width), jnp.float32),
            shape((tokens, width)),
            shape((head_count, PAD, joint_width)),
            shape((weight_rows, width), jnp.float32),
            shape((weight_rows, 128), jnp.float32),
            shape((8, 128), jnp.float32),
        ],
        [
            pair_grad.reshape(blk_count, head_count, tokens, pair_width),
            query_grad,
            joint,
            normed,
            x_all,
            small_grad,
            out_parts,
            output_terms,
            small,
            middle_grad,
            mixture,
        ],
        [
            vmem(head_count, half, tokens, pair_width),
            vmem(head_count, half - 1, tokens, pair_width),
            vmem(half, PAD, width),
            vmem(half - 1, PAD, width),
            wide_small(blk_count, head_count * weight_rows, 128),
            wide_small(half, head_count * weight_rows, 128),
            wide_small(half - 1, head_count * weight_rows, 128),
            vmem(blk_count, head_count * PAD, joint_width),
            vmem(half, head_count * PAD, joint_width),
            vmem(half - 1, head_count * PAD, joint_width),
            wide_small(blk_count, 8, 128),
            wide_small(half, 8, 128),
            wide_small(half - 1, 8, 128),
            vmem(others, tokens, width),
            vmem(head_count, tokens, width),
            vmem(head_count, tokens, width),
            vmem(head_count, PAD, joint_width),
            wide_small(head_count, weight_rows, 128),
            wide_small(head_count, weight_rows, 128),
            wide_small(head_count, 8, 128),
            wide_small(head_count, 8, 128),
            vmem(width, column_rows),
            vmem(column_rows, pair_width),
            wide_small(column_rows, width),
            dma(others),
            dma(others),
            dma(head_count + 4, half),
            dma(head_count + 4, half),
            dma(head_count + 4, half - 1),
            dma(head_count + 4, half - 1),
            dma(others),
            dma(others),
            dma(3, others),
            dma(3, others),
        ],
        3,
    )
    (down_grad,) = compute(
        part(finish_down, sizes), [shape(down_weight.shape, jnp.float32)], [down_in]
    )
    gate_grad, up_grad = compute(
        part(finish_early, sizes),
        [shape(gate_weight.shape, jnp.float32), shape(up_weight.shape, jnp.float32)],
        grad_pieces,
    )
    joint_grad_rows = joint_out[:, :weight_rows].astype(jnp.float32).transpose(1, 0, 2)

    def lanes_of(*spans):
        return jnp.concatenate(
            [joint_grad_rows[:, :, start:stop] for start, stop in spans], axis=2
        ).reshape(weight_rows, width)

    joint_grad = jnp.concatenate([lanes_of((0, 192)), lanes_of((256, 448))], axis=1)
    value_grad = lanes_of((512, 640), (448, 512))
    return (
        layer_out,
        input_grad,
        residual_grad[:, :ROUTED],
        gain_total[0, :weight_rows],
        small_total[:, GAIN_TWO_AT],
        joint_grad,
        value_grad,
        output_grad,
        small_total[:, ROUTER_AT : ROUTER_AT + ROUTED],
        small_total[:, MIX_AT : MIX_AT + 4],
        small_total[:, VECTOR_AT : VECTOR_AT + 2],
        gate_grad,
        up_grad,
        down_grad,
    )


def solution(mesh):
    body = fast_shards if mesh.shape["blk"] == EXPERTS else shards
    in_specs = (
        P(("head", "blk"), None),
        P(("head", "blk"), None),
        P(("head", "blk")),
        P(("head", "blk")),
        P(("head", "blk"), None),
        P(("head", "blk"), None),
        P(("head", "blk")),
        P(("head", "blk")),
        P(("head", "blk"), None),
        P(("head", "blk"), None),
        P(("head", "blk"), None),
        P(("head", "blk"), None),
        P(("head", "blk"), None),
        P(("head", "blk"), None),
        P("head", "blk"),
        P("head", "blk"),
        P("blk", "head"),
    )
    out_specs = (
        P(("head", "blk"), None),
        P(("head", "blk"), None),
        P(("head", "blk"), None),
        P(("head", "blk")),
        P(("head", "blk")),
        P(("head", "blk"), None),
        P(("head", "blk"), None),
        P(("head", "blk"), None),
        P(("head", "blk"), None),
        P(("head", "blk"), None),
        P(("head", "blk"), None),
        P("head", "blk"),
        P("head", "blk"),
        P("blk", "head"),
    )
    return jax.shard_map(body, mesh=mesh, in_specs=in_specs, out_specs=out_specs, check_vma=False)
```

```python
import functools
import types

import jax
import jax.numpy as jnp
from jax import lax
from jax.experimental import pallas as pl
from jax.experimental.pallas import tpu as pltpu
from jax.sharding import PartitionSpec as P

HEADS = 12
HEAD_DIM = 64
EXPERTS = 8
ROUTED = 12
TOP = 2
CONT_LEN = 1024
CAP = 24


EPS = 1e-06
HIGH = lax.Precision.HIGHEST


def silu_slope(pre):
    sigmoid_value = jax.nn.sigmoid(pre)
    return sigmoid_value * (1.0 + pre * (1.0 - sigmoid_value))


def visible_pairs(query_segment, query_position, key_segment, key_position, period):
    same_sequence = (query_segment[:, None] == key_segment[None, :]) & (
        key_position[None, :] <= query_position[:, None]
    )
    same_group = query_segment[:, None] // period == key_segment[None, :] // period
    shared = (
        (key_segment[None, :] % period == 0) & (query_segment[:, None] % period != 0) & same_group
    )
    return same_sequence | shared


def norm_back(grad_normed, source, inverse, gain):
    scaled = grad_normed * gain
    grad_source = inverse * scaled - source * inverse**3 * jnp.mean(
        scaled * source, axis=-1, keepdims=True
    )
    grad_gain = jnp.sum(grad_normed * source * inverse, axis=0)
    return (grad_source, grad_gain)


def around_blocks(pieces, combine, initial):
    return combine(
        initial,
        (
            lax.all_gather(pieces[0], "blk", axis=0, tiled=True),
            lax.all_gather(pieces[1], "blk", axis=0, tiled=True),
        ),
        jnp.int32(0),
    )


def softmax_last(logits):
    highest = jnp.max(logits, axis=-1, keepdims=True)
    raised = jnp.exp(logits - highest)
    return raised / jnp.sum(raised, axis=-1, keepdims=True)


def shards(
    inputs,
    cotangent,
    segment,
    position,
    routes,
    gate_residual,
    first_gain,
    second_gain,
    query_key_weight,
    value_weight,
    output_weight,
    router_weight,
    const_gate,
    const_vectors,
    gate_weight,
    up_weight,
    down_weight,
):
    tok_rows, width = inputs.shape
    head_count = lax.axis_size("head")
    blk_count = lax.axis_size("blk")
    local_heads = HEADS // head_count
    query_rows = head_count * tok_rows
    head_width = width // head_count
    width_split = blk_count // EXPERTS
    score_scale = HEAD_DIM ** (-0.5)
    period = tok_rows * blk_count // CONT_LEN + 1
    gathered = (
        lax.all_gather(first_gain, ("head", "blk"), axis=0, tiled=True),
        lax.all_gather(second_gain, ("head", "blk"), axis=0, tiled=True),
        lax.all_gather(query_key_weight, ("head", "blk"), axis=0, tiled=True),
        lax.all_gather(value_weight, ("head", "blk"), axis=0, tiled=True),
        lax.all_gather(output_weight, ("head", "blk"), axis=0, tiled=True),
        lax.all_gather(router_weight, ("head", "blk"), axis=0, tiled=True),
        lax.all_gather(const_gate, ("head", "blk"), axis=0, tiled=True),
        lax.all_gather(const_vectors, ("head", "blk"), axis=0, tiled=True),
        lax.all_gather(segment, ("head", "blk"), axis=0, tiled=True),
        lax.all_gather(position, ("head", "blk"), axis=0, tiled=True),
    )
    (
        gain_one,
        gain_two,
        full_joint,
        full_value,
        full_output,
        full_router,
        full_const,
        full_vectors,
        segment_all,
        position_all,
    ) = gathered
    gate_columns, up_columns, down_rows = (
        lax.all_gather(gate_weight, "head", axis=0, tiled=True),
        lax.all_gather(up_weight, "head", axis=0, tiled=True),
        lax.all_gather(down_weight, "head", axis=1, tiled=True),
    )
    gain_one = gain_one.astype(jnp.float32)
    gain_two = gain_two.astype(jnp.float32)
    source = inputs.astype(jnp.float32)
    inverse_one = lax.rsqrt(jnp.mean(source * source, axis=-1, keepdims=True) + EPS)
    normed_one = (source * inverse_one * gain_one).astype(jnp.bfloat16)
    joined = jnp.dot(normed_one, full_joint, preferred_element_type=jnp.float32)
    value_proj = jnp.dot(normed_one, full_value, preferred_element_type=jnp.float32)

    def head_layout(array):
        return array.astype(jnp.bfloat16).reshape(tok_rows, head_count, head_width)

    query_heads, key_heads, value_heads = (
        lax.all_to_all(
            head_layout(joined[:, :width]), "head", split_axis=1, concat_axis=0, tiled=True
        ),
        lax.all_to_all(
            head_layout(joined[:, width:]), "head", split_axis=1, concat_axis=0, tiled=True
        ),
        lax.all_to_all(head_layout(value_proj), "head", split_axis=1, concat_axis=0, tiled=True),
    )
    query_heads = query_heads.reshape(query_rows, local_heads, HEAD_DIM)
    key_heads = key_heads.reshape(query_rows, head_width)
    value_heads = value_heads.reshape(query_rows, head_width)
    blk_index = lax.axis_index("blk")
    segment_grid = segment_all.reshape(head_count, blk_count, tok_rows)
    position_grid = position_all.reshape(head_count, blk_count, tok_rows)
    query_segment = lax.dynamic_index_in_dim(segment_grid, blk_index, 1, keepdims=False).reshape(
        query_rows
    )
    query_position = lax.dynamic_index_in_dim(position_grid, blk_index, 1, keepdims=False).reshape(
        query_rows
    )
    key_segment = segment_grid.transpose(1, 0, 2).reshape(blk_count * query_rows)
    key_position = position_grid.transpose(1, 0, 2).reshape(blk_count * query_rows)

    def key_slices(pieces):
        piece_rows = pieces[0].shape[0]
        step_count = piece_rows // tok_rows
        return (
            pieces[0].reshape(step_count, tok_rows, local_heads, HEAD_DIM),
            pieces[1].reshape(step_count, tok_rows, local_heads, HEAD_DIM),
            key_segment.reshape(step_count, tok_rows),
            key_position.reshape(step_count, tok_rows),
        )

    def masked_scores(queries, block_keys, visible):
        scores = (
            jnp.einsum("qhd,khd->hqk", queries, block_keys, preferred_element_type=jnp.float32)
            * score_scale
        )
        return jnp.where(visible[None], scores, -jnp.inf)

    def attend_block(carried, block):
        block_keys, block_values, block_segment, block_position = block
        visible = visible_pairs(
            query_segment, query_position, block_segment, block_position, period
        )

        def attend_compute(state):
            top_score, running_total, weighted = state
            scores = masked_scores(query_heads, block_keys, visible)
            new_top = jnp.maximum(top_score, jnp.max(scores, axis=-1))
            anchor = jnp.where(new_top == -jnp.inf, 0.0, new_top)
            raised = jnp.exp(scores - anchor[..., None])
            factor = jnp.exp(top_score - anchor)
            running_total = running_total * factor + jnp.sum(raised, axis=-1)
            weighted = weighted * factor[..., None] + jnp.einsum(
                "hqk,khd->hqd",
                raised.astype(jnp.bfloat16),
                block_values,
                preferred_element_type=jnp.float32,
            )
            return (new_top, running_total, weighted)

        def unchanged(state):
            return state

        return (lax.cond(jnp.any(visible), attend_compute, unchanged, carried), None)

    def attend_piece(carried, pieces, first_row):
        result, unused = lax.scan(attend_block, carried, key_slices(pieces))
        return result

    start_state = (
        jnp.full((local_heads, query_rows), -jnp.inf, jnp.float32),
        jnp.zeros((local_heads, query_rows), jnp.float32),
        jnp.zeros((local_heads, query_rows, HEAD_DIM), jnp.float32),
    )
    top_score, running_total, weighted = around_blocks(
        (key_heads, value_heads), attend_piece, start_state
    )
    log_total = top_score + jnp.log(running_total)
    attended_local = (weighted / running_total[..., None]).transpose(1, 0, 2).astype(jnp.bfloat16)
    attended = lax.all_to_all(
        attended_local.reshape(query_rows, 1, head_width),
        "head",
        split_axis=0,
        concat_axis=1,
        tiled=True,
    ).reshape(tok_rows, width)
    middle = source + jnp.dot(attended, full_output, preferred_element_type=jnp.float32)
    inverse_two = lax.rsqrt(jnp.mean(middle * middle, axis=-1, keepdims=True) + EPS)
    normed_two = (middle * inverse_two * gain_two).astype(jnp.bfloat16)
    normed_float = normed_two.astype(jnp.float32)
    logits = jnp.dot(normed_two, full_router, preferred_element_type=jnp.float32) + gate_residual
    choose = (routes[:, :, None] == jnp.arange(ROUTED, dtype=jnp.int32)[None, None, :]).astype(
        jnp.float32
    )
    picked = jnp.sum(choose * logits[:, None, :], axis=-1)
    weighting = softmax_last(picked)
    pair_expert = routes.reshape(tok_rows * TOP)
    ffn_onehot = (pair_expert[:, None] == jnp.arange(EXPERTS, dtype=jnp.int32)[None, :]).astype(
        jnp.int32
    )
    pair_rank = jnp.sum((jnp.cumsum(ffn_onehot, axis=0) - ffn_onehot) * ffn_onehot, axis=-1)
    slot_match = (
        pair_rank[None, None, :] == jnp.arange(CAP, dtype=jnp.int32)[None, :, None]
    ).astype(jnp.int32)
    placement = (
        (ffn_onehot.T[:, None, :] * slot_match)
        .reshape(EXPERTS, CAP, tok_rows, TOP)
        .astype(jnp.float32)
    )
    select = jnp.sum(placement, axis=-1)
    gate_slot = jnp.einsum("ectj,tj->ect", placement, weighting, precision=HIGH)
    send_rows = jnp.einsum(
        "ect,td->ecd", select.astype(jnp.bfloat16), normed_two, preferred_element_type=jnp.float32
    ).astype(jnp.bfloat16)
    upstream = cotangent.astype(jnp.float32)
    slot_grad = jnp.einsum("ect,td->ecd", gate_slot, upstream, precision=HIGH).astype(jnp.bfloat16)
    rows_in = lax.all_to_all(
        jnp.repeat(send_rows, width_split, axis=0), "blk", split_axis=0, concat_axis=0, tiled=True
    )
    grads_in = lax.all_to_all(
        jnp.repeat(slot_grad, width_split, axis=0), "blk", split_axis=0, concat_axis=0, tiled=True
    )
    gate_pre = jnp.einsum("scd,df->scf", rows_in, gate_columns, preferred_element_type=jnp.float32)
    up_pre = jnp.einsum("scd,df->scf", rows_in, up_columns, preferred_element_type=jnp.float32)
    activated = jax.nn.silu(gate_pre)
    hidden = (activated * up_pre).astype(jnp.bfloat16)
    partial_out = jnp.einsum("scf,fd->scd", hidden, down_rows, preferred_element_type=jnp.float32)
    grad_hidden = jnp.einsum("scd,fd->scf", grads_in, down_rows, preferred_element_type=jnp.float32)
    grad_gate_pre = (grad_hidden * up_pre * silu_slope(gate_pre)).astype(jnp.bfloat16)
    grad_up_pre = (grad_hidden * activated).astype(jnp.bfloat16)
    grad_part = jnp.einsum(
        "scf,df->scd", grad_gate_pre, gate_columns, preferred_element_type=jnp.float32
    ) + jnp.einsum("scf,df->scd", grad_up_pre, up_columns, preferred_element_type=jnp.float32)
    back_out = lax.all_to_all(
        partial_out.astype(jnp.bfloat16), "blk", split_axis=0, concat_axis=0, tiled=True
    ).astype(partial_out.dtype)
    back_grad = lax.all_to_all(
        grad_part.astype(jnp.bfloat16), "blk", split_axis=0, concat_axis=0, tiled=True
    ).astype(grad_part.dtype)
    returned, grad_back, kept_rows, kept_grads, hidden, grad_gate_pre, grad_up_pre = (
        back_out,
        back_grad,
        rows_in,
        grads_in,
        hidden,
        grad_gate_pre,
        grad_up_pre,
    )
    expert_out = returned.reshape(EXPERTS, width_split, CAP, width).sum(axis=1)
    ffn_sum = jnp.einsum("ect,ecd->td", gate_slot, expert_out, precision=HIGH)
    mixing = softmax_last(
        jnp.dot(normed_two, full_const, preferred_element_type=jnp.float32).reshape(tok_rows, 2, 2)
    )
    vectors = full_vectors.astype(jnp.float32)
    copy_share = jnp.sum(weighting * (routes == EXPERTS + 1).astype(jnp.float32), axis=-1)
    const_share = jnp.stack(
        [
            jnp.sum(weighting * (routes == EXPERTS + 2 + const_index).astype(jnp.float32), axis=-1)
            for const_index in range(2)
        ],
        axis=1,
    )
    const_outs = [
        mixing[:, const_index, 0:1] * normed_float
        + mixing[:, const_index, 1:2] * vectors[:, const_index][None, :]
        for const_index in range(2)
    ]
    mixture = ffn_sum + copy_share[:, None] * normed_float
    for const_index in range(2):
        mixture = mixture + const_share[:, const_index : const_index + 1] * const_outs[const_index]
    layer_out = (middle + mixture).astype(jnp.bfloat16)
    output_dots = jnp.einsum("ecd,td->ect", expert_out, upstream, precision=HIGH)
    grad_weighting = jnp.einsum("ectj,ect->tj", placement, output_dots, precision=HIGH)
    copy_dot = jnp.sum(upstream * normed_float, axis=-1)
    grad_weighting = (
        grad_weighting + (routes == EXPERTS + 1).astype(jnp.float32) * copy_dot[:, None]
    )
    for const_index in range(2):
        const_dot = jnp.sum(upstream * const_outs[const_index], axis=-1)
        grad_weighting = (
            grad_weighting
            + (routes == EXPERTS + 2 + const_index).astype(jnp.float32) * const_dot[:, None]
        )
    grad_picked = weighting * (
        grad_weighting - jnp.sum(weighting * grad_weighting, axis=-1, keepdims=True)
    )
    grad_logits = jnp.einsum("tj,tjr->tr", grad_picked, choose, precision=HIGH)
    vector_dots = jnp.dot(upstream, vectors, precision=HIGH)
    grad_mixing = const_share[:, :, None] * jnp.stack(
        [jnp.broadcast_to(copy_dot[:, None], vector_dots.shape), vector_dots], axis=-1
    )
    grad_mix = (
        mixing * (grad_mixing - jnp.sum(mixing * grad_mixing, axis=-1, keepdims=True))
    ).reshape(tok_rows, 4)
    grad_const_weight = jnp.dot(normed_float.T, grad_mix, precision=HIGH)
    grad_vectors = jnp.einsum("ti,td->di", const_share * mixing[:, :, 1], upstream, precision=HIGH)
    grad_router_weight = jnp.dot(normed_float.T, grad_logits, precision=HIGH)
    direct_share = (
        copy_share + const_share[:, 0] * mixing[:, 0, 0] + const_share[:, 1] * mixing[:, 1, 0]
    )
    grad_normed_two = direct_share[:, None] * upstream
    grad_normed_two = grad_normed_two + jnp.dot(
        grad_mix, full_const.astype(jnp.float32).T, precision=HIGH
    )
    grad_normed_two = grad_normed_two + jnp.dot(
        grad_logits, full_router.astype(jnp.float32).T, precision=HIGH
    )
    grad_down_local = jnp.einsum(
        "scf,scd->fd", hidden, kept_grads, preferred_element_type=jnp.float32
    )
    grad_gate_local = jnp.einsum(
        "scd,scf->df", kept_rows, grad_gate_pre, preferred_element_type=jnp.float32
    )
    grad_up_local = jnp.einsum(
        "scd,scf->df", kept_rows, grad_up_pre, preferred_element_type=jnp.float32
    )
    grad_slots = grad_back.reshape(EXPERTS, width_split, CAP, width).sum(axis=1)
    grad_normed_two = grad_normed_two + jnp.einsum(
        "ect,ecd->td", select, grad_slots, precision=HIGH
    )
    grad_gate_sum, grad_up_sum, grad_down_sum = (
        lax.psum_scatter(
            grad_gate_local.astype(jnp.bfloat16), "head", scatter_dimension=0, tiled=True
        ).astype(jnp.float32),
        lax.psum_scatter(
            grad_up_local.astype(jnp.bfloat16), "head", scatter_dimension=0, tiled=True
        ).astype(jnp.float32),
        lax.psum_scatter(
            grad_down_local.astype(jnp.bfloat16), "head", scatter_dimension=1, tiled=True
        ).astype(jnp.float32),
    )
    grad_from_norm, grad_gain_two = norm_back(grad_normed_two, middle, inverse_two, gain_two)
    grad_middle = upstream + grad_from_norm
    branch_grad = grad_middle.astype(jnp.bfloat16)
    grad_out_weight = jnp.einsum(
        "tc,td->cd", attended, branch_grad, preferred_element_type=jnp.float32
    )
    grad_attended = jnp.einsum(
        "td,cd->tc", branch_grad, full_output, preferred_element_type=jnp.float32
    ).astype(jnp.bfloat16)
    grad_heads = lax.all_to_all(
        grad_attended.reshape(tok_rows, head_count, head_width),
        "head",
        split_axis=1,
        concat_axis=0,
        tiled=True,
    )
    grad_heads = grad_heads.reshape(query_rows, local_heads, HEAD_DIM)
    offset = jnp.sum(grad_heads.astype(jnp.float32) * attended_local.astype(jnp.float32), axis=-1).T

    def probe_block(queries, grads, lse_rows, offset_rows, block_keys, block_values, visible):
        scores = masked_scores(queries, block_keys, visible)
        probabilities = jnp.exp(scores - lse_rows[..., None])
        grad_probs = jnp.einsum(
            "qhd,khd->hqk", grads, block_values, preferred_element_type=jnp.float32
        )
        grad_scores = (probabilities * (grad_probs - offset_rows[..., None])).astype(jnp.bfloat16)
        return (probabilities, grad_scores)

    zero_query = jnp.zeros((query_rows, local_heads, HEAD_DIM), jnp.float32)

    def backward_block(grad_query, block):
        block_keys, block_values, block_segment, block_position = block
        visible = visible_pairs(
            query_segment, query_position, block_segment, block_position, period
        )

        def backward_compute(accumulated):
            probabilities, grad_scores = probe_block(
                query_heads, grad_heads, log_total, offset, block_keys, block_values, visible
            )
            grad_values = jnp.einsum(
                "hqk,qhd->khd",
                probabilities.astype(jnp.bfloat16),
                grad_heads,
                preferred_element_type=jnp.float32,
            )
            accumulated = (
                accumulated
                + jnp.einsum(
                    "hqk,khd->qhd", grad_scores, block_keys, preferred_element_type=jnp.float32
                )
                * score_scale
            )
            grad_keys = (
                jnp.einsum(
                    "hqk,qhd->khd", grad_scores, query_heads, preferred_element_type=jnp.float32
                )
                * score_scale
            )
            return (accumulated, jnp.concatenate([grad_keys, grad_values], axis=-1))

        def skipped(accumulated):
            return (
                accumulated,
                jnp.zeros((block_keys.shape[0], local_heads, 2 * HEAD_DIM), jnp.float32),
            )

        return lax.cond(jnp.any(visible), backward_compute, skipped, grad_query)

    def fold_back(carried, pieces, first_row):
        grad_query, stacked = lax.scan(backward_block, carried[0], key_slices(pieces))
        term_piece = stacked.reshape(pieces[0].shape[0], local_heads * 2 * HEAD_DIM)
        return (grad_query, term_piece)

    zero_term = jnp.zeros((blk_count * query_rows, local_heads * 2 * HEAD_DIM), jnp.float32)
    grad_query, key_term = around_blocks(
        (key_heads, value_heads), fold_back, (zero_query, zero_term)
    )
    key_sums = lax.psum_scatter(key_term, "blk", scatter_dimension=0, tiled=True).reshape(
        query_rows, local_heads, 2, HEAD_DIM
    )
    grad_key_heads = key_sums[:, :, 0].astype(jnp.bfloat16).reshape(query_rows, 1, head_width)
    grad_value_heads = key_sums[:, :, 1].astype(jnp.bfloat16).reshape(query_rows, 1, head_width)
    grad_query_heads = grad_query.astype(jnp.bfloat16).reshape(query_rows, 1, head_width)
    grad_query_tok, grad_key_tok, grad_value_tok = (
        lax.all_to_all(grad_query_heads, "head", split_axis=0, concat_axis=1, tiled=True),
        lax.all_to_all(grad_key_heads, "head", split_axis=0, concat_axis=1, tiled=True),
        lax.all_to_all(grad_value_heads, "head", split_axis=0, concat_axis=1, tiled=True),
    )
    grad_joined = jnp.concatenate(
        [grad_query_tok.reshape(tok_rows, width), grad_key_tok.reshape(tok_rows, width)], axis=1
    )
    grad_value_tok = grad_value_tok.reshape(tok_rows, width)
    grad_normed_one = jnp.einsum(
        "tc,dc->td", grad_joined, full_joint, preferred_element_type=jnp.float32
    ) + jnp.einsum("tc,dc->td", grad_value_tok, full_value, preferred_element_type=jnp.float32)
    grad_joint_weight = jnp.einsum(
        "td,tc->dc", normed_one, grad_joined, preferred_element_type=jnp.float32
    )
    grad_value_weight = jnp.einsum(
        "td,tc->dc", normed_one, grad_value_tok, preferred_element_type=jnp.float32
    )
    grad_from_first, grad_gain_one = norm_back(grad_normed_one, source, inverse_one, gain_one)
    grad_input = grad_middle + grad_from_first
    summed = (
        lax.psum_scatter(grad_gain_one, ("head", "blk"), scatter_dimension=0, tiled=True),
        lax.psum_scatter(grad_gain_two, ("head", "blk"), scatter_dimension=0, tiled=True),
        lax.psum_scatter(grad_joint_weight, ("head", "blk"), scatter_dimension=0, tiled=True),
        lax.psum_scatter(grad_value_weight, ("head", "blk"), scatter_dimension=0, tiled=True),
        lax.psum_scatter(grad_out_weight, ("head", "blk"), scatter_dimension=0, tiled=True),
        lax.psum_scatter(grad_router_weight, ("head", "blk"), scatter_dimension=0, tiled=True),
        lax.psum_scatter(grad_const_weight, ("head", "blk"), scatter_dimension=0, tiled=True),
        lax.psum_scatter(grad_vectors, ("head", "blk"), scatter_dimension=0, tiled=True),
    )
    return (
        layer_out,
        grad_input,
        grad_logits,
        summed[0],
        summed[1],
        summed[2],
        summed[3],
        summed[4],
        summed[5],
        summed[6],
        summed[7],
        grad_gate_sum,
        grad_up_sum,
        grad_down_sum,
    )


MESH = pl.DeviceIdType.MESH
SMALL = 24
ROUTER_AT, MIX_AT, VECTOR_AT, GAIN_ONE_AT, GAIN_TWO_AT = 0, 12, 16, 18, 19
PAD = 32
CHUNK = 4
FAR = 1 << 20
NT = (((1,), (1,)), ((), ()))
TN = (((0,), (0,)), ((), ()))


def mul(left, right):
    return jnp.dot(left, right, preferred_element_type=jnp.float32)


def mul_nt(left, right):
    return lax.dot_general(left, right, NT, preferred_element_type=jnp.float32)


def mul_tn(left, right):
    return lax.dot_general(left, right, TN, preferred_element_type=jnp.float32)


def low(values):
    return values.astype(jnp.bfloat16)


def wide(values):
    return values.astype(jnp.float32)


def halves(values):
    high = low(values)
    return high, low(values - wide(high))


def shape(dims, dtype=jnp.bfloat16):
    return jax.ShapeDtypeStruct(dims, dtype)


def compute(body, outs, ins, scratch=(), smem=0):
    specs = [pl.BlockSpec(memory_space=pltpu.SMEM)] * smem
    specs += [pl.BlockSpec(memory_space=pltpu.VMEM)] * (len(ins) - smem)
    return pl.pallas_call(
        body,
        out_shape=outs,
        in_specs=specs,
        out_specs=[pl.BlockSpec(memory_space=pltpu.VMEM)] * len(outs),
        scratch_shapes=list(scratch),
        compiler_params=pltpu.CompilerParams(vmem_limit_bytes=52 * 2**20),
    )(*ins)


def exchange(body, sizes, ins, outs, scratch, number, far=(), room=52):
    names = list(ins) + list(outs) + list(scratch)

    def run(*refs):
        body(Place(*sizes), types.SimpleNamespace(**dict(zip(names, refs))))

    def spec(name):
        return pl.BlockSpec(memory_space=pl.ANY if name in far else pltpu.VMEM)

    results = pl.pallas_call(
        run,
        out_shape=list(outs.values()),
        in_specs=[spec(name) for name in ins],
        out_specs=[spec(name) for name in outs],
        scratch_shapes=list(scratch.values()),
        compiler_params=pltpu.CompilerParams(
            collective_id=number, has_side_effects=True, vmem_limit_bytes=room * 2**20
        ),
    )(*ins.values())
    return types.SimpleNamespace(**dict(zip(outs, results)))


def vmem(*dims, dtype=jnp.bfloat16):
    return pltpu.VMEM(dims, dtype)


def vmem_wide(*dims):
    return pltpu.VMEM(dims, jnp.float32)


def greet(devices):
    barrier = pltpu.get_barrier_semaphore()
    for device in devices:
        pl.semaphore_signal(barrier, inc=1, device_id=device, device_id_type=MESH)


def greeted(count):
    pl.semaphore_wait(pltpu.get_barrier_semaphore(), count)


def meet(devices):
    greet(devices)
    greeted(len(devices))


class Place:
    def __init__(self, head_count, blk_count):
        self.head_count, self.blk_count = head_count, blk_count
        self.head, self.blk = lax.axis_index("head"), lax.axis_index("blk")
        self.half = blk_count // 2
        self.chip, self.core = self.blk // 2, self.blk % 2
        self.twin = self.blk + 1 - 2 * self.core

    def along(self, axis):
        if axis == "head":
            return self.head, self.head_count
        return self.blk, self.blk_count

    def device(self, axis, index):
        return (index, self.blk) if axis == "head" else (self.head, index)

    def others(self, axis):
        me, size = self.along(axis)
        return [self.device(axis, (me + step) % size) for step in range(1, size)]

    def partners(self):
        beside = self.chip + 1 - 2 * (self.chip % 2)
        beyond = (self.chip + self.half // 2) % self.half
        across = beside + self.half // 2 - self.half * (beside // (self.half // 2))
        return [across, beside, beyond]

    def chips(self):
        return [chip * 2 + self.core for chip in self.partners()]

    def exchange_order(self, axis):
        me, size = self.along(axis)
        if axis == "head":
            return [(step - 1, (me + step) % size, (me + size - step) % size) for step in range(1, size)]
        found = []
        for chip in self.partners():
            for core in (self.core, 1 - self.core):
                found.append(chip * 2 + core)
        found.append(self.twin)
        return [(number, blk, blk) for number, blk in enumerate(found)]

    def near(self):
        return [(self.head, self.twin)] + [(self.head, blk) for blk in self.chips()]


def dma(*dims):
    return pltpu.SemaphoreType.DMA(dims)


def remote(source, target, sent, got, device):
    return pltpu.make_async_remote_copy(
        src_ref=source,
        dst_ref=target,
        send_sem=sent,
        recv_sem=got,
        device_id=device,
        device_id_type=MESH,
    )


def send(source, target, sent, got, device):
    copy = remote(source, target, sent, got, device)
    copy.start()
    return copy


def keep(source, target, done):
    copy = pltpu.make_async_copy(source, target, done)
    copy.start()
    return copy


def scatter(place, axis, source, target, sent, got, wanted=lambda number: True):
    me, size = place.along(axis)
    copies = []
    for number, other, unused in place.exchange_order(axis):
        if not wanted(number):
            continue
        copies.append(
            send(
                source.at[other],
                target.at[me],
                sent.at[number],
                got.at[number],
                place.device(axis, other),
            )
        )
    return copies


def gather(place, axis, source, target, sent, got):
    me, size = place.along(axis)
    copies = []
    for step in range(1, size):
        other = (me + step) % size
        copies.append(
            send(
                source, target.at[me], sent.at[step - 1], got.at[step - 1], place.device(axis, other)
            )
        )
    return copies


class Spread:
    def __init__(self, place, ref, sent, got):
        self.place, self.ref, self.sent, self.got = place, ref, sent, got
        self.direct = [
            self.pass_on(step, place.blk, blk) for step, blk in enumerate(place.chips(), 1)
        ]
        self.rest = [self.pass_on(0, place.blk, place.twin)]

    def pass_on(self, lane, slot, blk):
        return send(
            self.ref.at[slot],
            self.ref.at[slot],
            self.sent.at[lane],
            self.got.at[lane],
            (self.place.head, blk),
        )

    def relay(self):
        place = self.place
        for step, slot in enumerate(place.chips(), 1):
            self.direct[step - 1].wait_recv()
            self.rest.append(self.pass_on(place.half - 1 + step, slot, place.twin))

    def wait(self):
        for copy in self.direct:
            copy.wait_send()
        for copy in self.rest:
            copy.wait()


class Fold:
    def __init__(self, place, terms, theirs, arrived, sent_twin, got_twin, sent, got):
        self.place, self.terms, self.theirs, self.arrived = place, terms, theirs, arrived
        self.sent, self.got = sent, got
        self.order = place.partners() + [place.chip]
        self.across = [
            send(
                terms.at[chip * 2 + 1 - place.core],
                theirs.at[step],
                sent_twin.at[step],
                got_twin.at[step],
                (place.head, place.twin),
            )
            for step, chip in enumerate(self.order)
        ]
        self.onward = []

    def add(self):
        place = self.place
        for step, chip in enumerate(self.order):
            self.across[step].wait_recv()
            total = wide(self.theirs[step]) + wide(self.terms[chip * 2 + place.core])
            self.theirs[step] = total.astype(self.theirs.dtype)
            if step < place.half - 1:
                self.onward.append(
                    send(
                        self.theirs.at[step],
                        self.arrived.at[step],
                        self.sent.at[step],
                        self.got.at[step],
                        (place.head, chip * 2 + place.core),
                    )
                )

    def total(self):
        total = wide(self.theirs[self.place.half - 1])
        for step, copy in enumerate(self.onward):
            copy.wait_recv()
            total = total + wide(self.arrived[step])
        return total

    def wait(self):
        for copy in self.across + self.onward:
            copy.wait_send()


def wait_all(*groups):
    for group in groups:
        for copy in group:
            copy.wait()


def far_block(number, head_count):
    head = lax.axis_index("head")
    found = 0
    for place in range(head_count):
        by_distance = sorted(range(head_count), key=lambda other: -abs(other - place))
        found = found + jnp.where(head == place, by_distance[number], 0)
    return found


def block_at(step, head_count):
    return (lax.axis_index("head") + step) % head_count


class LineGather:
    def __init__(self, place, ref, sent, got):
        self.place, self.ref, self.sent, self.got = place, ref, sent, got
        self.onward(0, place.head)
        self.back(0, place.head)

    def copy(self, way, hop, slot):
        head = self.place.head + 1 - 2 * way
        return remote(
            self.ref.at[slot],
            self.ref.at[slot],
            self.sent.at[way, hop],
            self.got.at[way, hop],
            (head, self.place.blk),
        )

    def sends(self, way, hop):
        head, last = self.place.head, self.place.head_count - 1
        if way == 0:
            return (head >= hop) & (head < last)
        return (head + hop <= last) & (head > 0)

    def has(self, way, hop):
        head, last = self.place.head, self.place.head_count - 1
        return head >= hop if way == 0 else head + hop <= last

    def onward(self, hop, slot):
        @pl.when(self.sends(0, hop))
        def _():
            self.copy(0, hop, slot).start()

    def back(self, hop, slot):
        @pl.when(self.sends(1, hop))
        def _():
            self.copy(1, hop, slot).start()

    def receive(self, hop):
        head, last = self.place.head, self.place.head_count - 1
        for way, slot in ((0, head - hop), (1, head + hop)):

            @pl.when(self.has(way, hop))
            def _():
                self.copy(way, hop - 1, slot).wait_recv()

            if hop < last:
                (self.onward, self.back)[way](hop, slot)

    def receive_all(self):
        for hop in range(1, self.place.head_count):
            self.receive(hop)

    def wait(self):
        for hop in range(self.place.head_count - 1):
            for way in range(2):

                @pl.when(self.sends(way, hop))
                def _():
                    self.copy(way, hop, self.place.head).wait_send()


class LineSum:
    def __init__(self, place, outbox, inbox, sent, got):
        self.place, self.outbox, self.inbox = place, outbox, inbox
        self.sent, self.got = sent, got

    def copy(self, way, slot):
        head = self.place.head + 1 - 2 * way
        return remote(
            self.outbox.at[slot],
            self.inbox.at[way, slot],
            self.sent.at[slot],
            self.got.at[way, slot],
            (head, self.place.blk),
        )

    def add(self, slot, term):
        head, last = self.place.head, self.place.head_count - 1
        self.outbox[slot] = low(term)
        for way, towards, first in ((0, slot > head, head == 0), (1, slot < head, head == last)):

            @pl.when(towards & jnp.logical_not(first))
            def _():
                self.copy(way, slot).wait_recv()
                self.outbox[slot] = low(wide(self.outbox[slot]) + wide(self.inbox[way, slot]))

            @pl.when(towards)
            def _():
                self.copy(way, slot).start()

    def total(self, term):
        head, last = self.place.head, self.place.head_count - 1
        for way, has in ((0, head > 0), (1, head < last)):

            @pl.when(has)
            def _():
                self.copy(way, head).wait_recv()

        for way, has in ((0, head > 0), (1, head < last)):
            term = term + jnp.where(has, wide(self.inbox[way, head]), 0.0)
        return term

    def wait(self):
        for slot in range(self.place.head_count):

            @pl.when(slot > self.place.head)
            def _():
                self.copy(0, slot).wait_send()

            @pl.when(slot < self.place.head)
            def _():
                self.copy(1, slot).wait_send()


def rows_at(block, tokens):
    return pl.ds(pl.multiple_of(block * tokens, tokens), tokens)


def lanes_joined(*parts):
    return jnp.concatenate(parts, axis=1)


def rows_joined(*parts):
    return jnp.concatenate(parts, axis=0)


def packed_rows(piece):
    half = piece.shape[1] // 2
    return lanes_joined(piece[:16], rows_joined(piece[16:, :half], piece[16:, half:]))


def unpacked_rows(packed):
    width = packed.shape[1] * 2 // 3
    rest = packed[:, width:]
    return rows_joined(packed[:, :width], lanes_joined(rest[:8], rest[8:]))


def own_pieces(product, rows, head_count, blk_count, blk):
    return rows_joined(
        *[
            product[(head * blk_count + blk) * rows : (head * blk_count + blk + 1) * rows]
            for head in range(head_count)
        ]
    )


def open_layer(place, r):
    head_count, blk_count = place.head_count, place.blk_count
    head, blk = place.head, place.blk
    tokens, width = r.x.shape
    rows = r.joint_rows.shape[0]
    columns = r.down_0.shape[1]
    head_width = width // head_count
    split = 2 * HEAD_DIM
    joint_width = r.joint.shape[1]
    greet(place.others("head") + place.near())
    names = ["router", "mix", "vectors", "gain_one", "gain_two", "joint_rows", "value_rows"]
    names += ["segment", "position", "routes", "residual", "output_rows", "x"]
    here = {
        name: keep(getattr(r, name), getattr(r, "my_" + name), r.local.at[number])
        for number, name in enumerate(names)
    }
    number = len(names)
    late_own = [keep(r.g, r.g_all.at[head], r.local.at[number])]
    for step, piece in enumerate((r.down_0, r.down_1, r.down_2, r.down_3)):
        at = rows_at(block_at(step, head_count), columns)
        late_own.append(keep(r.down.at[:, at], piece, r.local.at[number + 1 + step]))
    for name in names[:7]:
        here[name].wait()
    marks = rows_joined(
        *[
            wide(ref[...])
            for ref in (r.my_router, r.my_mix, r.my_vectors, r.my_gain_one, r.my_gain_two)
        ]
    )
    marks = rows_joined(marks, jnp.zeros((128 - marks.shape[0], rows), jnp.float32))
    marks = lanes_joined(marks, jnp.zeros((128, 128 - rows), jnp.float32))
    marks = marks.T[:rows]
    both = wide(r.my_joint_rows[...])
    third = wide(r.my_value_rows[...])
    filler = jnp.zeros((rows, HEAD_DIM), jnp.float32)
    for part in range(head_count):
        at = part * head_width
        piece = lanes_joined(
            both[:, at : at + head_width],
            filler,
            both[:, width + at : width + at + head_width],
            third[:, at + split : at + head_width],
            third[:, at : at + split],
            marks,
        )
        r.joint_own[part] = low(packed_rows(piece))
    r.joint_all[blk, head] = r.joint_own[head]
    for name in names[7:]:
        here[name].wait()
    facts = rows_joined(
        wide(r.my_segment[...]),
        wide(r.my_position[...]),
        wide(r.my_routes[...]),
        jnp.zeros((4, tokens), jnp.float32),
        r.my_residual[...],
        jnp.zeros((24 - 8 - ROUTED, tokens), jnp.float32),
    )
    r.facts_own[...] = facts
    r.facts[head] = facts
    r.marks_all[blk, head] = facts[:8]
    greeted(head_count - 1 + place.half)
    first = scatter(place, "head", r.joint_own, r.joint_all.at[blk], r.sent.at[0], r.got.at[0])
    first += gather(place, "head", r.facts_own, r.facts, r.sent.at[1], r.got.at[1])
    r.output_own[...] = low(packed_rows(wide(r.my_output_rows[...])))
    r.output_part[head] = r.output_own[...]
    r.x_all[head] = r.my_x[...]
    for copy in first:
        copy.wait_send()
    tokens_in = LineGather(place, r.x_all, r.sent_line.at[0], r.got_line.at[0])
    for copy in first:
        copy.wait_recv()
    for part in range(head_count):
        r.marks_all[blk, part] = r.facts[part, 0:8, :]
    joint_spread = Spread(place, r.joint_all, r.sent_joint, r.got_joint)
    marks_spread = Spread(place, r.marks_all, r.sent_marks, r.got_marks)
    tokens_in.receive(1)
    joint_spread.relay()
    marks_spread.relay()
    tokens_in.receive(2)
    joint_spread.wait()
    marks_spread.wait()
    column = lax.broadcasted_iota(jnp.int32, (8, 128), 1)
    places = jnp.zeros((8, 128), jnp.float32)
    for part in range(head_count):
        for other in range(blk_count):
            places = jnp.where(
                column == other * head_count + part, r.marks_all[other, part, :, 0:1], places
            )
    r.places[...] = places.astype(jnp.int32)
    for part in range(head_count):
        for other in range(blk_count):
            r.joint_wide[pl.ds((part * blk_count + other) * rows, rows), :] = unpacked_rows(
                wide(r.joint_all[other, part])
            )
    r.joint[...] = low(r.joint_wide[:, :joint_width])
    small_rows = r.joint_wide[:, joint_width:].T
    r.small[...] = small_rows[:SMALL]
    gain = small_rows[GAIN_ONE_AT : GAIN_ONE_AT + 1]
    for hop in range(3, head_count):
        tokens_in.receive(hop)
    outputs_in = LineGather(place, r.output_part, r.sent_line.at[1], r.got_line.at[1])
    late_own[0].wait()
    upstream_in = LineGather(place, r.g_all, r.sent_line.at[2], r.got_line.at[2])
    pair_spreads = []
    cut = r.queries.shape[1]
    for step in range(head_count):
        block = block_at(step, head_count)
        source = wide(r.x_all[block])
        inverse = lax.rsqrt(jnp.mean(source * source, axis=-1, keepdims=True) + EPS)
        rows_normed = low(source * inverse * gain)
        span = rows_at(block, tokens)
        r.normed[span, :] = rows_normed
        product = mul(rows_normed, r.joint[...])
        r.queries[span, :] = low(product[:, :cut])
        r.pairs_all[blk, block] = low(product[:, cut:])
        pair_spreads.append(
            Spread(place, r.pairs_all.at[:, block], r.sent_pairs.at[step], r.got_pairs.at[step])
        )
    for step, spread in enumerate(pair_spreads):
        if 0 < step + 1 < head_count:
            outputs_in.receive(step + 1)
            upstream_in.receive(step + 1)
        spread.relay()
    for spread in pair_spreads:
        spread.wait()
    for line in (tokens_in, outputs_in, upstream_in):
        line.wait()
    wait_all(late_own[1:])


def slots_of(head_count, facts, first, second):
    tokens = first.shape[2]
    earlier = low(
        wide(
            lax.broadcasted_iota(jnp.int32, (tokens, tokens), 0)
            < lax.broadcasted_iota(jnp.int32, (tokens, tokens), 1)
        )
    )
    expert = wide(lax.broadcasted_iota(jnp.int32, (2 * EXPERTS, tokens), 0))
    expert_at = wide(lax.broadcasted_iota(jnp.int32, (EXPERTS, CAP, tokens), 0))
    rank_at = wide(lax.broadcasted_iota(jnp.int32, (EXPERTS, CAP, tokens), 1))
    for head in range(head_count):
        routes = [facts[head, 2 + choice : 3 + choice, :] for choice in range(TOP)]
        named = jnp.where((routes[0] == expert) | (routes[1] == expert), 1.0, 0.0)
        count = mul(low(named), earlier)[:EXPERTS]
        fits = count[:, None, :] == rank_at
        for choice, out in enumerate((first, second)):
            match = (routes[choice][None] == expert_at) & fits
            out[head] = low(jnp.where(match, 1.0, 0.0).reshape(EXPERTS * CAP, tokens))


def place_upstream(place, r):
    head_count = place.head_count
    slots_of(head_count, r.facts, r.first, r.second)
    parts = []
    for number in range(head_count):
        block = far_block(number, head_count)
        found = mul(r.first[block] + r.second[block], r.g_all[block])
        parts.append(found.reshape(EXPERTS, CAP, found.shape[1]))
    r.upstream[...] = low(jnp.concatenate(parts, axis=1))


def visible_blocks(places, period, me, count, chosen, shift):
    mine, mine_at = places[0, me], places[1, me]

    def look(block, found):
        other, other_at = places[0, block], places[1, block]
        same = other == mine
        shared = (other // period == mine // period) & (other % period == 0) & (mine % period != 0)
        seen = (same & (other_at <= mine_at)) | shared
        chosen[found] = block
        shift[found] = jnp.where(same & (other_at == mine_at), 0, -FAR)
        return found + seen.astype(jnp.int32)

    found = lax.fori_loop(0, count, look, jnp.int32(0))
    for extra in range(CHUNK):
        chosen[found + extra] = jnp.int32(0)
        shift[found + extra] = jnp.int32(FAR)
    return (found + CHUNK - 1) // CHUNK


def chunk_mask(tokens, heads, shift, start):
    row = lax.broadcasted_iota(jnp.int32, (tokens, tokens), 0)
    column = lax.broadcasted_iota(jnp.int32, (tokens, tokens), 1)
    gap = row - column
    parts = [
        jnp.where(gap + shift[start + step] <= 0, 1.0, 0.0) for step in range(CHUNK)
    ]
    mask = jnp.concatenate(parts, axis=0)
    return jnp.concatenate([mask] * heads, axis=1) > 0.5


def chunk_rows(pairs, chosen, start, low_lane, high_lane):
    return jnp.concatenate(
        [pairs[chosen[start + step], :, low_lane:high_lane] for step in range(CHUNK)], axis=0
    )


def lanes_at(rows, first, last):
    lane = lax.broadcasted_iota(jnp.int32, rows.shape, 1)
    return jnp.where((lane >= first) & (lane < last), rows, jnp.zeros_like(rows))


def query_rows_of(queries, head, tokens):
    rows = queries[pl.ds(head * tokens, tokens), :]
    rows = low(wide(rows) * HEAD_DIM ** (-0.5))
    return jnp.concatenate(
        [lanes_at(rows, part * HEAD_DIM, (part + 1) * HEAD_DIM) for part in range(3)], axis=0
    )


def attend(sizes, period, places, queries, pairs, attended, totals, chosen, shift):
    head_count, blk_count = sizes
    blocks, tokens, lanes = pairs.shape
    heads = 3
    blk = lax.axis_index("blk")
    for head in range(head_count):
        chunks = visible_blocks(
            places, period, blk * head_count + head, blocks, chosen, shift
        )
        asked = query_rows_of(queries, head, tokens)

        def step(number, carried):
            top, total, weighted = carried
            start = number * CHUNK
            scores = mul_nt(chunk_rows(pairs, chosen, start, 0, 256), asked)
            scores = jnp.where(chunk_mask(tokens, heads, shift, start), scores, -jnp.inf)
            new_top = jnp.maximum(top, jnp.max(scores, axis=0, keepdims=True))
            raised = jnp.exp(scores - new_top)
            factor = jnp.exp(top - new_top)
            total = total * factor + jnp.sum(raised, axis=0, keepdims=True)
            mixed = mul_tn(chunk_rows(pairs, chosen, start, 128, lanes), low(raised))
            mixed = jnp.concatenate(
                [mixed[128:192, 0:128], mixed[192:256, 128:256], mixed[64:128, 256:384]], axis=1
            )
            return (new_top, total, weighted * factor + mixed)

        wide_lanes = heads * tokens
        top, total, weighted = lax.fori_loop(
            0,
            chunks,
            step,
            (
                jnp.full((1, wide_lanes), -1e30, jnp.float32),
                jnp.zeros((1, wide_lanes), jnp.float32),
                jnp.zeros((HEAD_DIM, wide_lanes), jnp.float32),
            ),
        )
        outcome = low(weighted / total)
        totals[head] = jnp.broadcast_to(top + jnp.log(total), totals.shape[1:])
        for part in range(heads):
            attended[head, part * HEAD_DIM : (part + 1) * HEAD_DIM, :] = outcome[
                :, part * tokens : (part + 1) * tokens
            ]


def attend_back(sizes, period, places, queries, pairs, attended, totals, given, query_grad, pair_grad, chosen, shift, summed):
    head_count, blk_count = sizes
    blocks, tokens, lanes = pairs.shape
    heads = 3
    blk = lax.axis_index("blk")
    summed[...] = jnp.zeros_like(summed)
    for head in range(head_count):
        chunks = visible_blocks(
            places, period, blk * head_count + head, blocks, chosen, shift
        )
        asked = query_rows_of(queries, head, tokens)
        turned = wide(given[head])
        own = rows_joined(jnp.zeros((HEAD_DIM, tokens), jnp.float32), turned[128:192], turned[0:128])
        own = low(own.T)
        back = jnp.concatenate(
            [lanes_at(own, 128, 192), lanes_at(own, 192, 256), lanes_at(own, 64, 128)], axis=0
        )
        dots = turned * wide(attended[head])
        offset = jnp.concatenate(
            [
                jnp.sum(dots[part * HEAD_DIM : (part + 1) * HEAD_DIM], axis=0, keepdims=True)
                for part in range(heads)
            ],
            axis=1,
        )
        total = totals[head, 0:1, :]

        def step(number, carried):
            start = number * CHUNK
            keys = chunk_rows(pairs, chosen, start, 0, 256)
            values = chunk_rows(pairs, chosen, start, 128, lanes)
            scores = mul_nt(keys, asked)
            raised = jnp.where(
                chunk_mask(tokens, heads, shift, start), jnp.exp(scores - total), 0.0
            )
            grad_raised = mul_nt(values, back)
            grad_scores = low(raised * (grad_raised - offset))
            key_part = mul(grad_scores, asked)
            value_part = mul(low(raised), back)
            both = jnp.concatenate(
                [
                    key_part[:, :128],
                    key_part[:, 128:] + value_part[:, :128],
                    value_part[:, 128:],
                ],
                axis=1,
            )
            for block in range(CHUNK):
                at = chosen[start + block]
                summed[at] = summed[at] + both[block * tokens : (block + 1) * tokens]
            found = mul_tn(keys, grad_scores)
            return carried + jnp.concatenate(
                [found[0:64, 0:128], found[64:128, 128:256], found[128:192, 256:384]], axis=1
            )

        found = lax.fori_loop(
            0, chunks, step, jnp.zeros((HEAD_DIM, heads * tokens), jnp.float32)
        )
        found = found * HEAD_DIM ** (-0.5)
        stacked = jnp.concatenate(
            [found[:, part * tokens : (part + 1) * tokens] for part in range(heads)]
            + [jnp.zeros((HEAD_DIM, tokens), jnp.float32)],
            axis=0,
        )
        query_grad[pl.ds(head * tokens, tokens), :] = low(stacked.T)
    pair_grad[...] = low(summed[...])


def ffn_rows(number, span, here, r, gate, up, down, lane):
    width = r.grads_in.shape[2]
    group = lane.shape[0]
    blk_count, span_rows = r.slots_in.shape[0], group // r.slots_in.shape[0]
    entry = r.slots_in[:, span, :].reshape(group, width + 128)
    rows = entry[:, :width]
    r.taken[here, :] = rows
    tail = wide(entry[:, width:])
    share = tail[:, 0:1] + tail[:, 64:65]
    scaled_rows = low(share * wide(r.grads_in[:, span, :].reshape(group, width)))
    r.scaled[here, :] = scaled_rows
    gate_pre = mul(rows, gate)
    up_pre = mul(rows, up)
    sigmoid = 1.0 / (1.0 + jnp.exp(-gate_pre))
    activated = gate_pre * sigmoid
    hidden_rows = low(activated * up_pre)
    r.hidden[here, :] = hidden_rows
    grad_hidden = mul(scaled_rows, down)
    gate_rows = low(grad_hidden * up_pre * sigmoid * (1.0 + gate_pre * (1.0 - sigmoid)))
    up_rows = low(grad_hidden * activated)
    r.grad_gate[here, :] = gate_rows
    r.grad_up[here, :] = up_rows
    dots = jnp.sum(wide(hidden_rows) * grad_hidden, axis=1, keepdims=True)
    grad_rows = mul_nt(gate_rows, gate) + mul_nt(up_rows, up)
    high, rest = halves(dots)
    tail_out = jnp.where(lane < 64, wide(high), wide(rest))
    r.back[:, span, :] = low(lanes_joined(grad_rows, tail_out)).reshape(
        blk_count, span_rows, width + 128
    )


def middle_layer(place, r):
    head_count, blk_count = place.head_count, place.blk_count
    head, blk = place.head, place.blk
    tokens, width = r.g.shape
    columns = r.gate_all.shape[2]
    head_width = r.gate_all.shape[1]
    rows = head_width // blk_count
    half_count = head_count // 2
    greet(place.others("head") + place.others("blk"))
    r.attended_all[head] = r.attended[...]
    for part in range(head_count):
        r.output_all[blk, part] = r.output_part[part]
    own_weights = [
        keep(ref.at[:, rows_at(head, columns)], held.at[head], r.local.at[number])
        for number, (ref, held) in enumerate(((r.gate, r.gate_all), (r.up, r.up_all)))
    ]
    for step, piece in enumerate((r.down_0, r.down_1, r.down_2, r.down_3)):
        r.down_all[(head + head_count - step) % head_count] = piece[...]
    greeted(head_count + blk_count - 2)
    rows_in = LineGather(place, r.attended_all, r.sent_line, r.got_line)
    output_spread = Spread(place, r.output_all, r.sent_output, r.got_output)
    place_upstream(place, r)
    r.grads_in[blk] = r.upstream[blk]
    routed = scatter(place, "blk", r.upstream, r.grads_in, r.sent_grads, r.got_grads)
    rows_in.receive(1)
    output_spread.relay()
    rows_in.receive(2)
    output_spread.wait()
    for part in range(head_count):
        for other in range(blk_count):
            r.output_wide[pl.ds((part * blk_count + other) * rows, rows), :] = unpacked_rows(
                wide(r.output_all[other, part])
            )
    r.output[...] = low(r.output_wide[...])
    router = low(r.small[0:16])
    expert = wide(lax.broadcasted_iota(jnp.int32, (16, tokens), 0))
    lane = lax.broadcasted_iota(jnp.int32, (EXPERTS * CAP, 128), 1)
    gain = r.small[GAIN_TWO_AT : GAIN_TWO_AT + 1]
    for hop in range(3, head_count):
        rows_in.receive(hop)
    weights_in = []
    for kind, (ref, held) in enumerate(((r.gate, r.gate_all), (r.up, r.up_all))):
        copies = []
        for away in range(1, head_count):
            other = (head + away) % head_count
            copies.append(
                send(
                    ref.at[:, rows_at(other, columns)],
                    held.at[head],
                    r.sent_weights.at[kind, away - 1],
                    r.got_weights.at[kind, away - 1],
                    (other, blk),
                )
            )
        weights_in.append(copies)
    parts = []
    for number in range(head_count):
        block = far_block(number, head_count)
        found = jnp.concatenate(
            [r.attended_all[source, block] for source in range(head_count)], axis=0
        ).T
        source = wide(r.x_all[block]) + mul(found, r.output[...])
        inverse = lax.rsqrt(jnp.mean(source * source, axis=-1, keepdims=True) + EPS)
        normed = low(source * inverse * gain)
        if number == head_count - 1:
            r.middle[...] = source
            r.normed[...] = normed
            r.attended_home[...] = low(wide(found).T)
        facts = r.facts[block]
        logits = mul_nt(router, normed) + facts[8:24]
        picked = [
            jnp.sum(
                jnp.where(facts[2 + choice : 3 + choice] == expert, logits, 0.0),
                axis=0,
                keepdims=True,
            )
            for choice in range(TOP)
        ]
        highest = jnp.maximum(picked[0], picked[1])
        raised = [jnp.exp(value - highest) for value in picked]
        total = raised[0] + raised[1]
        share = [value / total for value in raised]
        r.weights[block] = jnp.concatenate(
            share + [jnp.zeros((6, tokens), jnp.float32)], axis=0
        )
        places = [r.first[block], r.second[block]]
        of_slot = jnp.sum(
            wide(places[0]) * share[0] + wide(places[1]) * share[1], axis=1, keepdims=True
        )
        high, rest = halves(of_slot)
        entry = lanes_joined(
            mul(places[0] + places[1], normed), jnp.where(lane < 64, wide(high), wide(rest))
        )
        parts.append(entry.reshape(EXPERTS, CAP, width + 128))
        if number % 2:
            span = pl.ds((number - 1) * CAP, 2 * CAP)
            r.slots[:, span, :] = low(jnp.concatenate(parts, axis=1))
            parts = []
            r.slots_in[blk, span, :] = r.slots[blk, span, :]
            routed += scatter(
                place,
                "blk",
                r.slots.at[:, span],
                r.slots_in.at[:, span],
                r.sent_slots.at[number // 2],
                r.got_slots.at[number // 2],
            )
    rows_in.wait()
    wait_all(routed)
    wait_all(own_weights, *weights_in)

    depth = head_count * head_width
    gate, up, down = [
        ref[...].reshape(depth, columns) for ref in (r.gate_all, r.up_all, r.down_all)
    ]
    span_rows = 2 * CAP
    group = blk_count * span_rows
    lane = lax.broadcasted_iota(jnp.int32, (group, 128), 1)
    routed = []
    for number in range(half_count):
        span = pl.ds(number * span_rows, span_rows)
        here = pl.ds(number * group, group)
        ffn_rows(number, span, here, r, gate, up, down, lane)
        r.back_in[blk, span, :] = r.back[blk, span, :]
        routed.append(
            scatter(
                place,
                "blk",
                r.back.at[:, span],
                r.back_in.at[:, span],
                r.sent_back.at[number],
                r.got_back.at[number],
            )
        )
    r.down_parts[...] = low(mul(r.scaled[...].T, r.hidden[...])).reshape(r.down_parts.shape)
    r.down_in[head] = r.down_parts[head]
    far_away = head_count // 2 - 1
    down_copies = scatter(
        place, "head", r.down_parts, r.down_in, r.sent_down, r.got_down, lambda number: number != far_away
    )
    for number in range(half_count):
        span = pl.ds(number * span_rows, span_rows)
        here = pl.ds(number * group, group)
        r.outs[:, span, :] = low(mul_nt(r.hidden[here, :], down)).reshape(
            blk_count, span_rows, width
        )
    r.outs_in[blk] = r.outs[blk]
    out_copies = scatter(place, "blk", r.outs, r.outs_in, r.sent_outs, r.got_outs)
    r.turned[...] = r.taken[...].T
    for step, piece in enumerate((r.early_0, r.early_1, r.early_2, r.early_3)):
        here = rows_at(block_at(step, head_count), head_width)
        for kind, right in enumerate((r.grad_gate, r.grad_up)):
            piece[kind] = low(mul(r.turned[here, :], right[...]))
    narrow = lax.broadcasted_iota(jnp.int32, (tokens, 128), 1)
    shares_in = LineSum(place, r.parts, r.parts_in, r.sent_parts, r.got_parts)
    dot_copies = []
    for number in range(head_count):
        block = far_block(number, head_count)
        if number % 2 == 0:
            for copy in routed[number // 2]:
                copy.wait_recv()
            entries = wide(r.back_in[:, pl.ds(number * CAP, span_rows), :])
        entry = entries[:, (number % 2) * CAP : (number % 2 + 1) * CAP]
        entry = low(entry.reshape(EXPERTS * CAP, width + 128))
        found = [mul_tn(placed[block], entry) for placed in (r.first, r.second)]
        dots = [
            found[choice][:, width : width + 1] + found[choice][:, width + 64 : width + 65]
            for choice in range(TOP)
        ]
        dots = jnp.where(narrow == 0, dots[0], jnp.where(narrow == 1, dots[1], 0.0))
        r.dots[block] = dots.T[0:8]
        share = found[0][:, :width] + found[1][:, :width]
        if number < head_count - 1:
            away = (block + head_count - head) % head_count
            dot_copies.append(
                send(
                    r.dots.at[block],
                    r.dots_in.at[head],
                    r.sent_dots.at[away - 1],
                    r.got_dots.at[away - 1],
                    (block, blk),
                )
            )
            shares_in.add(block, share)
    down_copies += scatter(
        place, "head", r.down_parts, r.down_in, r.sent_down, r.got_down, lambda number: number == far_away
    )
    r.dots_in[head] = r.dots[head]
    grad_slots = shares_in.total(share)
    for copy in dot_copies:
        copy.wait_recv()
    at_home(
        (head_count, blk_count),
        grad_slots,
        r.dots_in,
        r.middle,
        r.normed,
        r.g,
        r.small,
        r.weights,
        r.facts,
        r.middle_grad,
        r.middle_low,
        r.residual_grad,
        r.small_grad,
        r.mixture,
    )
    r.given_parts[...] = low(mul_nt(r.output[...], r.middle_low[...])).reshape(
        r.given_parts.shape
    )
    r.given[head] = r.given_parts[head]
    given_copies = scatter(place, "head", r.given_parts, r.given, r.sent_given, r.got_given)
    product = mul(r.attended_home[...], r.middle_low[...])
    for other in range(blk_count):
        r.output_terms[other] = low(own_pieces(product, rows, head_count, blk_count, other))
    for copy in out_copies:
        copy.wait_recv()
    for number in range(head_count):
        block = far_block(number, head_count)
        if number % 2 == 0:
            entries = wide(r.outs_in[:, pl.ds(number * CAP, span_rows), :])
        entry = entries[:, (number % 2) * CAP : (number % 2 + 1) * CAP]
        entry = low(entry.reshape(EXPERTS * CAP, width))
        shares = r.weights[block].T
        r.out_parts[block] = low(
            shares[:, 0:1] * mul_tn(r.first[block], entry)
            + shares[:, 1:2] * mul_tn(r.second[block], entry)
        )
    for copies in routed + [out_copies, dot_copies]:
        for copy in copies:
            copy.wait_send()
    shares_in.wait()
    wait_all(down_copies, given_copies)
    pl.semaphore_signal(
        r.done, inc=1, device_id=(head, place.twin), device_id_type=MESH
    )
    pl.semaphore_wait(r.done, 1)


def at_home(sizes, grad_slots, dots_in, middle, normed, g, small, weights, facts_all, middle_grad, middle_low, residual_grad, small_grad, mixture):
    head_count, blk_count = sizes
    tokens, width = middle.shape
    mine = lax.axis_index("head")
    facts = facts_all[mine]
    share_rows = weights[mine]
    dots = dots_in[0]
    for head in range(1, head_count):
        dots = dots + dots_in[head]
    columns = rows_joined(share_rows, facts[0:8], dots).T
    share = [columns[:, choice : choice + 1] for choice in range(TOP)]
    route_of = [columns[:, 10 + choice : 11 + choice] for choice in range(TOP)]
    upstream = wide(g[...])
    normed_wide = wide(normed[...])
    source = middle[...]
    small_low = low(small[...])
    seen = mul_nt(normed[...], small_low)
    met = mul_nt(g[...], small_low)

    def weight_of(expert):
        return sum(
            share[choice] * jnp.where(route_of[choice] == expert, 1.0, 0.0)
            for choice in range(TOP)
        )

    copy_share = weight_of(EXPERTS + 1)
    const_share = [weight_of(EXPERTS + 2 + const) for const in range(2)]
    mixing = []
    for const in range(2):
        at = MIX_AT + 2 * const
        pair = [seen[:, at + part : at + part + 1] for part in range(2)]
        highest = jnp.maximum(pair[0], pair[1])
        raised = [jnp.exp(value - highest) for value in pair]
        total = raised[0] + raised[1]
        mixing.append([value / total for value in raised])
    copy_dot = jnp.sum(upstream * normed_wide, axis=-1, keepdims=True)
    vector_dot = [met[:, VECTOR_AT + const : VECTOR_AT + const + 1] for const in range(2)]
    const_dot = [
        mixing[const][0] * copy_dot + mixing[const][1] * vector_dot[const] for const in range(2)
    ]
    product = []
    for choice in range(TOP):
        value = columns[:, 16 + choice : 17 + choice]
        special = jnp.where(route_of[choice] == EXPERTS + 1, copy_dot, 0.0)
        for const in range(2):
            special = special + jnp.where(
                route_of[choice] == EXPERTS + 2 + const, const_dot[const], 0.0
            )
        product.append(value + share[choice] * special)
    both = product[0] + product[1]
    lane = lax.broadcasted_iota(jnp.int32, (tokens, 128), 1)
    lane_wide = wide(lane)
    routing = jnp.zeros((tokens, 128), jnp.float32)
    for choice in range(TOP):
        routing = routing + jnp.where(
            lane_wide == route_of[choice], product[choice] - share[choice] * both, 0.0
        )
    residual_grad[...] = routing.T[:ROUTED]
    vector_share = jnp.zeros((tokens, 128), jnp.float32)
    spread_grad = routing
    for const in range(2):
        grad_mix = [const_share[const] * copy_dot, const_share[const] * vector_dot[const]]
        mean = mixing[const][0] * grad_mix[0] + mixing[const][1] * grad_mix[1]
        for part in range(2):
            spread_grad = spread_grad + jnp.where(
                lane == MIX_AT + 2 * const + part,
                mixing[const][part] * (grad_mix[part] - mean),
                0.0,
            )
        vector_share = vector_share + jnp.where(
            lane == VECTOR_AT + const, const_share[const] * mixing[const][1], 0.0
        )
    direct = (
        copy_share + const_share[0] * mixing[0][0] + const_share[1] * mixing[1][0]
    )
    table = jnp.concatenate(
        [small_low[0:16], jnp.zeros((128 - 16, width), jnp.bfloat16)], axis=0
    )
    spread_high, spread_rest = halves(spread_grad)
    grad_normed = (
        direct * upstream + grad_slots + mul(spread_high, table) + mul(spread_rest, table)
    )
    inverse = lax.rsqrt(jnp.mean(source * source, axis=-1, keepdims=True) + EPS)
    scaled = grad_normed * small[GAIN_TWO_AT : GAIN_TWO_AT + 1]
    result = (
        upstream
        + inverse * scaled
        - source * inverse**3 * jnp.mean(scaled * source, axis=-1, keepdims=True)
    )
    middle_grad[...] = result
    middle_low[...] = low(result)
    gain_row = jnp.sum(grad_normed * source * inverse, axis=0, keepdims=True)
    vector_high, vector_rest = halves(vector_share)
    by_normed = mul_tn(spread_high, normed[...]) + mul_tn(spread_rest, normed[...])
    by_upstream = mul_tn(vector_high, g[...]) + mul_tn(vector_rest, g[...])
    row = lax.broadcasted_iota(jnp.int32, (SMALL, width), 0)
    small_grad[...] = jnp.where(
        row == GAIN_TWO_AT, gain_row, by_normed[:SMALL] + by_upstream[:SMALL]
    )
    vectors = [small[VECTOR_AT + const : VECTOR_AT + const + 1] for const in range(2)]
    mixed = copy_share * normed_wide
    for const in range(2):
        mixed = mixed + const_share[const] * (
            mixing[const][0] * normed_wide + mixing[const][1] * vectors[const]
        )
    mixture[...] = source + mixed


def close_layer(place, r):
    head_count, blk_count = place.head_count, place.blk_count
    head, blk = place.head, place.blk
    tokens, width = r.input_grad.shape
    rows = width // (head_count * blk_count)
    cut = r.query_grad.shape[1]
    joint_width = r.joint.shape[1]
    greet(place.others("head") + place.near())
    flat = jnp.concatenate(
        [r.small_grad[...], jnp.zeros((128 - SMALL, width), jnp.float32)], axis=0
    ).T
    for part in range(head_count):
        for other in range(blk_count):
            at = (part * blk_count + other) * rows
            r.small_terms[other, part * rows : (part + 1) * rows, :] = flat[at : at + rows]
    greeted(place.head_count - 1 + place.half)
    outs_in = LineSum(place, r.out_sums, r.out_in, r.sent_out, r.got_out)
    at_end = (head == 0) | (head == head_count - 1)

    @pl.when(at_end)
    def _():
        for number in range(head_count - 1):
            block = far_block(number, head_count)
            outs_in.add(block, wide(r.out_parts[block]))


    def fold(number, terms, theirs, arrived):
        return Fold(
            place,
            terms,
            theirs,
            arrived,
            r.sent_twin.at[number],
            r.got_twin.at[number],
            r.sent_blk.at[number],
            r.got_blk.at[number],
        )

    pair_folds = []
    for number in range(head_count):
        block = far_block(number, head_count)
        pair_folds.append(
            fold(
                number,
                r.pair_terms.at[:, block],
                r.theirs_pairs.at[number],
                r.arrived_pairs.at[number],
            )
        )
    output_fold = fold(head_count, r.output_terms, r.theirs_output, r.arrived_output)
    small_fold = fold(head_count + 1, r.small_terms, r.theirs_small, r.arrived_small)
    for one in pair_folds:
        one.add()
    output_fold.add()
    small_fold.add()
    r.turned[...] = r.normed[...].T
    r.early_rows[...] = mul_nt(r.query_grad[...], r.joint[:, :cut])
    early = mul(r.turned[...], r.query_grad[...])
    row_copies = []
    gain_row = jnp.zeros((1, width), jnp.float32)
    for number in range(head_count):
        block = far_block(number, head_count)
        here = rows_at(block, tokens)
        part = low(pair_folds[number].total())
        r.grads[here, :] = part
        grad_normed = r.early_rows[here, :] + mul_nt(part, r.joint[:, cut:])
        result = low(grad_normed)
        if number < head_count - 1:
            r.row_parts[number] = result
            away = (block + head_count - head) % head_count
            row_copies.append(
                send(
                    r.row_parts.at[number],
                    r.rows_in.at[head],
                    r.sent_rows.at[away - 1],
                    r.got_rows.at[away - 1],
                    (block, blk),
                )
            )

            @pl.when(jnp.logical_not(at_end))
            def _():
                outs_in.add(block, wide(r.out_parts[block]))

        else:
            r.rows_in[head] = result
        source = wide(r.x_all[block])
        inverse = lax.rsqrt(jnp.mean(source * source, axis=-1, keepdims=True) + EPS)
        gain_row = gain_row + jnp.sum(grad_normed * source * inverse, axis=0, keepdims=True)
    product = jnp.concatenate([early, mul(r.turned[...], r.grads[...])], axis=1)
    for other in range(blk_count):
        r.joint_terms[other] = low(own_pieces(product, rows, head_count, blk_count, other))
    joint_fold = fold(head_count + 2, r.joint_terms, r.theirs_joint, r.arrived_joint)
    owners = head_count * blk_count
    owner = lax.broadcasted_iota(jnp.int32, (owners, width), 0)
    column = lax.broadcasted_iota(jnp.int32, (owners, width), 1)
    owned = jnp.where(column // rows == owner, gain_row, 0.0)
    feature = lax.broadcasted_iota(jnp.int32, (width, 128), 0)
    target = lax.broadcasted_iota(jnp.int32, (width, 128), 1)
    moved = low(jnp.where(feature % rows == target, 1.0, 0.0))
    high, rest = halves(owned)
    by_owner = mul(high, moved) + mul(rest, moved)
    for other in range(blk_count):
        r.gain_terms[other] = jnp.concatenate(
            [
                by_owner[part * blk_count + other : part * blk_count + other + 1]
                for part in range(head_count)
            ]
            + [jnp.zeros((8 - head_count, 128), jnp.float32)],
            axis=0,
        )
    gain_fold = fold(head_count + 3, r.gain_terms, r.theirs_gain, r.arrived_gain)
    r.small_sums[...] = small_fold.total().reshape(head_count, rows, 128)
    r.small_in[head] = r.small_sums[head]
    last = scatter(place, "head", r.small_sums, r.small_in, r.sent_last.at[0], r.got_last.at[0])
    output_sum = output_fold.total()
    for part in range(head_count):
        r.output_sums[part] = low(packed_rows(output_sum[part * rows : (part + 1) * rows]))
    r.output_in[head] = r.output_sums[head]
    last += scatter(place, "head", r.output_sums, r.output_in, r.sent_last.at[3], r.got_last.at[3])
    joint_fold.add()
    gain_fold.add()
    joint_sum = joint_fold.total()
    filler = jnp.zeros((PAD - rows, joint_width), jnp.float32)
    for part in range(head_count):
        r.joint_sums[part] = low(rows_joined(joint_sum[part * rows : (part + 1) * rows], filler))
    r.joint_out[head] = r.joint_sums[head]
    last += scatter(place, "head", r.joint_sums, r.joint_out, r.sent_last.at[1], r.got_last.at[1])
    gain_now = gain_fold.total()
    for part in range(head_count):
        r.gain_sums[part] = jnp.broadcast_to(gain_now[part : part + 1], (8, 128))
    r.gain_in[head] = r.gain_sums[head]
    last += scatter(place, "head", r.gain_sums, r.gain_in, r.sent_last.at[2], r.got_last.at[2])
    total = r.mixture[...] + outs_in.total(wide(r.out_parts[head]))
    r.layer_out[...] = low(total)
    for copy in row_copies:
        copy.wait_recv()
    grad_normed = wide(r.rows_in[0])
    for part in range(1, head_count):
        grad_normed = grad_normed + wide(r.rows_in[part])
    source = wide(r.x_all[head])
    inverse = lax.rsqrt(jnp.mean(source * source, axis=-1, keepdims=True) + EPS)
    scaled = grad_normed * r.small[GAIN_ONE_AT : GAIN_ONE_AT + 1]
    r.input_grad[...] = (
        r.middle_grad[...]
        + inverse * scaled
        - source * inverse**3 * jnp.mean(scaled * source, axis=-1, keepdims=True)
    )
    for copy in last:
        copy.wait_recv()
    output_sum = wide(r.output_in[0])
    for part in range(1, head_count):
        output_sum = output_sum + wide(r.output_in[part])
    r.output_grad[...] = unpacked_rows(output_sum)
    r.small_total[...] = sum(r.small_in[part] for part in range(head_count))
    r.gain_total[...] = sum(r.gain_in[part] for part in range(head_count))
    for one in pair_folds + [output_fold, small_fold, joint_fold, gain_fold]:
        one.wait()
    outs_in.wait()
    for copy in row_copies + last:
        copy.wait_send()


def finish(
    sizes,
    piece_0,
    piece_1,
    piece_2,
    piece_3,
    down_in,
    joint_in,
    small_in,
    gain_in,
    sums_in,
    rows_in,
    layer_in,
    residual_in,
    gate,
    up,
    down,
    joint,
    value,
    gain_one,
    gain_two,
    router,
    mix,
    vectors,
    output,
    rows,
    layer,
    residual,
):
    head_count, blk_count = sizes
    mine = lax.axis_index("head")
    columns = piece_0.shape[2]
    for step, piece in enumerate((piece_0, piece_1, piece_2, piece_3)):
        source = (mine + head_count - step) % head_count
        at = rows_at(source, columns)
        gate[:, at] = wide(piece[0])
        up[:, at] = wide(piece[1])
    for source in range(head_count):
        down[:, source * columns : (source + 1) * columns] = wide(down_in[source])
    own_rows = joint.shape[0]
    parts = [wide(joint_in[source])[:own_rows] for source in range(head_count)]
    joint[...] = lanes_joined(
        *[part[:, 0:192] for part in parts], *[part[:, 256:448] for part in parts]
    )
    value[...] = lanes_joined(
        *[lanes_joined(part[:, 512:640], part[:, 448:512]) for part in parts]
    )
    flat = small_in[...]
    flat = jnp.concatenate(
        [flat, jnp.zeros((128 - own_rows, 128), jnp.float32)], axis=0
    ).T[:SMALL, :own_rows]
    gain_one[...] = gain_in[0:1, :own_rows]
    gain_two[...] = flat[GAIN_TWO_AT : GAIN_TWO_AT + 1]
    router[...] = flat[ROUTER_AT : ROUTER_AT + ROUTED]
    mix[...] = flat[MIX_AT : MIX_AT + 4]
    vectors[...] = flat[VECTOR_AT : VECTOR_AT + 2]
    output[...] = sums_in[...]
    rows[...] = rows_in[...]
    layer[...] = layer_in[...]
    residual[...] = residual_in[...]


def after(values, *signals):
    return lax.optimization_barrier((values, signals))[0]


def around_heads(pieces):
    count = len(pieces)
    return [pieces[0]] + [
        lax.ppermute(pieces[step], "head", [(i, (i + step) % count) for i in range(count)])
        for step in range(1, count)
    ]


def fast_shards(
    inputs,
    cotangent,
    segment,
    position,
    routes,
    gate_residual,
    first_gain,
    second_gain,
    query_key_weight,
    value_weight,
    output_weight,
    router_weight,
    const_gate,
    const_vectors,
    gate_weight,
    up_weight,
    down_weight,
):
    tokens, width = inputs.shape
    head_count = lax.axis_size("head")
    blk_count = lax.axis_size("blk")
    sizes = (head_count, blk_count)
    part = functools.partial
    half = blk_count // 2
    period = tokens * blk_count // CONT_LEN + 1
    head_width = width // head_count
    column_rows = head_count * tokens
    weight_rows = query_key_weight.shape[0]
    columns = gate_weight.shape[1] // head_count
    slot_rows = head_count * CAP
    slot_total = blk_count * slot_rows
    joint_width = 10 * HEAD_DIM
    pair_width = 6 * HEAD_DIM
    others, near = head_count - 1, blk_count - 1
    packed = width * 3 // 2
    joint_packed = (joint_width + 128) * 3 // 2

    opened_from = dict(
            x=inputs,
            joint_rows=query_key_weight,
            value_rows=value_weight,
            output_rows=output_weight,
            router=router_weight.T,
            mix=const_gate.T,
            vectors=const_vectors.T,
            gain_one=first_gain[None],
            gain_two=second_gain[None],
            segment=segment[None],
            position=position[None],
            routes=routes.T,
            residual=gate_residual.T,
            g=cotangent,
            down=down_weight.T,
    )
    opened = exchange(
        open_layer,
        sizes,
        opened_from,
        dict(
            x_all=shape((head_count, tokens, width)),
            facts=shape((head_count, 24, tokens), jnp.float32),
            places=shape((8, 128), jnp.int32),
            g_all=shape((head_count, tokens, width)),
            normed=shape((column_rows, width)),
            queries=shape((column_rows, 4 * HEAD_DIM)),
            pairs_all=shape((blk_count, head_count, tokens, pair_width)),
            joint=shape((width, joint_width)),
            output_part=shape((head_count, 16, packed)),
            small=shape((SMALL, width), jnp.float32),
            down_0=shape((head_width, columns)),
            down_1=shape((head_width, columns)),
            down_2=shape((head_width, columns)),
            down_3=shape((head_width, columns)),
        ),
        dict(
            my_router=vmem(ROUTED, weight_rows),
            my_mix=vmem(4, weight_rows),
            my_vectors=vmem(2, weight_rows),
            my_gain_one=vmem(1, weight_rows),
            my_gain_two=vmem(1, weight_rows),
            my_joint_rows=vmem(*query_key_weight.shape),
            my_value_rows=vmem(*value_weight.shape),
            my_segment=vmem(1, tokens, dtype=jnp.int32),
            my_position=vmem(1, tokens, dtype=jnp.int32),
            my_routes=vmem(TOP, tokens, dtype=jnp.int32),
            my_residual=vmem_wide(ROUTED, tokens),
            my_output_rows=vmem(*output_weight.shape),
            my_x=vmem(tokens, width),
            marks_all=vmem_wide(blk_count, head_count, 8, tokens),
            joint_own=vmem(head_count, 16, joint_packed),
            output_own=vmem(16, packed),
            facts_own=vmem_wide(24, tokens),
            joint_all=vmem(blk_count, head_count, 16, joint_packed),
            joint_wide=vmem_wide(width, joint_width + 128),
            local=dma(18),
            sent=dma(2, others),
            got=dma(2, others),
            sent_line=dma(3, 2, others),
            got_line=dma(3, 2, others),
            sent_joint=dma(near),
            got_joint=dma(near),
            sent_marks=dma(near),
            got_marks=dma(near),
            sent_pairs=dma(head_count, near),
            got_pairs=dma(head_count, near),
        ),
        0,
        far=tuple(opened_from) + ("g_all", "down_0", "down_1", "down_2", "down_3"),
        room=63,
    )
    down_pieces = around_heads([opened.down_0, opened.down_1, opened.down_2, opened.down_3])
    pairs_all = opened.pairs_all.reshape(blk_count * head_count, tokens, pair_width)
    lists = [
        pltpu.SMEM((blk_count * head_count + CHUNK,), jnp.int32),
        pltpu.SMEM((blk_count * head_count + CHUNK,), jnp.int32),
    ]
    attended, totals = compute(
        part(attend, sizes, period),
        [
            shape((head_count, head_width, tokens)),
            shape((head_count, 8, 3 * tokens), jnp.float32),
        ],
        [opened.places, opened.queries, pairs_all],
        lists,
        1,
    )
    halved = head_count // 2
    went = exchange(
        middle_layer,
        sizes,
        dict(
            attended=attended,
            g_all=opened.g_all,
            x_all=opened.x_all,
            output_part=opened.output_part,
            small=opened.small,
            facts=opened.facts,
            g=cotangent,
            gate=gate_weight,
            up=up_weight,
            down_0=down_pieces[0],
            down_1=down_pieces[1],
            down_2=down_pieces[2],
            down_3=down_pieces[3],
        ),
        dict(
            output_terms=shape((blk_count, head_count * weight_rows, width)),
            early_0=shape((2, head_width, columns)),
            early_1=shape((2, head_width, columns)),
            early_2=shape((2, head_width, columns)),
            early_3=shape((2, head_width, columns)),
            down_in=shape((head_count, head_width, columns)),
            out_parts=shape((head_count, tokens, width)),
            middle_grad=shape((tokens, width), jnp.float32),
            given=shape((head_count, head_width, tokens)),
            residual_grad=shape((ROUTED, tokens), jnp.float32),
            small_grad=shape((SMALL, width), jnp.float32),
            mixture=shape((tokens, width), jnp.float32),
        ),
        dict(
            attended_all=vmem(head_count, head_count, head_width, tokens),
            attended_home=vmem(width, tokens),
            first=vmem(head_count, EXPERTS * CAP, tokens),
            second=vmem(head_count, EXPERTS * CAP, tokens),
            upstream=vmem(EXPERTS, slot_rows, width),
            output=vmem(width, width),
            output_all=vmem(blk_count, head_count, 16, packed),
            output_wide=vmem_wide(width, width),
            slots=vmem(EXPERTS, slot_rows, width + 128),
            slots_in=vmem(blk_count, slot_rows, width + 128),
            grads_in=vmem(blk_count, slot_rows, width),
            middle=vmem_wide(tokens, width),
            normed=vmem(tokens, width),
            weights=vmem_wide(head_count, 8, tokens),
            gate_all=vmem(head_count, head_width, columns),
            up_all=vmem(head_count, head_width, columns),
            down_all=vmem(head_count, head_width, columns),
            taken=vmem(slot_total, width),
            turned=vmem(width, slot_total),
            hidden=vmem(slot_total, columns),
            grad_gate=vmem(slot_total, columns),
            grad_up=vmem(slot_total, columns),
            scaled=vmem(slot_total, width),
            back=vmem(blk_count, slot_rows, width + 128),
            outs=vmem(blk_count, slot_rows, width),
            back_in=vmem(blk_count, slot_rows, width + 128),
            outs_in=vmem(blk_count, slot_rows, width),
            parts=vmem(head_count, tokens, width),
            parts_in=vmem(2, head_count, tokens, width),
            dots=vmem_wide(head_count, 8, tokens),
            dots_in=vmem_wide(head_count, 8, tokens),
            down_parts=vmem(head_count, head_width, columns),
            middle_low=vmem(tokens, width),
            given_parts=vmem(head_count, head_width, tokens),
            local=dma(2),
            sent_line=dma(2, others),
            got_line=dma(2, others),
            sent_dots=dma(others),
            got_dots=dma(others),
            sent_output=dma(near),
            got_output=dma(near),
            sent_grads=dma(near),
            got_grads=dma(near),
            sent_weights=dma(2, others),
            got_weights=dma(2, others),
            sent_slots=dma(halved, near),
            got_slots=dma(halved, near),
            sent_back=dma(halved, near),
            got_back=dma(halved, near),
            sent_outs=dma(near),
            got_outs=dma(near),
            sent_down=dma(others),
            got_down=dma(others),
            sent_parts=dma(head_count),
            got_parts=dma(2, head_count),
            sent_given=dma(others),
            got_given=dma(others),
            done=pltpu.SemaphoreType.REGULAR,
        ),
        1,
        far=("gate", "up"),
    )
    grad_pieces = around_heads([went.early_0, went.early_1, went.early_2, went.early_3])
    query_grad, pair_grad = compute(
        part(attend_back, sizes, period),
        [shape(opened.queries.shape), shape(pairs_all.shape)],
        [
            opened.places,
            opened.queries,
            pairs_all,
            attended,
            totals,
            went.given,
        ],
        lists + [pltpu.VMEM(pairs_all.shape, jnp.float32)],
        1,
    )
    folds = head_count + 4
    closed = exchange(
        close_layer,
        sizes,
        dict(
            pair_terms=pair_grad.reshape(blk_count, head_count, tokens, pair_width),
            query_grad=query_grad,
            joint=opened.joint,
            normed=opened.normed,
            x_all=opened.x_all,
            small_grad=went.small_grad,
            out_parts=went.out_parts,
            output_terms=went.output_terms,
            small=opened.small,
            middle_grad=went.middle_grad,
            mixture=went.mixture,
        ),
        dict(
            input_grad=shape((tokens, width), jnp.float32),
            layer_out=shape((tokens, width)),
            joint_out=shape((head_count, PAD, joint_width)),
            output_grad=shape((weight_rows, width), jnp.float32),
            small_total=shape((weight_rows, 128), jnp.float32),
            gain_total=shape((8, 128), jnp.float32),
        ),
        dict(
            theirs_pairs=vmem(head_count, half, tokens, pair_width),
            arrived_pairs=vmem(head_count, half - 1, tokens, pair_width),
            theirs_output=vmem(half, head_count * weight_rows, width),
            arrived_output=vmem(half - 1, head_count * weight_rows, width),
            output_sums=vmem(head_count, 16, packed),
            output_in=vmem(head_count, 16, packed),
            small_terms=vmem_wide(blk_count, head_count * weight_rows, 128),
            theirs_small=vmem_wide(half, head_count * weight_rows, 128),
            arrived_small=vmem_wide(half - 1, head_count * weight_rows, 128),
            joint_terms=vmem(blk_count, head_count * weight_rows, joint_width),
            theirs_joint=vmem(half, head_count * weight_rows, joint_width),
            arrived_joint=vmem(half - 1, head_count * weight_rows, joint_width),
            gain_terms=vmem_wide(blk_count, 8, 128),
            theirs_gain=vmem_wide(half, 8, 128),
            arrived_gain=vmem_wide(half - 1, 8, 128),
            row_parts=vmem(others, tokens, width),
            rows_in=vmem(head_count, tokens, width),
            out_sums=vmem(head_count, tokens, width),
            out_in=vmem(2, head_count, tokens, width),
            joint_sums=vmem(head_count, PAD, joint_width),
            small_sums=vmem_wide(head_count, weight_rows, 128),
            small_in=vmem_wide(head_count, weight_rows, 128),
            gain_sums=vmem_wide(head_count, 8, 128),
            gain_in=vmem_wide(head_count, 8, 128),
            turned=vmem(width, column_rows),
            grads=vmem(column_rows, pair_width),
            early_rows=vmem_wide(column_rows, width),
            sent_out=dma(head_count),
            got_out=dma(2, head_count),
            sent_twin=dma(folds, half),
            got_twin=dma(folds, half),
            sent_blk=dma(folds, half - 1),
            got_blk=dma(folds, half - 1),
            sent_rows=dma(others),
            got_rows=dma(others),
            sent_last=dma(4, others),
            got_last=dma(4, others),
        ),
        2,
    )
    wide_shape = part(shape, dtype=jnp.float32)
    (
        gate_grad,
        up_grad,
        down_grad,
        joint_grad,
        value_grad,
        gain_one_grad,
        gain_two_grad,
        router_grad,
        mix_grad,
        vector_grad,
        output_grad,
        input_grad,
        layer_out,
        residual_grad,
    ) = compute(
        part(finish, sizes),
        [
            wide_shape(gate_weight.shape),
            wide_shape(up_weight.shape),
            wide_shape(gate_weight.shape),
            wide_shape(query_key_weight.shape),
            wide_shape(value_weight.shape),
            wide_shape((1, weight_rows)),
            wide_shape((1, weight_rows)),
            wide_shape((ROUTED, weight_rows)),
            wide_shape((4, weight_rows)),
            wide_shape((2, weight_rows)),
            wide_shape(output_weight.shape),
            wide_shape((tokens, width)),
            shape((tokens, width)),
            wide_shape((ROUTED, tokens)),
        ],
        grad_pieces
        + [
            went.down_in,
            closed.joint_out,
            closed.small_total,
            closed.gain_total,
            closed.output_grad,
            closed.input_grad,
            closed.layer_out,
            went.residual_grad,
        ],
    )
    return (
        layer_out,
        input_grad,
        residual_grad.T,
        gain_one_grad[0],
        gain_two_grad[0],
        joint_grad,
        value_grad,
        output_grad,
        router_grad.T,
        mix_grad.T,
        vector_grad.T,
        gate_grad,
        up_grad,
        down_grad.T,
    )


def solution(mesh):
    body = fast_shards if mesh.shape["blk"] == EXPERTS else shards
    in_specs = (
        P(("head", "blk"), None),
        P(("head", "blk"), None),
        P(("head", "blk")),
        P(("head", "blk")),
        P(("head", "blk"), None),
        P(("head", "blk"), None),
        P(("head", "blk")),
        P(("head", "blk")),
        P(("head", "blk"), None),
        P(("head", "blk"), None),
        P(("head", "blk"), None),
        P(("head", "blk"), None),
        P(("head", "blk"), None),
        P(("head", "blk"), None),
        P("head", "blk"),
        P("head", "blk"),
        P("blk", "head"),
    )
    out_specs = (
        P(("head", "blk"), None),
        P(("head", "blk"), None),
        P(("head", "blk"), None),
        P(("head", "blk")),
        P(("head", "blk")),
        P(("head", "blk"), None),
        P(("head", "blk"), None),
        P(("head", "blk"), None),
        P(("head", "blk"), None),
        P(("head", "blk"), None),
        P(("head", "blk"), None),
        P("head", "blk"),
        P("head", "blk"),
        P("blk", "head"),
    )
    return jax.shard_map(body, mesh=mesh, in_specs=in_specs, out_specs=out_specs, check_vma=False)
```

```python
import functools
import types

import jax
import jax.numpy as jnp
from jax import lax
from jax.experimental import pallas as pl
from jax.experimental.pallas import tpu as pltpu
from jax.sharding import PartitionSpec as P

HEADS = 12
HEAD_DIM = 64
EXPERTS = 8
ROUTED = 12
TOP = 2
CONT_LEN = 1024
CAP = 24


EPS = 1e-06
HIGH = lax.Precision.HIGHEST


def silu_slope(pre):
    sigmoid_value = jax.nn.sigmoid(pre)
    return sigmoid_value * (1.0 + pre * (1.0 - sigmoid_value))


def visible_pairs(query_segment, query_position, key_segment, key_position, period):
    same_sequence = (query_segment[:, None] == key_segment[None, :]) & (
        key_position[None, :] <= query_position[:, None]
    )
    same_group = query_segment[:, None] // period == key_segment[None, :] // period
    shared = (
        (key_segment[None, :] % period == 0) & (query_segment[:, None] % period != 0) & same_group
    )
    return same_sequence | shared


def norm_back(grad_normed, source, inverse, gain):
    scaled = grad_normed * gain
    grad_source = inverse * scaled - source * inverse**3 * jnp.mean(
        scaled * source, axis=-1, keepdims=True
    )
    grad_gain = jnp.sum(grad_normed * source * inverse, axis=0)
    return (grad_source, grad_gain)


def around_blocks(pieces, combine, initial):
    return combine(
        initial,
        (
            lax.all_gather(pieces[0], "blk", axis=0, tiled=True),
            lax.all_gather(pieces[1], "blk", axis=0, tiled=True),
        ),
        jnp.int32(0),
    )


def softmax_last(logits):
    highest = jnp.max(logits, axis=-1, keepdims=True)
    raised = jnp.exp(logits - highest)
    return raised / jnp.sum(raised, axis=-1, keepdims=True)


def shards(
    inputs,
    cotangent,
    segment,
    position,
    routes,
    gate_residual,
    first_gain,
    second_gain,
    query_key_weight,
    value_weight,
    output_weight,
    router_weight,
    const_gate,
    const_vectors,
    gate_weight,
    up_weight,
    down_weight,
):
    tok_rows, width = inputs.shape
    head_count = lax.axis_size("head")
    blk_count = lax.axis_size("blk")
    local_heads = HEADS // head_count
    query_rows = head_count * tok_rows
    head_width = width // head_count
    width_split = blk_count // EXPERTS
    score_scale = HEAD_DIM ** (-0.5)
    period = tok_rows * blk_count // CONT_LEN + 1
    gathered = (
        lax.all_gather(first_gain, ("head", "blk"), axis=0, tiled=True),
        lax.all_gather(second_gain, ("head", "blk"), axis=0, tiled=True),
        lax.all_gather(query_key_weight, ("head", "blk"), axis=0, tiled=True),
        lax.all_gather(value_weight, ("head", "blk"), axis=0, tiled=True),
        lax.all_gather(output_weight, ("head", "blk"), axis=0, tiled=True),
        lax.all_gather(router_weight, ("head", "blk"), axis=0, tiled=True),
        lax.all_gather(const_gate, ("head", "blk"), axis=0, tiled=True),
        lax.all_gather(const_vectors, ("head", "blk"), axis=0, tiled=True),
        lax.all_gather(segment, ("head", "blk"), axis=0, tiled=True),
        lax.all_gather(position, ("head", "blk"), axis=0, tiled=True),
    )
    (
        gain_one,
        gain_two,
        full_joint,
        full_value,
        full_output,
        full_router,
        full_const,
        full_vectors,
        segment_all,
        position_all,
    ) = gathered
    gate_columns, up_columns, down_rows = (
        lax.all_gather(gate_weight, "head", axis=0, tiled=True),
        lax.all_gather(up_weight, "head", axis=0, tiled=True),
        lax.all_gather(down_weight, "head", axis=1, tiled=True),
    )
    gain_one = gain_one.astype(jnp.float32)
    gain_two = gain_two.astype(jnp.float32)
    source = inputs.astype(jnp.float32)
    inverse_one = lax.rsqrt(jnp.mean(source * source, axis=-1, keepdims=True) + EPS)
    normed_one = (source * inverse_one * gain_one).astype(jnp.bfloat16)
    joined = jnp.dot(normed_one, full_joint, preferred_element_type=jnp.float32)
    value_proj = jnp.dot(normed_one, full_value, preferred_element_type=jnp.float32)

    def head_layout(array):
        return array.astype(jnp.bfloat16).reshape(tok_rows, head_count, head_width)

    query_heads, key_heads, value_heads = (
        lax.all_to_all(
            head_layout(joined[:, :width]), "head", split_axis=1, concat_axis=0, tiled=True
        ),
        lax.all_to_all(
            head_layout(joined[:, width:]), "head", split_axis=1, concat_axis=0, tiled=True
        ),
        lax.all_to_all(head_layout(value_proj), "head", split_axis=1, concat_axis=0, tiled=True),
    )
    query_heads = query_heads.reshape(query_rows, local_heads, HEAD_DIM)
    key_heads = key_heads.reshape(query_rows, head_width)
    value_heads = value_heads.reshape(query_rows, head_width)
    blk_index = lax.axis_index("blk")
    segment_grid = segment_all.reshape(head_count, blk_count, tok_rows)
    position_grid = position_all.reshape(head_count, blk_count, tok_rows)
    query_segment = lax.dynamic_index_in_dim(segment_grid, blk_index, 1, keepdims=False).reshape(
        query_rows
    )
    query_position = lax.dynamic_index_in_dim(position_grid, blk_index, 1, keepdims=False).reshape(
        query_rows
    )
    key_segment = segment_grid.transpose(1, 0, 2).reshape(blk_count * query_rows)
    key_position = position_grid.transpose(1, 0, 2).reshape(blk_count * query_rows)

    def key_slices(pieces):
        piece_rows = pieces[0].shape[0]
        step_count = piece_rows // tok_rows
        return (
            pieces[0].reshape(step_count, tok_rows, local_heads, HEAD_DIM),
            pieces[1].reshape(step_count, tok_rows, local_heads, HEAD_DIM),
            key_segment.reshape(step_count, tok_rows),
            key_position.reshape(step_count, tok_rows),
        )

    def masked_scores(queries, block_keys, visible):
        scores = (
            jnp.einsum("qhd,khd->hqk", queries, block_keys, preferred_element_type=jnp.float32)
            * score_scale
        )
        return jnp.where(visible[None], scores, -jnp.inf)

    def attend_block(carried, block):
        block_keys, block_values, block_segment, block_position = block
        visible = visible_pairs(
            query_segment, query_position, block_segment, block_position, period
        )

        def attend_compute(state):
            top_score, running_total, weighted = state
            scores = masked_scores(query_heads, block_keys, visible)
            new_top = jnp.maximum(top_score, jnp.max(scores, axis=-1))
            anchor = jnp.where(new_top == -jnp.inf, 0.0, new_top)
            raised = jnp.exp(scores - anchor[..., None])
            factor = jnp.exp(top_score - anchor)
            running_total = running_total * factor + jnp.sum(raised, axis=-1)
            weighted = weighted * factor[..., None] + jnp.einsum(
                "hqk,khd->hqd",
                raised.astype(jnp.bfloat16),
                block_values,
                preferred_element_type=jnp.float32,
            )
            return (new_top, running_total, weighted)

        def unchanged(state):
            return state

        return (lax.cond(jnp.any(visible), attend_compute, unchanged, carried), None)

    def attend_piece(carried, pieces, first_row):
        result, unused = lax.scan(attend_block, carried, key_slices(pieces))
        return result

    start_state = (
        jnp.full((local_heads, query_rows), -jnp.inf, jnp.float32),
        jnp.zeros((local_heads, query_rows), jnp.float32),
        jnp.zeros((local_heads, query_rows, HEAD_DIM), jnp.float32),
    )
    top_score, running_total, weighted = around_blocks(
        (key_heads, value_heads), attend_piece, start_state
    )
    log_total = top_score + jnp.log(running_total)
    attended_local = (weighted / running_total[..., None]).transpose(1, 0, 2).astype(jnp.bfloat16)
    attended = lax.all_to_all(
        attended_local.reshape(query_rows, 1, head_width),
        "head",
        split_axis=0,
        concat_axis=1,
        tiled=True,
    ).reshape(tok_rows, width)
    middle = source + jnp.dot(attended, full_output, preferred_element_type=jnp.float32)
    inverse_two = lax.rsqrt(jnp.mean(middle * middle, axis=-1, keepdims=True) + EPS)
    normed_two = (middle * inverse_two * gain_two).astype(jnp.bfloat16)
    normed_float = normed_two.astype(jnp.float32)
    logits = jnp.dot(normed_two, full_router, preferred_element_type=jnp.float32) + gate_residual
    choose = (routes[:, :, None] == jnp.arange(ROUTED, dtype=jnp.int32)[None, None, :]).astype(
        jnp.float32
    )
    picked = jnp.sum(choose * logits[:, None, :], axis=-1)
    weighting = softmax_last(picked)
    pair_expert = routes.reshape(tok_rows * TOP)
    ffn_onehot = (pair_expert[:, None] == jnp.arange(EXPERTS, dtype=jnp.int32)[None, :]).astype(
        jnp.int32
    )
    pair_rank = jnp.sum((jnp.cumsum(ffn_onehot, axis=0) - ffn_onehot) * ffn_onehot, axis=-1)
    slot_match = (
        pair_rank[None, None, :] == jnp.arange(CAP, dtype=jnp.int32)[None, :, None]
    ).astype(jnp.int32)
    placement = (
        (ffn_onehot.T[:, None, :] * slot_match)
        .reshape(EXPERTS, CAP, tok_rows, TOP)
        .astype(jnp.float32)
    )
    select = jnp.sum(placement, axis=-1)
    gate_slot = jnp.einsum("ectj,tj->ect", placement, weighting, precision=HIGH)
    send_rows = jnp.einsum(
        "ect,td->ecd", select.astype(jnp.bfloat16), normed_two, preferred_element_type=jnp.float32
    ).astype(jnp.bfloat16)
    upstream = cotangent.astype(jnp.float32)
    slot_grad = jnp.einsum("ect,td->ecd", gate_slot, upstream, precision=HIGH).astype(jnp.bfloat16)
    rows_in = lax.all_to_all(
        jnp.repeat(send_rows, width_split, axis=0), "blk", split_axis=0, concat_axis=0, tiled=True
    )
    grads_in = lax.all_to_all(
        jnp.repeat(slot_grad, width_split, axis=0), "blk", split_axis=0, concat_axis=0, tiled=True
    )
    gate_pre = jnp.einsum("scd,df->scf", rows_in, gate_columns, preferred_element_type=jnp.float32)
    up_pre = jnp.einsum("scd,df->scf", rows_in, up_columns, preferred_element_type=jnp.float32)
    activated = jax.nn.silu(gate_pre)
    hidden = (activated * up_pre).astype(jnp.bfloat16)
    partial_out = jnp.einsum("scf,fd->scd", hidden, down_rows, preferred_element_type=jnp.float32)
    grad_hidden = jnp.einsum("scd,fd->scf", grads_in, down_rows, preferred_element_type=jnp.float32)
    grad_gate_pre = (grad_hidden * up_pre * silu_slope(gate_pre)).astype(jnp.bfloat16)
    grad_up_pre = (grad_hidden * activated).astype(jnp.bfloat16)
    grad_part = jnp.einsum(
        "scf,df->scd", grad_gate_pre, gate_columns, preferred_element_type=jnp.float32
    ) + jnp.einsum("scf,df->scd", grad_up_pre, up_columns, preferred_element_type=jnp.float32)
    back_out = lax.all_to_all(
        partial_out.astype(jnp.bfloat16), "blk", split_axis=0, concat_axis=0, tiled=True
    ).astype(partial_out.dtype)
    back_grad = lax.all_to_all(
        grad_part.astype(jnp.bfloat16), "blk", split_axis=0, concat_axis=0, tiled=True
    ).astype(grad_part.dtype)
    returned, grad_back, kept_rows, kept_grads, hidden, grad_gate_pre, grad_up_pre = (
        back_out,
        back_grad,
        rows_in,
        grads_in,
        hidden,
        grad_gate_pre,
        grad_up_pre,
    )
    expert_out = returned.reshape(EXPERTS, width_split, CAP, width).sum(axis=1)
    ffn_sum = jnp.einsum("ect,ecd->td", gate_slot, expert_out, precision=HIGH)
    mixing = softmax_last(
        jnp.dot(normed_two, full_const, preferred_element_type=jnp.float32).reshape(tok_rows, 2, 2)
    )
    vectors = full_vectors.astype(jnp.float32)
    copy_share = jnp.sum(weighting * (routes == EXPERTS + 1).astype(jnp.float32), axis=-1)
    const_share = jnp.stack(
        [
            jnp.sum(weighting * (routes == EXPERTS + 2 + const_index).astype(jnp.float32), axis=-1)
            for const_index in range(2)
        ],
        axis=1,
    )
    const_outs = [
        mixing[:, const_index, 0:1] * normed_float
        + mixing[:, const_index, 1:2] * vectors[:, const_index][None, :]
        for const_index in range(2)
    ]
    mixture = ffn_sum + copy_share[:, None] * normed_float
    for const_index in range(2):
        mixture = mixture + const_share[:, const_index : const_index + 1] * const_outs[const_index]
    layer_out = (middle + mixture).astype(jnp.bfloat16)
    output_dots = jnp.einsum("ecd,td->ect", expert_out, upstream, precision=HIGH)
    grad_weighting = jnp.einsum("ectj,ect->tj", placement, output_dots, precision=HIGH)
    copy_dot = jnp.sum(upstream * normed_float, axis=-1)
    grad_weighting = (
        grad_weighting + (routes == EXPERTS + 1).astype(jnp.float32) * copy_dot[:, None]
    )
    for const_index in range(2):
        const_dot = jnp.sum(upstream * const_outs[const_index], axis=-1)
        grad_weighting = (
            grad_weighting
            + (routes == EXPERTS + 2 + const_index).astype(jnp.float32) * const_dot[:, None]
        )
    grad_picked = weighting * (
        grad_weighting - jnp.sum(weighting * grad_weighting, axis=-1, keepdims=True)
    )
    grad_logits = jnp.einsum("tj,tjr->tr", grad_picked, choose, precision=HIGH)
    vector_dots = jnp.dot(upstream, vectors, precision=HIGH)
    grad_mixing = const_share[:, :, None] * jnp.stack(
        [jnp.broadcast_to(copy_dot[:, None], vector_dots.shape), vector_dots], axis=-1
    )
    grad_mix = (
        mixing * (grad_mixing - jnp.sum(mixing * grad_mixing, axis=-1, keepdims=True))
    ).reshape(tok_rows, 4)
    grad_const_weight = jnp.dot(normed_float.T, grad_mix, precision=HIGH)
    grad_vectors = jnp.einsum("ti,td->di", const_share * mixing[:, :, 1], upstream, precision=HIGH)
    grad_router_weight = jnp.dot(normed_float.T, grad_logits, precision=HIGH)
    direct_share = (
        copy_share + const_share[:, 0] * mixing[:, 0, 0] + const_share[:, 1] * mixing[:, 1, 0]
    )
    grad_normed_two = direct_share[:, None] * upstream
    grad_normed_two = grad_normed_two + jnp.dot(
        grad_mix, full_const.astype(jnp.float32).T, precision=HIGH
    )
    grad_normed_two = grad_normed_two + jnp.dot(
        grad_logits, full_router.astype(jnp.float32).T, precision=HIGH
    )
    grad_down_local = jnp.einsum(
        "scf,scd->fd", hidden, kept_grads, preferred_element_type=jnp.float32
    )
    grad_gate_local = jnp.einsum(
        "scd,scf->df", kept_rows, grad_gate_pre, preferred_element_type=jnp.float32
    )
    grad_up_local = jnp.einsum(
        "scd,scf->df", kept_rows, grad_up_pre, preferred_element_type=jnp.float32
    )
    grad_slots = grad_back.reshape(EXPERTS, width_split, CAP, width).sum(axis=1)
    grad_normed_two = grad_normed_two + jnp.einsum(
        "ect,ecd->td", select, grad_slots, precision=HIGH
    )
    grad_gate_sum, grad_up_sum, grad_down_sum = (
        lax.psum_scatter(
            grad_gate_local.astype(jnp.bfloat16), "head", scatter_dimension=0, tiled=True
        ).astype(jnp.float32),
        lax.psum_scatter(
            grad_up_local.astype(jnp.bfloat16), "head", scatter_dimension=0, tiled=True
        ).astype(jnp.float32),
        lax.psum_scatter(
            grad_down_local.astype(jnp.bfloat16), "head", scatter_dimension=1, tiled=True
        ).astype(jnp.float32),
    )
    grad_from_norm, grad_gain_two = norm_back(grad_normed_two, middle, inverse_two, gain_two)
    grad_middle = upstream + grad_from_norm
    branch_grad = grad_middle.astype(jnp.bfloat16)
    grad_out_weight = jnp.einsum(
        "tc,td->cd", attended, branch_grad, preferred_element_type=jnp.float32
    )
    grad_attended = jnp.einsum(
        "td,cd->tc", branch_grad, full_output, preferred_element_type=jnp.float32
    ).astype(jnp.bfloat16)
    grad_heads = lax.all_to_all(
        grad_attended.reshape(tok_rows, head_count, head_width),
        "head",
        split_axis=1,
        concat_axis=0,
        tiled=True,
    )
    grad_heads = grad_heads.reshape(query_rows, local_heads, HEAD_DIM)
    offset = jnp.sum(grad_heads.astype(jnp.float32) * attended_local.astype(jnp.float32), axis=-1).T

    def probe_block(queries, grads, lse_rows, offset_rows, block_keys, block_values, visible):
        scores = masked_scores(queries, block_keys, visible)
        probabilities = jnp.exp(scores - lse_rows[..., None])
        grad_probs = jnp.einsum(
            "qhd,khd->hqk", grads, block_values, preferred_element_type=jnp.float32
        )
        grad_scores = (probabilities * (grad_probs - offset_rows[..., None])).astype(jnp.bfloat16)
        return (probabilities, grad_scores)

    zero_query = jnp.zeros((query_rows, local_heads, HEAD_DIM), jnp.float32)

    def backward_block(grad_query, block):
        block_keys, block_values, block_segment, block_position = block
        visible = visible_pairs(
            query_segment, query_position, block_segment, block_position, period
        )

        def backward_compute(accumulated):
            probabilities, grad_scores = probe_block(
                query_heads, grad_heads, log_total, offset, block_keys, block_values, visible
            )
            grad_values = jnp.einsum(
                "hqk,qhd->khd",
                probabilities.astype(jnp.bfloat16),
                grad_heads,
                preferred_element_type=jnp.float32,
            )
            accumulated = (
                accumulated
                + jnp.einsum(
                    "hqk,khd->qhd", grad_scores, block_keys, preferred_element_type=jnp.float32
                )
                * score_scale
            )
            grad_keys = (
                jnp.einsum(
                    "hqk,qhd->khd", grad_scores, query_heads, preferred_element_type=jnp.float32
                )
                * score_scale
            )
            return (accumulated, jnp.concatenate([grad_keys, grad_values], axis=-1))

        def skipped(accumulated):
            return (
                accumulated,
                jnp.zeros((block_keys.shape[0], local_heads, 2 * HEAD_DIM), jnp.float32),
            )

        return lax.cond(jnp.any(visible), backward_compute, skipped, grad_query)

    def fold_back(carried, pieces, first_row):
        grad_query, stacked = lax.scan(backward_block, carried[0], key_slices(pieces))
        term_piece = stacked.reshape(pieces[0].shape[0], local_heads * 2 * HEAD_DIM)
        return (grad_query, term_piece)

    zero_term = jnp.zeros((blk_count * query_rows, local_heads * 2 * HEAD_DIM), jnp.float32)
    grad_query, key_term = around_blocks(
        (key_heads, value_heads), fold_back, (zero_query, zero_term)
    )
    key_sums = lax.psum_scatter(key_term, "blk", scatter_dimension=0, tiled=True).reshape(
        query_rows, local_heads, 2, HEAD_DIM
    )
    grad_key_heads = key_sums[:, :, 0].astype(jnp.bfloat16).reshape(query_rows, 1, head_width)
    grad_value_heads = key_sums[:, :, 1].astype(jnp.bfloat16).reshape(query_rows, 1, head_width)
    grad_query_heads = grad_query.astype(jnp.bfloat16).reshape(query_rows, 1, head_width)
    grad_query_tok, grad_key_tok, grad_value_tok = (
        lax.all_to_all(grad_query_heads, "head", split_axis=0, concat_axis=1, tiled=True),
        lax.all_to_all(grad_key_heads, "head", split_axis=0, concat_axis=1, tiled=True),
        lax.all_to_all(grad_value_heads, "head", split_axis=0, concat_axis=1, tiled=True),
    )
    grad_joined = jnp.concatenate(
        [grad_query_tok.reshape(tok_rows, width), grad_key_tok.reshape(tok_rows, width)], axis=1
    )
    grad_value_tok = grad_value_tok.reshape(tok_rows, width)
    grad_normed_one = jnp.einsum(
        "tc,dc->td", grad_joined, full_joint, preferred_element_type=jnp.float32
    ) + jnp.einsum("tc,dc->td", grad_value_tok, full_value, preferred_element_type=jnp.float32)
    grad_joint_weight = jnp.einsum(
        "td,tc->dc", normed_one, grad_joined, preferred_element_type=jnp.float32
    )
    grad_value_weight = jnp.einsum(
        "td,tc->dc", normed_one, grad_value_tok, preferred_element_type=jnp.float32
    )
    grad_from_first, grad_gain_one = norm_back(grad_normed_one, source, inverse_one, gain_one)
    grad_input = grad_middle + grad_from_first
    summed = (
        lax.psum_scatter(grad_gain_one, ("head", "blk"), scatter_dimension=0, tiled=True),
        lax.psum_scatter(grad_gain_two, ("head", "blk"), scatter_dimension=0, tiled=True),
        lax.psum_scatter(grad_joint_weight, ("head", "blk"), scatter_dimension=0, tiled=True),
        lax.psum_scatter(grad_value_weight, ("head", "blk"), scatter_dimension=0, tiled=True),
        lax.psum_scatter(grad_out_weight, ("head", "blk"), scatter_dimension=0, tiled=True),
        lax.psum_scatter(grad_router_weight, ("head", "blk"), scatter_dimension=0, tiled=True),
        lax.psum_scatter(grad_const_weight, ("head", "blk"), scatter_dimension=0, tiled=True),
        lax.psum_scatter(grad_vectors, ("head", "blk"), scatter_dimension=0, tiled=True),
    )
    return (
        layer_out,
        grad_input,
        grad_logits,
        summed[0],
        summed[1],
        summed[2],
        summed[3],
        summed[4],
        summed[5],
        summed[6],
        summed[7],
        grad_gate_sum,
        grad_up_sum,
        grad_down_sum,
    )


MESH = pl.DeviceIdType.MESH
SMALL = 24
ROUTER_AT, MIX_AT, VECTOR_AT, GAIN_ONE_AT, GAIN_TWO_AT = 0, 12, 16, 18, 19
PAD = 32
CHUNK = 4
FAR = 1 << 20
NT = (((1,), (1,)), ((), ()))
TN = (((0,), (0,)), ((), ()))


def mul(left, right):
    return jnp.dot(left, right, preferred_element_type=jnp.float32)


def mul_nt(left, right):
    return lax.dot_general(left, right, NT, preferred_element_type=jnp.float32)


def mul_tn(left, right):
    return lax.dot_general(left, right, TN, preferred_element_type=jnp.float32)


def low(values):
    return values.astype(jnp.bfloat16)


def wide(values):
    return values.astype(jnp.float32)


def halves(values):
    high = low(values)
    return high, low(values - wide(high))


def shape(dims, dtype=jnp.bfloat16):
    return jax.ShapeDtypeStruct(dims, dtype)


def compute(body, outs, ins, scratch=(), smem=0):
    specs = [pl.BlockSpec(memory_space=pltpu.SMEM)] * smem
    specs += [pl.BlockSpec(memory_space=pltpu.VMEM)] * (len(ins) - smem)
    return pl.pallas_call(
        body,
        out_shape=outs,
        in_specs=specs,
        out_specs=[pl.BlockSpec(memory_space=pltpu.VMEM)] * len(outs),
        scratch_shapes=list(scratch),
        compiler_params=pltpu.CompilerParams(vmem_limit_bytes=52 * 2**20),
    )(*ins)


def exchange(body, sizes, ins, outs, scratch, number, far=(), room=52):
    names = list(ins) + list(outs) + list(scratch)

    def run(*refs):
        body(Place(*sizes), types.SimpleNamespace(**dict(zip(names, refs))))

    def spec(name):
        return pl.BlockSpec(memory_space=pl.ANY if name in far else pltpu.VMEM)

    results = pl.pallas_call(
        run,
        out_shape=list(outs.values()),
        in_specs=[spec(name) for name in ins],
        out_specs=[spec(name) for name in outs],
        scratch_shapes=list(scratch.values()),
        compiler_params=pltpu.CompilerParams(
            collective_id=number, has_side_effects=True, vmem_limit_bytes=room * 2**20
        ),
    )(*ins.values())
    return types.SimpleNamespace(**dict(zip(outs, results)))


def vmem(*dims, dtype=jnp.bfloat16):
    return pltpu.VMEM(dims, dtype)


def vmem_wide(*dims):
    return pltpu.VMEM(dims, jnp.float32)


def greet(devices):
    barrier = pltpu.get_barrier_semaphore()
    for device in devices:
        pl.semaphore_signal(barrier, inc=1, device_id=device, device_id_type=MESH)


def greeted(count):
    pl.semaphore_wait(pltpu.get_barrier_semaphore(), count)


def meet(devices):
    greet(devices)
    greeted(len(devices))


class Place:
    def __init__(self, head_count, blk_count):
        self.head_count, self.blk_count = head_count, blk_count
        self.head, self.blk = lax.axis_index("head"), lax.axis_index("blk")
        self.half = blk_count // 2
        self.chip, self.core = self.blk // 2, self.blk % 2
        self.twin = self.blk + 1 - 2 * self.core

    def along(self, axis):
        if axis == "head":
            return self.head, self.head_count
        return self.blk, self.blk_count

    def device(self, axis, index):
        return (index, self.blk) if axis == "head" else (self.head, index)

    def others(self, axis):
        me, size = self.along(axis)
        return [self.device(axis, (me + step) % size) for step in range(1, size)]

    def partners(self):
        beside = self.chip + 1 - 2 * (self.chip % 2)
        beyond = (self.chip + self.half // 2) % self.half
        across = beside + self.half // 2 - self.half * (beside // (self.half // 2))
        return [across, beside, beyond]

    def chips(self):
        return [chip * 2 + self.core for chip in self.partners()]

    def exchange_order(self, axis):
        me, size = self.along(axis)
        if axis == "head":
            return [(step - 1, (me + step) % size, (me + size - step) % size) for step in range(1, size)]
        found = []
        for chip in self.partners():
            for core in (self.core, 1 - self.core):
                found.append(chip * 2 + core)
        found.append(self.twin)
        return [(number, blk, blk) for number, blk in enumerate(found)]

    def near(self):
        return [(self.head, self.twin)] + [(self.head, blk) for blk in self.chips()]


def dma(*dims):
    return pltpu.SemaphoreType.DMA(dims)


def remote(source, target, sent, got, device):
    return pltpu.make_async_remote_copy(
        src_ref=source,
        dst_ref=target,
        send_sem=sent,
        recv_sem=got,
        device_id=device,
        device_id_type=MESH,
    )


def send(source, target, sent, got, device):
    copy = remote(source, target, sent, got, device)
    copy.start()
    return copy


def keep(source, target, done):
    copy = pltpu.make_async_copy(source, target, done)
    copy.start()
    return copy


def scatter(place, axis, source, target, sent, got, wanted=lambda number: True):
    me, size = place.along(axis)
    copies = []
    for number, other, unused in place.exchange_order(axis):
        if not wanted(number):
            continue
        copies.append(
            send(
                source.at[other],
                target.at[me],
                sent.at[number],
                got.at[number],
                place.device(axis, other),
            )
        )
    return copies


def gather(place, axis, source, target, sent, got):
    me, size = place.along(axis)
    copies = []
    for step in range(1, size):
        other = (me + step) % size
        copies.append(
            send(
                source, target.at[me], sent.at[step - 1], got.at[step - 1], place.device(axis, other)
            )
        )
    return copies


class Spread:
    def __init__(self, place, ref, sent, got):
        self.place, self.ref, self.sent, self.got = place, ref, sent, got
        self.direct = [
            self.pass_on(step, place.blk, blk) for step, blk in enumerate(place.chips(), 1)
        ]
        self.rest = [self.pass_on(0, place.blk, place.twin)]

    def pass_on(self, lane, slot, blk):
        return send(
            self.ref.at[slot],
            self.ref.at[slot],
            self.sent.at[lane],
            self.got.at[lane],
            (self.place.head, blk),
        )

    def relay(self):
        place = self.place
        for step, slot in enumerate(place.chips(), 1):
            self.direct[step - 1].wait_recv()
            self.rest.append(self.pass_on(place.half - 1 + step, slot, place.twin))

    def wait(self):
        for copy in self.direct:
            copy.wait_send()
        for copy in self.rest:
            copy.wait()


class Fold:
    def __init__(self, place, terms, theirs, arrived, sent_twin, got_twin, sent, got):
        self.place, self.terms, self.theirs, self.arrived = place, terms, theirs, arrived
        self.sent, self.got = sent, got
        self.order = place.partners() + [place.chip]
        self.across = [
            send(
                terms.at[chip * 2 + 1 - place.core],
                theirs.at[step],
                sent_twin.at[step],
                got_twin.at[step],
                (place.head, place.twin),
            )
            for step, chip in enumerate(self.order)
        ]
        self.onward = []

    def add(self):
        place = self.place
        for step, chip in enumerate(self.order):
            self.across[step].wait_recv()
            total = wide(self.theirs[step]) + wide(self.terms[chip * 2 + place.core])
            self.theirs[step] = total.astype(self.theirs.dtype)
            if step < place.half - 1:
                self.onward.append(
                    send(
                        self.theirs.at[step],
                        self.arrived.at[step],
                        self.sent.at[step],
                        self.got.at[step],
                        (place.head, chip * 2 + place.core),
                    )
                )

    def total(self):
        total = wide(self.theirs[self.place.half - 1])
        for step, copy in enumerate(self.onward):
            copy.wait_recv()
            total = total + wide(self.arrived[step])
        return total

    def wait(self):
        for copy in self.across + self.onward:
            copy.wait_send()


def wait_all(*groups):
    for group in groups:
        for copy in group:
            copy.wait()


def far_block(number, head_count):
    head = lax.axis_index("head")
    found = 0
    for place in range(head_count):
        by_distance = sorted(range(head_count), key=lambda other: -abs(other - place))
        found = found + jnp.where(head == place, by_distance[number], 0)
    return found


def block_at(step, head_count):
    return (lax.axis_index("head") + step) % head_count


class LineGather:
    def __init__(self, place, ref, sent, got):
        self.place, self.ref, self.sent, self.got = place, ref, sent, got
        self.onward(0, place.head)
        self.back(0, place.head)

    def copy(self, way, hop, slot):
        head = self.place.head + 1 - 2 * way
        return remote(
            self.ref.at[slot],
            self.ref.at[slot],
            self.sent.at[way, hop],
            self.got.at[way, hop],
            (head, self.place.blk),
        )

    def sends(self, way, hop):
        head, last = self.place.head, self.place.head_count - 1
        if way == 0:
            return (head >= hop) & (head < last)
        return (head + hop <= last) & (head > 0)

    def has(self, way, hop):
        head, last = self.place.head, self.place.head_count - 1
        return head >= hop if way == 0 else head + hop <= last

    def onward(self, hop, slot):
        @pl.when(self.sends(0, hop))
        def _():
            self.copy(0, hop, slot).start()

    def back(self, hop, slot):
        @pl.when(self.sends(1, hop))
        def _():
            self.copy(1, hop, slot).start()

    def receive(self, hop):
        head, last = self.place.head, self.place.head_count - 1
        for way, slot in ((0, head - hop), (1, head + hop)):

            @pl.when(self.has(way, hop))
            def _():
                self.copy(way, hop - 1, slot).wait_recv()

            if hop < last:
                (self.onward, self.back)[way](hop, slot)

    def receive_all(self):
        for hop in range(1, self.place.head_count):
            self.receive(hop)

    def wait(self):
        for hop in range(self.place.head_count - 1):
            for way in range(2):

                @pl.when(self.sends(way, hop))
                def _():
                    self.copy(way, hop, self.place.head).wait_send()


class LineSum:
    def __init__(self, place, outbox, inbox, sent, got):
        self.place, self.outbox, self.inbox = place, outbox, inbox
        self.sent, self.got = sent, got

    def copy(self, way, slot):
        head = self.place.head + 1 - 2 * way
        return remote(
            self.outbox.at[slot],
            self.inbox.at[way, slot],
            self.sent.at[slot],
            self.got.at[way, slot],
            (head, self.place.blk),
        )

    def add(self, slot, term):
        head, last = self.place.head, self.place.head_count - 1
        self.outbox[slot] = low(term)
        for way, towards, first in ((0, slot > head, head == 0), (1, slot < head, head == last)):

            @pl.when(towards & jnp.logical_not(first))
            def _():
                self.copy(way, slot).wait_recv()
                self.outbox[slot] = low(wide(self.outbox[slot]) + wide(self.inbox[way, slot]))

            @pl.when(towards)
            def _():
                self.copy(way, slot).start()

    def total(self, term):
        head, last = self.place.head, self.place.head_count - 1
        for way, has in ((0, head > 0), (1, head < last)):

            @pl.when(has)
            def _():
                self.copy(way, head).wait_recv()

        for way, has in ((0, head > 0), (1, head < last)):
            term = term + jnp.where(has, wide(self.inbox[way, head]), 0.0)
        return term

    def wait(self):
        for slot in range(self.place.head_count):

            @pl.when(slot > self.place.head)
            def _():
                self.copy(0, slot).wait_send()

            @pl.when(slot < self.place.head)
            def _():
                self.copy(1, slot).wait_send()


def rows_at(block, tokens):
    return pl.ds(pl.multiple_of(block * tokens, tokens), tokens)


def lanes_joined(*parts):
    return jnp.concatenate(parts, axis=1)


def rows_joined(*parts):
    return jnp.concatenate(parts, axis=0)


def packed_rows(piece):
    half = piece.shape[1] // 2
    return lanes_joined(piece[:16], rows_joined(piece[16:, :half], piece[16:, half:]))


def unpacked_rows(packed):
    width = packed.shape[1] * 2 // 3
    rest = packed[:, width:]
    return rows_joined(packed[:, :width], lanes_joined(rest[:8], rest[8:]))


def own_pieces(product, rows, head_count, blk_count, blk):
    return rows_joined(
        *[
            product[(head * blk_count + blk) * rows : (head * blk_count + blk + 1) * rows]
            for head in range(head_count)
        ]
    )


def open_layer(place, r):
    head_count, blk_count = place.head_count, place.blk_count
    head, blk = place.head, place.blk
    tokens, width = r.x.shape
    rows = r.joint_rows.shape[0]
    columns = r.down_0.shape[1]
    head_width = width // head_count
    split = 2 * HEAD_DIM
    joint_width = r.joint.shape[1]
    greet(place.others("head") + place.near())
    names = ["router", "mix", "vectors", "gain_one", "gain_two", "joint_rows", "value_rows"]
    names += ["segment", "position", "routes", "residual", "output_rows", "x"]
    here = {
        name: keep(getattr(r, name), getattr(r, "my_" + name), r.local.at[number])
        for number, name in enumerate(names)
    }
    number = len(names)
    late_own = [keep(r.g, r.g_all.at[head], r.local.at[number])]
    for step, piece in enumerate((r.down_0, r.down_1, r.down_2, r.down_3)):
        at = rows_at(block_at(step, head_count), columns)
        late_own.append(keep(r.down.at[:, at], piece, r.local.at[number + 1 + step]))
    for name in names[:7]:
        here[name].wait()
    marks = rows_joined(
        *[
            wide(ref[...])
            for ref in (r.my_router, r.my_mix, r.my_vectors, r.my_gain_one, r.my_gain_two)
        ]
    )
    marks = rows_joined(marks, jnp.zeros((128 - marks.shape[0], rows), jnp.float32))
    marks = lanes_joined(marks, jnp.zeros((128, 128 - rows), jnp.float32))
    marks = marks.T[:rows]
    both = wide(r.my_joint_rows[...])
    third = wide(r.my_value_rows[...])
    filler = jnp.zeros((rows, HEAD_DIM), jnp.float32)
    for part in range(head_count):
        at = part * head_width
        piece = lanes_joined(
            both[:, at : at + head_width],
            filler,
            both[:, width + at : width + at + head_width],
            third[:, at + split : at + head_width],
            third[:, at : at + split],
            marks,
        )
        r.joint_own[part] = low(packed_rows(piece))
    r.joint_all[blk, head] = r.joint_own[head]
    for name in names[7:]:
        here[name].wait()
    facts = rows_joined(
        wide(r.my_segment[...]),
        wide(r.my_position[...]),
        wide(r.my_routes[...]),
        jnp.zeros((4, tokens), jnp.float32),
        r.my_residual[...],
        jnp.zeros((24 - 8 - ROUTED, tokens), jnp.float32),
    )
    r.facts_own[...] = facts
    r.facts[head] = facts
    r.marks_all[blk, head] = facts[:8]
    greeted(head_count - 1 + place.half)
    first = scatter(place, "head", r.joint_own, r.joint_all.at[blk], r.sent.at[0], r.got.at[0])
    first += gather(place, "head", r.facts_own, r.facts, r.sent.at[1], r.got.at[1])
    r.output_own[...] = low(packed_rows(wide(r.my_output_rows[...])))
    r.output_part[head] = r.output_own[...]
    r.x_all[head] = r.my_x[...]
    for copy in first:
        copy.wait_send()
    tokens_in = LineGather(place, r.x_all, r.sent_line.at[0], r.got_line.at[0])
    for copy in first:
        copy.wait_recv()
    for part in range(head_count):
        r.marks_all[blk, part] = r.facts[part, 0:8, :]
    joint_spread = Spread(place, r.joint_all, r.sent_joint, r.got_joint)
    marks_spread = Spread(place, r.marks_all, r.sent_marks, r.got_marks)
    tokens_in.receive(1)
    joint_spread.relay()
    marks_spread.relay()
    tokens_in.receive(2)
    joint_spread.wait()
    marks_spread.wait()
    column = lax.broadcasted_iota(jnp.int32, (8, 128), 1)
    places = jnp.zeros((8, 128), jnp.float32)
    for part in range(head_count):
        for other in range(blk_count):
            places = jnp.where(
                column == other * head_count + part, r.marks_all[other, part, :, 0:1], places
            )
    r.places[...] = places.astype(jnp.int32)
    for part in range(head_count):
        for other in range(blk_count):
            r.joint_wide[pl.ds((part * blk_count + other) * rows, rows), :] = unpacked_rows(
                wide(r.joint_all[other, part])
            )
    r.joint[...] = low(r.joint_wide[:, :joint_width])
    small_rows = r.joint_wide[:, joint_width:].T
    r.small[...] = small_rows[:SMALL]
    gain = small_rows[GAIN_ONE_AT : GAIN_ONE_AT + 1]
    for hop in range(3, head_count):
        tokens_in.receive(hop)
    outputs_in = LineGather(place, r.output_part, r.sent_line.at[1], r.got_line.at[1])
    late_own[0].wait()
    upstream_in = LineGather(place, r.g_all, r.sent_line.at[2], r.got_line.at[2])
    pair_spreads = []
    cut = r.queries.shape[1]
    for step in range(head_count):
        block = block_at(step, head_count)
        source = wide(r.x_all[block])
        inverse = lax.rsqrt(jnp.mean(source * source, axis=-1, keepdims=True) + EPS)
        rows_normed = low(source * inverse * gain)
        span = rows_at(block, tokens)
        r.normed[span, :] = rows_normed
        product = mul(rows_normed, r.joint[...])
        r.queries[span, :] = low(product[:, :cut])
        r.pairs_all[blk, block] = low(product[:, cut:])
        pair_spreads.append(
            Spread(place, r.pairs_all.at[:, block], r.sent_pairs.at[step], r.got_pairs.at[step])
        )
    for step, spread in enumerate(pair_spreads):
        if 0 < step + 1 < head_count:
            outputs_in.receive(step + 1)
            upstream_in.receive(step + 1)
        spread.relay()
    for spread in pair_spreads:
        spread.wait()
    for line in (tokens_in, outputs_in, upstream_in):
        line.wait()
    wait_all(late_own[1:])


def slots_of(head_count, facts, first, second):
    tokens = first.shape[2]
    earlier = low(
        wide(
            lax.broadcasted_iota(jnp.int32, (tokens, tokens), 0)
            < lax.broadcasted_iota(jnp.int32, (tokens, tokens), 1)
        )
    )
    expert = wide(lax.broadcasted_iota(jnp.int32, (2 * EXPERTS, tokens), 0))
    expert_at = wide(lax.broadcasted_iota(jnp.int32, (EXPERTS, CAP, tokens), 0))
    rank_at = wide(lax.broadcasted_iota(jnp.int32, (EXPERTS, CAP, tokens), 1))
    for head in range(head_count):
        routes = [facts[head, 2 + choice : 3 + choice, :] for choice in range(TOP)]
        named = jnp.where((routes[0] == expert) | (routes[1] == expert), 1.0, 0.0)
        count = mul(low(named), earlier)[:EXPERTS]
        fits = count[:, None, :] == rank_at
        for choice, out in enumerate((first, second)):
            match = (routes[choice][None] == expert_at) & fits
            out[head] = low(jnp.where(match, 1.0, 0.0).reshape(EXPERTS * CAP, tokens))


def place_upstream(place, r):
    head_count = place.head_count
    slots_of(head_count, r.facts, r.first, r.second)
    parts = []
    for number in range(head_count):
        block = far_block(number, head_count)
        found = mul(r.first[block] + r.second[block], r.g_all[block])
        parts.append(found.reshape(EXPERTS, CAP, found.shape[1]))
    r.upstream[...] = low(jnp.concatenate(parts, axis=1))


def visible_blocks(places, period, me, count, chosen, shift, base=0):
    mine, mine_at = places[0, me], places[1, me]

    def look(block, found):
        other, other_at = places[0, block], places[1, block]
        same = other == mine
        shared = (other // period == mine // period) & (other % period == 0) & (mine % period != 0)
        seen = (same & (other_at <= mine_at)) | shared
        chosen[found] = block
        shift[found] = jnp.where(same & (other_at == mine_at), 0, -FAR)
        return found + seen.astype(jnp.int32)

    found = lax.fori_loop(0, count, look, base + jnp.int32(0)) - base
    for extra in range(CHUNK):
        chosen[base + found + extra] = jnp.int32(0)
        shift[base + found + extra] = jnp.int32(FAR)
    return (found + CHUNK - 1) // CHUNK


def chunk_mask(tokens, heads, shift, start):
    row = lax.broadcasted_iota(jnp.int32, (tokens, tokens), 0)
    column = lax.broadcasted_iota(jnp.int32, (tokens, tokens), 1)
    gap = row - column
    parts = [
        jnp.where(gap + shift[start + step] <= 0, 1.0, 0.0) for step in range(CHUNK)
    ]
    mask = jnp.concatenate(parts, axis=0)
    return jnp.concatenate([mask] * heads, axis=1) > 0.5


def chunk_rows(pairs, chosen, start, low_lane, high_lane):
    return jnp.concatenate(
        [pairs[chosen[start + step], :, low_lane:high_lane] for step in range(CHUNK)], axis=0
    )


def lanes_at(rows, first, last):
    lane = lax.broadcasted_iota(jnp.int32, rows.shape, 1)
    return jnp.where((lane >= first) & (lane < last), rows, jnp.zeros_like(rows))


def query_rows_of(queries, head, tokens):
    rows = queries[pl.ds(head * tokens, tokens), :]
    rows = low(wide(rows) * HEAD_DIM ** (-0.5))
    return jnp.concatenate(
        [lanes_at(rows, part * HEAD_DIM, (part + 1) * HEAD_DIM) for part in range(3)], axis=0
    )


def attend(sizes, period, places, queries, pairs, attended, totals, chosen, shift):
    head_count, blk_count = sizes
    blocks, tokens, lanes = pairs.shape
    heads = 3
    blk = lax.axis_index("blk")
    for head in range(head_count):
        chunks = visible_blocks(
            places, period, blk * head_count + head, blocks, chosen, shift
        )
        asked = query_rows_of(queries, head, tokens)

        def step(number, carried):
            top, total, weighted = carried
            start = number * CHUNK
            scores = mul_nt(chunk_rows(pairs, chosen, start, 0, 256), asked)
            scores = jnp.where(chunk_mask(tokens, heads, shift, start), scores, -jnp.inf)
            new_top = jnp.maximum(top, jnp.max(scores, axis=0, keepdims=True))
            raised = jnp.exp(scores - new_top)
            factor = jnp.exp(top - new_top)
            total = total * factor + jnp.sum(raised, axis=0, keepdims=True)
            mixed = mul_tn(chunk_rows(pairs, chosen, start, 128, lanes), low(raised))
            mixed = jnp.concatenate(
                [mixed[128:192, 0:128], mixed[192:256, 128:256], mixed[64:128, 256:384]], axis=1
            )
            return (new_top, total, weighted * factor + mixed)

        wide_lanes = heads * tokens
        top, total, weighted = lax.fori_loop(
            0,
            chunks,
            step,
            (
                jnp.full((1, wide_lanes), -1e30, jnp.float32),
                jnp.zeros((1, wide_lanes), jnp.float32),
                jnp.zeros((HEAD_DIM, wide_lanes), jnp.float32),
            ),
        )
        outcome = low(weighted / total)
        totals[head] = jnp.broadcast_to(top + jnp.log(total), totals.shape[1:])
        for part in range(heads):
            attended[head, part * HEAD_DIM : (part + 1) * HEAD_DIM, :] = outcome[
                :, part * tokens : (part + 1) * tokens
            ]


def attend_back(sizes, period, places, queries, pairs, attended, totals, given, query_grad, pair_grad, chosen, shift, owner, asked, back, offset, found, summed):
    head_count, blk_count = sizes
    blocks, tokens, lanes = pairs.shape
    heads = 3
    blk = lax.axis_index("blk")
    items = jnp.int32(0)
    for head in range(head_count):
        chunks = visible_blocks(
            places, period, blk * head_count + head, blocks, chosen, shift, items * CHUNK
        )

        def note(number, unused):
            owner[number] = jnp.int32(head)
            return unused

        lax.fori_loop(items, items + chunks, note, 0)
        items = items + chunks
        asked[head] = query_rows_of(queries, head, tokens)
        turned = wide(given[head])
        own = rows_joined(jnp.zeros((HEAD_DIM, tokens), jnp.float32), turned[128:192], turned[0:128])
        own = low(own.T)
        back[head] = rows_joined(
            lanes_at(own, 128, 192), lanes_at(own, 192, 256), lanes_at(own, 64, 128)
        )
        dots = turned * wide(attended[head])
        sums = lanes_joined(
            *[
                jnp.sum(dots[part * HEAD_DIM : (part + 1) * HEAD_DIM], axis=0, keepdims=True)
                for part in range(heads)
            ]
        )
        offset[head] = jnp.broadcast_to(sums, offset.shape[1:])
    owner[items] = jnp.int32(0)
    for extra in range(CHUNK):
        chosen[items * CHUNK + extra] = jnp.int32(0)
        shift[items * CHUNK + extra] = jnp.int32(FAR)
    summed[...] = jnp.zeros_like(summed)
    found[...] = jnp.zeros_like(found)

    def one(item):
        start = item * CHUNK
        head = owner[item]
        keys = chunk_rows(pairs, chosen, start, 0, 256)
        values = chunk_rows(pairs, chosen, start, 128, lanes)
        mine, given_back = asked[head], back[head]
        scores = mul_nt(keys, mine)
        raised = jnp.where(
            chunk_mask(tokens, heads, shift, start),
            jnp.exp(scores - totals[head, 0:1, :]),
            0.0,
        )
        grad_raised = mul_nt(values, given_back)
        grad_scores = low(raised * (grad_raised - offset[head, 0:1, :]))
        key_part = mul(grad_scores, mine)
        value_part = mul(low(raised), given_back)
        both = lanes_joined(
            key_part[:, :128], key_part[:, 128:] + value_part[:, :128], value_part[:, 128:]
        )
        query_part = mul_tn(keys, grad_scores)
        return (
            start,
            head,
            both,
            lanes_joined(
                query_part[0:64, 0:128], query_part[64:128, 128:256], query_part[128:192, 256:384]
            ),
        )

    def step(number, unused):
        results = [one(number * 2 + part) for part in range(2)]
        for start, head, both, query_part in results:
            found[head] = found[head] + query_part
            for block in range(CHUNK):
                at = chosen[start + block]
                summed[at] = summed[at] + both[block * tokens : (block + 1) * tokens]
        return unused

    lax.fori_loop(0, (items + 1) // 2, step, 0)
    for head in range(head_count):
        total = found[head] * HEAD_DIM ** (-0.5)
        stacked = rows_joined(
            *[total[:, part * tokens : (part + 1) * tokens] for part in range(heads)],
            jnp.zeros((HEAD_DIM, tokens), jnp.float32),
        )
        query_grad[pl.ds(head * tokens, tokens), :] = low(stacked.T)
    pair_grad[...] = low(summed[...])


def ffn_rows(number, span, here, r, gate, up, down, lane):
    width = r.grads_in.shape[2]
    group = lane.shape[0]
    blk_count, span_rows = r.slots_in.shape[0], group // r.slots_in.shape[0]
    entry = r.slots_in[:, span, :].reshape(group, width + 128)
    rows = entry[:, :width]
    r.taken[here, :] = rows
    tail = wide(entry[:, width:])
    share = tail[:, 0:1] + tail[:, 64:65]
    scaled_rows = low(share * wide(r.grads_in[:, span, :].reshape(group, width)))
    r.scaled[here, :] = scaled_rows
    gate_pre = mul(rows, gate)
    up_pre = mul(rows, up)
    sigmoid = 1.0 / (1.0 + jnp.exp(-gate_pre))
    activated = gate_pre * sigmoid
    hidden_rows = low(activated * up_pre)
    r.hidden[here, :] = hidden_rows
    grad_hidden = mul(scaled_rows, down)
    gate_rows = low(grad_hidden * up_pre * sigmoid * (1.0 + gate_pre * (1.0 - sigmoid)))
    up_rows = low(grad_hidden * activated)
    r.grad_gate[here, :] = gate_rows
    r.grad_up[here, :] = up_rows
    dots = jnp.sum(wide(hidden_rows) * grad_hidden, axis=1, keepdims=True)
    grad_rows = mul_nt(gate_rows, gate) + mul_nt(up_rows, up)
    high, rest = halves(dots)
    tail_out = jnp.where(lane < 64, wide(high), wide(rest))
    r.back[:, span, :] = low(lanes_joined(grad_rows, tail_out)).reshape(
        blk_count, span_rows, width + 128
    )


def middle_layer(place, r):
    head_count, blk_count = place.head_count, place.blk_count
    head, blk = place.head, place.blk
    tokens, width = r.g.shape
    columns = r.gate_all.shape[2]
    head_width = r.gate_all.shape[1]
    rows = head_width // blk_count
    half_count = head_count // 2
    greet(place.others("head") + place.others("blk"))
    r.attended_all[head] = r.attended[...]
    for part in range(head_count):
        r.output_all[blk, part] = r.output_part[part]
    own_weights = [
        keep(ref.at[:, rows_at(head, columns)], held.at[head], r.local.at[number])
        for number, (ref, held) in enumerate(((r.gate, r.gate_all), (r.up, r.up_all)))
    ]
    for step, piece in enumerate((r.down_0, r.down_1, r.down_2, r.down_3)):
        r.down_all[(head + head_count - step) % head_count] = piece[...]
    greeted(head_count + blk_count - 2)
    rows_in = LineGather(place, r.attended_all, r.sent_line, r.got_line)
    output_spread = Spread(place, r.output_all, r.sent_output, r.got_output)
    place_upstream(place, r)
    r.grads_in[blk] = r.upstream[blk]
    routed = scatter(place, "blk", r.upstream, r.grads_in, r.sent_grads, r.got_grads)
    rows_in.receive(1)
    output_spread.relay()
    rows_in.receive(2)
    output_spread.wait()
    for part in range(head_count):
        for other in range(blk_count):
            r.output_wide[pl.ds((part * blk_count + other) * rows, rows), :] = unpacked_rows(
                wide(r.output_all[other, part])
            )
    r.output[...] = low(r.output_wide[...])
    router = low(r.small[0:16])
    expert = wide(lax.broadcasted_iota(jnp.int32, (16, tokens), 0))
    lane = lax.broadcasted_iota(jnp.int32, (EXPERTS * CAP, 128), 1)
    gain = r.small[GAIN_TWO_AT : GAIN_TWO_AT + 1]
    for hop in range(3, head_count):
        rows_in.receive(hop)
    weights_in = []
    for kind, (ref, held) in enumerate(((r.gate, r.gate_all), (r.up, r.up_all))):
        copies = []
        for away in range(1, head_count):
            other = (head + away) % head_count
            copies.append(
                send(
                    ref.at[:, rows_at(other, columns)],
                    held.at[head],
                    r.sent_weights.at[kind, away - 1],
                    r.got_weights.at[kind, away - 1],
                    (other, blk),
                )
            )
        weights_in.append(copies)
    parts = []
    for number in range(head_count):
        block = far_block(number, head_count)
        found = jnp.concatenate(
            [r.attended_all[source, block] for source in range(head_count)], axis=0
        ).T
        source = wide(r.x_all[block]) + mul(found, r.output[...])
        inverse = lax.rsqrt(jnp.mean(source * source, axis=-1, keepdims=True) + EPS)
        normed = low(source * inverse * gain)
        if number == head_count - 1:
            r.middle[...] = source
            r.normed[...] = normed
            r.attended_home[...] = low(wide(found).T)
        facts = r.facts[block]
        logits = mul_nt(router, normed) + facts[8:24]
        picked = [
            jnp.sum(
                jnp.where(facts[2 + choice : 3 + choice] == expert, logits, 0.0),
                axis=0,
                keepdims=True,
            )
            for choice in range(TOP)
        ]
        highest = jnp.maximum(picked[0], picked[1])
        raised = [jnp.exp(value - highest) for value in picked]
        total = raised[0] + raised[1]
        share = [value / total for value in raised]
        r.weights[block] = jnp.concatenate(
            share + [jnp.zeros((6, tokens), jnp.float32)], axis=0
        )
        places = [r.first[block], r.second[block]]
        of_slot = jnp.sum(
            wide(places[0]) * share[0] + wide(places[1]) * share[1], axis=1, keepdims=True
        )
        high, rest = halves(of_slot)
        entry = lanes_joined(
            mul(places[0] + places[1], normed), jnp.where(lane < 64, wide(high), wide(rest))
        )
        parts.append(entry.reshape(EXPERTS, CAP, width + 128))
        if number % 2:
            span = pl.ds((number - 1) * CAP, 2 * CAP)
            r.slots[:, span, :] = low(jnp.concatenate(parts, axis=1))
            parts = []
            r.slots_in[blk, span, :] = r.slots[blk, span, :]
            routed += scatter(
                place,
                "blk",
                r.slots.at[:, span],
                r.slots_in.at[:, span],
                r.sent_slots.at[number // 2],
                r.got_slots.at[number // 2],
            )
    rows_in.wait()
    wait_all(routed)
    wait_all(own_weights, *weights_in)

    depth = head_count * head_width
    gate, up, down = [
        ref[...].reshape(depth, columns) for ref in (r.gate_all, r.up_all, r.down_all)
    ]
    span_rows = 2 * CAP
    group = blk_count * span_rows
    lane = lax.broadcasted_iota(jnp.int32, (group, 128), 1)
    routed = []
    for number in range(half_count):
        span = pl.ds(number * span_rows, span_rows)
        here = pl.ds(number * group, group)
        ffn_rows(number, span, here, r, gate, up, down, lane)
        r.back_in[blk, span, :] = r.back[blk, span, :]
        routed.append(
            scatter(
                place,
                "blk",
                r.back.at[:, span],
                r.back_in.at[:, span],
                r.sent_back.at[number],
                r.got_back.at[number],
            )
        )
    r.down_parts[...] = low(mul(r.scaled[...].T, r.hidden[...])).reshape(r.down_parts.shape)
    r.down_in[head] = r.down_parts[head]
    far_away = head_count // 2 - 1
    down_copies = scatter(
        place, "head", r.down_parts, r.down_in, r.sent_down, r.got_down, lambda number: number != far_away
    )
    cut = head_width // 2
    down_copies += scatter(
        place,
        "head",
        r.down_parts.at[:, pl.ds(0, cut)],
        r.down_in.at[:, pl.ds(0, cut)],
        r.sent_down,
        r.got_down,
        lambda number: number == far_away,
    )
    for number in range(half_count):
        span = pl.ds(number * span_rows, span_rows)
        here = pl.ds(number * group, group)
        r.outs[:, span, :] = low(mul_nt(r.hidden[here, :], down)).reshape(
            blk_count, span_rows, width
        )
    r.outs_in[blk] = r.outs[blk]
    out_copies = scatter(place, "blk", r.outs, r.outs_in, r.sent_outs, r.got_outs)
    r.turned[...] = r.taken[...].T
    for step, piece in enumerate((r.early_0, r.early_1, r.early_2, r.early_3)):
        here = rows_at(block_at(step, head_count), head_width)
        for kind, right in enumerate((r.grad_gate, r.grad_up)):
            piece[kind] = low(mul(r.turned[here, :], right[...]))
    narrow = lax.broadcasted_iota(jnp.int32, (tokens, 128), 1)
    shares_in = LineSum(place, r.parts, r.parts_in, r.sent_parts, r.got_parts)
    dot_copies = []
    for number in range(head_count):
        block = far_block(number, head_count)
        if number % 2 == 0:
            for copy in routed[number // 2]:
                copy.wait_recv()
            entries = wide(r.back_in[:, pl.ds(number * CAP, span_rows), :])
        entry = entries[:, (number % 2) * CAP : (number % 2 + 1) * CAP]
        entry = low(entry.reshape(EXPERTS * CAP, width + 128))
        found = [mul_tn(placed[block], entry) for placed in (r.first, r.second)]
        dots = [
            found[choice][:, width : width + 1] + found[choice][:, width + 64 : width + 65]
            for choice in range(TOP)
        ]
        dots = jnp.where(narrow == 0, dots[0], jnp.where(narrow == 1, dots[1], 0.0))
        r.dots[block] = dots.T[0:8]
        share = found[0][:, :width] + found[1][:, :width]
        if number < head_count - 1:
            away = (block + head_count - head) % head_count
            dot_copies.append(
                send(
                    r.dots.at[block],
                    r.dots_in.at[head],
                    r.sent_dots.at[away - 1],
                    r.got_dots.at[away - 1],
                    (block, blk),
                )
            )
            shares_in.add(block, share)
    down_copies += scatter(
        place,
        "head",
        r.down_parts.at[:, pl.ds(cut, cut)],
        r.down_in.at[:, pl.ds(cut, cut)],
        r.sent_down_rest,
        r.got_down_rest,
        lambda number: number == far_away,
    )
    home = home_early(place, r)
    r.dots_in[head] = r.dots[head]
    grad_slots = shares_in.total(share)
    for copy in dot_copies:
        copy.wait_recv()
    home_middle(place, r, home, grad_slots)
    r.given_parts[...] = low(mul_nt(r.output[...], r.middle_low[...])).reshape(
        r.given_parts.shape
    )
    r.given[head] = r.given_parts[head]
    given_copies = scatter(place, "head", r.given_parts, r.given, r.sent_given, r.got_given)
    for copy in out_copies:
        copy.wait_recv()
    for number in range(head_count):
        block = far_block(number, head_count)
        if number % 2 == 0:
            entries = wide(r.outs_in[:, pl.ds(number * CAP, span_rows), :])
        entry = entries[:, (number % 2) * CAP : (number % 2 + 1) * CAP]
        entry = low(entry.reshape(EXPERTS * CAP, width))
        shares = r.weights[block].T
        r.out_parts[block] = low(
            shares[:, 0:1] * mul_tn(r.first[block], entry)
            + shares[:, 1:2] * mul_tn(r.second[block], entry)
        )
    home_late(place, r, home)
    product = mul(r.attended_home[...], r.middle_low[...])
    for other in range(blk_count):
        r.output_terms[other] = low(own_pieces(product, rows, head_count, blk_count, other))
    for copies in routed + [out_copies, dot_copies]:
        for copy in copies:
            copy.wait_send()
    shares_in.wait()
    wait_all(down_copies, given_copies)
    pl.semaphore_signal(
        r.done, inc=1, device_id=(head, place.twin), device_id_type=MESH
    )
    pl.semaphore_wait(r.done, 1)


def home_early(place, r):
    head_count = place.head_count
    tokens, width = r.middle.shape
    share_rows = r.weights[place.head]
    columns = rows_joined(share_rows, r.facts[place.head, 0:8, :]).T
    share = [columns[:, choice : choice + 1] for choice in range(TOP)]
    route_of = [columns[:, 10 + choice : 11 + choice] for choice in range(TOP)]
    upstream = wide(r.g[...])
    normed_wide = wide(r.normed[...])
    small_low = low(r.small[...])
    seen = mul_nt(r.normed[...], small_low)
    met = mul_nt(r.g[...], small_low)

    def weight_of(expert):
        return sum(
            share[choice] * jnp.where(route_of[choice] == expert, 1.0, 0.0)
            for choice in range(TOP)
        )

    copy_share = weight_of(EXPERTS + 1)
    const_share = [weight_of(EXPERTS + 2 + const) for const in range(2)]
    mixing = []
    for const in range(2):
        at = MIX_AT + 2 * const
        pair = [seen[:, at + part : at + part + 1] for part in range(2)]
        highest = jnp.maximum(pair[0], pair[1])
        raised = [jnp.exp(value - highest) for value in pair]
        total = raised[0] + raised[1]
        mixing.append([value / total for value in raised])
    copy_dot = jnp.sum(upstream * normed_wide, axis=-1, keepdims=True)
    vector_dot = [met[:, VECTOR_AT + const : VECTOR_AT + const + 1] for const in range(2)]
    const_dot = [
        mixing[const][0] * copy_dot + mixing[const][1] * vector_dot[const] for const in range(2)
    ]
    special = []
    for choice in range(TOP):
        found = jnp.where(route_of[choice] == EXPERTS + 1, copy_dot, 0.0)
        for const in range(2):
            found = found + jnp.where(
                route_of[choice] == EXPERTS + 2 + const, const_dot[const], 0.0
            )
        special.append(share[choice] * found)
    lane = lax.broadcasted_iota(jnp.int32, (tokens, 128), 1)
    vector_share = jnp.zeros((tokens, 128), jnp.float32)
    mix_grad = jnp.zeros((tokens, 128), jnp.float32)
    for const in range(2):
        grad_mix = [const_share[const] * copy_dot, const_share[const] * vector_dot[const]]
        mean = mixing[const][0] * grad_mix[0] + mixing[const][1] * grad_mix[1]
        for part in range(2):
            mix_grad = mix_grad + jnp.where(
                lane == MIX_AT + 2 * const + part,
                mixing[const][part] * (grad_mix[part] - mean),
                0.0,
            )
        vector_share = vector_share + jnp.where(
            lane == VECTOR_AT + const, const_share[const] * mixing[const][1], 0.0
        )
    direct = copy_share + const_share[0] * mixing[0][0] + const_share[1] * mixing[1][0]
    r.direct[...] = direct * upstream
    source = r.middle[...]
    inverse = lax.rsqrt(jnp.mean(source * source, axis=-1, keepdims=True) + EPS)
    vectors = [r.small[VECTOR_AT + const : VECTOR_AT + const + 1] for const in range(2)]
    mixed = copy_share * normed_wide
    for const in range(2):
        mixed = mixed + const_share[const] * (
            mixing[const][0] * normed_wide + mixing[const][1] * vectors[const]
        )
    r.mixture[...] = source + mixed
    table = rows_joined(small_low[0:16], jnp.zeros((128 - 16, width), jnp.bfloat16))
    return types.SimpleNamespace(
        share=share,
        route_of=route_of,
        special=special,
        mix_grad=mix_grad,
        vector_share=vector_share,
        inverse=inverse,
        table=table,
    )


def home_middle(place, r, home, grad_slots):
    tokens, width = r.middle.shape
    dots = r.dots_in[0]
    for head in range(1, place.head_count):
        dots = dots + r.dots_in[head]
    dots = dots.T
    product = [dots[:, choice : choice + 1] + home.special[choice] for choice in range(TOP)]
    both = product[0] + product[1]
    lane = wide(lax.broadcasted_iota(jnp.int32, (tokens, 128), 1))
    routing = jnp.zeros((tokens, 128), jnp.float32)
    for choice in range(TOP):
        routing = routing + jnp.where(
            lane == home.route_of[choice], product[choice] - home.share[choice] * both, 0.0
        )
    spread_high, spread_rest = halves(routing + home.mix_grad)
    grad_normed = (
        r.direct[...] + grad_slots + mul(spread_high, home.table) + mul(spread_rest, home.table)
    )
    source = r.middle[...]
    scaled = grad_normed * r.small[GAIN_TWO_AT : GAIN_TWO_AT + 1]
    result = (
        wide(r.g[...])
        + home.inverse * scaled
        - source * home.inverse**3 * jnp.mean(scaled * source, axis=-1, keepdims=True)
    )
    r.middle_grad[...] = result
    r.middle_low[...] = low(result)
    r.direct[...] = grad_normed
    home.routing, home.spread = routing, (spread_high, spread_rest)


def home_late(place, r, home):
    width = r.middle.shape[1]
    r.residual_grad[...] = home.routing.T[:ROUTED]
    gain_row = jnp.sum(r.direct[...] * r.middle[...] * home.inverse, axis=0, keepdims=True)
    vector_high, vector_rest = halves(home.vector_share)
    by_normed = mul_tn(home.spread[0], r.normed[...]) + mul_tn(home.spread[1], r.normed[...])
    by_upstream = mul_tn(vector_high, r.g[...]) + mul_tn(vector_rest, r.g[...])
    row = lax.broadcasted_iota(jnp.int32, (SMALL, width), 0)
    r.small_grad[...] = jnp.where(
        row == GAIN_TWO_AT, gain_row, by_normed[:SMALL] + by_upstream[:SMALL]
    )


def close_layer(place, r):
    head_count, blk_count = place.head_count, place.blk_count
    head, blk = place.head, place.blk
    tokens, width = r.input_grad.shape
    rows = width // (head_count * blk_count)
    cut = r.query_grad.shape[1]
    joint_width = r.joint.shape[1]
    greet(place.others("head") + place.near())
    flat = jnp.concatenate(
        [r.small_grad[...], jnp.zeros((128 - SMALL, width), jnp.float32)], axis=0
    ).T
    for part in range(head_count):
        for other in range(blk_count):
            at = (part * blk_count + other) * rows
            r.small_terms[other, part * rows : (part + 1) * rows, :] = flat[at : at + rows]
    greeted(place.head_count - 1 + place.half)
    outs_in = LineSum(place, r.out_sums, r.out_in, r.sent_out, r.got_out)
    at_end = (head == 0) | (head == head_count - 1)

    @pl.when(at_end)
    def _():
        for number in range(head_count - 1):
            block = far_block(number, head_count)
            outs_in.add(block, wide(r.out_parts[block]))


    def fold(number, terms, theirs, arrived):
        return Fold(
            place,
            terms,
            theirs,
            arrived,
            r.sent_twin.at[number],
            r.got_twin.at[number],
            r.sent_blk.at[number],
            r.got_blk.at[number],
        )

    pair_folds = []
    for number in range(head_count):
        block = far_block(number, head_count)
        pair_folds.append(
            fold(
                number,
                r.pair_terms.at[:, block],
                r.theirs_pairs.at[number],
                r.arrived_pairs.at[number],
            )
        )
    output_fold = fold(head_count, r.output_terms, r.theirs_output, r.arrived_output)
    small_fold = fold(head_count + 1, r.small_terms, r.theirs_small, r.arrived_small)
    for one in pair_folds:
        one.add()
    output_fold.add()
    small_fold.add()
    r.turned[...] = r.normed[...].T
    r.early_rows[...] = mul_nt(r.query_grad[...], r.joint[:, :cut])
    early = mul(r.turned[...], r.query_grad[...])
    rows_in = LineSum(place, r.row_parts, r.rows_in, r.sent_rows, r.got_rows)
    for number in range(head_count - 1):
        block = far_block(number, head_count)

        @pl.when(jnp.logical_not(at_end))
        def _():
            outs_in.add(block, wide(r.out_parts[block]))

    gain_row = jnp.zeros((1, width), jnp.float32)
    for number in range(head_count):
        block = far_block(number, head_count)
        here = rows_at(block, tokens)
        part = low(pair_folds[number].total())
        r.grads[here, :] = part
        grad_normed = r.early_rows[here, :] + mul_nt(part, r.joint[:, cut:])
        if number < head_count - 1:
            rows_in.add(block, grad_normed)

        else:
            own_rows = grad_normed
        source = wide(r.x_all[block])
        inverse = lax.rsqrt(jnp.mean(source * source, axis=-1, keepdims=True) + EPS)
        gain_row = gain_row + jnp.sum(grad_normed * source * inverse, axis=0, keepdims=True)
    product = jnp.concatenate([early, mul(r.turned[...], r.grads[...])], axis=1)
    for other in range(blk_count):
        r.joint_terms[other] = low(own_pieces(product, rows, head_count, blk_count, other))
    joint_fold = fold(head_count + 2, r.joint_terms, r.theirs_joint, r.arrived_joint)
    owners = head_count * blk_count
    owner = lax.broadcasted_iota(jnp.int32, (owners, width), 0)
    column = lax.broadcasted_iota(jnp.int32, (owners, width), 1)
    owned = jnp.where(column // rows == owner, gain_row, 0.0)
    feature = lax.broadcasted_iota(jnp.int32, (width, 128), 0)
    target = lax.broadcasted_iota(jnp.int32, (width, 128), 1)
    moved = low(jnp.where(feature % rows == target, 1.0, 0.0))
    high, rest = halves(owned)
    by_owner = mul(high, moved) + mul(rest, moved)
    for other in range(blk_count):
        r.gain_terms[other] = jnp.concatenate(
            [
                by_owner[part * blk_count + other : part * blk_count + other + 1]
                for part in range(head_count)
            ]
            + [jnp.zeros((8 - head_count, 128), jnp.float32)],
            axis=0,
        )
    gain_fold = fold(head_count + 3, r.gain_terms, r.theirs_gain, r.arrived_gain)
    r.small_sums[...] = small_fold.total().reshape(head_count, rows, 128)
    r.small_in[head] = r.small_sums[head]
    last = scatter(place, "head", r.small_sums, r.small_in, r.sent_last.at[0], r.got_last.at[0])
    output_sum = output_fold.total()
    for part in range(head_count):
        r.output_sums[part] = low(packed_rows(output_sum[part * rows : (part + 1) * rows]))
    r.output_in[head] = r.output_sums[head]
    last += scatter(place, "head", r.output_sums, r.output_in, r.sent_last.at[3], r.got_last.at[3])
    joint_fold.add()
    gain_fold.add()
    joint_sum = joint_fold.total()
    filler = jnp.zeros((PAD - rows, joint_width), jnp.float32)
    for part in range(head_count):
        r.joint_sums[part] = low(rows_joined(joint_sum[part * rows : (part + 1) * rows], filler))
    r.joint_out[head] = r.joint_sums[head]
    last += scatter(place, "head", r.joint_sums, r.joint_out, r.sent_last.at[1], r.got_last.at[1])
    gain_now = gain_fold.total()
    for part in range(head_count):
        r.gain_sums[part] = jnp.broadcast_to(gain_now[part : part + 1], (8, 128))
    r.gain_in[head] = r.gain_sums[head]
    last += scatter(place, "head", r.gain_sums, r.gain_in, r.sent_last.at[2], r.got_last.at[2])
    total = r.mixture[...] + outs_in.total(wide(r.out_parts[head]))
    r.layer_out[...] = low(total)
    grad_normed = rows_in.total(own_rows)
    source = wide(r.x_all[head])
    inverse = lax.rsqrt(jnp.mean(source * source, axis=-1, keepdims=True) + EPS)
    scaled = grad_normed * r.small[GAIN_ONE_AT : GAIN_ONE_AT + 1]
    r.input_grad[...] = (
        r.middle_grad[...]
        + inverse * scaled
        - source * inverse**3 * jnp.mean(scaled * source, axis=-1, keepdims=True)
    )
    for copy in last:
        copy.wait_recv()
    output_sum = wide(r.output_in[0])
    for part in range(1, head_count):
        output_sum = output_sum + wide(r.output_in[part])
    r.output_grad[...] = unpacked_rows(output_sum)
    r.small_total[...] = sum(r.small_in[part] for part in range(head_count))
    r.gain_total[...] = sum(r.gain_in[part] for part in range(head_count))
    for one in pair_folds + [output_fold, small_fold, joint_fold, gain_fold]:
        one.wait()
    outs_in.wait()
    rows_in.wait()
    for copy in last:
        copy.wait_send()


def finish(
    sizes,
    piece_0,
    piece_1,
    piece_2,
    piece_3,
    down_in,
    joint_in,
    small_in,
    gain_in,
    sums_in,
    rows_in,
    layer_in,
    residual_in,
    gate,
    up,
    down,
    joint,
    value,
    gain_one,
    gain_two,
    router,
    mix,
    vectors,
    output,
    rows,
    layer,
    residual,
):
    head_count, blk_count = sizes
    mine = lax.axis_index("head")
    columns = piece_0.shape[2]
    for step, piece in enumerate((piece_0, piece_1, piece_2, piece_3)):
        source = (mine + head_count - step) % head_count
        at = rows_at(source, columns)
        gate[:, at] = wide(piece[0])
        up[:, at] = wide(piece[1])
    for source in range(head_count):
        down[:, source * columns : (source + 1) * columns] = wide(down_in[source])
    own_rows = joint.shape[0]
    parts = [wide(joint_in[source])[:own_rows] for source in range(head_count)]
    joint[...] = lanes_joined(
        *[part[:, 0:192] for part in parts], *[part[:, 256:448] for part in parts]
    )
    value[...] = lanes_joined(
        *[lanes_joined(part[:, 512:640], part[:, 448:512]) for part in parts]
    )
    flat = small_in[...]
    flat = jnp.concatenate(
        [flat, jnp.zeros((128 - own_rows, 128), jnp.float32)], axis=0
    ).T[:SMALL, :own_rows]
    gain_one[...] = gain_in[0:1, :own_rows]
    gain_two[...] = flat[GAIN_TWO_AT : GAIN_TWO_AT + 1]
    router[...] = flat[ROUTER_AT : ROUTER_AT + ROUTED]
    mix[...] = flat[MIX_AT : MIX_AT + 4]
    vectors[...] = flat[VECTOR_AT : VECTOR_AT + 2]
    output[...] = sums_in[...]
    rows[...] = rows_in[...]
    layer[...] = layer_in[...]
    residual[...] = residual_in[...]


def after(values, *signals):
    return lax.optimization_barrier((values, signals))[0]


def around_heads(pieces):
    count = len(pieces)
    return [pieces[0]] + [
        lax.ppermute(pieces[step], "head", [(i, (i + step) % count) for i in range(count)])
        for step in range(1, count)
    ]


def fast_shards(
    inputs,
    cotangent,
    segment,
    position,
    routes,
    gate_residual,
    first_gain,
    second_gain,
    query_key_weight,
    value_weight,
    output_weight,
    router_weight,
    const_gate,
    const_vectors,
    gate_weight,
    up_weight,
    down_weight,
):
    tokens, width = inputs.shape
    head_count = lax.axis_size("head")
    blk_count = lax.axis_size("blk")
    sizes = (head_count, blk_count)
    part = functools.partial
    half = blk_count // 2
    period = tokens * blk_count // CONT_LEN + 1
    head_width = width // head_count
    column_rows = head_count * tokens
    weight_rows = query_key_weight.shape[0]
    columns = gate_weight.shape[1] // head_count
    slot_rows = head_count * CAP
    slot_total = blk_count * slot_rows
    joint_width = 10 * HEAD_DIM
    pair_width = 6 * HEAD_DIM
    others, near = head_count - 1, blk_count - 1
    packed = width * 3 // 2
    joint_packed = (joint_width + 128) * 3 // 2

    opened_from = dict(
            x=inputs,
            joint_rows=query_key_weight,
            value_rows=value_weight,
            output_rows=output_weight,
            router=router_weight.T,
            mix=const_gate.T,
            vectors=const_vectors.T,
            gain_one=first_gain[None],
            gain_two=second_gain[None],
            segment=segment[None],
            position=position[None],
            routes=routes.T,
            residual=gate_residual.T,
            g=cotangent,
            down=down_weight.T,
    )
    opened = exchange(
        open_layer,
        sizes,
        opened_from,
        dict(
            x_all=shape((head_count, tokens, width)),
            facts=shape((head_count, 24, tokens), jnp.float32),
            places=shape((8, 128), jnp.int32),
            g_all=shape((head_count, tokens, width)),
            normed=shape((column_rows, width)),
            queries=shape((column_rows, 4 * HEAD_DIM)),
            pairs_all=shape((blk_count, head_count, tokens, pair_width)),
            joint=shape((width, joint_width)),
            output_part=shape((head_count, 16, packed)),
            small=shape((SMALL, width), jnp.float32),
            down_0=shape((head_width, columns)),
            down_1=shape((head_width, columns)),
            down_2=shape((head_width, columns)),
            down_3=shape((head_width, columns)),
        ),
        dict(
            my_router=vmem(ROUTED, weight_rows),
            my_mix=vmem(4, weight_rows),
            my_vectors=vmem(2, weight_rows),
            my_gain_one=vmem(1, weight_rows),
            my_gain_two=vmem(1, weight_rows),
            my_joint_rows=vmem(*query_key_weight.shape),
            my_value_rows=vmem(*value_weight.shape),
            my_segment=vmem(1, tokens, dtype=jnp.int32),
            my_position=vmem(1, tokens, dtype=jnp.int32),
            my_routes=vmem(TOP, tokens, dtype=jnp.int32),
            my_residual=vmem_wide(ROUTED, tokens),
            my_output_rows=vmem(*output_weight.shape),
            my_x=vmem(tokens, width),
            marks_all=vmem_wide(blk_count, head_count, 8, tokens),
            joint_own=vmem(head_count, 16, joint_packed),
            output_own=vmem(16, packed),
            facts_own=vmem_wide(24, tokens),
            joint_all=vmem(blk_count, head_count, 16, joint_packed),
            joint_wide=vmem_wide(width, joint_width + 128),
            local=dma(18),
            sent=dma(2, others),
            got=dma(2, others),
            sent_line=dma(3, 2, others),
            got_line=dma(3, 2, others),
            sent_joint=dma(near),
            got_joint=dma(near),
            sent_marks=dma(near),
            got_marks=dma(near),
            sent_pairs=dma(head_count, near),
            got_pairs=dma(head_count, near),
        ),
        0,
        far=tuple(opened_from) + ("g_all", "down_0", "down_1", "down_2", "down_3"),
        room=63,
    )
    down_pieces = around_heads([opened.down_0, opened.down_1, opened.down_2, opened.down_3])
    pairs_all = opened.pairs_all.reshape(blk_count * head_count, tokens, pair_width)
    lists = [
        pltpu.SMEM((blk_count * head_count + CHUNK,), jnp.int32),
        pltpu.SMEM((blk_count * head_count + CHUNK,), jnp.int32),
    ]
    items_at_most = head_count * (blk_count * head_count // CHUNK + 1) + 1
    long_lists = [pltpu.SMEM((items_at_most * CHUNK + CHUNK,), jnp.int32)] * 2
    attended, totals = compute(
        part(attend, sizes, period),
        [
            shape((head_count, head_width, tokens)),
            shape((head_count, 8, 3 * tokens), jnp.float32),
        ],
        [opened.places, opened.queries, pairs_all],
        lists,
        1,
    )
    halved = head_count // 2
    went = exchange(
        middle_layer,
        sizes,
        dict(
            attended=attended,
            g_all=opened.g_all,
            x_all=opened.x_all,
            output_part=opened.output_part,
            small=opened.small,
            facts=opened.facts,
            g=cotangent,
            gate=gate_weight,
            up=up_weight,
            down_0=down_pieces[0],
            down_1=down_pieces[1],
            down_2=down_pieces[2],
            down_3=down_pieces[3],
        ),
        dict(
            output_terms=shape((blk_count, head_count * weight_rows, width)),
            early_0=shape((2, head_width, columns)),
            early_1=shape((2, head_width, columns)),
            early_2=shape((2, head_width, columns)),
            early_3=shape((2, head_width, columns)),
            down_in=shape((head_count, head_width, columns)),
            out_parts=shape((head_count, tokens, width)),
            middle_grad=shape((tokens, width), jnp.float32),
            given=shape((head_count, head_width, tokens)),
            residual_grad=shape((ROUTED, tokens), jnp.float32),
            small_grad=shape((SMALL, width), jnp.float32),
            mixture=shape((tokens, width), jnp.float32),
        ),
        dict(
            attended_all=vmem(head_count, head_count, head_width, tokens),
            attended_home=vmem(width, tokens),
            first=vmem(head_count, EXPERTS * CAP, tokens),
            second=vmem(head_count, EXPERTS * CAP, tokens),
            upstream=vmem(EXPERTS, slot_rows, width),
            output=vmem(width, width),
            output_all=vmem(blk_count, head_count, 16, packed),
            output_wide=vmem_wide(width, width),
            slots=vmem(EXPERTS, slot_rows, width + 128),
            slots_in=vmem(blk_count, slot_rows, width + 128),
            grads_in=vmem(blk_count, slot_rows, width),
            middle=vmem_wide(tokens, width),
            normed=vmem(tokens, width),
            weights=vmem_wide(head_count, 8, tokens),
            gate_all=vmem(head_count, head_width, columns),
            up_all=vmem(head_count, head_width, columns),
            down_all=vmem(head_count, head_width, columns),
            taken=vmem(slot_total, width),
            turned=vmem(width, slot_total),
            hidden=vmem(slot_total, columns),
            grad_gate=vmem(slot_total, columns),
            grad_up=vmem(slot_total, columns),
            scaled=vmem(slot_total, width),
            back=vmem(blk_count, slot_rows, width + 128),
            outs=vmem(blk_count, slot_rows, width),
            back_in=vmem(blk_count, slot_rows, width + 128),
            outs_in=vmem(blk_count, slot_rows, width),
            parts=vmem(head_count, tokens, width),
            parts_in=vmem(2, head_count, tokens, width),
            dots=vmem_wide(head_count, 8, tokens),
            dots_in=vmem_wide(head_count, 8, tokens),
            down_parts=vmem(head_count, head_width, columns),
            middle_low=vmem(tokens, width),
            direct=vmem_wide(tokens, width),
            given_parts=vmem(head_count, head_width, tokens),
            local=dma(2),
            sent_line=dma(2, others),
            got_line=dma(2, others),
            sent_dots=dma(others),
            got_dots=dma(others),
            sent_output=dma(near),
            got_output=dma(near),
            sent_grads=dma(near),
            got_grads=dma(near),
            sent_weights=dma(2, others),
            got_weights=dma(2, others),
            sent_slots=dma(halved, near),
            got_slots=dma(halved, near),
            sent_back=dma(halved, near),
            got_back=dma(halved, near),
            sent_outs=dma(near),
            got_outs=dma(near),
            sent_down=dma(others),
            got_down=dma(others),
            sent_down_rest=dma(others),
            got_down_rest=dma(others),
            sent_parts=dma(head_count),
            got_parts=dma(2, head_count),
            sent_given=dma(others),
            got_given=dma(others),
            done=pltpu.SemaphoreType.REGULAR,
        ),
        1,
        far=("gate", "up"),
    )
    grad_pieces = around_heads([went.early_0, went.early_1, went.early_2, went.early_3])
    query_grad, pair_grad = compute(
        part(attend_back, sizes, period),
        [shape(opened.queries.shape), shape(pairs_all.shape)],
        [
            opened.places,
            opened.queries,
            pairs_all,
            attended,
            totals,
            went.given,
        ],
        long_lists
        + [
            pltpu.SMEM((items_at_most,), jnp.int32),
            vmem(head_count, 3 * tokens, 4 * HEAD_DIM),
            vmem(head_count, 3 * tokens, 4 * HEAD_DIM),
            vmem_wide(head_count, 8, 3 * tokens),
            vmem_wide(head_count, HEAD_DIM, 3 * tokens),
            vmem_wide(*pairs_all.shape),
        ],
        1,
    )
    folds = head_count + 4
    closed = exchange(
        close_layer,
        sizes,
        dict(
            pair_terms=pair_grad.reshape(blk_count, head_count, tokens, pair_width),
            query_grad=query_grad,
            joint=opened.joint,
            normed=opened.normed,
            x_all=opened.x_all,
            small_grad=went.small_grad,
            out_parts=went.out_parts,
            output_terms=went.output_terms,
            small=opened.small,
            middle_grad=went.middle_grad,
            mixture=went.mixture,
        ),
        dict(
            input_grad=shape((tokens, width), jnp.float32),
            layer_out=shape((tokens, width)),
            joint_out=shape((head_count, PAD, joint_width)),
            output_grad=shape((weight_rows, width), jnp.float32),
            small_total=shape((weight_rows, 128), jnp.float32),
            gain_total=shape((8, 128), jnp.float32),
        ),
        dict(
            theirs_pairs=vmem(head_count, half, tokens, pair_width),
            arrived_pairs=vmem(head_count, half - 1, tokens, pair_width),
            theirs_output=vmem(half, head_count * weight_rows, width),
            arrived_output=vmem(half - 1, head_count * weight_rows, width),
            output_sums=vmem(head_count, 16, packed),
            output_in=vmem(head_count, 16, packed),
            small_terms=vmem_wide(blk_count, head_count * weight_rows, 128),
            theirs_small=vmem_wide(half, head_count * weight_rows, 128),
            arrived_small=vmem_wide(half - 1, head_count * weight_rows, 128),
            joint_terms=vmem(blk_count, head_count * weight_rows, joint_width),
            theirs_joint=vmem(half, head_count * weight_rows, joint_width),
            arrived_joint=vmem(half - 1, head_count * weight_rows, joint_width),
            gain_terms=vmem_wide(blk_count, 8, 128),
            theirs_gain=vmem_wide(half, 8, 128),
            arrived_gain=vmem_wide(half - 1, 8, 128),
            row_parts=vmem(head_count, tokens, width),
            rows_in=vmem(2, head_count, tokens, width),
            out_sums=vmem(head_count, tokens, width),
            out_in=vmem(2, head_count, tokens, width),
            joint_sums=vmem(head_count, PAD, joint_width),
            small_sums=vmem_wide(head_count, weight_rows, 128),
            small_in=vmem_wide(head_count, weight_rows, 128),
            gain_sums=vmem_wide(head_count, 8, 128),
            gain_in=vmem_wide(head_count, 8, 128),
            turned=vmem(width, column_rows),
            grads=vmem(column_rows, pair_width),
            early_rows=vmem_wide(column_rows, width),
            sent_out=dma(head_count),
            got_out=dma(2, head_count),
            sent_twin=dma(folds, half),
            got_twin=dma(folds, half),
            sent_blk=dma(folds, half - 1),
            got_blk=dma(folds, half - 1),
            sent_rows=dma(head_count),
            got_rows=dma(2, head_count),
            sent_last=dma(4, others),
            got_last=dma(4, others),
        ),
        2,
    )
    wide_shape = part(shape, dtype=jnp.float32)
    (
        gate_grad,
        up_grad,
        down_grad,
        joint_grad,
        value_grad,
        gain_one_grad,
        gain_two_grad,
        router_grad,
        mix_grad,
        vector_grad,
        output_grad,
        input_grad,
        layer_out,
        residual_grad,
    ) = compute(
        part(finish, sizes),
        [
            wide_shape(gate_weight.shape),
            wide_shape(up_weight.shape),
            wide_shape(gate_weight.shape),
            wide_shape(query_key_weight.shape),
            wide_shape(value_weight.shape),
            wide_shape((1, weight_rows)),
            wide_shape((1, weight_rows)),
            wide_shape((ROUTED, weight_rows)),
            wide_shape((4, weight_rows)),
            wide_shape((2, weight_rows)),
            wide_shape(output_weight.shape),
            wide_shape((tokens, width)),
            shape((tokens, width)),
            wide_shape((ROUTED, tokens)),
        ],
        grad_pieces
        + [
            went.down_in,
            closed.joint_out,
            closed.small_total,
            closed.gain_total,
            closed.output_grad,
            closed.input_grad,
            closed.layer_out,
            went.residual_grad,
        ],
    )
    return (
        layer_out,
        input_grad,
        residual_grad.T,
        gain_one_grad[0],
        gain_two_grad[0],
        joint_grad,
        value_grad,
        output_grad,
        router_grad.T,
        mix_grad.T,
        vector_grad.T,
        gate_grad,
        up_grad,
        down_grad.T,
    )


def solution(mesh):
    body = fast_shards if mesh.shape["blk"] == EXPERTS else shards
    in_specs = (
        P(("head", "blk"), None),
        P(("head", "blk"), None),
        P(("head", "blk")),
        P(("head", "blk")),
        P(("head", "blk"), None),
        P(("head", "blk"), None),
        P(("head", "blk")),
        P(("head", "blk")),
        P(("head", "blk"), None),
        P(("head", "blk"), None),
        P(("head", "blk"), None),
        P(("head", "blk"), None),
        P(("head", "blk"), None),
        P(("head", "blk"), None),
        P("head", "blk"),
        P("head", "blk"),
        P("blk", "head"),
    )
    out_specs = (
        P(("head", "blk"), None),
        P(("head", "blk"), None),
        P(("head", "blk"), None),
        P(("head", "blk")),
        P(("head", "blk")),
        P(("head", "blk"), None),
        P(("head", "blk"), None),
        P(("head", "blk"), None),
        P(("head", "blk"), None),
        P(("head", "blk"), None),
        P(("head", "blk"), None),
        P("head", "blk"),
        P("head", "blk"),
        P("blk", "head"),
    )
    return jax.shard_map(body, mesh=mesh, in_specs=in_specs, out_specs=out_specs, check_vma=False)
```

```python
import functools
import types

import jax
import jax.numpy as jnp
from jax import lax
from jax.experimental import pallas as pl
from jax.experimental.pallas import tpu as pltpu
from jax.sharding import PartitionSpec as P

HEADS = 12
HEAD_DIM = 64
EXPERTS = 8
ROUTED = 12
TOP = 2
CONT_LEN = 1024
CAP = 24


EPS = 1e-06
HIGH = lax.Precision.HIGHEST


def silu_slope(pre):
    sigmoid_value = jax.nn.sigmoid(pre)
    return sigmoid_value * (1.0 + pre * (1.0 - sigmoid_value))


def visible_pairs(query_segment, query_position, key_segment, key_position, period):
    same_sequence = (query_segment[:, None] == key_segment[None, :]) & (
        key_position[None, :] <= query_position[:, None]
    )
    same_group = query_segment[:, None] // period == key_segment[None, :] // period
    shared = (
        (key_segment[None, :] % period == 0) & (query_segment[:, None] % period != 0) & same_group
    )
    return same_sequence | shared


def norm_back(grad_normed, source, inverse, gain):
    scaled = grad_normed * gain
    grad_source = inverse * scaled - source * inverse**3 * jnp.mean(
        scaled * source, axis=-1, keepdims=True
    )
    grad_gain = jnp.sum(grad_normed * source * inverse, axis=0)
    return (grad_source, grad_gain)


def around_blocks(pieces, combine, initial):
    return combine(
        initial,
        (
            lax.all_gather(pieces[0], "blk", axis=0, tiled=True),
            lax.all_gather(pieces[1], "blk", axis=0, tiled=True),
        ),
        jnp.int32(0),
    )


def softmax_last(logits):
    highest = jnp.max(logits, axis=-1, keepdims=True)
    raised = jnp.exp(logits - highest)
    return raised / jnp.sum(raised, axis=-1, keepdims=True)


def shards(
    inputs,
    cotangent,
    segment,
    position,
    routes,
    gate_residual,
    first_gain,
    second_gain,
    query_key_weight,
    value_weight,
    output_weight,
    router_weight,
    const_gate,
    const_vectors,
    gate_weight,
    up_weight,
    down_weight,
):
    tok_rows, width = inputs.shape
    head_count = lax.axis_size("head")
    blk_count = lax.axis_size("blk")
    local_heads = HEADS // head_count
    query_rows = head_count * tok_rows
    head_width = width // head_count
    width_split = blk_count // EXPERTS
    score_scale = HEAD_DIM ** (-0.5)
    period = tok_rows * blk_count // CONT_LEN + 1
    gathered = (
        lax.all_gather(first_gain, ("head", "blk"), axis=0, tiled=True),
        lax.all_gather(second_gain, ("head", "blk"), axis=0, tiled=True),
        lax.all_gather(query_key_weight, ("head", "blk"), axis=0, tiled=True),
        lax.all_gather(value_weight, ("head", "blk"), axis=0, tiled=True),
        lax.all_gather(output_weight, ("head", "blk"), axis=0, tiled=True),
        lax.all_gather(router_weight, ("head", "blk"), axis=0, tiled=True),
        lax.all_gather(const_gate, ("head", "blk"), axis=0, tiled=True),
        lax.all_gather(const_vectors, ("head", "blk"), axis=0, tiled=True),
        lax.all_gather(segment, ("head", "blk"), axis=0, tiled=True),
        lax.all_gather(position, ("head", "blk"), axis=0, tiled=True),
    )
    (
        gain_one,
        gain_two,
        full_joint,
        full_value,
        full_output,
        full_router,
        full_const,
        full_vectors,
        segment_all,
        position_all,
    ) = gathered
    gate_columns, up_columns, down_rows = (
        lax.all_gather(gate_weight, "head", axis=0, tiled=True),
        lax.all_gather(up_weight, "head", axis=0, tiled=True),
        lax.all_gather(down_weight, "head", axis=1, tiled=True),
    )
    gain_one = gain_one.astype(jnp.float32)
    gain_two = gain_two.astype(jnp.float32)
    source = inputs.astype(jnp.float32)
    inverse_one = lax.rsqrt(jnp.mean(source * source, axis=-1, keepdims=True) + EPS)
    normed_one = (source * inverse_one * gain_one).astype(jnp.bfloat16)
    joined = jnp.dot(normed_one, full_joint, preferred_element_type=jnp.float32)
    value_proj = jnp.dot(normed_one, full_value, preferred_element_type=jnp.float32)

    def head_layout(array):
        return array.astype(jnp.bfloat16).reshape(tok_rows, head_count, head_width)

    query_heads, key_heads, value_heads = (
        lax.all_to_all(
            head_layout(joined[:, :width]), "head", split_axis=1, concat_axis=0, tiled=True
        ),
        lax.all_to_all(
            head_layout(joined[:, width:]), "head", split_axis=1, concat_axis=0, tiled=True
        ),
        lax.all_to_all(head_layout(value_proj), "head", split_axis=1, concat_axis=0, tiled=True),
    )
    query_heads = query_heads.reshape(query_rows, local_heads, HEAD_DIM)
    key_heads = key_heads.reshape(query_rows, head_width)
    value_heads = value_heads.reshape(query_rows, head_width)
    blk_index = lax.axis_index("blk")
    segment_grid = segment_all.reshape(head_count, blk_count, tok_rows)
    position_grid = position_all.reshape(head_count, blk_count, tok_rows)
    query_segment = lax.dynamic_index_in_dim(segment_grid, blk_index, 1, keepdims=False).reshape(
        query_rows
    )
    query_position = lax.dynamic_index_in_dim(position_grid, blk_index, 1, keepdims=False).reshape(
        query_rows
    )
    key_segment = segment_grid.transpose(1, 0, 2).reshape(blk_count * query_rows)
    key_position = position_grid.transpose(1, 0, 2).reshape(blk_count * query_rows)

    def key_slices(pieces):
        piece_rows = pieces[0].shape[0]
        step_count = piece_rows // tok_rows
        return (
            pieces[0].reshape(step_count, tok_rows, local_heads, HEAD_DIM),
            pieces[1].reshape(step_count, tok_rows, local_heads, HEAD_DIM),
            key_segment.reshape(step_count, tok_rows),
            key_position.reshape(step_count, tok_rows),
        )

    def masked_scores(queries, block_keys, visible):
        scores = (
            jnp.einsum("qhd,khd->hqk", queries, block_keys, preferred_element_type=jnp.float32)
            * score_scale
        )
        return jnp.where(visible[None], scores, -jnp.inf)

    def attend_block(carried, block):
        block_keys, block_values, block_segment, block_position = block
        visible = visible_pairs(
            query_segment, query_position, block_segment, block_position, period
        )

        def attend_compute(state):
            top_score, running_total, weighted = state
            scores = masked_scores(query_heads, block_keys, visible)
            new_top = jnp.maximum(top_score, jnp.max(scores, axis=-1))
            anchor = jnp.where(new_top == -jnp.inf, 0.0, new_top)
            raised = jnp.exp(scores - anchor[..., None])
            factor = jnp.exp(top_score - anchor)
            running_total = running_total * factor + jnp.sum(raised, axis=-1)
            weighted = weighted * factor[..., None] + jnp.einsum(
                "hqk,khd->hqd",
                raised.astype(jnp.bfloat16),
                block_values,
                preferred_element_type=jnp.float32,
            )
            return (new_top, running_total, weighted)

        def unchanged(state):
            return state

        return (lax.cond(jnp.any(visible), attend_compute, unchanged, carried), None)

    def attend_piece(carried, pieces, first_row):
        result, unused = lax.scan(attend_block, carried, key_slices(pieces))
        return result

    start_state = (
        jnp.full((local_heads, query_rows), -jnp.inf, jnp.float32),
        jnp.zeros((local_heads, query_rows), jnp.float32),
        jnp.zeros((local_heads, query_rows, HEAD_DIM), jnp.float32),
    )
    top_score, running_total, weighted = around_blocks(
        (key_heads, value_heads), attend_piece, start_state
    )
    log_total = top_score + jnp.log(running_total)
    attended_local = (weighted / running_total[..., None]).transpose(1, 0, 2).astype(jnp.bfloat16)
    attended = lax.all_to_all(
        attended_local.reshape(query_rows, 1, head_width),
        "head",
        split_axis=0,
        concat_axis=1,
        tiled=True,
    ).reshape(tok_rows, width)
    middle = source + jnp.dot(attended, full_output, preferred_element_type=jnp.float32)
    inverse_two = lax.rsqrt(jnp.mean(middle * middle, axis=-1, keepdims=True) + EPS)
    normed_two = (middle * inverse_two * gain_two).astype(jnp.bfloat16)
    normed_float = normed_two.astype(jnp.float32)
    logits = jnp.dot(normed_two, full_router, preferred_element_type=jnp.float32) + gate_residual
    choose = (routes[:, :, None] == jnp.arange(ROUTED, dtype=jnp.int32)[None, None, :]).astype(
        jnp.float32
    )
    picked = jnp.sum(choose * logits[:, None, :], axis=-1)
    weighting = softmax_last(picked)
    pair_expert = routes.reshape(tok_rows * TOP)
    ffn_onehot = (pair_expert[:, None] == jnp.arange(EXPERTS, dtype=jnp.int32)[None, :]).astype(
        jnp.int32
    )
    pair_rank = jnp.sum((jnp.cumsum(ffn_onehot, axis=0) - ffn_onehot) * ffn_onehot, axis=-1)
    slot_match = (
        pair_rank[None, None, :] == jnp.arange(CAP, dtype=jnp.int32)[None, :, None]
    ).astype(jnp.int32)
    placement = (
        (ffn_onehot.T[:, None, :] * slot_match)
        .reshape(EXPERTS, CAP, tok_rows, TOP)
        .astype(jnp.float32)
    )
    select = jnp.sum(placement, axis=-1)
    gate_slot = jnp.einsum("ectj,tj->ect", placement, weighting, precision=HIGH)
    send_rows = jnp.einsum(
        "ect,td->ecd", select.astype(jnp.bfloat16), normed_two, preferred_element_type=jnp.float32
    ).astype(jnp.bfloat16)
    upstream = cotangent.astype(jnp.float32)
    slot_grad = jnp.einsum("ect,td->ecd", gate_slot, upstream, precision=HIGH).astype(jnp.bfloat16)
    rows_in = lax.all_to_all(
        jnp.repeat(send_rows, width_split, axis=0), "blk", split_axis=0, concat_axis=0, tiled=True
    )
    grads_in = lax.all_to_all(
        jnp.repeat(slot_grad, width_split, axis=0), "blk", split_axis=0, concat_axis=0, tiled=True
    )
    gate_pre = jnp.einsum("scd,df->scf", rows_in, gate_columns, preferred_element_type=jnp.float32)
    up_pre = jnp.einsum("scd,df->scf", rows_in, up_columns, preferred_element_type=jnp.float32)
    activated = jax.nn.silu(gate_pre)
    hidden = (activated * up_pre).astype(jnp.bfloat16)
    partial_out = jnp.einsum("scf,fd->scd", hidden, down_rows, preferred_element_type=jnp.float32)
    grad_hidden = jnp.einsum("scd,fd->scf", grads_in, down_rows, preferred_element_type=jnp.float32)
    grad_gate_pre = (grad_hidden * up_pre * silu_slope(gate_pre)).astype(jnp.bfloat16)
    grad_up_pre = (grad_hidden * activated).astype(jnp.bfloat16)
    grad_part = jnp.einsum(
        "scf,df->scd", grad_gate_pre, gate_columns, preferred_element_type=jnp.float32
    ) + jnp.einsum("scf,df->scd", grad_up_pre, up_columns, preferred_element_type=jnp.float32)
    back_out = lax.all_to_all(
        partial_out.astype(jnp.bfloat16), "blk", split_axis=0, concat_axis=0, tiled=True
    ).astype(partial_out.dtype)
    back_grad = lax.all_to_all(
        grad_part.astype(jnp.bfloat16), "blk", split_axis=0, concat_axis=0, tiled=True
    ).astype(grad_part.dtype)
    returned, grad_back, kept_rows, kept_grads, hidden, grad_gate_pre, grad_up_pre = (
        back_out,
        back_grad,
        rows_in,
        grads_in,
        hidden,
        grad_gate_pre,
        grad_up_pre,
    )
    expert_out = returned.reshape(EXPERTS, width_split, CAP, width).sum(axis=1)
    ffn_sum = jnp.einsum("ect,ecd->td", gate_slot, expert_out, precision=HIGH)
    mixing = softmax_last(
        jnp.dot(normed_two, full_const, preferred_element_type=jnp.float32).reshape(tok_rows, 2, 2)
    )
    vectors = full_vectors.astype(jnp.float32)
    copy_share = jnp.sum(weighting * (routes == EXPERTS + 1).astype(jnp.float32), axis=-1)
    const_share = jnp.stack(
        [
            jnp.sum(weighting * (routes == EXPERTS + 2 + const_index).astype(jnp.float32), axis=-1)
            for const_index in range(2)
        ],
        axis=1,
    )
    const_outs = [
        mixing[:, const_index, 0:1] * normed_float
        + mixing[:, const_index, 1:2] * vectors[:, const_index][None, :]
        for const_index in range(2)
    ]
    mixture = ffn_sum + copy_share[:, None] * normed_float
    for const_index in range(2):
        mixture = mixture + const_share[:, const_index : const_index + 1] * const_outs[const_index]
    layer_out = (middle + mixture).astype(jnp.bfloat16)
    output_dots = jnp.einsum("ecd,td->ect", expert_out, upstream, precision=HIGH)
    grad_weighting = jnp.einsum("ectj,ect->tj", placement, output_dots, precision=HIGH)
    copy_dot = jnp.sum(upstream * normed_float, axis=-1)
    grad_weighting = (
        grad_weighting + (routes == EXPERTS + 1).astype(jnp.float32) * copy_dot[:, None]
    )
    for const_index in range(2):
        const_dot = jnp.sum(upstream * const_outs[const_index], axis=-1)
        grad_weighting = (
            grad_weighting
            + (routes == EXPERTS + 2 + const_index).astype(jnp.float32) * const_dot[:, None]
        )
    grad_picked = weighting * (
        grad_weighting - jnp.sum(weighting * grad_weighting, axis=-1, keepdims=True)
    )
    grad_logits = jnp.einsum("tj,tjr->tr", grad_picked, choose, precision=HIGH)
    vector_dots = jnp.dot(upstream, vectors, precision=HIGH)
    grad_mixing = const_share[:, :, None] * jnp.stack(
        [jnp.broadcast_to(copy_dot[:, None], vector_dots.shape), vector_dots], axis=-1
    )
    grad_mix = (
        mixing * (grad_mixing - jnp.sum(mixing * grad_mixing, axis=-1, keepdims=True))
    ).reshape(tok_rows, 4)
    grad_const_weight = jnp.dot(normed_float.T, grad_mix, precision=HIGH)
    grad_vectors = jnp.einsum("ti,td->di", const_share * mixing[:, :, 1], upstream, precision=HIGH)
    grad_router_weight = jnp.dot(normed_float.T, grad_logits, precision=HIGH)
    direct_share = (
        copy_share + const_share[:, 0] * mixing[:, 0, 0] + const_share[:, 1] * mixing[:, 1, 0]
    )
    grad_normed_two = direct_share[:, None] * upstream
    grad_normed_two = grad_normed_two + jnp.dot(
        grad_mix, full_const.astype(jnp.float32).T, precision=HIGH
    )
    grad_normed_two = grad_normed_two + jnp.dot(
        grad_logits, full_router.astype(jnp.float32).T, precision=HIGH
    )
    grad_down_local = jnp.einsum(
        "scf,scd->fd", hidden, kept_grads, preferred_element_type=jnp.float32
    )
    grad_gate_local = jnp.einsum(
        "scd,scf->df", kept_rows, grad_gate_pre, preferred_element_type=jnp.float32
    )
    grad_up_local = jnp.einsum(
        "scd,scf->df", kept_rows, grad_up_pre, preferred_element_type=jnp.float32
    )
    grad_slots = grad_back.reshape(EXPERTS, width_split, CAP, width).sum(axis=1)
    grad_normed_two = grad_normed_two + jnp.einsum(
        "ect,ecd->td", select, grad_slots, precision=HIGH
    )
    grad_gate_sum, grad_up_sum, grad_down_sum = (
        lax.psum_scatter(
            grad_gate_local.astype(jnp.bfloat16), "head", scatter_dimension=0, tiled=True
        ).astype(jnp.float32),
        lax.psum_scatter(
            grad_up_local.astype(jnp.bfloat16), "head", scatter_dimension=0, tiled=True
        ).astype(jnp.float32),
        lax.psum_scatter(
            grad_down_local.astype(jnp.bfloat16), "head", scatter_dimension=1, tiled=True
        ).astype(jnp.float32),
    )
    grad_from_norm, grad_gain_two = norm_back(grad_normed_two, middle, inverse_two, gain_two)
    grad_middle = upstream + grad_from_norm
    branch_grad = grad_middle.astype(jnp.bfloat16)
    grad_out_weight = jnp.einsum(
        "tc,td->cd", attended, branch_grad, preferred_element_type=jnp.float32
    )
    grad_attended = jnp.einsum(
        "td,cd->tc", branch_grad, full_output, preferred_element_type=jnp.float32
    ).astype(jnp.bfloat16)
    grad_heads = lax.all_to_all(
        grad_attended.reshape(tok_rows, head_count, head_width),
        "head",
        split_axis=1,
        concat_axis=0,
        tiled=True,
    )
    grad_heads = grad_heads.reshape(query_rows, local_heads, HEAD_DIM)
    offset = jnp.sum(grad_heads.astype(jnp.float32) * attended_local.astype(jnp.float32), axis=-1).T

    def probe_block(queries, grads, lse_rows, offset_rows, block_keys, block_values, visible):
        scores = masked_scores(queries, block_keys, visible)
        probabilities = jnp.exp(scores - lse_rows[..., None])
        grad_probs = jnp.einsum(
            "qhd,khd->hqk", grads, block_values, preferred_element_type=jnp.float32
        )
        grad_scores = (probabilities * (grad_probs - offset_rows[..., None])).astype(jnp.bfloat16)
        return (probabilities, grad_scores)

    zero_query = jnp.zeros((query_rows, local_heads, HEAD_DIM), jnp.float32)

    def backward_block(grad_query, block):
        block_keys, block_values, block_segment, block_position = block
        visible = visible_pairs(
            query_segment, query_position, block_segment, block_position, period
        )

        def backward_compute(accumulated):
            probabilities, grad_scores = probe_block(
                query_heads, grad_heads, log_total, offset, block_keys, block_values, visible
            )
            grad_values = jnp.einsum(
                "hqk,qhd->khd",
                probabilities.astype(jnp.bfloat16),
                grad_heads,
                preferred_element_type=jnp.float32,
            )
            accumulated = (
                accumulated
                + jnp.einsum(
                    "hqk,khd->qhd", grad_scores, block_keys, preferred_element_type=jnp.float32
                )
                * score_scale
            )
            grad_keys = (
                jnp.einsum(
                    "hqk,qhd->khd", grad_scores, query_heads, preferred_element_type=jnp.float32
                )
                * score_scale
            )
            return (accumulated, jnp.concatenate([grad_keys, grad_values], axis=-1))

        def skipped(accumulated):
            return (
                accumulated,
                jnp.zeros((block_keys.shape[0], local_heads, 2 * HEAD_DIM), jnp.float32),
            )

        return lax.cond(jnp.any(visible), backward_compute, skipped, grad_query)

    def fold_back(carried, pieces, first_row):
        grad_query, stacked = lax.scan(backward_block, carried[0], key_slices(pieces))
        term_piece = stacked.reshape(pieces[0].shape[0], local_heads * 2 * HEAD_DIM)
        return (grad_query, term_piece)

    zero_term = jnp.zeros((blk_count * query_rows, local_heads * 2 * HEAD_DIM), jnp.float32)
    grad_query, key_term = around_blocks(
        (key_heads, value_heads), fold_back, (zero_query, zero_term)
    )
    key_sums = lax.psum_scatter(key_term, "blk", scatter_dimension=0, tiled=True).reshape(
        query_rows, local_heads, 2, HEAD_DIM
    )
    grad_key_heads = key_sums[:, :, 0].astype(jnp.bfloat16).reshape(query_rows, 1, head_width)
    grad_value_heads = key_sums[:, :, 1].astype(jnp.bfloat16).reshape(query_rows, 1, head_width)
    grad_query_heads = grad_query.astype(jnp.bfloat16).reshape(query_rows, 1, head_width)
    grad_query_tok, grad_key_tok, grad_value_tok = (
        lax.all_to_all(grad_query_heads, "head", split_axis=0, concat_axis=1, tiled=True),
        lax.all_to_all(grad_key_heads, "head", split_axis=0, concat_axis=1, tiled=True),
        lax.all_to_all(grad_value_heads, "head", split_axis=0, concat_axis=1, tiled=True),
    )
    grad_joined = jnp.concatenate(
        [grad_query_tok.reshape(tok_rows, width), grad_key_tok.reshape(tok_rows, width)], axis=1
    )
    grad_value_tok = grad_value_tok.reshape(tok_rows, width)
    grad_normed_one = jnp.einsum(
        "tc,dc->td", grad_joined, full_joint, preferred_element_type=jnp.float32
    ) + jnp.einsum("tc,dc->td", grad_value_tok, full_value, preferred_element_type=jnp.float32)
    grad_joint_weight = jnp.einsum(
        "td,tc->dc", normed_one, grad_joined, preferred_element_type=jnp.float32
    )
    grad_value_weight = jnp.einsum(
        "td,tc->dc", normed_one, grad_value_tok, preferred_element_type=jnp.float32
    )
    grad_from_first, grad_gain_one = norm_back(grad_normed_one, source, inverse_one, gain_one)
    grad_input = grad_middle + grad_from_first
    summed = (
        lax.psum_scatter(grad_gain_one, ("head", "blk"), scatter_dimension=0, tiled=True),
        lax.psum_scatter(grad_gain_two, ("head", "blk"), scatter_dimension=0, tiled=True),
        lax.psum_scatter(grad_joint_weight, ("head", "blk"), scatter_dimension=0, tiled=True),
        lax.psum_scatter(grad_value_weight, ("head", "blk"), scatter_dimension=0, tiled=True),
        lax.psum_scatter(grad_out_weight, ("head", "blk"), scatter_dimension=0, tiled=True),
        lax.psum_scatter(grad_router_weight, ("head", "blk"), scatter_dimension=0, tiled=True),
        lax.psum_scatter(grad_const_weight, ("head", "blk"), scatter_dimension=0, tiled=True),
        lax.psum_scatter(grad_vectors, ("head", "blk"), scatter_dimension=0, tiled=True),
    )
    return (
        layer_out,
        grad_input,
        grad_logits,
        summed[0],
        summed[1],
        summed[2],
        summed[3],
        summed[4],
        summed[5],
        summed[6],
        summed[7],
        grad_gate_sum,
        grad_up_sum,
        grad_down_sum,
    )


MESH = pl.DeviceIdType.MESH
SMALL = 24
ROUTER_AT, MIX_AT, VECTOR_AT, GAIN_ONE_AT, GAIN_TWO_AT = 0, 12, 16, 18, 19
PAD = 32
CHUNK = 4
FAR = 1 << 20
NT = (((1,), (1,)), ((), ()))
TN = (((0,), (0,)), ((), ()))


def mul(left, right):
    return jnp.dot(left, right, preferred_element_type=jnp.float32)


def mul_nt(left, right):
    return lax.dot_general(left, right, NT, preferred_element_type=jnp.float32)


def mul_tn(left, right):
    return lax.dot_general(left, right, TN, preferred_element_type=jnp.float32)


def low(values):
    return values.astype(jnp.bfloat16)


def wide(values):
    return values.astype(jnp.float32)


def halves(values):
    high = low(values)
    return high, low(values - wide(high))


def shape(dims, dtype=jnp.bfloat16):
    return jax.ShapeDtypeStruct(dims, dtype)


def compute(body, outs, ins, scratch=(), smem=0):
    specs = [pl.BlockSpec(memory_space=pltpu.SMEM)] * smem
    specs += [pl.BlockSpec(memory_space=pltpu.VMEM)] * (len(ins) - smem)
    return pl.pallas_call(
        body,
        out_shape=outs,
        in_specs=specs,
        out_specs=[pl.BlockSpec(memory_space=pltpu.VMEM)] * len(outs),
        scratch_shapes=list(scratch),
        compiler_params=pltpu.CompilerParams(vmem_limit_bytes=52 * 2**20),
    )(*ins)


def exchange(body, sizes, ins, outs, scratch, number, far=(), room=52):
    names = list(ins) + list(outs) + list(scratch)

    def run(*refs):
        body(Place(*sizes), types.SimpleNamespace(**dict(zip(names, refs))))

    def spec(name):
        return pl.BlockSpec(memory_space=pl.ANY if name in far else pltpu.VMEM)

    results = pl.pallas_call(
        run,
        out_shape=list(outs.values()),
        in_specs=[spec(name) for name in ins],
        out_specs=[spec(name) for name in outs],
        scratch_shapes=list(scratch.values()),
        compiler_params=pltpu.CompilerParams(
            collective_id=number, has_side_effects=True, vmem_limit_bytes=room * 2**20
        ),
    )(*ins.values())
    return types.SimpleNamespace(**dict(zip(outs, results)))


def vmem(*dims, dtype=jnp.bfloat16):
    return pltpu.VMEM(dims, dtype)


def vmem_wide(*dims):
    return pltpu.VMEM(dims, jnp.float32)


def greet(devices):
    barrier = pltpu.get_barrier_semaphore()
    for device in devices:
        pl.semaphore_signal(barrier, inc=1, device_id=device, device_id_type=MESH)


def greeted(count):
    pl.semaphore_wait(pltpu.get_barrier_semaphore(), count)


def meet(devices):
    greet(devices)
    greeted(len(devices))


class Place:
    def __init__(self, head_count, blk_count):
        self.head_count, self.blk_count = head_count, blk_count
        self.head, self.blk = lax.axis_index("head"), lax.axis_index("blk")
        self.half = blk_count // 2
        self.chip, self.core = self.blk // 2, self.blk % 2
        self.twin = self.blk + 1 - 2 * self.core

    def along(self, axis):
        if axis == "head":
            return self.head, self.head_count
        return self.blk, self.blk_count

    def device(self, axis, index):
        return (index, self.blk) if axis == "head" else (self.head, index)

    def others(self, axis):
        me, size = self.along(axis)
        return [self.device(axis, (me + step) % size) for step in range(1, size)]

    def partners(self):
        beside = self.chip + 1 - 2 * (self.chip % 2)
        beyond = (self.chip + self.half // 2) % self.half
        across = beside + self.half // 2 - self.half * (beside // (self.half // 2))
        return [across, beside, beyond]

    def chips(self):
        return [chip * 2 + self.core for chip in self.partners()]

    def exchange_order(self, axis):
        me, size = self.along(axis)
        if axis == "head":
            return [(step - 1, (me + step) % size, (me + size - step) % size) for step in range(1, size)]
        found = []
        for chip in self.partners():
            for core in (self.core, 1 - self.core):
                found.append(chip * 2 + core)
        found.append(self.twin)
        return [(number, blk, blk) for number, blk in enumerate(found)]

    def near(self):
        return [(self.head, self.twin)] + [(self.head, blk) for blk in self.chips()]


def dma(*dims):
    return pltpu.SemaphoreType.DMA(dims)


def remote(source, target, sent, got, device):
    return pltpu.make_async_remote_copy(
        src_ref=source,
        dst_ref=target,
        send_sem=sent,
        recv_sem=got,
        device_id=device,
        device_id_type=MESH,
    )


def send(source, target, sent, got, device):
    copy = remote(source, target, sent, got, device)
    copy.start()
    return copy


def keep(source, target, done):
    copy = pltpu.make_async_copy(source, target, done)
    copy.start()
    return copy


def scatter(place, axis, source, target, sent, got, wanted=lambda number: True):
    me, size = place.along(axis)
    copies = []
    for number, other, unused in place.exchange_order(axis):
        if not wanted(number):
            continue
        copies.append(
            send(
                source.at[other],
                target.at[me],
                sent.at[number],
                got.at[number],
                place.device(axis, other),
            )
        )
    return copies


def gather(place, axis, source, target, sent, got):
    me, size = place.along(axis)
    copies = []
    for step in range(1, size):
        other = (me + step) % size
        copies.append(
            send(
                source, target.at[me], sent.at[step - 1], got.at[step - 1], place.device(axis, other)
            )
        )
    return copies


class Spread:
    def __init__(self, place, ref, sent, got):
        self.place, self.ref, self.sent, self.got = place, ref, sent, got
        self.direct = [
            self.pass_on(step, place.blk, blk) for step, blk in enumerate(place.chips(), 1)
        ]
        self.rest = [self.pass_on(0, place.blk, place.twin)]

    def pass_on(self, lane, slot, blk):
        return send(
            self.ref.at[slot],
            self.ref.at[slot],
            self.sent.at[lane],
            self.got.at[lane],
            (self.place.head, blk),
        )

    def relay(self):
        place = self.place
        for step, slot in enumerate(place.chips(), 1):
            self.direct[step - 1].wait_recv()
            self.rest.append(self.pass_on(place.half - 1 + step, slot, place.twin))

    def wait(self):
        for copy in self.direct:
            copy.wait_send()
        for copy in self.rest:
            copy.wait()


class Fold:
    def __init__(self, place, terms, theirs, arrived, sent_twin, got_twin, sent, got):
        self.place, self.terms, self.theirs, self.arrived = place, terms, theirs, arrived
        self.sent, self.got = sent, got
        self.order = place.partners() + [place.chip]
        self.across = [
            send(
                terms.at[chip * 2 + 1 - place.core],
                theirs.at[step],
                sent_twin.at[step],
                got_twin.at[step],
                (place.head, place.twin),
            )
            for step, chip in enumerate(self.order)
        ]
        self.onward = []

    def add(self):
        place = self.place
        for step, chip in enumerate(self.order):
            self.across[step].wait_recv()
            total = wide(self.theirs[step]) + wide(self.terms[chip * 2 + place.core])
            self.theirs[step] = total.astype(self.theirs.dtype)
            if step < place.half - 1:
                self.onward.append(
                    send(
                        self.theirs.at[step],
                        self.arrived.at[step],
                        self.sent.at[step],
                        self.got.at[step],
                        (place.head, chip * 2 + place.core),
                    )
                )

    def total(self):
        total = wide(self.theirs[self.place.half - 1])
        for step, copy in enumerate(self.onward):
            copy.wait_recv()
            total = total + wide(self.arrived[step])
        return total

    def wait(self):
        for copy in self.across + self.onward:
            copy.wait_send()


def wait_all(*groups):
    for group in groups:
        for copy in group:
            copy.wait()


def far_block(number, head_count):
    head = lax.axis_index("head")
    found = 0
    for place in range(head_count):
        by_distance = sorted(range(head_count), key=lambda other: -abs(other - place))
        found = found + jnp.where(head == place, by_distance[number], 0)
    return found


def block_at(step, head_count):
    return (lax.axis_index("head") + step) % head_count


class LineGather:
    def __init__(self, place, ref, sent, got):
        self.place, self.ref, self.sent, self.got = place, ref, sent, got
        self.onward(0, place.head)
        self.back(0, place.head)

    def copy(self, way, hop, slot):
        head = self.place.head + 1 - 2 * way
        return remote(
            self.ref.at[slot],
            self.ref.at[slot],
            self.sent.at[way, hop],
            self.got.at[way, hop],
            (head, self.place.blk),
        )

    def sends(self, way, hop):
        head, last = self.place.head, self.place.head_count - 1
        if way == 0:
            return (head >= hop) & (head < last)
        return (head + hop <= last) & (head > 0)

    def has(self, way, hop):
        head, last = self.place.head, self.place.head_count - 1
        return head >= hop if way == 0 else head + hop <= last

    def onward(self, hop, slot):
        @pl.when(self.sends(0, hop))
        def _():
            self.copy(0, hop, slot).start()

    def back(self, hop, slot):
        @pl.when(self.sends(1, hop))
        def _():
            self.copy(1, hop, slot).start()

    def receive(self, hop):
        head, last = self.place.head, self.place.head_count - 1
        for way, slot in ((0, head - hop), (1, head + hop)):

            @pl.when(self.has(way, hop))
            def _():
                self.copy(way, hop - 1, slot).wait_recv()

            if hop < last:
                (self.onward, self.back)[way](hop, slot)

    def receive_all(self):
        for hop in range(1, self.place.head_count):
            self.receive(hop)

    def wait(self):
        for hop in range(self.place.head_count - 1):
            for way in range(2):

                @pl.when(self.sends(way, hop))
                def _():
                    self.copy(way, hop, self.place.head).wait_send()


class LineSum:
    def __init__(self, place, outbox, inbox, sent, got):
        self.place, self.outbox, self.inbox = place, outbox, inbox
        self.sent, self.got = sent, got

    def copy(self, way, slot):
        head = self.place.head + 1 - 2 * way
        return remote(
            self.outbox.at[slot],
            self.inbox.at[way, slot],
            self.sent.at[slot],
            self.got.at[way, slot],
            (head, self.place.blk),
        )

    def add(self, slot, term):
        head, last = self.place.head, self.place.head_count - 1
        self.outbox[slot] = low(term)
        for way, towards, first in ((0, slot > head, head == 0), (1, slot < head, head == last)):

            @pl.when(towards & jnp.logical_not(first))
            def _():
                self.copy(way, slot).wait_recv()
                self.outbox[slot] = low(wide(self.outbox[slot]) + wide(self.inbox[way, slot]))

            @pl.when(towards)
            def _():
                self.copy(way, slot).start()

    def total(self, term):
        head, last = self.place.head, self.place.head_count - 1
        for way, has in ((0, head > 0), (1, head < last)):

            @pl.when(has)
            def _():
                self.copy(way, head).wait_recv()

        for way, has in ((0, head > 0), (1, head < last)):
            term = term + jnp.where(has, wide(self.inbox[way, head]), 0.0)
        return term

    def wait(self):
        for slot in range(self.place.head_count):

            @pl.when(slot > self.place.head)
            def _():
                self.copy(0, slot).wait_send()

            @pl.when(slot < self.place.head)
            def _():
                self.copy(1, slot).wait_send()


def rows_at(block, tokens):
    return pl.ds(pl.multiple_of(block * tokens, tokens), tokens)


def lanes_joined(*parts):
    return jnp.concatenate(parts, axis=1)


def rows_joined(*parts):
    return jnp.concatenate(parts, axis=0)


def packed_rows(piece):
    half = piece.shape[1] // 2
    return lanes_joined(piece[:16], rows_joined(piece[16:, :half], piece[16:, half:]))


def unpacked_rows(packed):
    width = packed.shape[1] * 2 // 3
    rest = packed[:, width:]
    return rows_joined(packed[:, :width], lanes_joined(rest[:8], rest[8:]))


def own_pieces(product, rows, head_count, blk_count, blk):
    return rows_joined(
        *[
            product[(head * blk_count + blk) * rows : (head * blk_count + blk + 1) * rows]
            for head in range(head_count)
        ]
    )


def open_layer(place, r):
    head_count, blk_count = place.head_count, place.blk_count
    head, blk = place.head, place.blk
    tokens, width = r.x.shape
    rows = r.joint_rows.shape[0]
    columns = r.down_0.shape[1]
    head_width = width // head_count
    split = 2 * HEAD_DIM
    joint_width = r.joint.shape[1]
    greet(place.others("head") + place.near())
    names = ["router", "mix", "vectors", "gain_one", "gain_two", "joint_rows", "value_rows"]
    names += ["segment", "position", "routes", "residual", "output_rows", "x"]
    here = {
        name: keep(getattr(r, name), getattr(r, "my_" + name), r.local.at[number])
        for number, name in enumerate(names)
    }
    number = len(names)
    late_own = [keep(r.g, r.g_all.at[head], r.local.at[number])]
    for step, piece in enumerate((r.down_0, r.down_1, r.down_2, r.down_3)):
        at = rows_at(block_at(step, head_count), columns)
        late_own.append(keep(r.down.at[:, at], piece, r.local.at[number + 1 + step]))
    for name in names[:7]:
        here[name].wait()
    marks = rows_joined(
        *[
            wide(ref[...])
            for ref in (r.my_router, r.my_mix, r.my_vectors, r.my_gain_one, r.my_gain_two)
        ]
    )
    marks = rows_joined(marks, jnp.zeros((128 - marks.shape[0], rows), jnp.float32))
    marks = lanes_joined(marks, jnp.zeros((128, 128 - rows), jnp.float32))
    marks = marks.T[:rows]
    both = wide(r.my_joint_rows[...])
    third = wide(r.my_value_rows[...])
    filler = jnp.zeros((rows, HEAD_DIM), jnp.float32)
    for part in range(head_count):
        at = part * head_width
        piece = lanes_joined(
            both[:, at : at + head_width],
            filler,
            both[:, width + at : width + at + head_width],
            third[:, at + split : at + head_width],
            third[:, at : at + split],
            marks,
        )
        r.joint_own[part] = low(packed_rows(piece))
    r.joint_all[blk, head] = r.joint_own[head]
    for name in names[7:]:
        here[name].wait()
    facts = rows_joined(
        wide(r.my_segment[...]),
        wide(r.my_position[...]),
        wide(r.my_routes[...]),
        jnp.zeros((4, tokens), jnp.float32),
        r.my_residual[...],
        jnp.zeros((24 - 8 - ROUTED, tokens), jnp.float32),
    )
    r.facts_own[...] = facts
    r.facts[head] = facts
    r.marks_all[blk, head] = facts[:8]
    greeted(head_count - 1 + place.half)
    first = scatter(place, "head", r.joint_own, r.joint_all.at[blk], r.sent.at[0], r.got.at[0])
    first += gather(place, "head", r.facts_own, r.facts, r.sent.at[1], r.got.at[1])
    r.output_own[...] = low(packed_rows(wide(r.my_output_rows[...])))
    r.output_part[head] = r.output_own[...]
    r.x_all[head] = r.my_x[...]
    for copy in first:
        copy.wait_send()
    tokens_in = LineGather(place, r.x_all, r.sent_line.at[0], r.got_line.at[0])
    for copy in first:
        copy.wait_recv()
    for part in range(head_count):
        r.marks_all[blk, part] = r.facts[part, 0:8, :]
    joint_spread = Spread(place, r.joint_all, r.sent_joint, r.got_joint)
    marks_spread = Spread(place, r.marks_all, r.sent_marks, r.got_marks)
    tokens_in.receive(1)
    joint_spread.relay()
    marks_spread.relay()
    tokens_in.receive(2)
    joint_spread.wait()
    marks_spread.wait()
    column = lax.broadcasted_iota(jnp.int32, (8, 128), 1)
    places = jnp.zeros((8, 128), jnp.float32)
    for part in range(head_count):
        for other in range(blk_count):
            places = jnp.where(
                column == other * head_count + part, r.marks_all[other, part, :, 0:1], places
            )
    r.places[...] = places.astype(jnp.int32)
    for part in range(head_count):
        for other in range(blk_count):
            r.joint_wide[pl.ds((part * blk_count + other) * rows, rows), :] = unpacked_rows(
                wide(r.joint_all[other, part])
            )
    r.joint[...] = low(r.joint_wide[:, :joint_width])
    small_rows = r.joint_wide[:, joint_width:].T
    r.small[...] = small_rows[:SMALL]
    gain = small_rows[GAIN_ONE_AT : GAIN_ONE_AT + 1]
    for hop in range(3, head_count):
        tokens_in.receive(hop)
    outputs_in = LineGather(place, r.output_part, r.sent_line.at[1], r.got_line.at[1])
    late_own[0].wait()
    upstream_in = LineGather(place, r.g_all, r.sent_line.at[2], r.got_line.at[2])
    pair_spreads = []
    cut = r.queries.shape[1]
    for step in range(head_count):
        block = block_at(step, head_count)
        source = wide(r.x_all[block])
        inverse = lax.rsqrt(jnp.mean(source * source, axis=-1, keepdims=True) + EPS)
        rows_normed = low(source * inverse * gain)
        span = rows_at(block, tokens)
        r.normed[span, :] = rows_normed
        product = mul(rows_normed, r.joint[...])
        r.queries[span, :] = low(product[:, :cut])
        r.pairs_all[blk, block] = low(product[:, cut:])
        pair_spreads.append(
            Spread(place, r.pairs_all.at[:, block], r.sent_pairs.at[step], r.got_pairs.at[step])
        )
    for step, spread in enumerate(pair_spreads):
        if 0 < step + 1 < head_count:
            outputs_in.receive(step + 1)
            upstream_in.receive(step + 1)
        spread.relay()
    for spread in pair_spreads:
        spread.wait()
    for line in (tokens_in, outputs_in, upstream_in):
        line.wait()
    wait_all(late_own[1:])


def slots_of(head_count, facts, first, second):
    tokens = first.shape[2]
    earlier = low(
        wide(
            lax.broadcasted_iota(jnp.int32, (tokens, tokens), 0)
            < lax.broadcasted_iota(jnp.int32, (tokens, tokens), 1)
        )
    )
    expert = wide(lax.broadcasted_iota(jnp.int32, (2 * EXPERTS, tokens), 0))
    expert_at = wide(lax.broadcasted_iota(jnp.int32, (EXPERTS, CAP, tokens), 0))
    rank_at = wide(lax.broadcasted_iota(jnp.int32, (EXPERTS, CAP, tokens), 1))
    for head in range(head_count):
        routes = [facts[head, 2 + choice : 3 + choice, :] for choice in range(TOP)]
        named = jnp.where((routes[0] == expert) | (routes[1] == expert), 1.0, 0.0)
        count = mul(low(named), earlier)[:EXPERTS]
        fits = count[:, None, :] == rank_at
        for choice, out in enumerate((first, second)):
            match = (routes[choice][None] == expert_at) & fits
            out[head] = low(jnp.where(match, 1.0, 0.0).reshape(EXPERTS * CAP, tokens))


def place_upstream(place, r):
    head_count = place.head_count
    slots_of(head_count, r.facts, r.first, r.second)
    parts = []
    for number in range(head_count):
        block = far_block(number, head_count)
        found = mul(r.first[block] + r.second[block], r.g_all[block])
        parts.append(found.reshape(EXPERTS, CAP, found.shape[1]))
    r.upstream[...] = low(jnp.concatenate(parts, axis=1))


def visible_blocks(places, period, me, count, chosen, shift, base=0):
    mine, mine_at = places[0, me], places[1, me]

    def look(block, found):
        other, other_at = places[0, block], places[1, block]
        same = other == mine
        shared = (other // period == mine // period) & (other % period == 0) & (mine % period != 0)
        seen = (same & (other_at <= mine_at)) | shared
        chosen[found] = block
        shift[found] = jnp.where(same & (other_at == mine_at), 0, -FAR)
        return found + seen.astype(jnp.int32)

    found = lax.fori_loop(0, count, look, base + jnp.int32(0)) - base
    for extra in range(CHUNK):
        chosen[base + found + extra] = jnp.int32(0)
        shift[base + found + extra] = jnp.int32(FAR)
    return (found + CHUNK - 1) // CHUNK


def chunk_mask(tokens, heads, shift, start):
    row = lax.broadcasted_iota(jnp.int32, (tokens, tokens), 0)
    column = lax.broadcasted_iota(jnp.int32, (tokens, tokens), 1)
    gap = row - column
    parts = [
        jnp.where(gap + shift[start + step] <= 0, 0.0, -jnp.inf) for step in range(CHUNK)
    ]
    return jnp.concatenate([jnp.concatenate(parts, axis=0)] * heads, axis=1)


def chunk_rows(pairs, chosen, start, low_lane, high_lane):
    return jnp.concatenate(
        [pairs[chosen[start + step], :, low_lane:high_lane] for step in range(CHUNK)], axis=0
    )


def lanes_at(rows, first, last):
    lane = lax.broadcasted_iota(jnp.int32, rows.shape, 1)
    return jnp.where((lane >= first) & (lane < last), rows, jnp.zeros_like(rows))


def query_rows_of(queries, head, tokens):
    rows = queries[pl.ds(head * tokens, tokens), :]
    rows = low(wide(rows) * HEAD_DIM ** (-0.5))
    return jnp.concatenate(
        [lanes_at(rows, part * HEAD_DIM, (part + 1) * HEAD_DIM) for part in range(3)], axis=0
    )


def attend(sizes, period, places, queries, pairs, attended, totals, chosen, shift):
    head_count, blk_count = sizes
    blocks, tokens, lanes = pairs.shape
    heads = 3
    blk = lax.axis_index("blk")
    for head in range(head_count):
        chunks = visible_blocks(
            places, period, blk * head_count + head, blocks, chosen, shift
        )
        asked = query_rows_of(queries, head, tokens)

        def step(number, carried):
            top, total, weighted = carried
            start = number * CHUNK
            scores = mul_nt(chunk_rows(pairs, chosen, start, 0, 256), asked)
            scores = scores + chunk_mask(tokens, heads, shift, start)
            new_top = jnp.maximum(top, jnp.max(scores, axis=0, keepdims=True))
            raised = jnp.exp(scores - new_top)
            factor = jnp.exp(top - new_top)
            total = total * factor + jnp.sum(raised, axis=0, keepdims=True)
            mixed = mul_tn(chunk_rows(pairs, chosen, start, 128, lanes), low(raised))
            mixed = jnp.concatenate(
                [mixed[128:192, 0:128], mixed[192:256, 128:256], mixed[64:128, 256:384]], axis=1
            )
            return (new_top, total, weighted * factor + mixed)

        wide_lanes = heads * tokens
        top, total, weighted = lax.fori_loop(
            0,
            chunks,
            step,
            (
                jnp.full((1, wide_lanes), -1e30, jnp.float32),
                jnp.zeros((1, wide_lanes), jnp.float32),
                jnp.zeros((HEAD_DIM, wide_lanes), jnp.float32),
            ),
        )
        outcome = low(weighted / total)
        totals[head] = jnp.broadcast_to(top + jnp.log(total), totals.shape[1:])
        for part in range(heads):
            attended[head, part * HEAD_DIM : (part + 1) * HEAD_DIM, :] = outcome[
                :, part * tokens : (part + 1) * tokens
            ]


def attend_back(sizes, period, places, queries, pairs, attended, totals, given, query_grad, pair_grad, chosen, shift, owner, asked, back, offset, found, summed):
    head_count, blk_count = sizes
    blocks, tokens, lanes = pairs.shape
    heads = 3
    blk = lax.axis_index("blk")
    items = jnp.int32(0)
    for head in range(head_count):
        chunks = visible_blocks(
            places, period, blk * head_count + head, blocks, chosen, shift, items * CHUNK
        )

        def note(number, unused):
            owner[number] = jnp.int32(head)
            return unused

        lax.fori_loop(items, items + chunks, note, 0)
        items = items + chunks
        asked[head] = query_rows_of(queries, head, tokens)
        turned = wide(given[head])
        own = rows_joined(jnp.zeros((HEAD_DIM, tokens), jnp.float32), turned[128:192], turned[0:128])
        own = low(own.T)
        back[head] = rows_joined(
            lanes_at(own, 128, 192), lanes_at(own, 192, 256), lanes_at(own, 64, 128)
        )
        dots = turned * wide(attended[head])
        sums = lanes_joined(
            *[
                jnp.sum(dots[part * HEAD_DIM : (part + 1) * HEAD_DIM], axis=0, keepdims=True)
                for part in range(heads)
            ]
        )
        offset[head] = jnp.broadcast_to(sums, offset.shape[1:])
    owner[items] = jnp.int32(0)
    for extra in range(CHUNK):
        chosen[items * CHUNK + extra] = jnp.int32(0)
        shift[items * CHUNK + extra] = jnp.int32(FAR)
    summed[...] = jnp.zeros_like(summed)
    found[...] = jnp.zeros_like(found)

    def one(item):
        start = item * CHUNK
        head = owner[item]
        keys = chunk_rows(pairs, chosen, start, 0, 256)
        values = chunk_rows(pairs, chosen, start, 128, lanes)
        mine, given_back = asked[head], back[head]
        scores = mul_nt(keys, mine)
        scores = scores + chunk_mask(tokens, heads, shift, start)
        raised = jnp.exp(scores - totals[head, 0:1, :])
        grad_raised = mul_nt(values, given_back)
        grad_scores = low(raised * (grad_raised - offset[head, 0:1, :]))
        key_part = mul(grad_scores, mine)
        value_part = mul(low(raised), given_back)
        both = lanes_joined(
            key_part[:, :128], key_part[:, 128:] + value_part[:, :128], value_part[:, 128:]
        )
        query_part = mul_tn(keys, grad_scores)
        return (
            start,
            head,
            both,
            lanes_joined(
                query_part[0:64, 0:128], query_part[64:128, 128:256], query_part[128:192, 256:384]
            ),
        )

    def step(number, unused):
        results = [one(number * 2 + part) for part in range(2)]
        for start, head, both, query_part in results:
            found[head] = found[head] + query_part
            for block in range(CHUNK):
                at = chosen[start + block]
                summed[at] = summed[at] + both[block * tokens : (block + 1) * tokens]
        return unused

    lax.fori_loop(0, (items + 1) // 2, step, 0)
    for head in range(head_count):
        total = found[head] * HEAD_DIM ** (-0.5)
        stacked = rows_joined(
            *[total[:, part * tokens : (part + 1) * tokens] for part in range(heads)],
            jnp.zeros((HEAD_DIM, tokens), jnp.float32),
        )
        query_grad[pl.ds(head * tokens, tokens), :] = low(stacked.T)
    pair_grad[...] = low(summed[...])


def ffn_rows(number, span, here, r, gate, up, down, lane):
    width = r.grads_in.shape[2]
    group = lane.shape[0]
    blk_count, span_rows = r.slots_in.shape[0], group // r.slots_in.shape[0]
    entry = r.slots_in[:, span, :].reshape(group, width + 128)
    rows = entry[:, :width]
    r.taken[here, :] = rows
    tail = wide(entry[:, width:])
    share = tail[:, 0:1] + tail[:, 64:65]
    scaled_rows = low(share * wide(r.grads_in[:, span, :].reshape(group, width)))
    r.scaled[here, :] = scaled_rows
    gate_pre = mul(rows, gate)
    up_pre = mul(rows, up)
    sigmoid = 1.0 / (1.0 + jnp.exp(-gate_pre))
    activated = gate_pre * sigmoid
    hidden_rows = low(activated * up_pre)
    r.hidden[here, :] = hidden_rows
    grad_hidden = mul(scaled_rows, down)
    gate_rows = low(grad_hidden * up_pre * sigmoid * (1.0 + gate_pre * (1.0 - sigmoid)))
    up_rows = low(grad_hidden * activated)
    r.grad_gate[here, :] = gate_rows
    r.grad_up[here, :] = up_rows
    dots = jnp.sum(wide(hidden_rows) * grad_hidden, axis=1, keepdims=True)
    grad_rows = mul_nt(gate_rows, gate) + mul_nt(up_rows, up)
    high, rest = halves(dots)
    tail_out = jnp.where(lane < 64, wide(high), wide(rest))
    r.back[:, span, :] = low(lanes_joined(grad_rows, tail_out)).reshape(
        blk_count, span_rows, width + 128
    )


def middle_layer(place, r):
    head_count, blk_count = place.head_count, place.blk_count
    head, blk = place.head, place.blk
    tokens, width = r.g.shape
    columns = r.gate_all.shape[2]
    head_width = r.gate_all.shape[1]
    rows = head_width // blk_count
    half_count = head_count // 2
    greet(place.others("head") + place.others("blk"))
    r.attended_all[head] = r.attended[...]
    for part in range(head_count):
        r.output_all[blk, part] = r.output_part[part]
    own_weights = [
        keep(ref.at[:, rows_at(head, columns)], held.at[head], r.local.at[number])
        for number, (ref, held) in enumerate(((r.gate, r.gate_all), (r.up, r.up_all)))
    ]
    for step, piece in enumerate((r.down_0, r.down_1, r.down_2, r.down_3)):
        r.down_all[(head + head_count - step) % head_count] = piece[...]
    greeted(head_count + blk_count - 2)
    rows_in = LineGather(place, r.attended_all, r.sent_line, r.got_line)
    output_spread = Spread(place, r.output_all, r.sent_output, r.got_output)
    place_upstream(place, r)
    r.grads_in[blk] = r.upstream[blk]
    routed = scatter(place, "blk", r.upstream, r.grads_in, r.sent_grads, r.got_grads)
    rows_in.receive(1)
    output_spread.relay()
    rows_in.receive(2)
    output_spread.wait()
    for part in range(head_count):
        for other in range(blk_count):
            r.output_wide[pl.ds((part * blk_count + other) * rows, rows), :] = unpacked_rows(
                wide(r.output_all[other, part])
            )
    r.output[...] = low(r.output_wide[...])
    router = low(r.small[0:16])
    expert = wide(lax.broadcasted_iota(jnp.int32, (16, tokens), 0))
    lane = lax.broadcasted_iota(jnp.int32, (EXPERTS * CAP, 128), 1)
    gain = r.small[GAIN_TWO_AT : GAIN_TWO_AT + 1]
    for hop in range(3, head_count):
        rows_in.receive(hop)
    weights_in = []
    for kind, (ref, held) in enumerate(((r.gate, r.gate_all), (r.up, r.up_all))):
        copies = []
        for away in range(1, head_count):
            other = (head + away) % head_count
            copies.append(
                send(
                    ref.at[:, rows_at(other, columns)],
                    held.at[head],
                    r.sent_weights.at[kind, away - 1],
                    r.got_weights.at[kind, away - 1],
                    (other, blk),
                )
            )
        weights_in.append(copies)
    parts = []
    for number in range(head_count):
        block = far_block(number, head_count)
        found = jnp.concatenate(
            [r.attended_all[source, block] for source in range(head_count)], axis=0
        ).T
        source = wide(r.x_all[block]) + mul(found, r.output[...])
        inverse = lax.rsqrt(jnp.mean(source * source, axis=-1, keepdims=True) + EPS)
        normed = low(source * inverse * gain)
        if number == head_count - 1:
            r.middle[...] = source
            r.normed[...] = normed
            r.attended_home[...] = low(wide(found).T)
        facts = r.facts[block]
        logits = mul_nt(router, normed) + facts[8:24]
        picked = [
            jnp.sum(
                jnp.where(facts[2 + choice : 3 + choice] == expert, logits, 0.0),
                axis=0,
                keepdims=True,
            )
            for choice in range(TOP)
        ]
        highest = jnp.maximum(picked[0], picked[1])
        raised = [jnp.exp(value - highest) for value in picked]
        total = raised[0] + raised[1]
        share = [value / total for value in raised]
        r.weights[block] = jnp.concatenate(
            share + [jnp.zeros((6, tokens), jnp.float32)], axis=0
        )
        places = [r.first[block], r.second[block]]
        of_slot = jnp.sum(
            wide(places[0]) * share[0] + wide(places[1]) * share[1], axis=1, keepdims=True
        )
        high, rest = halves(of_slot)
        entry = lanes_joined(
            mul(places[0] + places[1], normed), jnp.where(lane < 64, wide(high), wide(rest))
        )
        parts.append(entry.reshape(EXPERTS, CAP, width + 128))
        if number % 2:
            span = pl.ds((number - 1) * CAP, 2 * CAP)
            r.slots[:, span, :] = low(jnp.concatenate(parts, axis=1))
            parts = []
            r.slots_in[blk, span, :] = r.slots[blk, span, :]
            routed += scatter(
                place,
                "blk",
                r.slots.at[:, span],
                r.slots_in.at[:, span],
                r.sent_slots.at[number // 2],
                r.got_slots.at[number // 2],
            )
    rows_in.wait()
    wait_all(routed)
    wait_all(own_weights, *weights_in)

    depth = head_count * head_width
    gate, up, down = [
        ref[...].reshape(depth, columns) for ref in (r.gate_all, r.up_all, r.down_all)
    ]
    span_rows = 2 * CAP
    group = blk_count * span_rows
    lane = lax.broadcasted_iota(jnp.int32, (group, 128), 1)
    routed = []
    for number in range(half_count):
        span = pl.ds(number * span_rows, span_rows)
        here = pl.ds(number * group, group)
        ffn_rows(number, span, here, r, gate, up, down, lane)
        r.back_in[blk, span, :] = r.back[blk, span, :]
        routed.append(
            scatter(
                place,
                "blk",
                r.back.at[:, span],
                r.back_in.at[:, span],
                r.sent_back.at[number],
                r.got_back.at[number],
            )
        )
    r.down_parts[...] = low(mul(r.scaled[...].T, r.hidden[...])).reshape(r.down_parts.shape)
    r.down_in[head] = r.down_parts[head]
    far_away = head_count // 2 - 1
    down_copies = scatter(
        place, "head", r.down_parts, r.down_in, r.sent_down, r.got_down, lambda number: number != far_away
    )
    cut = head_width // 4 * 3
    down_copies += scatter(
        place,
        "head",
        r.down_parts.at[:, pl.ds(0, cut)],
        r.down_in.at[:, pl.ds(0, cut)],
        r.sent_down,
        r.got_down,
        lambda number: number == far_away,
    )
    for number in range(half_count):
        span = pl.ds(number * span_rows, span_rows)
        here = pl.ds(number * group, group)
        r.outs[:, span, :] = low(mul_nt(r.hidden[here, :], down)).reshape(
            blk_count, span_rows, width
        )
    r.outs_in[blk] = r.outs[blk]
    out_copies = scatter(place, "blk", r.outs, r.outs_in, r.sent_outs, r.got_outs)
    r.turned[...] = r.taken[...].T
    for step, piece in enumerate((r.early_0, r.early_1, r.early_2, r.early_3)):
        here = rows_at(block_at(step, head_count), head_width)
        for kind, right in enumerate((r.grad_gate, r.grad_up)):
            piece[kind] = low(mul(r.turned[here, :], right[...]))
    narrow = lax.broadcasted_iota(jnp.int32, (tokens, 128), 1)
    shares_in = LineSum(place, r.parts, r.parts_in, r.sent_parts, r.got_parts)
    dot_copies = []
    for number in range(head_count):
        block = far_block(number, head_count)
        if number % 2 == 0:
            for copy in routed[number // 2]:
                copy.wait_recv()
            entries = wide(r.back_in[:, pl.ds(number * CAP, span_rows), :])
        entry = entries[:, (number % 2) * CAP : (number % 2 + 1) * CAP]
        entry = low(entry.reshape(EXPERTS * CAP, width + 128))
        found = [mul_tn(placed[block], entry) for placed in (r.first, r.second)]
        dots = [
            found[choice][:, width : width + 1] + found[choice][:, width + 64 : width + 65]
            for choice in range(TOP)
        ]
        dots = jnp.where(narrow == 0, dots[0], jnp.where(narrow == 1, dots[1], 0.0))
        r.dots[block] = dots.T[0:8]
        share = found[0][:, :width] + found[1][:, :width]
        if number < head_count - 1:
            away = (block + head_count - head) % head_count
            dot_copies.append(
                send(
                    r.dots.at[block],
                    r.dots_in.at[head],
                    r.sent_dots.at[away - 1],
                    r.got_dots.at[away - 1],
                    (block, blk),
                )
            )
            shares_in.add(block, share)
    down_copies += scatter(
        place,
        "head",
        r.down_parts.at[:, pl.ds(cut, head_width - cut)],
        r.down_in.at[:, pl.ds(cut, head_width - cut)],
        r.sent_down_rest,
        r.got_down_rest,
        lambda number: number == far_away,
    )
    home = home_early(place, r)
    r.dots_in[head] = r.dots[head]
    grad_slots = shares_in.total(share)
    for copy in dot_copies:
        copy.wait_recv()
    home_middle(place, r, home, grad_slots)
    r.given_parts[...] = low(mul_nt(r.output[...], r.middle_low[...])).reshape(
        r.given_parts.shape
    )
    r.given[head] = r.given_parts[head]
    given_copies = scatter(place, "head", r.given_parts, r.given, r.sent_given, r.got_given)
    for copy in out_copies:
        copy.wait_recv()
    for number in range(head_count):
        block = far_block(number, head_count)
        if number % 2 == 0:
            entries = wide(r.outs_in[:, pl.ds(number * CAP, span_rows), :])
        entry = entries[:, (number % 2) * CAP : (number % 2 + 1) * CAP]
        entry = low(entry.reshape(EXPERTS * CAP, width))
        shares = r.weights[block].T
        r.out_parts[block] = low(
            shares[:, 0:1] * mul_tn(r.first[block], entry)
            + shares[:, 1:2] * mul_tn(r.second[block], entry)
        )
    home_late(place, r, home)
    product = mul(r.attended_home[...], r.middle_low[...])
    for other in range(blk_count):
        r.output_terms[other] = low(own_pieces(product, rows, head_count, blk_count, other))
    for copies in routed + [out_copies, dot_copies]:
        for copy in copies:
            copy.wait_send()
    shares_in.wait()
    wait_all(down_copies, given_copies)
    pl.semaphore_signal(
        r.done, inc=1, device_id=(head, place.twin), device_id_type=MESH
    )
    pl.semaphore_wait(r.done, 1)


def home_early(place, r):
    head_count = place.head_count
    tokens, width = r.middle.shape
    share_rows = r.weights[place.head]
    columns = rows_joined(share_rows, r.facts[place.head, 0:8, :]).T
    share = [columns[:, choice : choice + 1] for choice in range(TOP)]
    route_of = [columns[:, 10 + choice : 11 + choice] for choice in range(TOP)]
    upstream = wide(r.g[...])
    normed_wide = wide(r.normed[...])
    small_low = low(r.small[...])
    seen = mul_nt(r.normed[...], small_low)
    met = mul_nt(r.g[...], small_low)

    def weight_of(expert):
        return sum(
            share[choice] * jnp.where(route_of[choice] == expert, 1.0, 0.0)
            for choice in range(TOP)
        )

    copy_share = weight_of(EXPERTS + 1)
    const_share = [weight_of(EXPERTS + 2 + const) for const in range(2)]
    mixing = []
    for const in range(2):
        at = MIX_AT + 2 * const
        pair = [seen[:, at + part : at + part + 1] for part in range(2)]
        highest = jnp.maximum(pair[0], pair[1])
        raised = [jnp.exp(value - highest) for value in pair]
        total = raised[0] + raised[1]
        mixing.append([value / total for value in raised])
    copy_dot = jnp.sum(upstream * normed_wide, axis=-1, keepdims=True)
    vector_dot = [met[:, VECTOR_AT + const : VECTOR_AT + const + 1] for const in range(2)]
    const_dot = [
        mixing[const][0] * copy_dot + mixing[const][1] * vector_dot[const] for const in range(2)
    ]
    special = []
    for choice in range(TOP):
        found = jnp.where(route_of[choice] == EXPERTS + 1, copy_dot, 0.0)
        for const in range(2):
            found = found + jnp.where(
                route_of[choice] == EXPERTS + 2 + const, const_dot[const], 0.0
            )
        special.append(share[choice] * found)
    lane = lax.broadcasted_iota(jnp.int32, (tokens, 128), 1)
    vector_share = jnp.zeros((tokens, 128), jnp.float32)
    mix_grad = jnp.zeros((tokens, 128), jnp.float32)
    for const in range(2):
        grad_mix = [const_share[const] * copy_dot, const_share[const] * vector_dot[const]]
        mean = mixing[const][0] * grad_mix[0] + mixing[const][1] * grad_mix[1]
        for part in range(2):
            mix_grad = mix_grad + jnp.where(
                lane == MIX_AT + 2 * const + part,
                mixing[const][part] * (grad_mix[part] - mean),
                0.0,
            )
        vector_share = vector_share + jnp.where(
            lane == VECTOR_AT + const, const_share[const] * mixing[const][1], 0.0
        )
    direct = copy_share + const_share[0] * mixing[0][0] + const_share[1] * mixing[1][0]
    r.direct[...] = direct * upstream
    source = r.middle[...]
    inverse = lax.rsqrt(jnp.mean(source * source, axis=-1, keepdims=True) + EPS)
    vectors = [r.small[VECTOR_AT + const : VECTOR_AT + const + 1] for const in range(2)]
    mixed = copy_share * normed_wide
    for const in range(2):
        mixed = mixed + const_share[const] * (
            mixing[const][0] * normed_wide + mixing[const][1] * vectors[const]
        )
    r.mixture[...] = source + mixed
    table = rows_joined(small_low[0:16], jnp.zeros((128 - 16, width), jnp.bfloat16))
    return types.SimpleNamespace(
        share=share,
        route_of=route_of,
        special=special,
        mix_grad=mix_grad,
        vector_share=vector_share,
        inverse=inverse,
        table=table,
    )


def home_middle(place, r, home, grad_slots):
    tokens, width = r.middle.shape
    dots = r.dots_in[0]
    for head in range(1, place.head_count):
        dots = dots + r.dots_in[head]
    dots = dots.T
    product = [dots[:, choice : choice + 1] + home.special[choice] for choice in range(TOP)]
    both = product[0] + product[1]
    lane = wide(lax.broadcasted_iota(jnp.int32, (tokens, 128), 1))
    routing = jnp.zeros((tokens, 128), jnp.float32)
    for choice in range(TOP):
        routing = routing + jnp.where(
            lane == home.route_of[choice], product[choice] - home.share[choice] * both, 0.0
        )
    spread_high, spread_rest = halves(routing + home.mix_grad)
    grad_normed = (
        r.direct[...] + grad_slots + mul(spread_high, home.table) + mul(spread_rest, home.table)
    )
    source = r.middle[...]
    scaled = grad_normed * r.small[GAIN_TWO_AT : GAIN_TWO_AT + 1]
    result = (
        wide(r.g[...])
        + home.inverse * scaled
        - source * home.inverse**3 * jnp.mean(scaled * source, axis=-1, keepdims=True)
    )
    r.middle_grad[...] = result
    r.middle_low[...] = low(result)
    r.direct[...] = grad_normed
    home.routing, home.spread = routing, (spread_high, spread_rest)


def home_late(place, r, home):
    width = r.middle.shape[1]
    r.residual_grad[...] = home.routing.T[:ROUTED]
    gain_row = jnp.sum(r.direct[...] * r.middle[...] * home.inverse, axis=0, keepdims=True)
    vector_high, vector_rest = halves(home.vector_share)
    by_normed = mul_tn(home.spread[0], r.normed[...]) + mul_tn(home.spread[1], r.normed[...])
    by_upstream = mul_tn(vector_high, r.g[...]) + mul_tn(vector_rest, r.g[...])
    row = lax.broadcasted_iota(jnp.int32, (SMALL, width), 0)
    r.small_grad[...] = jnp.where(
        row == GAIN_TWO_AT, gain_row, by_normed[:SMALL] + by_upstream[:SMALL]
    )


def close_layer(place, r):
    head_count, blk_count = place.head_count, place.blk_count
    head, blk = place.head, place.blk
    tokens, width = r.input_grad.shape
    rows = width // (head_count * blk_count)
    cut = r.query_grad.shape[1]
    joint_width = r.joint.shape[1]
    greet(place.others("head") + place.near())
    flat = jnp.concatenate(
        [r.small_grad[...], jnp.zeros((128 - SMALL, width), jnp.float32)], axis=0
    ).T
    for part in range(head_count):
        for other in range(blk_count):
            at = (part * blk_count + other) * rows
            r.small_terms[other, part * rows : (part + 1) * rows, :] = flat[at : at + rows]
    greeted(place.head_count - 1 + place.half)
    outs_in = LineSum(place, r.out_sums, r.out_in, r.sent_out, r.got_out)
    at_end = (head == 0) | (head == head_count - 1)

    @pl.when(at_end)
    def _():
        for number in range(head_count - 1):
            block = far_block(number, head_count)
            outs_in.add(block, wide(r.out_parts[block]))


    def fold(number, terms, theirs, arrived):
        return Fold(
            place,
            terms,
            theirs,
            arrived,
            r.sent_twin.at[number],
            r.got_twin.at[number],
            r.sent_blk.at[number],
            r.got_blk.at[number],
        )

    pair_folds = []
    for number in range(head_count):
        block = far_block(number, head_count)
        pair_folds.append(
            fold(
                number,
                r.pair_terms.at[:, block],
                r.theirs_pairs.at[number],
                r.arrived_pairs.at[number],
            )
        )
    output_fold = fold(head_count, r.output_terms, r.theirs_output, r.arrived_output)
    small_fold = fold(head_count + 1, r.small_terms, r.theirs_small, r.arrived_small)
    for one in pair_folds:
        one.add()
    output_fold.add()
    small_fold.add()
    r.turned[...] = r.normed[...].T
    r.early_rows[...] = mul_nt(r.query_grad[...], r.joint[:, :cut])
    early = mul(r.turned[...], r.query_grad[...])
    rows_in = LineSum(place, r.row_parts, r.rows_in, r.sent_rows, r.got_rows)
    for number in range(head_count - 1):
        block = far_block(number, head_count)

        @pl.when(jnp.logical_not(at_end))
        def _():
            outs_in.add(block, wide(r.out_parts[block]))

    gain_row = jnp.zeros((1, width), jnp.float32)
    for number in range(head_count):
        block = far_block(number, head_count)
        here = rows_at(block, tokens)
        part = low(pair_folds[number].total())
        r.grads[here, :] = part
        grad_normed = r.early_rows[here, :] + mul_nt(part, r.joint[:, cut:])
        if number < head_count - 1:
            rows_in.add(block, grad_normed)

        else:
            own_rows = grad_normed
        source = wide(r.x_all[block])
        inverse = lax.rsqrt(jnp.mean(source * source, axis=-1, keepdims=True) + EPS)
        gain_row = gain_row + jnp.sum(grad_normed * source * inverse, axis=0, keepdims=True)
    product = jnp.concatenate([early, mul(r.turned[...], r.grads[...])], axis=1)
    for other in range(blk_count):
        r.joint_terms[other] = low(own_pieces(product, rows, head_count, blk_count, other))
    joint_fold = fold(head_count + 2, r.joint_terms, r.theirs_joint, r.arrived_joint)
    owners = head_count * blk_count
    owner = lax.broadcasted_iota(jnp.int32, (owners, width), 0)
    column = lax.broadcasted_iota(jnp.int32, (owners, width), 1)
    owned = jnp.where(column // rows == owner, gain_row, 0.0)
    feature = lax.broadcasted_iota(jnp.int32, (width, 128), 0)
    target = lax.broadcasted_iota(jnp.int32, (width, 128), 1)
    moved = low(jnp.where(feature % rows == target, 1.0, 0.0))
    high, rest = halves(owned)
    by_owner = mul(high, moved) + mul(rest, moved)
    for other in range(blk_count):
        r.gain_terms[other] = jnp.concatenate(
            [
                by_owner[part * blk_count + other : part * blk_count + other + 1]
                for part in range(head_count)
            ]
            + [jnp.zeros((8 - head_count, 128), jnp.float32)],
            axis=0,
        )
    gain_fold = fold(head_count + 3, r.gain_terms, r.theirs_gain, r.arrived_gain)
    r.small_sums[...] = small_fold.total().reshape(head_count, rows, 128)
    r.small_in[head] = r.small_sums[head]
    last = scatter(place, "head", r.small_sums, r.small_in, r.sent_last.at[0], r.got_last.at[0])
    output_sum = output_fold.total()
    for part in range(head_count):
        r.output_sums[part] = low(packed_rows(output_sum[part * rows : (part + 1) * rows]))
    r.output_in[head] = r.output_sums[head]
    last += scatter(place, "head", r.output_sums, r.output_in, r.sent_last.at[3], r.got_last.at[3])
    joint_fold.add()
    gain_fold.add()
    joint_sum = joint_fold.total()
    filler = jnp.zeros((PAD - rows, joint_width), jnp.float32)
    for part in range(head_count):
        r.joint_sums[part] = low(rows_joined(joint_sum[part * rows : (part + 1) * rows], filler))
    r.joint_out[head] = r.joint_sums[head]
    last += scatter(place, "head", r.joint_sums, r.joint_out, r.sent_last.at[1], r.got_last.at[1])
    gain_now = gain_fold.total()
    for part in range(head_count):
        r.gain_sums[part] = jnp.broadcast_to(gain_now[part : part + 1], (8, 128))
    r.gain_in[head] = r.gain_sums[head]
    last += scatter(place, "head", r.gain_sums, r.gain_in, r.sent_last.at[2], r.got_last.at[2])
    total = r.mixture[...] + outs_in.total(wide(r.out_parts[head]))
    r.layer_out[...] = low(total)
    grad_normed = rows_in.total(own_rows)
    source = wide(r.x_all[head])
    inverse = lax.rsqrt(jnp.mean(source * source, axis=-1, keepdims=True) + EPS)
    scaled = grad_normed * r.small[GAIN_ONE_AT : GAIN_ONE_AT + 1]
    r.input_grad[...] = (
        r.middle_grad[...]
        + inverse * scaled
        - source * inverse**3 * jnp.mean(scaled * source, axis=-1, keepdims=True)
    )
    for copy in last:
        copy.wait_recv()
    output_sum = wide(r.output_in[0])
    for part in range(1, head_count):
        output_sum = output_sum + wide(r.output_in[part])
    r.output_grad[...] = unpacked_rows(output_sum)
    r.small_total[...] = sum(r.small_in[part] for part in range(head_count))
    r.gain_total[...] = sum(r.gain_in[part] for part in range(head_count))
    for one in pair_folds + [output_fold, small_fold, joint_fold, gain_fold]:
        one.wait()
    outs_in.wait()
    rows_in.wait()
    for copy in last:
        copy.wait_send()


def finish(
    sizes,
    piece_0,
    piece_1,
    piece_2,
    piece_3,
    down_in,
    joint_in,
    small_in,
    gain_in,
    sums_in,
    rows_in,
    layer_in,
    residual_in,
    gate,
    up,
    down,
    joint,
    value,
    gain_one,
    gain_two,
    router,
    mix,
    vectors,
    output,
    rows,
    layer,
    residual,
):
    head_count, blk_count = sizes
    mine = lax.axis_index("head")
    columns = piece_0.shape[2]
    for step, piece in enumerate((piece_0, piece_1, piece_2, piece_3)):
        source = (mine + head_count - step) % head_count
        at = rows_at(source, columns)
        gate[:, at] = wide(piece[0])
        up[:, at] = wide(piece[1])
    for source in range(head_count):
        down[:, source * columns : (source + 1) * columns] = wide(down_in[source])
    own_rows = joint.shape[0]
    parts = [wide(joint_in[source])[:own_rows] for source in range(head_count)]
    joint[...] = lanes_joined(
        *[part[:, 0:192] for part in parts], *[part[:, 256:448] for part in parts]
    )
    value[...] = lanes_joined(
        *[lanes_joined(part[:, 512:640], part[:, 448:512]) for part in parts]
    )
    flat = small_in[...]
    flat = jnp.concatenate(
        [flat, jnp.zeros((128 - own_rows, 128), jnp.float32)], axis=0
    ).T[:SMALL, :own_rows]
    gain_one[...] = gain_in[0:1, :own_rows]
    gain_two[...] = flat[GAIN_TWO_AT : GAIN_TWO_AT + 1]
    router[...] = flat[ROUTER_AT : ROUTER_AT + ROUTED]
    mix[...] = flat[MIX_AT : MIX_AT + 4]
    vectors[...] = flat[VECTOR_AT : VECTOR_AT + 2]
    output[...] = sums_in[...]
    rows[...] = rows_in[...]
    layer[...] = layer_in[...]
    residual[...] = residual_in[...]


def after(values, *signals):
    return lax.optimization_barrier((values, signals))[0]


def around_heads(pieces):
    count = len(pieces)
    return [pieces[0]] + [
        lax.ppermute(pieces[step], "head", [(i, (i + step) % count) for i in range(count)])
        for step in range(1, count)
    ]


def fast_shards(
    inputs,
    cotangent,
    segment,
    position,
    routes,
    gate_residual,
    first_gain,
    second_gain,
    query_key_weight,
    value_weight,
    output_weight,
    router_weight,
    const_gate,
    const_vectors,
    gate_weight,
    up_weight,
    down_weight,
):
    tokens, width = inputs.shape
    head_count = lax.axis_size("head")
    blk_count = lax.axis_size("blk")
    sizes = (head_count, blk_count)
    part = functools.partial
    half = blk_count // 2
    period = tokens * blk_count // CONT_LEN + 1
    head_width = width // head_count
    column_rows = head_count * tokens
    weight_rows = query_key_weight.shape[0]
    columns = gate_weight.shape[1] // head_count
    slot_rows = head_count * CAP
    slot_total = blk_count * slot_rows
    joint_width = 10 * HEAD_DIM
    pair_width = 6 * HEAD_DIM
    others, near = head_count - 1, blk_count - 1
    packed = width * 3 // 2
    joint_packed = (joint_width + 128) * 3 // 2

    opened_from = dict(
            x=inputs,
            joint_rows=query_key_weight,
            value_rows=value_weight,
            output_rows=output_weight,
            router=router_weight.T,
            mix=const_gate.T,
            vectors=const_vectors.T,
            gain_one=first_gain[None],
            gain_two=second_gain[None],
            segment=segment[None],
            position=position[None],
            routes=routes.T,
            residual=gate_residual.T,
            g=cotangent,
            down=down_weight.T,
    )
    opened = exchange(
        open_layer,
        sizes,
        opened_from,
        dict(
            x_all=shape((head_count, tokens, width)),
            facts=shape((head_count, 24, tokens), jnp.float32),
            places=shape((8, 128), jnp.int32),
            g_all=shape((head_count, tokens, width)),
            normed=shape((column_rows, width)),
            queries=shape((column_rows, 4 * HEAD_DIM)),
            pairs_all=shape((blk_count, head_count, tokens, pair_width)),
            joint=shape((width, joint_width)),
            output_part=shape((head_count, 16, packed)),
            small=shape((SMALL, width), jnp.float32),
            down_0=shape((head_width, columns)),
            down_1=shape((head_width, columns)),
            down_2=shape((head_width, columns)),
            down_3=shape((head_width, columns)),
        ),
        dict(
            my_router=vmem(ROUTED, weight_rows),
            my_mix=vmem(4, weight_rows),
            my_vectors=vmem(2, weight_rows),
            my_gain_one=vmem(1, weight_rows),
            my_gain_two=vmem(1, weight_rows),
            my_joint_rows=vmem(*query_key_weight.shape),
            my_value_rows=vmem(*value_weight.shape),
            my_segment=vmem(1, tokens, dtype=jnp.int32),
            my_position=vmem(1, tokens, dtype=jnp.int32),
            my_routes=vmem(TOP, tokens, dtype=jnp.int32),
            my_residual=vmem_wide(ROUTED, tokens),
            my_output_rows=vmem(*output_weight.shape),
            my_x=vmem(tokens, width),
            marks_all=vmem_wide(blk_count, head_count, 8, tokens),
            joint_own=vmem(head_count, 16, joint_packed),
            output_own=vmem(16, packed),
            facts_own=vmem_wide(24, tokens),
            joint_all=vmem(blk_count, head_count, 16, joint_packed),
            joint_wide=vmem_wide(width, joint_width + 128),
            local=dma(18),
            sent=dma(2, others),
            got=dma(2, others),
            sent_line=dma(3, 2, others),
            got_line=dma(3, 2, others),
            sent_joint=dma(near),
            got_joint=dma(near),
            sent_marks=dma(near),
            got_marks=dma(near),
            sent_pairs=dma(head_count, near),
            got_pairs=dma(head_count, near),
        ),
        0,
        far=tuple(opened_from) + ("g_all", "down_0", "down_1", "down_2", "down_3"),
        room=63,
    )
    down_pieces = around_heads([opened.down_0, opened.down_1, opened.down_2, opened.down_3])
    pairs_all = opened.pairs_all.reshape(blk_count * head_count, tokens, pair_width)
    lists = [
        pltpu.SMEM((blk_count * head_count + CHUNK,), jnp.int32),
        pltpu.SMEM((blk_count * head_count + CHUNK,), jnp.int32),
    ]
    items_at_most = head_count * (blk_count * head_count // CHUNK + 1) + 1
    long_lists = [pltpu.SMEM((items_at_most * CHUNK + CHUNK,), jnp.int32)] * 2
    attended, totals = compute(
        part(attend, sizes, period),
        [
            shape((head_count, head_width, tokens)),
            shape((head_count, 8, 3 * tokens), jnp.float32),
        ],
        [opened.places, opened.queries, pairs_all],
        lists,
        1,
    )
    halved = head_count // 2
    went = exchange(
        middle_layer,
        sizes,
        dict(
            attended=attended,
            g_all=opened.g_all,
            x_all=opened.x_all,
            output_part=opened.output_part,
            small=opened.small,
            facts=opened.facts,
            g=cotangent,
            gate=gate_weight,
            up=up_weight,
            down_0=down_pieces[0],
            down_1=down_pieces[1],
            down_2=down_pieces[2],
            down_3=down_pieces[3],
        ),
        dict(
            output_terms=shape((blk_count, head_count * weight_rows, width)),
            early_0=shape((2, head_width, columns)),
            early_1=shape((2, head_width, columns)),
            early_2=shape((2, head_width, columns)),
            early_3=shape((2, head_width, columns)),
            down_in=shape((head_count, head_width, columns)),
            out_parts=shape((head_count, tokens, width)),
            middle_grad=shape((tokens, width), jnp.float32),
            given=shape((head_count, head_width, tokens)),
            residual_grad=shape((ROUTED, tokens), jnp.float32),
            small_grad=shape((SMALL, width), jnp.float32),
            mixture=shape((tokens, width), jnp.float32),
        ),
        dict(
            attended_all=vmem(head_count, head_count, head_width, tokens),
            attended_home=vmem(width, tokens),
            first=vmem(head_count, EXPERTS * CAP, tokens),
            second=vmem(head_count, EXPERTS * CAP, tokens),
            upstream=vmem(EXPERTS, slot_rows, width),
            output=vmem(width, width),
            output_all=vmem(blk_count, head_count, 16, packed),
            output_wide=vmem_wide(width, width),
            slots=vmem(EXPERTS, slot_rows, width + 128),
            slots_in=vmem(blk_count, slot_rows, width + 128),
            grads_in=vmem(blk_count, slot_rows, width),
            middle=vmem_wide(tokens, width),
            normed=vmem(tokens, width),
            weights=vmem_wide(head_count, 8, tokens),
            gate_all=vmem(head_count, head_width, columns),
            up_all=vmem(head_count, head_width, columns),
            down_all=vmem(head_count, head_width, columns),
            taken=vmem(slot_total, width),
            turned=vmem(width, slot_total),
            hidden=vmem(slot_total, columns),
            grad_gate=vmem(slot_total, columns),
            grad_up=vmem(slot_total, columns),
            scaled=vmem(slot_total, width),
            back=vmem(blk_count, slot_rows, width + 128),
            outs=vmem(blk_count, slot_rows, width),
            back_in=vmem(blk_count, slot_rows, width + 128),
            outs_in=vmem(blk_count, slot_rows, width),
            parts=vmem(head_count, tokens, width),
            parts_in=vmem(2, head_count, tokens, width),
            dots=vmem_wide(head_count, 8, tokens),
            dots_in=vmem_wide(head_count, 8, tokens),
            down_parts=vmem(head_count, head_width, columns),
            middle_low=vmem(tokens, width),
            direct=vmem_wide(tokens, width),
            given_parts=vmem(head_count, head_width, tokens),
            local=dma(2),
            sent_line=dma(2, others),
            got_line=dma(2, others),
            sent_dots=dma(others),
            got_dots=dma(others),
            sent_output=dma(near),
            got_output=dma(near),
            sent_grads=dma(near),
            got_grads=dma(near),
            sent_weights=dma(2, others),
            got_weights=dma(2, others),
            sent_slots=dma(halved, near),
            got_slots=dma(halved, near),
            sent_back=dma(halved, near),
            got_back=dma(halved, near),
            sent_outs=dma(near),
            got_outs=dma(near),
            sent_down=dma(others),
            got_down=dma(others),
            sent_down_rest=dma(others),
            got_down_rest=dma(others),
            sent_parts=dma(head_count),
            got_parts=dma(2, head_count),
            sent_given=dma(others),
            got_given=dma(others),
            done=pltpu.SemaphoreType.REGULAR,
        ),
        1,
        far=("gate", "up"),
    )
    grad_pieces = around_heads([went.early_0, went.early_1, went.early_2, went.early_3])
    query_grad, pair_grad = compute(
        part(attend_back, sizes, period),
        [shape(opened.queries.shape), shape(pairs_all.shape)],
        [
            opened.places,
            opened.queries,
            pairs_all,
            attended,
            totals,
            went.given,
        ],
        long_lists
        + [
            pltpu.SMEM((items_at_most,), jnp.int32),
            vmem(head_count, 3 * tokens, 4 * HEAD_DIM),
            vmem(head_count, 3 * tokens, 4 * HEAD_DIM),
            vmem_wide(head_count, 8, 3 * tokens),
            vmem_wide(head_count, HEAD_DIM, 3 * tokens),
            vmem_wide(*pairs_all.shape),
        ],
        1,
    )
    folds = head_count + 4
    closed = exchange(
        close_layer,
        sizes,
        dict(
            pair_terms=pair_grad.reshape(blk_count, head_count, tokens, pair_width),
            query_grad=query_grad,
            joint=opened.joint,
            normed=opened.normed,
            x_all=opened.x_all,
            small_grad=went.small_grad,
            out_parts=went.out_parts,
            output_terms=went.output_terms,
            small=opened.small,
            middle_grad=went.middle_grad,
            mixture=went.mixture,
        ),
        dict(
            input_grad=shape((tokens, width), jnp.float32),
            layer_out=shape((tokens, width)),
            joint_out=shape((head_count, PAD, joint_width)),
            output_grad=shape((weight_rows, width), jnp.float32),
            small_total=shape((weight_rows, 128), jnp.float32),
            gain_total=shape((8, 128), jnp.float32),
        ),
        dict(
            theirs_pairs=vmem(head_count, half, tokens, pair_width),
            arrived_pairs=vmem(head_count, half - 1, tokens, pair_width),
            theirs_output=vmem(half, head_count * weight_rows, width),
            arrived_output=vmem(half - 1, head_count * weight_rows, width),
            output_sums=vmem(head_count, 16, packed),
            output_in=vmem(head_count, 16, packed),
            small_terms=vmem_wide(blk_count, head_count * weight_rows, 128),
            theirs_small=vmem_wide(half, head_count * weight_rows, 128),
            arrived_small=vmem_wide(half - 1, head_count * weight_rows, 128),
            joint_terms=vmem(blk_count, head_count * weight_rows, joint_width),
            theirs_joint=vmem(half, head_count * weight_rows, joint_width),
            arrived_joint=vmem(half - 1, head_count * weight_rows, joint_width),
            gain_terms=vmem_wide(blk_count, 8, 128),
            theirs_gain=vmem_wide(half, 8, 128),
            arrived_gain=vmem_wide(half - 1, 8, 128),
            row_parts=vmem(head_count, tokens, width),
            rows_in=vmem(2, head_count, tokens, width),
            out_sums=vmem(head_count, tokens, width),
            out_in=vmem(2, head_count, tokens, width),
            joint_sums=vmem(head_count, PAD, joint_width),
            small_sums=vmem_wide(head_count, weight_rows, 128),
            small_in=vmem_wide(head_count, weight_rows, 128),
            gain_sums=vmem_wide(head_count, 8, 128),
            gain_in=vmem_wide(head_count, 8, 128),
            turned=vmem(width, column_rows),
            grads=vmem(column_rows, pair_width),
            early_rows=vmem_wide(column_rows, width),
            sent_out=dma(head_count),
            got_out=dma(2, head_count),
            sent_twin=dma(folds, half),
            got_twin=dma(folds, half),
            sent_blk=dma(folds, half - 1),
            got_blk=dma(folds, half - 1),
            sent_rows=dma(head_count),
            got_rows=dma(2, head_count),
            sent_last=dma(4, others),
            got_last=dma(4, others),
        ),
        2,
    )
    wide_shape = part(shape, dtype=jnp.float32)
    (
        gate_grad,
        up_grad,
        down_grad,
        joint_grad,
        value_grad,
        gain_one_grad,
        gain_two_grad,
        router_grad,
        mix_grad,
        vector_grad,
        output_grad,
        input_grad,
        layer_out,
        residual_grad,
    ) = compute(
        part(finish, sizes),
        [
            wide_shape(gate_weight.shape),
            wide_shape(up_weight.shape),
            wide_shape(gate_weight.shape),
            wide_shape(query_key_weight.shape),
            wide_shape(value_weight.shape),
            wide_shape((1, weight_rows)),
            wide_shape((1, weight_rows)),
            wide_shape((ROUTED, weight_rows)),
            wide_shape((4, weight_rows)),
            wide_shape((2, weight_rows)),
            wide_shape(output_weight.shape),
            wide_shape((tokens, width)),
            shape((tokens, width)),
            wide_shape((ROUTED, tokens)),
        ],
        grad_pieces
        + [
            went.down_in,
            closed.joint_out,
            closed.small_total,
            closed.gain_total,
            closed.output_grad,
            closed.input_grad,
            closed.layer_out,
            went.residual_grad,
        ],
    )
    return (
        layer_out,
        input_grad,
        residual_grad.T,
        gain_one_grad[0],
        gain_two_grad[0],
        joint_grad,
        value_grad,
        output_grad,
        router_grad.T,
        mix_grad.T,
        vector_grad.T,
        gate_grad,
        up_grad,
        down_grad.T,
    )


def solution(mesh):
    body = fast_shards if mesh.shape["blk"] == EXPERTS else shards
    in_specs = (
        P(("head", "blk"), None),
        P(("head", "blk"), None),
        P(("head", "blk")),
        P(("head", "blk")),
        P(("head", "blk"), None),
        P(("head", "blk"), None),
        P(("head", "blk")),
        P(("head", "blk")),
        P(("head", "blk"), None),
        P(("head", "blk"), None),
        P(("head", "blk"), None),
        P(("head", "blk"), None),
        P(("head", "blk"), None),
        P(("head", "blk"), None),
        P("head", "blk"),
        P("head", "blk"),
        P("blk", "head"),
    )
    out_specs = (
        P(("head", "blk"), None),
        P(("head", "blk"), None),
        P(("head", "blk"), None),
        P(("head", "blk")),
        P(("head", "blk")),
        P(("head", "blk"), None),
        P(("head", "blk"), None),
        P(("head", "blk"), None),
        P(("head", "blk"), None),
        P(("head", "blk"), None),
        P(("head", "blk"), None),
        P("head", "blk"),
        P("head", "blk"),
        P("blk", "head"),
    )
    return jax.shard_map(body, mesh=mesh, in_specs=in_specs, out_specs=out_specs, check_vma=False)
```

```python
import functools
import types

import jax
import jax.numpy as jnp
from jax import lax
from jax.experimental import pallas as pl
from jax.experimental.pallas import tpu as pltpu
from jax.sharding import PartitionSpec as P

HEADS = 12
HEAD_DIM = 64
EXPERTS = 8
ROUTED = 12
TOP = 2
CONT_LEN = 1024
CAP = 24


EPS = 1e-06
HIGH = lax.Precision.HIGHEST


def silu_slope(pre):
    sigmoid_value = jax.nn.sigmoid(pre)
    return sigmoid_value * (1.0 + pre * (1.0 - sigmoid_value))


def visible_pairs(query_segment, query_position, key_segment, key_position, period):
    same_sequence = (query_segment[:, None] == key_segment[None, :]) & (
        key_position[None, :] <= query_position[:, None]
    )
    same_group = query_segment[:, None] // period == key_segment[None, :] // period
    shared = (
        (key_segment[None, :] % period == 0) & (query_segment[:, None] % period != 0) & same_group
    )
    return same_sequence | shared


def norm_back(grad_normed, source, inverse, gain):
    scaled = grad_normed * gain
    grad_source = inverse * scaled - source * inverse**3 * jnp.mean(
        scaled * source, axis=-1, keepdims=True
    )
    grad_gain = jnp.sum(grad_normed * source * inverse, axis=0)
    return (grad_source, grad_gain)


def around_blocks(pieces, combine, initial):
    return combine(
        initial,
        (
            lax.all_gather(pieces[0], "blk", axis=0, tiled=True),
            lax.all_gather(pieces[1], "blk", axis=0, tiled=True),
        ),
        jnp.int32(0),
    )


def softmax_last(logits):
    highest = jnp.max(logits, axis=-1, keepdims=True)
    raised = jnp.exp(logits - highest)
    return raised / jnp.sum(raised, axis=-1, keepdims=True)


def shards(
    inputs,
    cotangent,
    segment,
    position,
    routes,
    gate_residual,
    first_gain,
    second_gain,
    query_key_weight,
    value_weight,
    output_weight,
    router_weight,
    const_gate,
    const_vectors,
    gate_weight,
    up_weight,
    down_weight,
):
    tok_rows, width = inputs.shape
    head_count = lax.axis_size("head")
    blk_count = lax.axis_size("blk")
    local_heads = HEADS // head_count
    query_rows = head_count * tok_rows
    head_width = width // head_count
    width_split = blk_count // EXPERTS
    score_scale = HEAD_DIM ** (-0.5)
    period = tok_rows * blk_count // CONT_LEN + 1
    gathered = (
        lax.all_gather(first_gain, ("head", "blk"), axis=0, tiled=True),
        lax.all_gather(second_gain, ("head", "blk"), axis=0, tiled=True),
        lax.all_gather(query_key_weight, ("head", "blk"), axis=0, tiled=True),
        lax.all_gather(value_weight, ("head", "blk"), axis=0, tiled=True),
        lax.all_gather(output_weight, ("head", "blk"), axis=0, tiled=True),
        lax.all_gather(router_weight, ("head", "blk"), axis=0, tiled=True),
        lax.all_gather(const_gate, ("head", "blk"), axis=0, tiled=True),
        lax.all_gather(const_vectors, ("head", "blk"), axis=0, tiled=True),
        lax.all_gather(segment, ("head", "blk"), axis=0, tiled=True),
        lax.all_gather(position, ("head", "blk"), axis=0, tiled=True),
    )
    (
        gain_one,
        gain_two,
        full_joint,
        full_value,
        full_output,
        full_router,
        full_const,
        full_vectors,
        segment_all,
        position_all,
    ) = gathered
    gate_columns, up_columns, down_rows = (
        lax.all_gather(gate_weight, "head", axis=0, tiled=True),
        lax.all_gather(up_weight, "head", axis=0, tiled=True),
        lax.all_gather(down_weight, "head", axis=1, tiled=True),
    )
    gain_one = gain_one.astype(jnp.float32)
    gain_two = gain_two.astype(jnp.float32)
    source = inputs.astype(jnp.float32)
    inverse_one = lax.rsqrt(jnp.mean(source * source, axis=-1, keepdims=True) + EPS)
    normed_one = (source * inverse_one * gain_one).astype(jnp.bfloat16)
    joined = jnp.dot(normed_one, full_joint, preferred_element_type=jnp.float32)
    value_proj = jnp.dot(normed_one, full_value, preferred_element_type=jnp.float32)

    def head_layout(array):
        return array.astype(jnp.bfloat16).reshape(tok_rows, head_count, head_width)

    query_heads, key_heads, value_heads = (
        lax.all_to_all(
            head_layout(joined[:, :width]), "head", split_axis=1, concat_axis=0, tiled=True
        ),
        lax.all_to_all(
            head_layout(joined[:, width:]), "head", split_axis=1, concat_axis=0, tiled=True
        ),
        lax.all_to_all(head_layout(value_proj), "head", split_axis=1, concat_axis=0, tiled=True),
    )
    query_heads = query_heads.reshape(query_rows, local_heads, HEAD_DIM)
    key_heads = key_heads.reshape(query_rows, head_width)
    value_heads = value_heads.reshape(query_rows, head_width)
    blk_index = lax.axis_index("blk")
    segment_grid = segment_all.reshape(head_count, blk_count, tok_rows)
    position_grid = position_all.reshape(head_count, blk_count, tok_rows)
    query_segment = lax.dynamic_index_in_dim(segment_grid, blk_index, 1, keepdims=False).reshape(
        query_rows
    )
    query_position = lax.dynamic_index_in_dim(position_grid, blk_index, 1, keepdims=False).reshape(
        query_rows
    )
    key_segment = segment_grid.transpose(1, 0, 2).reshape(blk_count * query_rows)
    key_position = position_grid.transpose(1, 0, 2).reshape(blk_count * query_rows)

    def key_slices(pieces):
        piece_rows = pieces[0].shape[0]
        step_count = piece_rows // tok_rows
        return (
            pieces[0].reshape(step_count, tok_rows, local_heads, HEAD_DIM),
            pieces[1].reshape(step_count, tok_rows, local_heads, HEAD_DIM),
            key_segment.reshape(step_count, tok_rows),
            key_position.reshape(step_count, tok_rows),
        )

    def masked_scores(queries, block_keys, visible):
        scores = (
            jnp.einsum("qhd,khd->hqk", queries, block_keys, preferred_element_type=jnp.float32)
            * score_scale
        )
        return jnp.where(visible[None], scores, -jnp.inf)

    def attend_block(carried, block):
        block_keys, block_values, block_segment, block_position = block
        visible = visible_pairs(
            query_segment, query_position, block_segment, block_position, period
        )

        def attend_compute(state):
            top_score, running_total, weighted = state
            scores = masked_scores(query_heads, block_keys, visible)
            new_top = jnp.maximum(top_score, jnp.max(scores, axis=-1))
            anchor = jnp.where(new_top == -jnp.inf, 0.0, new_top)
            raised = jnp.exp(scores - anchor[..., None])
            factor = jnp.exp(top_score - anchor)
            running_total = running_total * factor + jnp.sum(raised, axis=-1)
            weighted = weighted * factor[..., None] + jnp.einsum(
                "hqk,khd->hqd",
                raised.astype(jnp.bfloat16),
                block_values,
                preferred_element_type=jnp.float32,
            )
            return (new_top, running_total, weighted)

        def unchanged(state):
            return state

        return (lax.cond(jnp.any(visible), attend_compute, unchanged, carried), None)

    def attend_piece(carried, pieces, first_row):
        result, unused = lax.scan(attend_block, carried, key_slices(pieces))
        return result

    start_state = (
        jnp.full((local_heads, query_rows), -jnp.inf, jnp.float32),
        jnp.zeros((local_heads, query_rows), jnp.float32),
        jnp.zeros((local_heads, query_rows, HEAD_DIM), jnp.float32),
    )
    top_score, running_total, weighted = around_blocks(
        (key_heads, value_heads), attend_piece, start_state
    )
    log_total = top_score + jnp.log(running_total)
    attended_local = (weighted / running_total[..., None]).transpose(1, 0, 2).astype(jnp.bfloat16)
    attended = lax.all_to_all(
        attended_local.reshape(query_rows, 1, head_width),
        "head",
        split_axis=0,
        concat_axis=1,
        tiled=True,
    ).reshape(tok_rows, width)
    middle = source + jnp.dot(attended, full_output, preferred_element_type=jnp.float32)
    inverse_two = lax.rsqrt(jnp.mean(middle * middle, axis=-1, keepdims=True) + EPS)
    normed_two = (middle * inverse_two * gain_two).astype(jnp.bfloat16)
    normed_float = normed_two.astype(jnp.float32)
    logits = jnp.dot(normed_two, full_router, preferred_element_type=jnp.float32) + gate_residual
    choose = (routes[:, :, None] == jnp.arange(ROUTED, dtype=jnp.int32)[None, None, :]).astype(
        jnp.float32
    )
    picked = jnp.sum(choose * logits[:, None, :], axis=-1)
    weighting = softmax_last(picked)
    pair_expert = routes.reshape(tok_rows * TOP)
    ffn_onehot = (pair_expert[:, None] == jnp.arange(EXPERTS, dtype=jnp.int32)[None, :]).astype(
        jnp.int32
    )
    pair_rank = jnp.sum((jnp.cumsum(ffn_onehot, axis=0) - ffn_onehot) * ffn_onehot, axis=-1)
    slot_match = (
        pair_rank[None, None, :] == jnp.arange(CAP, dtype=jnp.int32)[None, :, None]
    ).astype(jnp.int32)
    placement = (
        (ffn_onehot.T[:, None, :] * slot_match)
        .reshape(EXPERTS, CAP, tok_rows, TOP)
        .astype(jnp.float32)
    )
    select = jnp.sum(placement, axis=-1)
    gate_slot = jnp.einsum("ectj,tj->ect", placement, weighting, precision=HIGH)
    send_rows = jnp.einsum(
        "ect,td->ecd", select.astype(jnp.bfloat16), normed_two, preferred_element_type=jnp.float32
    ).astype(jnp.bfloat16)
    upstream = cotangent.astype(jnp.float32)
    slot_grad = jnp.einsum("ect,td->ecd", gate_slot, upstream, precision=HIGH).astype(jnp.bfloat16)
    rows_in = lax.all_to_all(
        jnp.repeat(send_rows, width_split, axis=0), "blk", split_axis=0, concat_axis=0, tiled=True
    )
    grads_in = lax.all_to_all(
        jnp.repeat(slot_grad, width_split, axis=0), "blk", split_axis=0, concat_axis=0, tiled=True
    )
    gate_pre = jnp.einsum("scd,df->scf", rows_in, gate_columns, preferred_element_type=jnp.float32)
    up_pre = jnp.einsum("scd,df->scf", rows_in, up_columns, preferred_element_type=jnp.float32)
    activated = jax.nn.silu(gate_pre)
    hidden = (activated * up_pre).astype(jnp.bfloat16)
    partial_out = jnp.einsum("scf,fd->scd", hidden, down_rows, preferred_element_type=jnp.float32)
    grad_hidden = jnp.einsum("scd,fd->scf", grads_in, down_rows, preferred_element_type=jnp.float32)
    grad_gate_pre = (grad_hidden * up_pre * silu_slope(gate_pre)).astype(jnp.bfloat16)
    grad_up_pre = (grad_hidden * activated).astype(jnp.bfloat16)
    grad_part = jnp.einsum(
        "scf,df->scd", grad_gate_pre, gate_columns, preferred_element_type=jnp.float32
    ) + jnp.einsum("scf,df->scd", grad_up_pre, up_columns, preferred_element_type=jnp.float32)
    back_out = lax.all_to_all(
        partial_out.astype(jnp.bfloat16), "blk", split_axis=0, concat_axis=0, tiled=True
    ).astype(partial_out.dtype)
    back_grad = lax.all_to_all(
        grad_part.astype(jnp.bfloat16), "blk", split_axis=0, concat_axis=0, tiled=True
    ).astype(grad_part.dtype)
    returned, grad_back, kept_rows, kept_grads, hidden, grad_gate_pre, grad_up_pre = (
        back_out,
        back_grad,
        rows_in,
        grads_in,
        hidden,
        grad_gate_pre,
        grad_up_pre,
    )
    expert_out = returned.reshape(EXPERTS, width_split, CAP, width).sum(axis=1)
    ffn_sum = jnp.einsum("ect,ecd->td", gate_slot, expert_out, precision=HIGH)
    mixing = softmax_last(
        jnp.dot(normed_two, full_const, preferred_element_type=jnp.float32).reshape(tok_rows, 2, 2)
    )
    vectors = full_vectors.astype(jnp.float32)
    copy_share = jnp.sum(weighting * (routes == EXPERTS + 1).astype(jnp.float32), axis=-1)
    const_share = jnp.stack(
        [
            jnp.sum(weighting * (routes == EXPERTS + 2 + const_index).astype(jnp.float32), axis=-1)
            for const_index in range(2)
        ],
        axis=1,
    )
    const_outs = [
        mixing[:, const_index, 0:1] * normed_float
        + mixing[:, const_index, 1:2] * vectors[:, const_index][None, :]
        for const_index in range(2)
    ]
    mixture = ffn_sum + copy_share[:, None] * normed_float
    for const_index in range(2):
        mixture = mixture + const_share[:, const_index : const_index + 1] * const_outs[const_index]
    layer_out = (middle + mixture).astype(jnp.bfloat16)
    output_dots = jnp.einsum("ecd,td->ect", expert_out, upstream, precision=HIGH)
    grad_weighting = jnp.einsum("ectj,ect->tj", placement, output_dots, precision=HIGH)
    copy_dot = jnp.sum(upstream * normed_float, axis=-1)
    grad_weighting = (
        grad_weighting + (routes == EXPERTS + 1).astype(jnp.float32) * copy_dot[:, None]
    )
    for const_index in range(2):
        const_dot = jnp.sum(upstream * const_outs[const_index], axis=-1)
        grad_weighting = (
            grad_weighting
            + (routes == EXPERTS + 2 + const_index).astype(jnp.float32) * const_dot[:, None]
        )
    grad_picked = weighting * (
        grad_weighting - jnp.sum(weighting * grad_weighting, axis=-1, keepdims=True)
    )
    grad_logits = jnp.einsum("tj,tjr->tr", grad_picked, choose, precision=HIGH)
    vector_dots = jnp.dot(upstream, vectors, precision=HIGH)
    grad_mixing = const_share[:, :, None] * jnp.stack(
        [jnp.broadcast_to(copy_dot[:, None], vector_dots.shape), vector_dots], axis=-1
    )
    grad_mix = (
        mixing * (grad_mixing - jnp.sum(mixing * grad_mixing, axis=-1, keepdims=True))
    ).reshape(tok_rows, 4)
    grad_const_weight = jnp.dot(normed_float.T, grad_mix, precision=HIGH)
    grad_vectors = jnp.einsum("ti,td->di", const_share * mixing[:, :, 1], upstream, precision=HIGH)
    grad_router_weight = jnp.dot(normed_float.T, grad_logits, precision=HIGH)
    direct_share = (
        copy_share + const_share[:, 0] * mixing[:, 0, 0] + const_share[:, 1] * mixing[:, 1, 0]
    )
    grad_normed_two = direct_share[:, None] * upstream
    grad_normed_two = grad_normed_two + jnp.dot(
        grad_mix, full_const.astype(jnp.float32).T, precision=HIGH
    )
    grad_normed_two = grad_normed_two + jnp.dot(
        grad_logits, full_router.astype(jnp.float32).T, precision=HIGH
    )
    grad_down_local = jnp.einsum(
        "scf,scd->fd", hidden, kept_grads, preferred_element_type=jnp.float32
    )
    grad_gate_local = jnp.einsum(
        "scd,scf->df", kept_rows, grad_gate_pre, preferred_element_type=jnp.float32
    )
    grad_up_local = jnp.einsum(
        "scd,scf->df", kept_rows, grad_up_pre, preferred_element_type=jnp.float32
    )
    grad_slots = grad_back.reshape(EXPERTS, width_split, CAP, width).sum(axis=1)
    grad_normed_two = grad_normed_two + jnp.einsum(
        "ect,ecd->td", select, grad_slots, precision=HIGH
    )
    grad_gate_sum, grad_up_sum, grad_down_sum = (
        lax.psum_scatter(
            grad_gate_local.astype(jnp.bfloat16), "head", scatter_dimension=0, tiled=True
        ).astype(jnp.float32),
        lax.psum_scatter(
            grad_up_local.astype(jnp.bfloat16), "head", scatter_dimension=0, tiled=True
        ).astype(jnp.float32),
        lax.psum_scatter(
            grad_down_local.astype(jnp.bfloat16), "head", scatter_dimension=1, tiled=True
        ).astype(jnp.float32),
    )
    grad_from_norm, grad_gain_two = norm_back(grad_normed_two, middle, inverse_two, gain_two)
    grad_middle = upstream + grad_from_norm
    branch_grad = grad_middle.astype(jnp.bfloat16)
    grad_out_weight = jnp.einsum(
        "tc,td->cd", attended, branch_grad, preferred_element_type=jnp.float32
    )
    grad_attended = jnp.einsum(
        "td,cd->tc", branch_grad, full_output, preferred_element_type=jnp.float32
    ).astype(jnp.bfloat16)
    grad_heads = lax.all_to_all(
        grad_attended.reshape(tok_rows, head_count, head_width),
        "head",
        split_axis=1,
        concat_axis=0,
        tiled=True,
    )
    grad_heads = grad_heads.reshape(query_rows, local_heads, HEAD_DIM)
    offset = jnp.sum(grad_heads.astype(jnp.float32) * attended_local.astype(jnp.float32), axis=-1).T

    def probe_block(queries, grads, lse_rows, offset_rows, block_keys, block_values, visible):
        scores = masked_scores(queries, block_keys, visible)
        probabilities = jnp.exp(scores - lse_rows[..., None])
        grad_probs = jnp.einsum(
            "qhd,khd->hqk", grads, block_values, preferred_element_type=jnp.float32
        )
        grad_scores = (probabilities * (grad_probs - offset_rows[..., None])).astype(jnp.bfloat16)
        return (probabilities, grad_scores)

    zero_query = jnp.zeros((query_rows, local_heads, HEAD_DIM), jnp.float32)

    def backward_block(grad_query, block):
        block_keys, block_values, block_segment, block_position = block
        visible = visible_pairs(
            query_segment, query_position, block_segment, block_position, period
        )

        def backward_compute(accumulated):
            probabilities, grad_scores = probe_block(
                query_heads, grad_heads, log_total, offset, block_keys, block_values, visible
            )
            grad_values = jnp.einsum(
                "hqk,qhd->khd",
                probabilities.astype(jnp.bfloat16),
                grad_heads,
                preferred_element_type=jnp.float32,
            )
            accumulated = (
                accumulated
                + jnp.einsum(
                    "hqk,khd->qhd", grad_scores, block_keys, preferred_element_type=jnp.float32
                )
                * score_scale
            )
            grad_keys = (
                jnp.einsum(
                    "hqk,qhd->khd", grad_scores, query_heads, preferred_element_type=jnp.float32
                )
                * score_scale
            )
            return (accumulated, jnp.concatenate([grad_keys, grad_values], axis=-1))

        def skipped(accumulated):
            return (
                accumulated,
                jnp.zeros((block_keys.shape[0], local_heads, 2 * HEAD_DIM), jnp.float32),
            )

        return lax.cond(jnp.any(visible), backward_compute, skipped, grad_query)

    def fold_back(carried, pieces, first_row):
        grad_query, stacked = lax.scan(backward_block, carried[0], key_slices(pieces))
        term_piece = stacked.reshape(pieces[0].shape[0], local_heads * 2 * HEAD_DIM)
        return (grad_query, term_piece)

    zero_term = jnp.zeros((blk_count * query_rows, local_heads * 2 * HEAD_DIM), jnp.float32)
    grad_query, key_term = around_blocks(
        (key_heads, value_heads), fold_back, (zero_query, zero_term)
    )
    key_sums = lax.psum_scatter(key_term, "blk", scatter_dimension=0, tiled=True).reshape(
        query_rows, local_heads, 2, HEAD_DIM
    )
    grad_key_heads = key_sums[:, :, 0].astype(jnp.bfloat16).reshape(query_rows, 1, head_width)
    grad_value_heads = key_sums[:, :, 1].astype(jnp.bfloat16).reshape(query_rows, 1, head_width)
    grad_query_heads = grad_query.astype(jnp.bfloat16).reshape(query_rows, 1, head_width)
    grad_query_tok, grad_key_tok, grad_value_tok = (
        lax.all_to_all(grad_query_heads, "head", split_axis=0, concat_axis=1, tiled=True),
        lax.all_to_all(grad_key_heads, "head", split_axis=0, concat_axis=1, tiled=True),
        lax.all_to_all(grad_value_heads, "head", split_axis=0, concat_axis=1, tiled=True),
    )
    grad_joined = jnp.concatenate(
        [grad_query_tok.reshape(tok_rows, width), grad_key_tok.reshape(tok_rows, width)], axis=1
    )
    grad_value_tok = grad_value_tok.reshape(tok_rows, width)
    grad_normed_one = jnp.einsum(
        "tc,dc->td", grad_joined, full_joint, preferred_element_type=jnp.float32
    ) + jnp.einsum("tc,dc->td", grad_value_tok, full_value, preferred_element_type=jnp.float32)
    grad_joint_weight = jnp.einsum(
        "td,tc->dc", normed_one, grad_joined, preferred_element_type=jnp.float32
    )
    grad_value_weight = jnp.einsum(
        "td,tc->dc", normed_one, grad_value_tok, preferred_element_type=jnp.float32
    )
    grad_from_first, grad_gain_one = norm_back(grad_normed_one, source, inverse_one, gain_one)
    grad_input = grad_middle + grad_from_first
    summed = (
        lax.psum_scatter(grad_gain_one, ("head", "blk"), scatter_dimension=0, tiled=True),
        lax.psum_scatter(grad_gain_two, ("head", "blk"), scatter_dimension=0, tiled=True),
        lax.psum_scatter(grad_joint_weight, ("head", "blk"), scatter_dimension=0, tiled=True),
        lax.psum_scatter(grad_value_weight, ("head", "blk"), scatter_dimension=0, tiled=True),
        lax.psum_scatter(grad_out_weight, ("head", "blk"), scatter_dimension=0, tiled=True),
        lax.psum_scatter(grad_router_weight, ("head", "blk"), scatter_dimension=0, tiled=True),
        lax.psum_scatter(grad_const_weight, ("head", "blk"), scatter_dimension=0, tiled=True),
        lax.psum_scatter(grad_vectors, ("head", "blk"), scatter_dimension=0, tiled=True),
    )
    return (
        layer_out,
        grad_input,
        grad_logits,
        summed[0],
        summed[1],
        summed[2],
        summed[3],
        summed[4],
        summed[5],
        summed[6],
        summed[7],
        grad_gate_sum,
        grad_up_sum,
        grad_down_sum,
    )


MESH = pl.DeviceIdType.MESH
SMALL = 24
ROUTER_AT, MIX_AT, VECTOR_AT, GAIN_ONE_AT, GAIN_TWO_AT = 0, 12, 16, 18, 19
PAD = 32
CHUNK = 4
FAR = 1 << 20
NT = (((1,), (1,)), ((), ()))
TN = (((0,), (0,)), ((), ()))


def mul(left, right):
    return jnp.dot(left, right, preferred_element_type=jnp.float32)


def mul_nt(left, right):
    return lax.dot_general(left, right, NT, preferred_element_type=jnp.float32)


def mul_tn(left, right):
    return lax.dot_general(left, right, TN, preferred_element_type=jnp.float32)


def low(values):
    return values.astype(jnp.bfloat16)


def wide(values):
    return values.astype(jnp.float32)


def halves(values):
    high = low(values)
    return high, low(values - wide(high))


def shape(dims, dtype=jnp.bfloat16):
    return jax.ShapeDtypeStruct(dims, dtype)


def compute(body, outs, ins, scratch=(), smem=0):
    specs = [pl.BlockSpec(memory_space=pltpu.SMEM)] * smem
    specs += [pl.BlockSpec(memory_space=pltpu.VMEM)] * (len(ins) - smem)
    return pl.pallas_call(
        body,
        out_shape=outs,
        in_specs=specs,
        out_specs=[pl.BlockSpec(memory_space=pltpu.VMEM)] * len(outs),
        scratch_shapes=list(scratch),
        compiler_params=pltpu.CompilerParams(vmem_limit_bytes=52 * 2**20),
    )(*ins)


def exchange(body, sizes, ins, outs, scratch, number, far=(), room=52):
    names = list(ins) + list(outs) + list(scratch)

    def run(*refs):
        body(Place(*sizes), types.SimpleNamespace(**dict(zip(names, refs))))

    def spec(name):
        return pl.BlockSpec(memory_space=pl.ANY if name in far else pltpu.VMEM)

    results = pl.pallas_call(
        run,
        out_shape=list(outs.values()),
        in_specs=[spec(name) for name in ins],
        out_specs=[spec(name) for name in outs],
        scratch_shapes=list(scratch.values()),
        compiler_params=pltpu.CompilerParams(
            collective_id=number, has_side_effects=True, vmem_limit_bytes=room * 2**20
        ),
    )(*ins.values())
    return types.SimpleNamespace(**dict(zip(outs, results)))


def vmem(*dims, dtype=jnp.bfloat16):
    return pltpu.VMEM(dims, dtype)


def vmem_wide(*dims):
    return pltpu.VMEM(dims, jnp.float32)


def greet(devices):
    barrier = pltpu.get_barrier_semaphore()
    for device in devices:
        pl.semaphore_signal(barrier, inc=1, device_id=device, device_id_type=MESH)


def greeted(count):
    pl.semaphore_wait(pltpu.get_barrier_semaphore(), count)


def meet(devices):
    greet(devices)
    greeted(len(devices))


class Place:
    def __init__(self, head_count, blk_count):
        self.head_count, self.blk_count = head_count, blk_count
        self.head, self.blk = lax.axis_index("head"), lax.axis_index("blk")
        self.half = blk_count // 2
        self.chip, self.core = self.blk // 2, self.blk % 2
        self.twin = self.blk + 1 - 2 * self.core

    def along(self, axis):
        if axis == "head":
            return self.head, self.head_count
        return self.blk, self.blk_count

    def device(self, axis, index):
        return (index, self.blk) if axis == "head" else (self.head, index)

    def others(self, axis):
        me, size = self.along(axis)
        return [self.device(axis, (me + step) % size) for step in range(1, size)]

    def partners(self):
        beside = self.chip + 1 - 2 * (self.chip % 2)
        beyond = (self.chip + self.half // 2) % self.half
        across = beside + self.half // 2 - self.half * (beside // (self.half // 2))
        return [across, beside, beyond]

    def chips(self):
        return [chip * 2 + self.core for chip in self.partners()]

    def exchange_order(self, axis):
        me, size = self.along(axis)
        if axis == "head":
            return [(step - 1, (me + step) % size, (me + size - step) % size) for step in range(1, size)]
        found = []
        for chip in self.partners():
            for core in (self.core, 1 - self.core):
                found.append(chip * 2 + core)
        found.append(self.twin)
        return [(number, blk, blk) for number, blk in enumerate(found)]

    def near(self):
        return [(self.head, self.twin)] + [(self.head, blk) for blk in self.chips()]


def dma(*dims):
    return pltpu.SemaphoreType.DMA(dims)


def remote(source, target, sent, got, device):
    return pltpu.make_async_remote_copy(
        src_ref=source,
        dst_ref=target,
        send_sem=sent,
        recv_sem=got,
        device_id=device,
        device_id_type=MESH,
    )


def send(source, target, sent, got, device):
    copy = remote(source, target, sent, got, device)
    copy.start()
    return copy


def keep(source, target, done):
    copy = pltpu.make_async_copy(source, target, done)
    copy.start()
    return copy


def scatter(place, axis, source, target, sent, got, wanted=lambda number: True):
    me, size = place.along(axis)
    copies = []
    for number, other, unused in place.exchange_order(axis):
        if not wanted(number):
            continue
        copies.append(
            send(
                source.at[other],
                target.at[me],
                sent.at[number],
                got.at[number],
                place.device(axis, other),
            )
        )
    return copies


def gather(place, axis, source, target, sent, got):
    me, size = place.along(axis)
    copies = []
    for step in range(1, size):
        other = (me + step) % size
        copies.append(
            send(
                source, target.at[me], sent.at[step - 1], got.at[step - 1], place.device(axis, other)
            )
        )
    return copies


class Spread:
    def __init__(self, place, ref, sent, got):
        self.place, self.ref, self.sent, self.got = place, ref, sent, got
        self.direct = [
            self.pass_on(step, place.blk, blk) for step, blk in enumerate(place.chips(), 1)
        ]
        self.rest = [self.pass_on(0, place.blk, place.twin)]

    def pass_on(self, lane, slot, blk):
        return send(
            self.ref.at[slot],
            self.ref.at[slot],
            self.sent.at[lane],
            self.got.at[lane],
            (self.place.head, blk),
        )

    def relay(self):
        place = self.place
        for step, slot in enumerate(place.chips(), 1):
            self.direct[step - 1].wait_recv()
            self.rest.append(self.pass_on(place.half - 1 + step, slot, place.twin))

    def wait(self):
        for copy in self.direct:
            copy.wait_send()
        for copy in self.rest:
            copy.wait()


class Fold:
    def __init__(self, place, terms, theirs, arrived, sent_twin, got_twin, sent, got):
        self.place, self.terms, self.theirs, self.arrived = place, terms, theirs, arrived
        self.sent, self.got = sent, got
        self.order = place.partners() + [place.chip]
        self.across = [
            send(
                terms.at[chip * 2 + 1 - place.core],
                theirs.at[step],
                sent_twin.at[step],
                got_twin.at[step],
                (place.head, place.twin),
            )
            for step, chip in enumerate(self.order)
        ]
        self.onward = []

    def add(self):
        place = self.place
        for step, chip in enumerate(self.order):
            self.across[step].wait_recv()
            total = wide(self.theirs[step]) + wide(self.terms[chip * 2 + place.core])
            self.theirs[step] = total.astype(self.theirs.dtype)
            if step < place.half - 1:
                self.onward.append(
                    send(
                        self.theirs.at[step],
                        self.arrived.at[step],
                        self.sent.at[step],
                        self.got.at[step],
                        (place.head, chip * 2 + place.core),
                    )
                )

    def total(self):
        total = wide(self.theirs[self.place.half - 1])
        for step, copy in enumerate(self.onward):
            copy.wait_recv()
            total = total + wide(self.arrived[step])
        return total

    def wait(self):
        for copy in self.across + self.onward:
            copy.wait_send()


def wait_all(*groups):
    for group in groups:
        for copy in group:
            copy.wait()


def far_block(number, head_count):
    head = lax.axis_index("head")
    found = 0
    for place in range(head_count):
        by_distance = sorted(range(head_count), key=lambda other: -abs(other - place))
        found = found + jnp.where(head == place, by_distance[number], 0)
    return found


def block_at(step, head_count):
    return (lax.axis_index("head") + step) % head_count


class LineGather:
    def __init__(self, place, ref, sent, got):
        self.place, self.ref, self.sent, self.got = place, ref, sent, got
        self.onward(0, place.head)
        self.back(0, place.head)

    def copy(self, way, hop, slot):
        head = self.place.head + 1 - 2 * way
        return remote(
            self.ref.at[slot],
            self.ref.at[slot],
            self.sent.at[way, hop],
            self.got.at[way, hop],
            (head, self.place.blk),
        )

    def sends(self, way, hop):
        head, last = self.place.head, self.place.head_count - 1
        if way == 0:
            return (head >= hop) & (head < last)
        return (head + hop <= last) & (head > 0)

    def has(self, way, hop):
        head, last = self.place.head, self.place.head_count - 1
        return head >= hop if way == 0 else head + hop <= last

    def onward(self, hop, slot):
        @pl.when(self.sends(0, hop))
        def _():
            self.copy(0, hop, slot).start()

    def back(self, hop, slot):
        @pl.when(self.sends(1, hop))
        def _():
            self.copy(1, hop, slot).start()

    def receive(self, hop):
        head, last = self.place.head, self.place.head_count - 1
        for way, slot in ((0, head - hop), (1, head + hop)):

            @pl.when(self.has(way, hop))
            def _():
                self.copy(way, hop - 1, slot).wait_recv()

            if hop < last:
                (self.onward, self.back)[way](hop, slot)

    def receive_all(self):
        for hop in range(1, self.place.head_count):
            self.receive(hop)

    def wait(self):
        for hop in range(self.place.head_count - 1):
            for way in range(2):

                @pl.when(self.sends(way, hop))
                def _():
                    self.copy(way, hop, self.place.head).wait_send()


class LineSum:
    def __init__(self, place, outbox, inbox, sent, got):
        self.place, self.outbox, self.inbox = place, outbox, inbox
        self.sent, self.got = sent, got

    def copy(self, way, slot):
        head = self.place.head + 1 - 2 * way
        return remote(
            self.outbox.at[slot],
            self.inbox.at[way, slot],
            self.sent.at[slot],
            self.got.at[way, slot],
            (head, self.place.blk),
        )

    def add(self, slot, term):
        head, last = self.place.head, self.place.head_count - 1
        self.outbox[slot] = low(term)
        for way, towards, first in ((0, slot > head, head == 0), (1, slot < head, head == last)):

            @pl.when(towards & jnp.logical_not(first))
            def _():
                self.copy(way, slot).wait_recv()
                self.outbox[slot] = low(wide(self.outbox[slot]) + wide(self.inbox[way, slot]))

            @pl.when(towards)
            def _():
                self.copy(way, slot).start()

    def total(self, term):
        head, last = self.place.head, self.place.head_count - 1
        for way, has in ((0, head > 0), (1, head < last)):

            @pl.when(has)
            def _():
                self.copy(way, head).wait_recv()

        for way, has in ((0, head > 0), (1, head < last)):
            term = term + jnp.where(has, wide(self.inbox[way, head]), 0.0)
        return term

    def wait(self):
        for slot in range(self.place.head_count):

            @pl.when(slot > self.place.head)
            def _():
                self.copy(0, slot).wait_send()

            @pl.when(slot < self.place.head)
            def _():
                self.copy(1, slot).wait_send()


def rows_at(block, tokens):
    return pl.ds(pl.multiple_of(block * tokens, tokens), tokens)


def lanes_joined(*parts):
    return jnp.concatenate(parts, axis=1)


def rows_joined(*parts):
    return jnp.concatenate(parts, axis=0)


def packed_rows(piece):
    half = piece.shape[1] // 2
    return lanes_joined(piece[:16], rows_joined(piece[16:, :half], piece[16:, half:]))


def unpacked_rows(packed):
    width = packed.shape[1] * 2 // 3
    rest = packed[:, width:]
    return rows_joined(packed[:, :width], lanes_joined(rest[:8], rest[8:]))


def own_pieces(product, rows, head_count, blk_count, blk):
    return rows_joined(
        *[
            product[(head * blk_count + blk) * rows : (head * blk_count + blk + 1) * rows]
            for head in range(head_count)
        ]
    )


def open_layer(place, r):
    head_count, blk_count = place.head_count, place.blk_count
    head, blk = place.head, place.blk
    tokens, width = r.x.shape
    rows = r.joint_rows.shape[0]
    columns = r.down_0.shape[1]
    head_width = width // head_count
    split = 2 * HEAD_DIM
    joint_width = r.joint.shape[1]
    greet(place.others("head") + place.near())
    names = ["router", "mix", "vectors", "gain_one", "gain_two", "joint_rows", "value_rows"]
    names += ["segment", "position", "routes", "residual", "output_rows", "x"]
    here = {
        name: keep(getattr(r, name), getattr(r, "my_" + name), r.local.at[number])
        for number, name in enumerate(names)
    }
    number = len(names)
    late_own = [keep(r.g, r.g_all.at[head], r.local.at[number])]
    for step, piece in enumerate((r.down_0, r.down_1, r.down_2, r.down_3)):
        at = rows_at(block_at(step, head_count), columns)
        late_own.append(keep(r.down.at[:, at], piece, r.local.at[number + 1 + step]))
    for name in names[:7]:
        here[name].wait()
    marks = rows_joined(
        *[
            wide(ref[...])
            for ref in (r.my_router, r.my_mix, r.my_vectors, r.my_gain_one, r.my_gain_two)
        ]
    )
    marks = rows_joined(marks, jnp.zeros((128 - marks.shape[0], rows), jnp.float32))
    marks = lanes_joined(marks, jnp.zeros((128, 128 - rows), jnp.float32))
    marks = marks.T[:rows]
    both = wide(r.my_joint_rows[...])
    third = wide(r.my_value_rows[...])
    filler = jnp.zeros((rows, HEAD_DIM), jnp.float32)
    for part in range(head_count):
        at = part * head_width
        piece = lanes_joined(
            both[:, at : at + head_width],
            filler,
            both[:, width + at : width + at + head_width],
            third[:, at + split : at + head_width],
            third[:, at : at + split],
            marks,
        )
        r.joint_own[part] = low(packed_rows(piece))
    r.joint_all[blk, head] = r.joint_own[head]
    for name in names[7:]:
        here[name].wait()
    facts = rows_joined(
        wide(r.my_segment[...]),
        wide(r.my_position[...]),
        wide(r.my_routes[...]),
        jnp.zeros((4, tokens), jnp.float32),
        r.my_residual[...],
        jnp.zeros((24 - 8 - ROUTED, tokens), jnp.float32),
    )
    r.facts_own[...] = facts
    r.facts[head] = facts
    r.marks_all[blk, head] = facts[:8]
    greeted(head_count - 1 + place.half)
    first = scatter(place, "head", r.joint_own, r.joint_all.at[blk], r.sent.at[0], r.got.at[0])
    first += gather(place, "head", r.facts_own, r.facts, r.sent.at[1], r.got.at[1])
    r.output_own[...] = low(packed_rows(wide(r.my_output_rows[...])))
    r.output_part[head] = r.output_own[...]
    r.x_all[head] = r.my_x[...]
    for copy in first:
        copy.wait_send()
    tokens_in = LineGather(place, r.x_all, r.sent_line.at[0], r.got_line.at[0])
    for copy in first:
        copy.wait_recv()
    for part in range(head_count):
        r.marks_all[blk, part] = r.facts[part, 0:8, :]
    joint_spread = Spread(place, r.joint_all, r.sent_joint, r.got_joint)
    marks_spread = Spread(place, r.marks_all, r.sent_marks, r.got_marks)
    tokens_in.receive(1)
    joint_spread.relay()
    marks_spread.relay()
    tokens_in.receive(2)
    joint_spread.wait()
    marks_spread.wait()
    column = lax.broadcasted_iota(jnp.int32, (8, 128), 1)
    places = jnp.zeros((8, 128), jnp.float32)
    for part in range(head_count):
        for other in range(blk_count):
            places = jnp.where(
                column == other * head_count + part, r.marks_all[other, part, :, 0:1], places
            )
    r.places[...] = places.astype(jnp.int32)
    for part in range(head_count):
        for other in range(blk_count):
            r.joint_wide[pl.ds((part * blk_count + other) * rows, rows), :] = unpacked_rows(
                wide(r.joint_all[other, part])
            )
    r.joint[...] = low(r.joint_wide[:, :joint_width])
    small_rows = r.joint_wide[:, joint_width:].T
    r.small[...] = small_rows[:SMALL]
    gain = small_rows[GAIN_ONE_AT : GAIN_ONE_AT + 1]
    for hop in range(3, head_count):
        tokens_in.receive(hop)
    outputs_in = LineGather(place, r.output_part, r.sent_line.at[1], r.got_line.at[1])
    late_own[0].wait()
    upstream_in = LineGather(place, r.g_all, r.sent_line.at[2], r.got_line.at[2])
    pair_spreads = []
    cut = r.queries.shape[1]
    for step in range(head_count):
        block = block_at(step, head_count)
        source = wide(r.x_all[block])
        inverse = lax.rsqrt(jnp.mean(source * source, axis=-1, keepdims=True) + EPS)
        rows_normed = low(source * inverse * gain)
        span = rows_at(block, tokens)
        r.normed[span, :] = rows_normed
        product = mul(rows_normed, r.joint[...])
        r.queries[span, :] = low(product[:, :cut])
        r.pairs_all[blk, block] = low(product[:, cut:])
        pair_spreads.append(
            Spread(place, r.pairs_all.at[:, block], r.sent_pairs.at[step], r.got_pairs.at[step])
        )
    for step, spread in enumerate(pair_spreads):
        if 0 < step + 1 < head_count:
            outputs_in.receive(step + 1)
            upstream_in.receive(step + 1)
        spread.relay()
    for spread in pair_spreads:
        spread.wait()
    for line in (tokens_in, outputs_in, upstream_in):
        line.wait()
    wait_all(late_own[1:])


def slots_of(head_count, facts, first, second):
    tokens = first.shape[2]
    earlier = low(
        wide(
            lax.broadcasted_iota(jnp.int32, (tokens, tokens), 0)
            < lax.broadcasted_iota(jnp.int32, (tokens, tokens), 1)
        )
    )
    expert = wide(lax.broadcasted_iota(jnp.int32, (2 * EXPERTS, tokens), 0))
    expert_at = wide(lax.broadcasted_iota(jnp.int32, (EXPERTS, CAP, tokens), 0))
    rank_at = wide(lax.broadcasted_iota(jnp.int32, (EXPERTS, CAP, tokens), 1))
    for head in range(head_count):
        routes = [facts[head, 2 + choice : 3 + choice, :] for choice in range(TOP)]
        named = jnp.where((routes[0] == expert) | (routes[1] == expert), 1.0, 0.0)
        count = mul(low(named), earlier)[:EXPERTS]
        fits = count[:, None, :] == rank_at
        for choice, out in enumerate((first, second)):
            match = (routes[choice][None] == expert_at) & fits
            out[head] = low(jnp.where(match, 1.0, 0.0).reshape(EXPERTS * CAP, tokens))


def place_upstream(place, r):
    head_count = place.head_count
    slots_of(head_count, r.facts, r.first, r.second)
    parts = []
    for number in range(head_count):
        block = far_block(number, head_count)
        found = mul(r.first[block] + r.second[block], r.g_all[block])
        parts.append(found.reshape(EXPERTS, CAP, found.shape[1]))
    r.upstream[...] = low(jnp.concatenate(parts, axis=1))


def visible_blocks(places, period, me, count, chosen, shift, base=0):
    mine, mine_at = places[0, me], places[1, me]

    def look(block, found):
        other, other_at = places[0, block], places[1, block]
        same = other == mine
        shared = (other // period == mine // period) & (other % period == 0) & (mine % period != 0)
        seen = (same & (other_at <= mine_at)) | shared
        chosen[found] = block
        shift[found] = jnp.where(same & (other_at == mine_at), 0, -FAR)
        return found + seen.astype(jnp.int32)

    found = lax.fori_loop(0, count, look, base + jnp.int32(0)) - base
    for extra in range(CHUNK):
        chosen[base + found + extra] = jnp.int32(0)
        shift[base + found + extra] = jnp.int32(FAR)
    return (found + CHUNK - 1) // CHUNK


def chunk_mask(tokens, heads, shift, start):
    row = lax.broadcasted_iota(jnp.int32, (tokens, tokens), 0)
    column = lax.broadcasted_iota(jnp.int32, (tokens, tokens), 1)
    gap = row - column
    parts = [
        jnp.where(gap + shift[start + step] <= 0, 0.0, -jnp.inf) for step in range(CHUNK)
    ]
    return jnp.concatenate([jnp.concatenate(parts, axis=0)] * heads, axis=1)


def chunk_rows(pairs, chosen, start, low_lane, high_lane):
    return jnp.concatenate(
        [pairs[chosen[start + step], :, low_lane:high_lane] for step in range(CHUNK)], axis=0
    )


def lanes_at(rows, first, last):
    lane = lax.broadcasted_iota(jnp.int32, rows.shape, 1)
    return jnp.where((lane >= first) & (lane < last), rows, jnp.zeros_like(rows))


def query_rows_of(queries, head, tokens):
    rows = queries[pl.ds(head * tokens, tokens), :]
    rows = low(wide(rows) * HEAD_DIM ** (-0.5))
    return jnp.concatenate(
        [lanes_at(rows, part * HEAD_DIM, (part + 1) * HEAD_DIM) for part in range(3)], axis=0
    )


def attend(sizes, period, places, queries, pairs, attended, totals, chosen, shift):
    head_count, blk_count = sizes
    blocks, tokens, lanes = pairs.shape
    heads = 3
    blk = lax.axis_index("blk")
    for head in range(head_count):
        chunks = visible_blocks(
            places, period, blk * head_count + head, blocks, chosen, shift
        )
        asked = query_rows_of(queries, head, tokens)

        def step(number, carried):
            top, total, weighted = carried
            start = number * CHUNK
            scores = mul_nt(chunk_rows(pairs, chosen, start, 0, 256), asked)
            scores = scores + chunk_mask(tokens, heads, shift, start)
            new_top = jnp.maximum(top, jnp.max(scores, axis=0, keepdims=True))
            raised = jnp.exp(scores - new_top)
            factor = jnp.exp(top - new_top)
            total = total * factor + jnp.sum(raised, axis=0, keepdims=True)
            mixed = mul_tn(chunk_rows(pairs, chosen, start, 128, lanes), low(raised))
            mixed = jnp.concatenate(
                [mixed[128:192, 0:128], mixed[192:256, 128:256], mixed[64:128, 256:384]], axis=1
            )
            return (new_top, total, weighted * factor + mixed)

        wide_lanes = heads * tokens
        top, total, weighted = lax.fori_loop(
            0,
            chunks,
            step,
            (
                jnp.full((1, wide_lanes), -1e30, jnp.float32),
                jnp.zeros((1, wide_lanes), jnp.float32),
                jnp.zeros((HEAD_DIM, wide_lanes), jnp.float32),
            ),
        )
        outcome = low(weighted / total)
        totals[head] = jnp.broadcast_to(top + jnp.log(total), totals.shape[1:])
        for part in range(heads):
            attended[head, part * HEAD_DIM : (part + 1) * HEAD_DIM, :] = outcome[
                :, part * tokens : (part + 1) * tokens
            ]


def attend_back(sizes, period, places, queries, pairs, attended, totals, given, query_grad, pair_grad, chosen, shift, owner, asked, back, offset, found, summed):
    head_count, blk_count = sizes
    blocks, tokens, lanes = pairs.shape
    heads = 3
    blk = lax.axis_index("blk")
    items = jnp.int32(0)
    for head in range(head_count):
        chunks = visible_blocks(
            places, period, blk * head_count + head, blocks, chosen, shift, items * CHUNK
        )

        def note(number, unused):
            owner[number] = jnp.int32(head)
            return unused

        lax.fori_loop(items, items + chunks, note, 0)
        items = items + chunks
        asked[head] = query_rows_of(queries, head, tokens)
        turned = wide(given[head])
        own = rows_joined(jnp.zeros((HEAD_DIM, tokens), jnp.float32), turned[128:192], turned[0:128])
        own = low(own.T)
        back[head] = rows_joined(
            lanes_at(own, 128, 192), lanes_at(own, 192, 256), lanes_at(own, 64, 128)
        )
        dots = turned * wide(attended[head])
        sums = lanes_joined(
            *[
                jnp.sum(dots[part * HEAD_DIM : (part + 1) * HEAD_DIM], axis=0, keepdims=True)
                for part in range(heads)
            ]
        )
        offset[head] = jnp.broadcast_to(sums, offset.shape[1:])
    owner[items] = jnp.int32(0)
    for extra in range(CHUNK):
        chosen[items * CHUNK + extra] = jnp.int32(0)
        shift[items * CHUNK + extra] = jnp.int32(FAR)
    summed[...] = jnp.zeros_like(summed)
    found[...] = jnp.zeros_like(found)

    def one(item):
        start = item * CHUNK
        head = owner[item]
        keys = chunk_rows(pairs, chosen, start, 0, 256)
        values = chunk_rows(pairs, chosen, start, 128, lanes)
        mine, given_back = asked[head], back[head]
        scores = mul_nt(keys, mine)
        scores = scores + chunk_mask(tokens, heads, shift, start)
        raised = jnp.exp(scores - totals[head, 0:1, :])
        grad_raised = mul_nt(values, given_back)
        grad_scores = low(raised * (grad_raised - offset[head, 0:1, :]))
        key_part = mul(grad_scores, mine)
        value_part = mul(low(raised), given_back)
        both = lanes_joined(
            key_part[:, :128], key_part[:, 128:] + value_part[:, :128], value_part[:, 128:]
        )
        query_part = mul_tn(keys, grad_scores)
        return (
            start,
            head,
            both,
            lanes_joined(
                query_part[0:64, 0:128], query_part[64:128, 128:256], query_part[128:192, 256:384]
            ),
        )

    def step(number, unused):
        results = [one(number * 2 + part) for part in range(2)]
        for start, head, both, query_part in results:
            found[head] = found[head] + query_part
            for block in range(CHUNK):
                at = chosen[start + block]
                summed[at] = summed[at] + both[block * tokens : (block + 1) * tokens]
        return unused

    lax.fori_loop(0, (items + 1) // 2, step, 0)
    for head in range(head_count):
        total = found[head] * HEAD_DIM ** (-0.5)
        stacked = rows_joined(
            *[total[:, part * tokens : (part + 1) * tokens] for part in range(heads)],
            jnp.zeros((HEAD_DIM, tokens), jnp.float32),
        )
        query_grad[pl.ds(head * tokens, tokens), :] = low(stacked.T)
    pair_grad[...] = low(summed[...])


def ffn_rows(number, span, here, r, gate, up, down, lane):
    width = r.grads_in.shape[2]
    group = lane.shape[0]
    blk_count, span_rows = r.slots_in.shape[0], group // r.slots_in.shape[0]
    entry = r.slots_in[:, span, :].reshape(group, width + 128)
    rows = entry[:, :width]
    r.taken[here, :] = rows
    tail = wide(entry[:, width:])
    share = tail[:, 0:1] + tail[:, 64:65]
    scaled_rows = low(share * wide(r.grads_in[:, span, :].reshape(group, width)))
    r.scaled[here, :] = scaled_rows
    gate_pre = mul(rows, gate)
    up_pre = mul(rows, up)
    sigmoid = 1.0 / (1.0 + jnp.exp(-gate_pre))
    activated = gate_pre * sigmoid
    hidden_rows = low(activated * up_pre)
    r.hidden[here, :] = hidden_rows
    grad_hidden = mul(scaled_rows, down)
    gate_rows = low(grad_hidden * up_pre * sigmoid * (1.0 + gate_pre * (1.0 - sigmoid)))
    up_rows = low(grad_hidden * activated)
    r.grad_gate[here, :] = gate_rows
    r.grad_up[here, :] = up_rows
    dots = jnp.sum(wide(hidden_rows) * grad_hidden, axis=1, keepdims=True)
    grad_rows = mul_nt(gate_rows, gate) + mul_nt(up_rows, up)
    high, rest = halves(dots)
    tail_out = jnp.where(lane < 64, wide(high), wide(rest))
    r.back[:, span, :] = low(lanes_joined(grad_rows, tail_out)).reshape(
        blk_count, span_rows, width + 128
    )


def middle_layer(place, r):
    head_count, blk_count = place.head_count, place.blk_count
    head, blk = place.head, place.blk
    tokens, width = r.g.shape
    columns = r.gate_all.shape[2]
    head_width = r.gate_all.shape[1]
    rows = head_width // blk_count
    half_count = head_count // 2
    greet(place.others("head") + place.others("blk"))
    r.attended_all[head] = r.attended[...]
    for part in range(head_count):
        r.output_all[blk, part] = r.output_part[part]
    own_weights = [
        keep(ref.at[:, rows_at(head, columns)], held.at[head], r.local.at[number])
        for number, (ref, held) in enumerate(((r.gate, r.gate_all), (r.up, r.up_all)))
    ]
    for step, piece in enumerate((r.down_0, r.down_1, r.down_2, r.down_3)):
        r.down_all[(head + head_count - step) % head_count] = piece[...]
    greeted(head_count + blk_count - 2)
    rows_in = LineGather(place, r.attended_all, r.sent_line, r.got_line)
    output_spread = Spread(place, r.output_all, r.sent_output, r.got_output)
    place_upstream(place, r)
    r.grads_in[blk] = r.upstream[blk]
    routed = scatter(place, "blk", r.upstream, r.grads_in, r.sent_grads, r.got_grads)
    rows_in.receive(1)
    output_spread.relay()
    rows_in.receive(2)
    output_spread.wait()
    for part in range(head_count):
        for other in range(blk_count):
            r.output_wide[pl.ds((part * blk_count + other) * rows, rows), :] = unpacked_rows(
                wide(r.output_all[other, part])
            )
    r.output[...] = low(r.output_wide[...])
    router = low(r.small[0:16])
    expert = wide(lax.broadcasted_iota(jnp.int32, (16, tokens), 0))
    lane = lax.broadcasted_iota(jnp.int32, (EXPERTS * CAP, 128), 1)
    gain = r.small[GAIN_TWO_AT : GAIN_TWO_AT + 1]
    for hop in range(3, head_count):
        rows_in.receive(hop)
    weights_in = []
    for kind, (ref, held) in enumerate(((r.gate, r.gate_all), (r.up, r.up_all))):
        copies = []
        for away in range(1, head_count):
            other = (head + away) % head_count
            copies.append(
                send(
                    ref.at[:, rows_at(other, columns)],
                    held.at[head],
                    r.sent_weights.at[kind, away - 1],
                    r.got_weights.at[kind, away - 1],
                    (other, blk),
                )
            )
        weights_in.append(copies)
    parts = []
    for number in range(head_count):
        block = far_block(number, head_count)
        found = jnp.concatenate(
            [r.attended_all[source, block] for source in range(head_count)], axis=0
        ).T
        source = wide(r.x_all[block]) + mul(found, r.output[...])
        inverse = lax.rsqrt(jnp.mean(source * source, axis=-1, keepdims=True) + EPS)
        normed = low(source * inverse * gain)
        if number == head_count - 1:
            r.middle[...] = source
            r.normed[...] = normed
            r.attended_home[...] = low(wide(found).T)
        facts = r.facts[block]
        logits = mul_nt(router, normed) + facts[8:24]
        picked = [
            jnp.sum(
                jnp.where(facts[2 + choice : 3 + choice] == expert, logits, 0.0),
                axis=0,
                keepdims=True,
            )
            for choice in range(TOP)
        ]
        highest = jnp.maximum(picked[0], picked[1])
        raised = [jnp.exp(value - highest) for value in picked]
        total = raised[0] + raised[1]
        share = [value / total for value in raised]
        r.weights[block] = jnp.concatenate(
            share + [jnp.zeros((6, tokens), jnp.float32)], axis=0
        )
        places = [r.first[block], r.second[block]]
        of_slot = jnp.sum(
            wide(places[0]) * share[0] + wide(places[1]) * share[1], axis=1, keepdims=True
        )
        high, rest = halves(of_slot)
        entry = lanes_joined(
            mul(places[0] + places[1], normed), jnp.where(lane < 64, wide(high), wide(rest))
        )
        parts.append(entry.reshape(EXPERTS, CAP, width + 128))
        if number % 2:
            span = pl.ds((number - 1) * CAP, 2 * CAP)
            r.slots[:, span, :] = low(jnp.concatenate(parts, axis=1))
            parts = []
            r.slots_in[blk, span, :] = r.slots[blk, span, :]
            routed += scatter(
                place,
                "blk",
                r.slots.at[:, span],
                r.slots_in.at[:, span],
                r.sent_slots.at[number // 2],
                r.got_slots.at[number // 2],
            )
    rows_in.wait()
    wait_all(routed)
    wait_all(own_weights, *weights_in)

    depth = head_count * head_width
    gate, up, down = [
        ref[...].reshape(depth, columns) for ref in (r.gate_all, r.up_all, r.down_all)
    ]
    span_rows = 2 * CAP
    group = blk_count * span_rows
    lane = lax.broadcasted_iota(jnp.int32, (group, 128), 1)
    routed = []
    for number in range(half_count):
        span = pl.ds(number * span_rows, span_rows)
        here = pl.ds(number * group, group)
        ffn_rows(number, span, here, r, gate, up, down, lane)
        r.back_in[blk, span, :] = r.back[blk, span, :]
        routed.append(
            scatter(
                place,
                "blk",
                r.back.at[:, span],
                r.back_in.at[:, span],
                r.sent_back.at[number],
                r.got_back.at[number],
            )
        )
    r.down_parts[...] = low(mul(r.scaled[...].T, r.hidden[...])).reshape(r.down_parts.shape)
    r.down_in[head] = r.down_parts[head]
    far_away = head_count // 2 - 1
    cut = head_width // 4 * 3
    down_copies = scatter(
        place,
        "head",
        r.down_parts.at[:, pl.ds(0, cut)],
        r.down_in.at[:, pl.ds(0, cut)],
        r.sent_down,
        r.got_down,
        lambda number: number == far_away,
    )
    down_copies += scatter(
        place, "head", r.down_parts, r.down_in, r.sent_down, r.got_down, lambda number: number != far_away
    )
    for number in range(half_count):
        span = pl.ds(number * span_rows, span_rows)
        here = pl.ds(number * group, group)
        r.outs[:, span, :] = low(mul_nt(r.hidden[here, :], down)).reshape(
            blk_count, span_rows, width
        )
    r.outs_in[blk] = r.outs[blk]
    out_copies = scatter(place, "blk", r.outs, r.outs_in, r.sent_outs, r.got_outs)
    r.turned[...] = r.taken[...].T
    for step, piece in enumerate((r.early_0, r.early_1, r.early_2, r.early_3)):
        here = rows_at(block_at(step, head_count), head_width)
        for kind, right in enumerate((r.grad_gate, r.grad_up)):
            piece[kind] = low(mul(r.turned[here, :], right[...]))
    narrow = lax.broadcasted_iota(jnp.int32, (tokens, 128), 1)
    shares_in = LineSum(place, r.parts, r.parts_in, r.sent_parts, r.got_parts)
    dot_copies = []
    for number in range(head_count):
        block = far_block(number, head_count)
        if number % 2 == 0:
            for copy in routed[number // 2]:
                copy.wait_recv()
            entries = wide(r.back_in[:, pl.ds(number * CAP, span_rows), :])
        entry = entries[:, (number % 2) * CAP : (number % 2 + 1) * CAP]
        entry = low(entry.reshape(EXPERTS * CAP, width + 128))
        found = [mul_tn(placed[block], entry) for placed in (r.first, r.second)]
        dots = [
            found[choice][:, width : width + 1] + found[choice][:, width + 64 : width + 65]
            for choice in range(TOP)
        ]
        dots = jnp.where(narrow == 0, dots[0], jnp.where(narrow == 1, dots[1], 0.0))
        r.dots[block] = dots.T[0:8]
        share = found[0][:, :width] + found[1][:, :width]
        if number < head_count - 1:
            away = (block + head_count - head) % head_count
            dot_copies.append(
                send(
                    r.dots.at[block],
                    r.dots_in.at[head],
                    r.sent_dots.at[away - 1],
                    r.got_dots.at[away - 1],
                    (block, blk),
                )
            )
            shares_in.add(block, share)
    down_copies += scatter(
        place,
        "head",
        r.down_parts.at[:, pl.ds(cut, head_width - cut)],
        r.down_in.at[:, pl.ds(cut, head_width - cut)],
        r.sent_down_rest,
        r.got_down_rest,
        lambda number: number == far_away,
    )
    home = home_early(place, r)
    r.dots_in[head] = r.dots[head]
    grad_slots = shares_in.total(share)
    for copy in dot_copies:
        copy.wait_recv()
    home_middle(place, r, home, grad_slots)
    r.given_parts[...] = low(mul_nt(r.output[...], r.middle_low[...])).reshape(
        r.given_parts.shape
    )
    r.given[head] = r.given_parts[head]
    given_copies = scatter(place, "head", r.given_parts, r.given, r.sent_given, r.got_given)
    for copy in out_copies:
        copy.wait_recv()
    for number in range(head_count):
        block = far_block(number, head_count)
        if number % 2 == 0:
            entries = wide(r.outs_in[:, pl.ds(number * CAP, span_rows), :])
        entry = entries[:, (number % 2) * CAP : (number % 2 + 1) * CAP]
        entry = low(entry.reshape(EXPERTS * CAP, width))
        shares = r.weights[block].T
        r.out_parts[block] = low(
            shares[:, 0:1] * mul_tn(r.first[block], entry)
            + shares[:, 1:2] * mul_tn(r.second[block], entry)
        )
    home_late(place, r, home)
    product = mul(r.attended_home[...], r.middle_low[...])
    for other in range(blk_count):
        r.output_terms[other] = low(own_pieces(product, rows, head_count, blk_count, other))
    for copies in routed + [out_copies, dot_copies]:
        for copy in copies:
            copy.wait_send()
    shares_in.wait()
    wait_all(down_copies, given_copies)
    pl.semaphore_signal(
        r.done, inc=1, device_id=(head, place.twin), device_id_type=MESH
    )
    pl.semaphore_wait(r.done, 1)


def home_early(place, r):
    head_count = place.head_count
    tokens, width = r.middle.shape
    share_rows = r.weights[place.head]
    columns = rows_joined(share_rows, r.facts[place.head, 0:8, :]).T
    share = [columns[:, choice : choice + 1] for choice in range(TOP)]
    route_of = [columns[:, 10 + choice : 11 + choice] for choice in range(TOP)]
    upstream = wide(r.g[...])
    normed_wide = wide(r.normed[...])
    small_low = low(r.small[...])
    seen = mul_nt(r.normed[...], small_low)
    met = mul_nt(r.g[...], small_low)

    def weight_of(expert):
        return sum(
            share[choice] * jnp.where(route_of[choice] == expert, 1.0, 0.0)
            for choice in range(TOP)
        )

    copy_share = weight_of(EXPERTS + 1)
    const_share = [weight_of(EXPERTS + 2 + const) for const in range(2)]
    mixing = []
    for const in range(2):
        at = MIX_AT + 2 * const
        pair = [seen[:, at + part : at + part + 1] for part in range(2)]
        highest = jnp.maximum(pair[0], pair[1])
        raised = [jnp.exp(value - highest) for value in pair]
        total = raised[0] + raised[1]
        mixing.append([value / total for value in raised])
    copy_dot = jnp.sum(upstream * normed_wide, axis=-1, keepdims=True)
    vector_dot = [met[:, VECTOR_AT + const : VECTOR_AT + const + 1] for const in range(2)]
    const_dot = [
        mixing[const][0] * copy_dot + mixing[const][1] * vector_dot[const] for const in range(2)
    ]
    special = []
    for choice in range(TOP):
        found = jnp.where(route_of[choice] == EXPERTS + 1, copy_dot, 0.0)
        for const in range(2):
            found = found + jnp.where(
                route_of[choice] == EXPERTS + 2 + const, const_dot[const], 0.0
            )
        special.append(share[choice] * found)
    lane = lax.broadcasted_iota(jnp.int32, (tokens, 128), 1)
    vector_share = jnp.zeros((tokens, 128), jnp.float32)
    mix_grad = jnp.zeros((tokens, 128), jnp.float32)
    for const in range(2):
        grad_mix = [const_share[const] * copy_dot, const_share[const] * vector_dot[const]]
        mean = mixing[const][0] * grad_mix[0] + mixing[const][1] * grad_mix[1]
        for part in range(2):
            mix_grad = mix_grad + jnp.where(
                lane == MIX_AT + 2 * const + part,
                mixing[const][part] * (grad_mix[part] - mean),
                0.0,
            )
        vector_share = vector_share + jnp.where(
            lane == VECTOR_AT + const, const_share[const] * mixing[const][1], 0.0
        )
    direct = copy_share + const_share[0] * mixing[0][0] + const_share[1] * mixing[1][0]
    r.direct[...] = direct * upstream
    source = r.middle[...]
    inverse = lax.rsqrt(jnp.mean(source * source, axis=-1, keepdims=True) + EPS)
    vectors = [r.small[VECTOR_AT + const : VECTOR_AT + const + 1] for const in range(2)]
    mixed = copy_share * normed_wide
    for const in range(2):
        mixed = mixed + const_share[const] * (
            mixing[const][0] * normed_wide + mixing[const][1] * vectors[const]
        )
    r.mixture[...] = source + mixed
    table = rows_joined(small_low[0:16], jnp.zeros((128 - 16, width), jnp.bfloat16))
    return types.SimpleNamespace(
        share=share,
        route_of=route_of,
        special=special,
        mix_grad=mix_grad,
        vector_share=vector_share,
        inverse=inverse,
        table=table,
    )


def home_middle(place, r, home, grad_slots):
    tokens, width = r.middle.shape
    dots = r.dots_in[0]
    for head in range(1, place.head_count):
        dots = dots + r.dots_in[head]
    dots = dots.T
    product = [dots[:, choice : choice + 1] + home.special[choice] for choice in range(TOP)]
    both = product[0] + product[1]
    lane = wide(lax.broadcasted_iota(jnp.int32, (tokens, 128), 1))
    routing = jnp.zeros((tokens, 128), jnp.float32)
    for choice in range(TOP):
        routing = routing + jnp.where(
            lane == home.route_of[choice], product[choice] - home.share[choice] * both, 0.0
        )
    spread_high, spread_rest = halves(routing + home.mix_grad)
    grad_normed = (
        r.direct[...] + grad_slots + mul(spread_high, home.table) + mul(spread_rest, home.table)
    )
    source = r.middle[...]
    scaled = grad_normed * r.small[GAIN_TWO_AT : GAIN_TWO_AT + 1]
    result = (
        wide(r.g[...])
        + home.inverse * scaled
        - source * home.inverse**3 * jnp.mean(scaled * source, axis=-1, keepdims=True)
    )
    r.middle_grad[...] = result
    r.middle_low[...] = low(result)
    r.direct[...] = grad_normed
    home.routing, home.spread = routing, (spread_high, spread_rest)


def home_late(place, r, home):
    width = r.middle.shape[1]
    r.residual_grad[...] = home.routing.T[:ROUTED]
    gain_row = jnp.sum(r.direct[...] * r.middle[...] * home.inverse, axis=0, keepdims=True)
    vector_high, vector_rest = halves(home.vector_share)
    by_normed = mul_tn(home.spread[0], r.normed[...]) + mul_tn(home.spread[1], r.normed[...])
    by_upstream = mul_tn(vector_high, r.g[...]) + mul_tn(vector_rest, r.g[...])
    row = lax.broadcasted_iota(jnp.int32, (SMALL, width), 0)
    r.small_grad[...] = jnp.where(
        row == GAIN_TWO_AT, gain_row, by_normed[:SMALL] + by_upstream[:SMALL]
    )


def close_layer(place, r):
    head_count, blk_count = place.head_count, place.blk_count
    head, blk = place.head, place.blk
    tokens, width = r.input_grad.shape
    rows = width // (head_count * blk_count)
    cut = r.query_grad.shape[1]
    joint_width = r.joint.shape[1]
    greet(place.others("head") + place.near())
    flat = jnp.concatenate(
        [r.small_grad[...], jnp.zeros((128 - SMALL, width), jnp.float32)], axis=0
    ).T
    for part in range(head_count):
        for other in range(blk_count):
            at = (part * blk_count + other) * rows
            r.small_terms[other, part * rows : (part + 1) * rows, :] = flat[at : at + rows]
    greeted(place.head_count - 1 + place.half)
    outs_in = LineSum(place, r.out_sums, r.out_in, r.sent_out, r.got_out)
    at_end = (head == 0) | (head == head_count - 1)

    @pl.when(at_end)
    def _():
        for number in range(head_count - 1):
            block = far_block(number, head_count)
            outs_in.add(block, wide(r.out_parts[block]))


    def fold(number, terms, theirs, arrived):
        return Fold(
            place,
            terms,
            theirs,
            arrived,
            r.sent_twin.at[number],
            r.got_twin.at[number],
            r.sent_blk.at[number],
            r.got_blk.at[number],
        )

    pair_folds = []
    for number in range(head_count):
        block = far_block(number, head_count)
        pair_folds.append(
            fold(
                number,
                r.pair_terms.at[:, block],
                r.theirs_pairs.at[number],
                r.arrived_pairs.at[number],
            )
        )
    output_fold = fold(head_count, r.output_terms, r.theirs_output, r.arrived_output)
    small_fold = fold(head_count + 1, r.small_terms, r.theirs_small, r.arrived_small)
    for one in pair_folds:
        one.add()
    output_fold.add()
    small_fold.add()
    r.turned[...] = r.normed[...].T
    r.early_rows[...] = mul_nt(r.query_grad[...], r.joint[:, :cut])
    early = mul(r.turned[...], r.query_grad[...])
    rows_in = LineSum(place, r.row_parts, r.rows_in, r.sent_rows, r.got_rows)
    for number in range(head_count - 1):
        block = far_block(number, head_count)

        @pl.when(jnp.logical_not(at_end))
        def _():
            outs_in.add(block, wide(r.out_parts[block]))

    gain_row = jnp.zeros((1, width), jnp.float32)
    for number in range(head_count):
        block = far_block(number, head_count)
        here = rows_at(block, tokens)
        part = low(pair_folds[number].total())
        r.grads[here, :] = part
        grad_normed = r.early_rows[here, :] + mul_nt(part, r.joint[:, cut:])
        if number < head_count - 1:
            rows_in.add(block, grad_normed)

        else:
            own_rows = grad_normed
        source = wide(r.x_all[block])
        inverse = lax.rsqrt(jnp.mean(source * source, axis=-1, keepdims=True) + EPS)
        gain_row = gain_row + jnp.sum(grad_normed * source * inverse, axis=0, keepdims=True)
    product = jnp.concatenate([early, mul(r.turned[...], r.grads[...])], axis=1)
    for other in range(blk_count):
        r.joint_terms[other] = low(own_pieces(product, rows, head_count, blk_count, other))
    joint_fold = fold(head_count + 2, r.joint_terms, r.theirs_joint, r.arrived_joint)
    owners = head_count * blk_count
    owner = lax.broadcasted_iota(jnp.int32, (owners, width), 0)
    column = lax.broadcasted_iota(jnp.int32, (owners, width), 1)
    owned = jnp.where(column // rows == owner, gain_row, 0.0)
    feature = lax.broadcasted_iota(jnp.int32, (width, 128), 0)
    target = lax.broadcasted_iota(jnp.int32, (width, 128), 1)
    moved = low(jnp.where(feature % rows == target, 1.0, 0.0))
    high, rest = halves(owned)
    by_owner = mul(high, moved) + mul(rest, moved)
    for other in range(blk_count):
        r.gain_terms[other] = jnp.concatenate(
            [
                by_owner[part * blk_count + other : part * blk_count + other + 1]
                for part in range(head_count)
            ]
            + [jnp.zeros((8 - head_count, 128), jnp.float32)],
            axis=0,
        )
    gain_fold = fold(head_count + 3, r.gain_terms, r.theirs_gain, r.arrived_gain)
    r.small_sums[...] = small_fold.total().reshape(head_count, rows, 128)
    r.small_in[head] = r.small_sums[head]
    last = scatter(place, "head", r.small_sums, r.small_in, r.sent_last.at[0], r.got_last.at[0])
    output_sum = output_fold.total()
    for part in range(head_count):
        r.output_sums[part] = low(packed_rows(output_sum[part * rows : (part + 1) * rows]))
    r.output_in[head] = r.output_sums[head]
    last += scatter(place, "head", r.output_sums, r.output_in, r.sent_last.at[3], r.got_last.at[3])
    joint_fold.add()
    gain_fold.add()
    joint_sum = joint_fold.total()
    filler = jnp.zeros((PAD - rows, joint_width), jnp.float32)
    for part in range(head_count):
        r.joint_sums[part] = low(rows_joined(joint_sum[part * rows : (part + 1) * rows], filler))
    r.joint_out[head] = r.joint_sums[head]
    last += scatter(place, "head", r.joint_sums, r.joint_out, r.sent_last.at[1], r.got_last.at[1])
    gain_now = gain_fold.total()
    for part in range(head_count):
        r.gain_sums[part] = jnp.broadcast_to(gain_now[part : part + 1], (8, 128))
    r.gain_in[head] = r.gain_sums[head]
    last += scatter(place, "head", r.gain_sums, r.gain_in, r.sent_last.at[2], r.got_last.at[2])
    total = r.mixture[...] + outs_in.total(wide(r.out_parts[head]))
    r.layer_out[...] = low(total)
    grad_normed = rows_in.total(own_rows)
    source = wide(r.x_all[head])
    inverse = lax.rsqrt(jnp.mean(source * source, axis=-1, keepdims=True) + EPS)
    scaled = grad_normed * r.small[GAIN_ONE_AT : GAIN_ONE_AT + 1]
    r.input_grad[...] = (
        r.middle_grad[...]
        + inverse * scaled
        - source * inverse**3 * jnp.mean(scaled * source, axis=-1, keepdims=True)
    )
    for copy in last:
        copy.wait_recv()
    output_sum = wide(r.output_in[0])
    for part in range(1, head_count):
        output_sum = output_sum + wide(r.output_in[part])
    r.output_grad[...] = unpacked_rows(output_sum)
    r.small_total[...] = sum(r.small_in[part] for part in range(head_count))
    r.gain_total[...] = sum(r.gain_in[part] for part in range(head_count))
    for one in pair_folds + [output_fold, small_fold, joint_fold, gain_fold]:
        one.wait()
    outs_in.wait()
    rows_in.wait()
    for copy in last:
        copy.wait_send()


def finish(
    sizes,
    piece_0,
    piece_1,
    piece_2,
    piece_3,
    down_in,
    joint_in,
    small_in,
    gain_in,
    sums_in,
    rows_in,
    layer_in,
    residual_in,
    gate,
    up,
    down,
    joint,
    value,
    gain_one,
    gain_two,
    router,
    mix,
    vectors,
    output,
    rows,
    layer,
    residual,
):
    head_count, blk_count = sizes
    mine = lax.axis_index("head")
    columns = piece_0.shape[2]
    for step, piece in enumerate((piece_0, piece_1, piece_2, piece_3)):
        source = (mine + head_count - step) % head_count
        at = rows_at(source, columns)
        gate[:, at] = wide(piece[0])
        up[:, at] = wide(piece[1])
    for source in range(head_count):
        down[:, source * columns : (source + 1) * columns] = wide(down_in[source])
    own_rows = joint.shape[0]
    parts = [wide(joint_in[source])[:own_rows] for source in range(head_count)]
    joint[...] = lanes_joined(
        *[part[:, 0:192] for part in parts], *[part[:, 256:448] for part in parts]
    )
    value[...] = lanes_joined(
        *[lanes_joined(part[:, 512:640], part[:, 448:512]) for part in parts]
    )
    flat = small_in[...]
    flat = jnp.concatenate(
        [flat, jnp.zeros((128 - own_rows, 128), jnp.float32)], axis=0
    ).T[:SMALL, :own_rows]
    gain_one[...] = gain_in[0:1, :own_rows]
    gain_two[...] = flat[GAIN_TWO_AT : GAIN_TWO_AT + 1]
    router[...] = flat[ROUTER_AT : ROUTER_AT + ROUTED]
    mix[...] = flat[MIX_AT : MIX_AT + 4]
    vectors[...] = flat[VECTOR_AT : VECTOR_AT + 2]
    output[...] = sums_in[...]
    rows[...] = rows_in[...]
    layer[...] = layer_in[...]
    residual[...] = residual_in[...]


def after(values, *signals):
    return lax.optimization_barrier((values, signals))[0]


def around_heads(pieces):
    count = len(pieces)
    return [pieces[0]] + [
        lax.ppermute(pieces[step], "head", [(i, (i + step) % count) for i in range(count)])
        for step in range(1, count)
    ]


def fast_shards(
    inputs,
    cotangent,
    segment,
    position,
    routes,
    gate_residual,
    first_gain,
    second_gain,
    query_key_weight,
    value_weight,
    output_weight,
    router_weight,
    const_gate,
    const_vectors,
    gate_weight,
    up_weight,
    down_weight,
):
    tokens, width = inputs.shape
    head_count = lax.axis_size("head")
    blk_count = lax.axis_size("blk")
    sizes = (head_count, blk_count)
    part = functools.partial
    half = blk_count // 2
    period = tokens * blk_count // CONT_LEN + 1
    head_width = width // head_count
    column_rows = head_count * tokens
    weight_rows = query_key_weight.shape[0]
    columns = gate_weight.shape[1] // head_count
    slot_rows = head_count * CAP
    slot_total = blk_count * slot_rows
    joint_width = 10 * HEAD_DIM
    pair_width = 6 * HEAD_DIM
    others, near = head_count - 1, blk_count - 1
    packed = width * 3 // 2
    joint_packed = (joint_width + 128) * 3 // 2

    opened_from = dict(
            x=inputs,
            joint_rows=query_key_weight,
            value_rows=value_weight,
            output_rows=output_weight,
            router=router_weight.T,
            mix=const_gate.T,
            vectors=const_vectors.T,
            gain_one=first_gain[None],
            gain_two=second_gain[None],
            segment=segment[None],
            position=position[None],
            routes=routes.T,
            residual=gate_residual.T,
            g=cotangent,
            down=down_weight.T,
    )
    opened = exchange(
        open_layer,
        sizes,
        opened_from,
        dict(
            x_all=shape((head_count, tokens, width)),
            facts=shape((head_count, 24, tokens), jnp.float32),
            places=shape((8, 128), jnp.int32),
            g_all=shape((head_count, tokens, width)),
            normed=shape((column_rows, width)),
            queries=shape((column_rows, 4 * HEAD_DIM)),
            pairs_all=shape((blk_count, head_count, tokens, pair_width)),
            joint=shape((width, joint_width)),
            output_part=shape((head_count, 16, packed)),
            small=shape((SMALL, width), jnp.float32),
            down_0=shape((head_width, columns)),
            down_1=shape((head_width, columns)),
            down_2=shape((head_width, columns)),
            down_3=shape((head_width, columns)),
        ),
        dict(
            my_router=vmem(ROUTED, weight_rows),
            my_mix=vmem(4, weight_rows),
            my_vectors=vmem(2, weight_rows),
            my_gain_one=vmem(1, weight_rows),
            my_gain_two=vmem(1, weight_rows),
            my_joint_rows=vmem(*query_key_weight.shape),
            my_value_rows=vmem(*value_weight.shape),
            my_segment=vmem(1, tokens, dtype=jnp.int32),
            my_position=vmem(1, tokens, dtype=jnp.int32),
            my_routes=vmem(TOP, tokens, dtype=jnp.int32),
            my_residual=vmem_wide(ROUTED, tokens),
            my_output_rows=vmem(*output_weight.shape),
            my_x=vmem(tokens, width),
            marks_all=vmem_wide(blk_count, head_count, 8, tokens),
            joint_own=vmem(head_count, 16, joint_packed),
            output_own=vmem(16, packed),
            facts_own=vmem_wide(24, tokens),
            joint_all=vmem(blk_count, head_count, 16, joint_packed),
            joint_wide=vmem_wide(width, joint_width + 128),
            local=dma(18),
            sent=dma(2, others),
            got=dma(2, others),
            sent_line=dma(3, 2, others),
            got_line=dma(3, 2, others),
            sent_joint=dma(near),
            got_joint=dma(near),
            sent_marks=dma(near),
            got_marks=dma(near),
            sent_pairs=dma(head_count, near),
            got_pairs=dma(head_count, near),
        ),
        0,
        far=tuple(opened_from) + ("g_all", "down_0", "down_1", "down_2", "down_3"),
        room=63,
    )
    down_pieces = around_heads([opened.down_0, opened.down_1, opened.down_2, opened.down_3])
    pairs_all = opened.pairs_all.reshape(blk_count * head_count, tokens, pair_width)
    lists = [
        pltpu.SMEM((blk_count * head_count + CHUNK,), jnp.int32),
        pltpu.SMEM((blk_count * head_count + CHUNK,), jnp.int32),
    ]
    items_at_most = head_count * (blk_count * head_count // CHUNK + 1) + 1
    long_lists = [pltpu.SMEM((items_at_most * CHUNK + CHUNK,), jnp.int32)] * 2
    attended, totals = compute(
        part(attend, sizes, period),
        [
            shape((head_count, head_width, tokens)),
            shape((head_count, 8, 3 * tokens), jnp.float32),
        ],
        [opened.places, opened.queries, pairs_all],
        lists,
        1,
    )
    halved = head_count // 2
    went = exchange(
        middle_layer,
        sizes,
        dict(
            attended=attended,
            g_all=opened.g_all,
            x_all=opened.x_all,
            output_part=opened.output_part,
            small=opened.small,
            facts=opened.facts,
            g=cotangent,
            gate=gate_weight,
            up=up_weight,
            down_0=down_pieces[0],
            down_1=down_pieces[1],
            down_2=down_pieces[2],
            down_3=down_pieces[3],
        ),
        dict(
            output_terms=shape((blk_count, head_count * weight_rows, width)),
            early_0=shape((2, head_width, columns)),
            early_1=shape((2, head_width, columns)),
            early_2=shape((2, head_width, columns)),
            early_3=shape((2, head_width, columns)),
            down_in=shape((head_count, head_width, columns)),
            out_parts=shape((head_count, tokens, width)),
            middle_grad=shape((tokens, width), jnp.float32),
            given=shape((head_count, head_width, tokens)),
            residual_grad=shape((ROUTED, tokens), jnp.float32),
            small_grad=shape((SMALL, width), jnp.float32),
            mixture=shape((tokens, width), jnp.float32),
        ),
        dict(
            attended_all=vmem(head_count, head_count, head_width, tokens),
            attended_home=vmem(width, tokens),
            first=vmem(head_count, EXPERTS * CAP, tokens),
            second=vmem(head_count, EXPERTS * CAP, tokens),
            upstream=vmem(EXPERTS, slot_rows, width),
            output=vmem(width, width),
            output_all=vmem(blk_count, head_count, 16, packed),
            output_wide=vmem_wide(width, width),
            slots=vmem(EXPERTS, slot_rows, width + 128),
            slots_in=vmem(blk_count, slot_rows, width + 128),
            grads_in=vmem(blk_count, slot_rows, width),
            middle=vmem_wide(tokens, width),
            normed=vmem(tokens, width),
            weights=vmem_wide(head_count, 8, tokens),
            gate_all=vmem(head_count, head_width, columns),
            up_all=vmem(head_count, head_width, columns),
            down_all=vmem(head_count, head_width, columns),
            taken=vmem(slot_total, width),
            turned=vmem(width, slot_total),
            hidden=vmem(slot_total, columns),
            grad_gate=vmem(slot_total, columns),
            grad_up=vmem(slot_total, columns),
            scaled=vmem(slot_total, width),
            back=vmem(blk_count, slot_rows, width + 128),
            outs=vmem(blk_count, slot_rows, width),
            back_in=vmem(blk_count, slot_rows, width + 128),
            outs_in=vmem(blk_count, slot_rows, width),
            parts=vmem(head_count, tokens, width),
            parts_in=vmem(2, head_count, tokens, width),
            dots=vmem_wide(head_count, 8, tokens),
            dots_in=vmem_wide(head_count, 8, tokens),
            down_parts=vmem(head_count, head_width, columns),
            middle_low=vmem(tokens, width),
            direct=vmem_wide(tokens, width),
            given_parts=vmem(head_count, head_width, tokens),
            local=dma(2),
            sent_line=dma(2, others),
            got_line=dma(2, others),
            sent_dots=dma(others),
            got_dots=dma(others),
            sent_output=dma(near),
            got_output=dma(near),
            sent_grads=dma(near),
            got_grads=dma(near),
            sent_weights=dma(2, others),
            got_weights=dma(2, others),
            sent_slots=dma(halved, near),
            got_slots=dma(halved, near),
            sent_back=dma(halved, near),
            got_back=dma(halved, near),
            sent_outs=dma(near),
            got_outs=dma(near),
            sent_down=dma(others),
            got_down=dma(others),
            sent_down_rest=dma(others),
            got_down_rest=dma(others),
            sent_parts=dma(head_count),
            got_parts=dma(2, head_count),
            sent_given=dma(others),
            got_given=dma(others),
            done=pltpu.SemaphoreType.REGULAR,
        ),
        1,
        far=("gate", "up"),
    )
    grad_pieces = around_heads([went.early_0, went.early_1, went.early_2, went.early_3])
    query_grad, pair_grad = compute(
        part(attend_back, sizes, period),
        [shape(opened.queries.shape), shape(pairs_all.shape)],
        [
            opened.places,
            opened.queries,
            pairs_all,
            attended,
            totals,
            went.given,
        ],
        long_lists
        + [
            pltpu.SMEM((items_at_most,), jnp.int32),
            vmem(head_count, 3 * tokens, 4 * HEAD_DIM),
            vmem(head_count, 3 * tokens, 4 * HEAD_DIM),
            vmem_wide(head_count, 8, 3 * tokens),
            vmem_wide(head_count, HEAD_DIM, 3 * tokens),
            vmem_wide(*pairs_all.shape),
        ],
        1,
    )
    folds = head_count + 4
    closed = exchange(
        close_layer,
        sizes,
        dict(
            pair_terms=pair_grad.reshape(blk_count, head_count, tokens, pair_width),
            query_grad=query_grad,
            joint=opened.joint,
            normed=opened.normed,
            x_all=opened.x_all,
            small_grad=went.small_grad,
            out_parts=went.out_parts,
            output_terms=went.output_terms,
            small=opened.small,
            middle_grad=went.middle_grad,
            mixture=went.mixture,
        ),
        dict(
            input_grad=shape((tokens, width), jnp.float32),
            layer_out=shape((tokens, width)),
            joint_out=shape((head_count, PAD, joint_width)),
            output_grad=shape((weight_rows, width), jnp.float32),
            small_total=shape((weight_rows, 128), jnp.float32),
            gain_total=shape((8, 128), jnp.float32),
        ),
        dict(
            theirs_pairs=vmem(head_count, half, tokens, pair_width),
            arrived_pairs=vmem(head_count, half - 1, tokens, pair_width),
            theirs_output=vmem(half, head_count * weight_rows, width),
            arrived_output=vmem(half - 1, head_count * weight_rows, width),
            output_sums=vmem(head_count, 16, packed),
            output_in=vmem(head_count, 16, packed),
            small_terms=vmem_wide(blk_count, head_count * weight_rows, 128),
            theirs_small=vmem_wide(half, head_count * weight_rows, 128),
            arrived_small=vmem_wide(half - 1, head_count * weight_rows, 128),
            joint_terms=vmem(blk_count, head_count * weight_rows, joint_width),
            theirs_joint=vmem(half, head_count * weight_rows, joint_width),
            arrived_joint=vmem(half - 1, head_count * weight_rows, joint_width),
            gain_terms=vmem_wide(blk_count, 8, 128),
            theirs_gain=vmem_wide(half, 8, 128),
            arrived_gain=vmem_wide(half - 1, 8, 128),
            row_parts=vmem(head_count, tokens, width),
            rows_in=vmem(2, head_count, tokens, width),
            out_sums=vmem(head_count, tokens, width),
            out_in=vmem(2, head_count, tokens, width),
            joint_sums=vmem(head_count, PAD, joint_width),
            small_sums=vmem_wide(head_count, weight_rows, 128),
            small_in=vmem_wide(head_count, weight_rows, 128),
            gain_sums=vmem_wide(head_count, 8, 128),
            gain_in=vmem_wide(head_count, 8, 128),
            turned=vmem(width, column_rows),
            grads=vmem(column_rows, pair_width),
            early_rows=vmem_wide(column_rows, width),
            sent_out=dma(head_count),
            got_out=dma(2, head_count),
            sent_twin=dma(folds, half),
            got_twin=dma(folds, half),
            sent_blk=dma(folds, half - 1),
            got_blk=dma(folds, half - 1),
            sent_rows=dma(head_count),
            got_rows=dma(2, head_count),
            sent_last=dma(4, others),
            got_last=dma(4, others),
        ),
        2,
    )
    wide_shape = part(shape, dtype=jnp.float32)
    (
        gate_grad,
        up_grad,
        down_grad,
        joint_grad,
        value_grad,
        gain_one_grad,
        gain_two_grad,
        router_grad,
        mix_grad,
        vector_grad,
        output_grad,
        input_grad,
        layer_out,
        residual_grad,
    ) = compute(
        part(finish, sizes),
        [
            wide_shape(gate_weight.shape),
            wide_shape(up_weight.shape),
            wide_shape(gate_weight.shape),
            wide_shape(query_key_weight.shape),
            wide_shape(value_weight.shape),
            wide_shape((1, weight_rows)),
            wide_shape((1, weight_rows)),
            wide_shape((ROUTED, weight_rows)),
            wide_shape((4, weight_rows)),
            wide_shape((2, weight_rows)),
            wide_shape(output_weight.shape),
            wide_shape((tokens, width)),
            shape((tokens, width)),
            wide_shape((ROUTED, tokens)),
        ],
        grad_pieces
        + [
            went.down_in,
            closed.joint_out,
            closed.small_total,
            closed.gain_total,
            closed.output_grad,
            closed.input_grad,
            closed.layer_out,
            went.residual_grad,
        ],
    )
    return (
        layer_out,
        input_grad,
        residual_grad.T,
        gain_one_grad[0],
        gain_two_grad[0],
        joint_grad,
        value_grad,
        output_grad,
        router_grad.T,
        mix_grad.T,
        vector_grad.T,
        gate_grad,
        up_grad,
        down_grad.T,
    )


def solution(mesh):
    body = fast_shards if mesh.shape["blk"] == EXPERTS else shards
    in_specs = (
        P(("head", "blk"), None),
        P(("head", "blk"), None),
        P(("head", "blk")),
        P(("head", "blk")),
        P(("head", "blk"), None),
        P(("head", "blk"), None),
        P(("head", "blk")),
        P(("head", "blk")),
        P(("head", "blk"), None),
        P(("head", "blk"), None),
        P(("head", "blk"), None),
        P(("head", "blk"), None),
        P(("head", "blk"), None),
        P(("head", "blk"), None),
        P("head", "blk"),
        P("head", "blk"),
        P("blk", "head"),
    )
    out_specs = (
        P(("head", "blk"), None),
        P(("head", "blk"), None),
        P(("head", "blk"), None),
        P(("head", "blk")),
        P(("head", "blk")),
        P(("head", "blk"), None),
        P(("head", "blk"), None),
        P(("head", "blk"), None),
        P(("head", "blk"), None),
        P(("head", "blk"), None),
        P(("head", "blk"), None),
        P("head", "blk"),
        P("head", "blk"),
        P("blk", "head"),
    )
    return jax.shard_map(body, mesh=mesh, in_specs=in_specs, out_specs=out_specs, check_vma=False)
```
